32 devices in a mesh: dp: 4 (over x, core), ctx: 2 (over y), tp: 4 (over z).
Axes of the slice: x: 2, y: 2, z: 4, core: 2. Of those that a mesh axis runs over, the one named last changes fastest.
Arguments:
- block_in: bfloat16 [8, 1024, 2048], P('dp', 'ctx', 'tp'), may hold values from -6 to 6
- doc_starts: int32 [8, 3], P('dp'), may hold values from 0 to 1023, as said below
- query_weight: bfloat16 [2048, 2048], P('dp', 'tp'), may hold values from -0.125 to 0.125
- key_weight: bfloat16 [2048, 2048], P('dp', 'tp'), may hold values from -0.125 to 0.125
- value_weight: bfloat16 [2048, 2048], P('dp', 'tp'), may hold values from -0.125 to 0.125
- output_weight: bfloat16 [2048, 2048], P('tp', 'dp'), may hold values from -0.5 to 0.5
- up_weight: bfloat16 [2048, 8192], P('dp', 'tp'), may hold values from -0.125 to 0.125
- down_weight: bfloat16 [8192, 2048], P('tp', 'dp'), may hold values from -0.0625 to 0.0625
- query_bias: bfloat16 [2048], P(('tp', 'dp')), may hold values from -3 to 3
- key_bias: bfloat16 [2048], P(('tp', 'dp')), may hold values from -3 to 3
- value_bias: bfloat16 [2048], P(('tp', 'dp')), may hold values from -3 to 3
- up_bias: bfloat16 [8192], P(('tp', 'dp')), may hold values from -3 to 3
- output_bias: bfloat16 [2048], P(('tp', 'dp')), may hold values from -3 to 3
- norm_gain: bfloat16 [2048], P(('tp', 'dp')), may hold values from 0.2 to 4.2
- norm_shift: bfloat16 [2048], P(('tp', 'dp')), may hold values from -3 to 3
- cotangent: bfloat16 [8, 1024, 2048], P('dp', 'ctx', 'tp'), may hold values from -6 to 6
Outputs:
- block_out: bfloat16 [8, 1024, 2048], P('dp', 'ctx', 'tp')
- in_grad: float32 [8, 1024, 2048], P('dp', 'ctx', 'tp')
- query_weight_grad: float32 [2048, 2048], P('dp', 'tp')
- key_weight_grad: float32 [2048, 2048], P('dp', 'tp')
- value_weight_grad: float32 [2048, 2048], P('dp', 'tp')
- output_weight_grad: float32 [2048, 2048], P('tp', 'dp')
- up_weight_grad: float32 [2048, 8192], P('dp', 'tp')
- down_weight_grad: float32 [8192, 2048], P('tp', 'dp')
- query_bias_grad: float32 [2048], P(('tp', 'dp'))
- key_bias_grad: float32 [2048], P(('tp', 'dp'))
- value_bias_grad: float32 [2048], P(('tp', 'dp'))
- up_bias_grad: float32 [8192], P(('tp', 'dp'))
- output_bias_grad: float32 [2048], P(('tp', 'dp'))
- gain_grad: float32 [2048], P(('tp', 'dp'))
- shift_grad: float32 [2048], P(('tp', 'dp'))
The draws below stay inside these ranges and needn't reach their ends.
Inputs may be any that keep to these rules, and one draw needn't show every extreme that they name: `doc_starts`: each sequence has 3 ascending starts: the first is 0, the second lies among the first 512 tokens, the third among the last 512 tokens, so the middle document reaches from the first index of ctx to the last.
All inputs are finite; a program needn't handle non-finite values.
Results may differ from the reference program's by a relative error of at most 0.025.
Values may be sent and summed in bfloat16 or wider, within the bound.
No kernel may reach another device: no remote copies, remote signals or barrier semaphores. Data moves between devices by JAX's collectives and lax.ppermute only.
A program may use at most 256 MiB of HBM per device.

```python
import math
import jax
import jax.numpy as jnp
from jax import lax

HEADS = 32
HEAD_DIM = 64
ROT = 32
FF = 8192
D = 2048
SEQ_DEV = 512
SEQS_ALL = 8
LEN = 1024


def draw_doc_starts(key, part):
    key = jax.random.fold_in(key, 11)
    key_second, key_third, key_chosen = jax.random.split(key, 3)
    second = jax.random.randint(key_second, (SEQS_ALL,), 1, SEQ_DEV)
    third_start = jax.random.randint(key_third, (SEQS_ALL,), LEN - SEQ_DEV + 1, LEN)
    chosen = jax.random.randint(key_chosen, (), 0, SEQS_ALL)
    third_start = jnp.where(jnp.arange(SEQS_ALL) == chosen, LEN - 1, third_start)
    opening = jnp.zeros((SEQS_ALL,), jnp.int32)
    return jnp.stack([opening, second.astype(jnp.int32), third_start.astype(jnp.int32)], axis=1).astype(jnp.int32)


def gain_ramp(key, lowest, highest_value):
    fraction = jnp.arange(D, dtype=jnp.float32) / (D - 1)
    ramp = lowest * jnp.exp(fraction * jnp.log(highest_value / lowest))
    jitter = jax.random.uniform(key, (D,), jnp.float32, 0.8, 1.2)
    return ramp * jitter


def draw_norm_gain(key, part):
    key = jax.random.fold_in(key, 23)
    gains = gain_ramp(key, 0.3, 3.0)
    return gains.astype(jnp.bfloat16)


def levels(own_key, extent, cuts, least, top_value):
    loudness = 1.0
    for position, parts in cuts:
        heights = jax.random.uniform(jax.random.fold_in(jax.random.fold_in(own_key, 6), position), (parts,), jnp.float32, least / len(cuts), top_value / len(cuts))
        loudness = loudness * jnp.repeat(jnp.exp(heights), extent[position] // parts).reshape((-1,) + (1,) * (len(extent) - 1 - position))
    return loudness


def gaussian(rng, shape, deviation, most, cuts=(), kind=jnp.bfloat16):
    factor_of = levels(rng, shape, cuts, -0.22, 0.18) if cuts else 1.0
    drawn = jax.random.normal(rng, shape, jnp.float32) * deviation * factor_of
    return jnp.minimum(jnp.maximum(drawn, -most), most).astype(kind)


def setup_inputs(seed: int = 0) -> dict:
    streams_of = jax.random.split(jax.random.key(seed), 17)
    return {
        "block_in": gaussian(streams_of[0], (SEQS_ALL, LEN, D), 1.0, 6.0, ((0, 4), (1, 2), (2, 4))),
        "doc_starts": draw_doc_starts(jax.random.fold_in(streams_of[16], 71), 0),
        "query_weight": gaussian(streams_of[2], (D, D), D ** -0.5, 0.125, ((0, 4), (1, 4))),
        "key_weight": gaussian(streams_of[3], (D, D), D ** -0.5, 0.125, ((0, 4), (1, 4))),
        "value_weight": gaussian(streams_of[4], (D, D), D ** -0.5, 0.125, ((0, 4), (1, 4))),
        "output_weight": gaussian(streams_of[5], (D, D), (D // 16) ** -0.5, 0.5, ((0, 4), (1, 4))),
        "up_weight": gaussian(streams_of[6], (D, FF), D ** -0.5, 0.125, ((0, 4), (1, 4))),
        "down_weight": gaussian(streams_of[7], (FF, D), FF ** -0.5, 0.0625, ((0, 4), (1, 4))),
        "query_bias": gaussian(streams_of[8], (D,), 0.5, 3.0, ((0, 16),)),
        "key_bias": gaussian(streams_of[9], (D,), 0.5, 3.0, ((0, 16),)),
        "value_bias": gaussian(streams_of[10], (D,), 0.5, 3.0, ((0, 16),)),
        "up_bias": gaussian(streams_of[11], (FF,), 0.5, 3.0, ((0, 16),)),
        "output_bias": gaussian(streams_of[12], (D,), 0.5, 3.0, ((0, 16),)),
        "norm_gain": draw_norm_gain(jax.random.fold_in(streams_of[16], 71), 0),
        "norm_shift": gaussian(streams_of[14], (D,), 0.5, 3.0, ((0, 16),)),
        "cotangent": gaussian(streams_of[15], (SEQS_ALL, LEN, D), 1.0, 6.0, ((0, 4), (1, 2), (2, 4))),
    }


@jax.custom_vjp
def low(v):
    return lax.optimization_barrier(v.astype(jnp.bfloat16)).astype(jnp.float32)

@jax.custom_vjp
def low_back(v):
    return v

def low_keep(v):
    return (low(v), None)

def low_pass(kept, grad):
    return (grad,)

def back_keep(v):
    return (v, None)

def back_low(kept, grad):
    return (low(grad),)
low.defvjp(low_keep, low_pass)
low_back.defvjp(back_keep, back_low)
epsilon = 1e-05
masked_score = -1e+30
highest = lax.Precision.HIGHEST

def product(left_side, right_side):
    return jnp.dot(left_side, right_side, precision=highest, preferred_element_type=jnp.float32)

def gelu_tanh(values):
    inner = math.sqrt(2.0 / math.pi) * (values + 0.044715 * values * values * values)
    return 0.5 * values * (1.0 + jnp.tanh(inner))

def rotate(values, cosine_table, sine_table):
    halfway = ROT // 2
    first_half = values[..., :halfway]
    second_half = values[..., halfway:ROT]
    cosine_part = cosine_table[:, None, :]
    sine_part = sine_table[:, None, :]
    return jnp.concatenate([first_half * cosine_part - second_half * sine_part, second_half * cosine_part + first_half * sine_part, values[..., ROT:]], axis=-1)

def attend(queries, keys_rot, values_heads, positions, document_ids):
    block_rows = math.gcd(LEN, 512)
    score_scale = HEAD_DIM ** (-0.5)

    def one_block(block_index):
        offset = block_index * block_rows
        query_block = lax.dynamic_slice_in_dim(queries, offset, block_rows, 0)
        query_positions = lax.dynamic_slice_in_dim(positions, offset, block_rows, 0)
        query_documents = lax.dynamic_slice_in_dim(document_ids, offset, block_rows, 0)
        raw_scores = jnp.einsum('qhd,khd->hqk', query_block, keys_rot, precision=highest) * score_scale
        scores = low_back(raw_scores)
        allowed = (query_documents[:, None] == document_ids[None, :]) & (positions[None, :] <= query_positions[:, None])
        scores = jnp.where(allowed[None], scores, masked_score)
        row_peak = lax.optimization_barrier(jnp.max(scores, axis=2, keepdims=True))
        expo_terms = jnp.exp(scores - row_peak)
        soft_weights = expo_terms / lax.optimization_barrier(jnp.sum(expo_terms, axis=2, keepdims=True))
        return jnp.einsum('hqk,khd->qhd', low(soft_weights), values_heads, precision=highest)
    blocks = lax.map(jax.checkpoint(one_block), jnp.arange(LEN // block_rows, dtype=jnp.int32))
    return blocks.reshape(LEN, HEADS * HEAD_DIM)

def forward(inputs, starts, params):
    query_weight, key_weight, value_weight, output_weight, up_weight, down_weight, query_bias, key_bias, value_bias, up_bias, output_bias, norm_gain, norm_shift = params
    positions = jnp.arange(LEN, dtype=jnp.int32)
    before = starts[None, :] <= positions[:, None]
    document_ids = lax.optimization_barrier(jnp.sum(before.astype(jnp.int32), axis=1))
    opening = lax.optimization_barrier(jnp.max(jnp.where(before, starts[None, :], 0), axis=1))
    relative = (positions - opening).astype(jnp.float32)
    halfway = ROT // 2
    frequency = jnp.exp(jnp.arange(halfway, dtype=jnp.float32) * (-math.log(10000.0) / halfway))
    angles = relative[:, None] * frequency[None, :]
    cosine_table = jnp.cos(angles)
    sine_table = jnp.sin(angles)
    average = lax.optimization_barrier(jnp.mean(inputs, axis=1, keepdims=True))
    centred = inputs - average
    variance = lax.optimization_barrier(jnp.mean(centred * centred, axis=1, keepdims=True))
    standard = centred * lax.rsqrt(variance + epsilon)
    normed = low(standard * norm_gain + norm_shift)

    def heads_of(values):
        return values.reshape(LEN, HEADS, HEAD_DIM)
    queries = low(rotate(heads_of(low_back(product(normed, query_weight) + query_bias)), cosine_table, sine_table))
    keys_rot = low(rotate(heads_of(low_back(product(normed, key_weight) + key_bias)), cosine_table, sine_table))
    values_heads = heads_of(low(low_back(product(normed, value_weight) + value_bias)))
    attention = low(low_back(attend(queries, keys_rot, values_heads, positions, document_ids)))
    hidden = low(gelu_tanh(low_back(product(normed, up_weight) + up_bias)))
    return inputs + product(attention, output_weight) + product(hidden, down_weight) + output_bias

def reference(block_in, doc_starts, query_weight, key_weight, value_weight, output_weight, up_weight, down_weight, query_bias, key_bias, value_bias, up_bias, output_bias, norm_gain, norm_shift, cotangent):
    params = tuple((weight.astype(jnp.float32) for weight in (query_weight, key_weight, value_weight, output_weight, up_weight, down_weight, query_bias, key_bias, value_bias, up_bias, output_bias, norm_gain, norm_shift)))
    zeroes = tuple((jnp.zeros_like(weight) for weight in params))

    def one_sequence(summed_grads, sequence):
        inputs, starts, seq_cotangent = sequence

        def apply_block(block_input, block_params):
            return forward(block_input, starts, block_params)
        result, pullback = jax.vjp(apply_block, inputs, params)
        input_grad, param_grads = pullback(seq_cotangent)
        summed_grads = jax.tree.map(lambda former, latter: former + latter, summed_grads, param_grads)
        return (summed_grads, (result.astype(jnp.bfloat16), input_grad))
    summed_grads, (block_out, in_grad) = lax.scan(one_sequence, zeroes, (block_in.astype(jnp.float32), doc_starts, cotangent.astype(jnp.float32)))
    return (block_out, in_grad, summed_grads[0], summed_grads[1], summed_grads[2], summed_grads[3], summed_grads[4], summed_grads[5], summed_grads[6], summed_grads[7], summed_grads[8], summed_grads[9], summed_grads[10], summed_grads[11], summed_grads[12])
```

```python
import functools
import math

import jax
import jax.numpy as jnp
from jax import lax
from jax.experimental import pallas as pl
from jax.experimental.pallas import tpu as pltpu
from jax.sharding import PartitionSpec as P

HEAD_DIM = 64
ROT = 32
D = 2048
N_DP = 4
N_TP = 4
CH = D // N_TP
EPS = 1e-05
NEG = -1e30
VMEM = 56 * 2**20

bf16 = jnp.bfloat16
f32 = jnp.float32


def dot_nn(a, b):
    return lax.dot_general(a, b, (((1,), (0,)), ((), ())), preferred_element_type=f32)


def dot_nt(a, b):
    return lax.dot_general(a, b, (((1,), (1,)), ((), ())), preferred_element_type=f32)


def dot_tn(a, b):
    return lax.dot_general(a, b, (((0,), (0,)), ((), ())), preferred_element_type=f32)


def spec(block, index):
    return pl.BlockSpec(block, index)


def whole(*block):
    zeros = (0,) * len(block)
    return pl.BlockSpec(block, lambda g, *_: zeros)


def shaped(shape, dtype=bf16):
    return jax.ShapeDtypeStruct(tuple(shape), dtype)


def call(body, name, grid, info, ins, in_specs, outs, out_specs, flops, scratch=()):
    moved = sum(math.prod(a.shape) * a.dtype.itemsize for a in (*ins, *outs))
    return pl.pallas_call(
        body,
        grid_spec=pltpu.PrefetchScalarGridSpec(
            num_scalar_prefetch=1,
            grid=(grid,),
            in_specs=in_specs,
            out_specs=out_specs,
            scratch_shapes=list(scratch),
        ),
        out_shape=outs,
        compiler_params=pltpu.CompilerParams(vmem_limit_bytes=VMEM),
        cost_estimate=pl.CostEstimate(
            flops=int(flops), bytes_accessed=int(moved), transcendentals=0
        ),
        name=name,
    )(info, *ins)


def columns(index, width=CH):
    return pl.ds(pl.multiple_of(index * width, width), width)


def place(pieces, axis, shape, name):
    starts = jnp.stack([jnp.asarray(at, jnp.int32) for _, at in pieces])
    arrays = [a for a, _ in pieces]

    def body(at_ref, *refs):
        *sources, out, sems = refs
        copies = []
        for n, source in enumerate(sources):
            size = arrays[n].shape[axis]
            window = pl.ds(pl.multiple_of(at_ref[n], 256), size)
            target = out.at[window, :] if axis == 0 else out.at[:, window]
            copies.append(pltpu.make_async_copy(source, target, sems.at[n]))
        for copy in copies:
            copy.start()
        for copy in copies:
            copy.wait()

    anywhere = pl.BlockSpec(memory_space=pl.ANY)
    return pl.pallas_call(
        body,
        grid_spec=pltpu.PrefetchScalarGridSpec(
            num_scalar_prefetch=1,
            grid=(1,),
            in_specs=[anywhere] * len(arrays),
            out_specs=anywhere,
            scratch_shapes=[pltpu.SemaphoreType.DMA((len(arrays),))],
        ),
        out_shape=shaped(shape),
        compiler_params=pltpu.CompilerParams(vmem_limit_bytes=VMEM),
        cost_estimate=pl.CostEstimate(
            flops=0, bytes_accessed=4 * math.prod(shape), transcendentals=0
        ),
        name=name,
    )(starts, *arrays)


def swap(array, axis, bit, size):
    return lax.ppermute(array, axis, [(i, i ^ bit) for i in range(size)])


def gather_shards(own, axis, d, c, two, name):
    size = own.shape[axis]
    shape = list(own.shape)
    shape[axis] = size * N_DP
    if two:
        half = size // 2
        mine = lax.dynamic_slice_in_dim(own, c * half, half, axis)
        first = swap(mine, "dp", 2, N_DP)
        second = swap(first, "ctx", 1, 2)
        near = swap(own, "dp", 1, N_DP)
        far = [(first, c * half), (second, (1 - c) * half)]
        pieces = [(own, d * size), (near, (d ^ 1) * size)]
        pieces += [(a, (d ^ 2) * size + at) for a, at in far]
        pieces += [(swap(a, "dp", 1, N_DP), (d ^ 3) * size + at) for a, at in far]
    else:
        near = swap(own, "dp", 1, N_DP)
        across = swap(own, "dp", 2, N_DP)
        pieces = [
            (own, d * size),
            (near, (d ^ 1) * size),
            (across, (d ^ 2) * size),
            (swap(across, "dp", 1, N_DP), (d ^ 3) * size),
        ]
    return place(pieces, axis, shape, name)


def rotary_tables(starts, positions):
    before = starts[:, None, :] <= positions[None, :, None]
    opening = jnp.max(jnp.where(before, starts[:, None, :], 0), axis=2)
    relative = (positions[None, :] - opening).astype(f32)
    half = ROT // 2
    frequency = jnp.exp(jnp.arange(half, dtype=f32) * (-math.log(10000.0) / half))
    angles = relative[:, :, None] * frequency
    cosine, sine = jnp.cos(angles), jnp.sin(angles)
    ones = jnp.ones(cosine.shape[:2] + (HEAD_DIM - ROT,), f32)
    none = jnp.zeros_like(ones)
    gap = jnp.zeros_like(sine)

    def lanes(*parts):
        return jnp.concatenate(parts * 2, axis=2)

    return (
        lanes(cosine, cosine, ones),
        lanes(-sine, gap, none),
        lanes(gap, sine, none),
    ), opening


def turn(x, own, up, down):
    return x * own + pltpu.roll(x, 112, 1) * up + pltpu.roll(x, 16, 1) * down


def turn_back(x, own, up, down):
    return x * own - pltpu.roll(x, 112, 1) * up - pltpu.roll(x, 16, 1) * down


def norm_qkv_body(
    info, x0, xa, xc, xb, gain, shift, w, bias, own, up, down, xf, normed, avg, inv, q, kv
):
    j = pl.program_id(0)
    t = info[0]
    rows = x0.shape[0]

    @pl.when(j == 0)
    def _():
        for part, step in ((x0, 0), (xa, 3), (xc, 1), (xb, 2)):
            xf[:, columns((t + step) % N_TP)] = part[...]

        tile = 128

        def rows_of(i, carry):
            window = pl.ds(pl.multiple_of(i * tile, tile), tile)
            x = xf[window, :].astype(f32)
            average = jnp.sum(x, axis=1, keepdims=True) * (1.0 / D)
            centred = x - average
            variance = jnp.sum(centred * centred, axis=1, keepdims=True) * (1.0 / D)
            root = lax.rsqrt(variance + EPS)
            avg[window, :] = average
            inv[window, :] = root
            normed[window, :] = (
                centred * root * gain[...].astype(f32) + shift[...].astype(f32)
            ).astype(bf16)
            return carry

        lax.fori_loop(0, rows // tile, rows_of, 0)

    y = dot_nn(normed[...], w[...]) + bias[...].astype(f32)

    def rotated():
        parts = [
            turn(y[:, 128 * n : 128 * n + 128], own[...], up[...], down[...])
            for n in range(CH // 128)
        ]
        return jnp.concatenate(parts, axis=1).astype(bf16)

    @pl.when(j == 0)
    def _():
        q[...] = rotated()

    @pl.when(j == 1)
    def _():
        kv[0] = rotated()

    @pl.when(j == 2)
    def _():
        kv[0] = y.astype(bf16)


def norm_qkv(info, parts, gain, shift, w, bias, tables):
    rows = parts[0].shape[0]
    outs = (
        shaped((rows, D)),
        shaped((rows, D)),
        shaped((rows, 1), f32),
        shaped((rows, 1), f32),
        shaped((rows, CH)),
        shaped((2, rows, CH)),
    )
    return call(
        norm_qkv_body,
        "norm_qkv",
        3,
        info,
        (*parts, gain, shift, w, bias, *tables),
        [whole(rows, CH)] * 4
        + [whole(1, D)] * 2
        + [spec((D, CH), lambda j, *_: (0, j)), spec((1, CH), lambda j, *_: (0, j))]
        + [whole(rows, 128)] * 3,
        outs,
        [
            whole(rows, D),
            whole(rows, D),
            whole(rows, 1),
            whole(rows, 1),
            whole(rows, CH),
            spec((1, rows, CH), lambda j, *_: (jnp.maximum(j - 1, 0), 0, 0)),
        ],
        2 * rows * D * 3 * CH,
    )


def mlp_up_body(info, n0, n1, w, bias, h0, h1, g0, g1):
    root = math.sqrt(2.0 / math.pi)
    for n, h, g in ((n0, h0, g0), (n1, h1, g1)):
        u = dot_nn(n[...], w[...]) + bias[...].astype(f32)
        square = u * u
        t = jnp.tanh(root * u * (1.0 + 0.044715 * square))
        h[...] = (0.5 * u * (1.0 + t)).astype(bf16)
        slope = root * (1.0 + 3 * 0.044715 * square)
        g[...] = (0.5 * (1.0 + t) + 0.5 * u * (1.0 - t * t) * slope).astype(bf16)


def mlp_up(info, normed, w, bias):
    rows, units = normed[0].shape[0], w.shape[1]
    block = spec((rows, CH), lambda j, *_: (0, j))
    return call(
        mlp_up_body,
        "mlp_up",
        units // CH,
        info,
        (*normed, w, bias),
        [whole(rows, D)] * 2
        + [spec((D, CH), lambda j, *_: (0, j)), spec((1, CH), lambda j, *_: (0, j))],
        (shaped((rows, units)),) * 4,
        [block] * 4,
        4 * rows * D * units,
    )


def back_out_body(info, c0, ca, cc, cb, w, slope, cf, bias_grad, datt, dup):
    j = pl.program_id(0)
    t = info[0]

    @pl.when(j == 0)
    def _():
        for part, step in ((c0, 0), (ca, 3), (cc, 1), (cb, 2)):
            cf[:, columns((t + step) % N_TP)] = part[...]
        bias_grad[...] = jnp.sum(c0[...].astype(f32), axis=0, keepdims=True)

    y = dot_nt(cf[...], w[...])

    @pl.when(j == 0)
    def _():
        datt[...] = y.astype(bf16)

    @pl.when(j > 0)
    def _():
        dup[...] = (y * slope[...].astype(f32)).astype(bf16)


def back_out(info, parts, w, slope):
    rows, units = slope.shape
    later = spec((rows, CH), lambda j, *_: (0, jnp.maximum(j - 1, 0)))
    return call(
        back_out_body,
        "back_out",
        w.shape[0] // CH,
        info,
        (*parts, w, slope),
        [whole(rows, CH)] * 4 + [spec((CH, D), lambda j, *_: (j, 0)), later],
        (
            shaped((rows, D)),
            shaped((1, CH), f32),
            shaped((rows, CH)),
            shaped((rows, units)),
        ),
        [whole(rows, D), whole(1, CH), whole(rows, CH), later],
        2 * rows * D * w.shape[0],
    )


def attention_body(
    blocks, info, low, q, kv, kvp, do, own, up, down, ownp, upp, downp,
    att, dq, dkv, dkvp, scores, probs,
):
    rows = q.shape[0]
    before, start = info[1], info[1] * rows
    lane = lax.broadcasted_iota(jnp.int32, (rows, 128), 1)
    key_row = lax.broadcasted_iota(jnp.int32, (rows, 1), 0)
    query_at = start + lax.broadcasted_iota(jnp.int32, (1, rows), 1)
    first = low[0]
    do_t = do[...].astype(f32).T
    nothing = jnp.zeros((), bf16)
    outputs = []
    for head in range(2):
        mine = (lane < HEAD_DIM) if head == 0 else (lane >= HEAD_DIM)
        half = slice(HEAD_DIM * head, HEAD_DIM * (head + 1))
        qh = jnp.where(mine, q[...] * jnp.asarray(HEAD_DIM**-0.5, bf16), nothing)
        dh = jnp.where(mine, do[...], nothing)

        key_at = start + key_row
        s = dot_nt(kv[0], qh)
        s = jnp.where((key_at >= first) & (key_at <= query_at), s, NEG)
        scores[blocks] = s
        peak = jnp.max(s, axis=0, keepdims=True)

        def score(n, peak):
            s = dot_nt(kvp[n, 0], qh)
            s = jnp.where(n * rows + key_row >= first, s, NEG)
            scores[n] = s
            return jnp.maximum(peak, jnp.max(s, axis=0, keepdims=True))

        peak = lax.fori_loop(0, before, score, peak)

        def expo(n, total):
            e = jnp.exp(scores[n] - peak)
            scores[n] = e
            return total + jnp.sum(e, axis=0, keepdims=True)

        total = expo(blocks, jnp.zeros((1, rows), f32))
        total = lax.fori_loop(0, before, expo, total)
        scale = 1.0 / total

        def weigh(n, values):
            p = (scores[n] * scale).astype(bf16)
            probs[n] = p
            return dot_tn(values, p)

        out_t = weigh(blocks, kv[1])
        out_t = lax.fori_loop(0, before, lambda n, acc: acc + weigh(n, kvp[n, 1]), out_t)
        delta = jnp.sum(out_t[half] * do_t[half], axis=0, keepdims=True)

        def back(n, keys, values):
            dp = dot_nt(values, dh)
            ds = ((scores[n] * scale) * (dp - delta)).astype(bf16)
            return dot_nn(ds, qh), dot_nn(probs[n], dh), dot_tn(keys, ds)

        dk, dv, dq_t = back(blocks, kv[0], kv[1])
        if head == 0:
            dk_sum, dv_sum = dk, dv
        else:
            dk_sum, dv_sum = dk_sum + dk, dv_sum + dv

        def back_before(n, acc):
            dk, dv, more = back(n, kvp[n, 0], kvp[n, 1])
            dk = turn_back(dk, ownp[n], upp[n], downp[n])
            if head == 0:
                dkvp[n, 0] = dk.astype(bf16)
                dkvp[n, 1] = dv.astype(bf16)
            else:
                dkvp[n, 0] = (dkvp[n, 0].astype(f32) + dk).astype(bf16)
                dkvp[n, 1] = (dkvp[n, 1].astype(f32) + dv).astype(bf16)
            return acc + more

        dq_t = lax.fori_loop(0, before, back_before, dq_t)
        outputs.append((out_t[half], dq_t[half]))

    def clear(n, carry):
        dkvp[n] = jnp.zeros(dkvp.shape[1:], bf16)
        return carry

    lax.fori_loop(before, blocks, clear, 0)
    att[...] = jnp.concatenate([outputs[0][0], outputs[1][0]], axis=0).T.astype(bf16)
    grad = jnp.concatenate([outputs[0][1], outputs[1][1]], axis=0).T * HEAD_DIM**-0.5
    dq[...] = turn_back(grad, own[...], up[...], down[...]).astype(bf16)
    dkv[0] = turn_back(dk_sum, own[...], up[...], down[...]).astype(bf16)
    dkv[1] = dv_sum.astype(bf16)


def attention(info, low, q, kv, kvp, do, tables, tables_before):
    rows, width = q.shape
    blocks = kvp.shape[0]
    token = spec((rows, 128), lambda g, *_: (0, g))
    pair = spec((2, rows, 128), lambda g, *_: (0, 0, g))
    pairs = spec((blocks, 2, rows, 128), lambda g, *_: (0, 0, 0, g))
    return call(
        functools.partial(attention_body, blocks),
        "attention",
        width // 128,
        info,
        (low, q, kv, kvp, do, *tables, *tables_before),
        [whole(1, rows), token, pair, pairs, token]
        + [whole(rows, 128)] * 3
        + [whole(blocks, rows, 128)] * 3,
        (
            shaped((rows, width)),
            shaped((rows, width)),
            shaped((2, rows, width)),
            shaped((blocks, 2, rows, width)),
        ),
        [token, token, pair, pairs],
        48 * rows * rows * width,
        [
            pltpu.VMEM((blocks + 1, rows, rows), f32),
            pltpu.VMEM((blocks + 1, rows, rows), bf16),
        ],
    )


ORDER = (2, 3, 1, 0)


def relative(step):
    return jnp.where(step < 2, step + 2, 3 - step)


def out_body(info, att, hidden, w, *outs):
    j = pl.program_id(0)
    y = dot_nn(att[...], w[:CH, :]) + dot_nn(hidden[...], w[CH:, :])
    y = y.astype(bf16)
    for step, r in enumerate(ORDER):

        @pl.when(j == step)
        def _(r=r):
            outs[r][...] = y


def project_out(info, att, hidden, w):
    rows, units = hidden.shape
    return call(
        out_body,
        "project_out",
        N_TP,
        info,
        (att, hidden, w),
        [
            whole(rows, CH),
            whole(rows, units),
            spec((CH + units, CH), lambda j, info: (0, (info[0] + relative(j)) % N_TP)),
        ],
        (shaped((rows, CH)),) * N_TP,
        [whole(rows, CH)] * N_TP,
        2 * rows * D * (CH + units),
    )


def back_in_body(info, dq, dkv, dup, wq, wu, xf, gain, avg, inv, *outs):
    j = pl.program_id(0)
    *chunks, row_sums, column_sums = outs
    y = dot_nt(dup[...], wu[...])
    y = y + dot_nt(dq[...], wq[:, :CH])
    y = y + dot_nt(dkv[0], wq[:, CH : 2 * CH])
    y = y + dot_nt(dkv[1], wq[:, 2 * CH :])
    yb = y.astype(bf16)
    for step, r in enumerate(ORDER):

        @pl.when(j == step)
        def _(r=r):
            chunks[r][...] = yb

    standard = (xf[...].astype(f32) - avg[...]) * inv[...]
    cross = y * standard
    weight = gain[...].astype(f32)
    column_sums[0, 0:1, :] = jnp.sum(cross, axis=0, keepdims=True)
    column_sums[0, 1:2, :] = jnp.sum(y, axis=0, keepdims=True)
    plain_row = jnp.sum(y * weight, axis=1, keepdims=True)
    cross_row = jnp.sum(cross * weight, axis=1, keepdims=True)

    @pl.when(j == 0)
    def _():
        row_sums[:, 0:1] = plain_row
        row_sums[:, 1:2] = cross_row

    @pl.when(j > 0)
    def _():
        row_sums[:, 0:1] += plain_row
        row_sums[:, 1:2] += cross_row


def back_in(info, dq, dkv, dup, wq, wu, xf, gain, avg, inv):
    rows, units = dup.shape

    def chunk(j, info):
        return (info[0] + relative(j)) % N_TP

    return call(
        back_in_body,
        "back_in",
        N_TP,
        info,
        (dq, dkv, dup, wq, wu, xf, gain, avg, inv),
        [
            whole(rows, CH),
            whole(2, rows, CH),
            whole(rows, units),
            spec((CH, 3 * CH), lambda j, info: (chunk(j, info), 0)),
            spec((CH, units), lambda j, info: (chunk(j, info), 0)),
            spec((rows, CH), lambda j, info: (0, chunk(j, info))),
            spec((1, CH), lambda j, info: (0, chunk(j, info))),
            whole(rows, 1),
            whole(rows, 1),
        ],
        (shaped((rows, CH)),) * N_TP + (shaped((rows, 2), f32), shaped((N_TP, 2, CH), f32)),
        [whole(rows, CH)] * N_TP
        + [
            whole(rows, 2),
            spec((1, 2, CH), lambda j, info: (chunk(j, info), 0, 0)),
        ],
        2 * rows * D * (3 * CH + units),
    )


KEPT = ((0, 0), (2, 1))
GIVEN = ((1, 0), (3, 1))


def grad_up_body(info, n0, n1, g0, g1, kept, given, sums):
    d = info[2]
    left, right = g0[...], g1[...]
    for target, which in ((given, GIVEN), (kept, KEPT)):
        for r, at in which:
            rows = columns(d ^ r)
            target[at, 0] = (dot_tn(n0[:, rows], left) + dot_tn(n1[:, rows], right)).astype(bf16)
    sums[...] = jnp.sum(left.astype(f32), axis=0, keepdims=True) + jnp.sum(
        right.astype(f32), axis=0, keepdims=True
    )


def grad_up(info, normed, dup):
    rows, units = dup[0].shape
    count = units // CH
    block = spec((rows, CH), lambda j, *_: (0, j))
    message = spec((2, 1, CH, CH), lambda j, *_: (0, j, 0, 0))
    return call(
        grad_up_body,
        "grad_up",
        count,
        info,
        (*normed, *dup),
        [whole(rows, D)] * 2 + [block] * 2,
        (shaped((2, count, CH, CH)),) * 2 + (shaped((1, units), f32),),
        [message, message, spec((1, CH), lambda j, *_: (0, j))],
        4 * rows * D * units,
    )


def grad_down_body(info, h0, h1, c0, c1, kept, given):
    j = pl.program_id(0)
    y = (dot_tn(h0[...], c0[...]) + dot_tn(h1[...], c1[...])).astype(bf16)

    def store(target):
        for n in range(target.shape[1]):
            target[0, n] = y[CH * n : CH * (n + 1), :]

    @pl.when(j < 2)
    def _():
        store(given)

    @pl.when(j >= 2)
    def _():
        store(kept)


def grad_down(info, hidden, ct):
    rows, units = hidden[0].shape
    count = units // CH
    block = spec(
        (rows, CH),
        lambda j, info: (0, info[2] ^ jnp.where(j < 2, 2 * j + 1, 2 * j - 4)),
    )
    return call(
        grad_down_body,
        "grad_down",
        N_DP,
        info,
        (*hidden, *ct),
        [whole(rows, units)] * 2 + [block] * 2,
        (shaped((2, count, CH, CH)),) * 2,
        [
            spec((1, count, CH, CH), lambda j, *_: (jnp.maximum(j - 2, 0), 0, 0, 0)),
            spec((1, count, CH, CH), lambda j, *_: (jnp.minimum(j, 1), 0, 0, 0)),
        ],
        4 * rows * D * units,
    )


def grad_heads_body(
    info, n0, n1, c0, c1, a0, a1, q0, q1, kv0, kv1, kept, given, sums
):
    j = pl.program_id(0)
    d = info[2]

    def store(lefts, rights, of_rows):
        for target, which in ((given, GIVEN), (kept, KEPT)):
            for r, at in which:
                window = columns(d ^ r)
                if of_rows:
                    y = sum(dot_tn(a[:, window], b) for a, b in zip(lefts, rights))
                else:
                    y = sum(dot_tn(b, a[:, window]) for a, b in zip(lefts, rights))
                target[at, 0] = y.astype(bf16)

    def add_up(rights):
        sums[0] = sum(jnp.sum(b.astype(f32), axis=0, keepdims=True) for b in rights)

    @pl.when(j == 0)
    def _():
        rights = (a0[...], a1[...])
        store((c0, c1), rights, False)
        add_up(rights)

    @pl.when(j == 1)
    def _():
        rights = (q0[...], q1[...])
        store((n0, n1), rights, True)
        add_up(rights)

    @pl.when(j > 1)
    def _():
        rights = (kv0[0], kv1[0])
        store((n0, n1), rights, True)
        add_up(rights)


def grad_heads(info, normed, ct, att, dq, dkv):
    rows = normed[0].shape[0]
    message = spec((2, 1, CH, CH), lambda j, *_: (0, j, 0, 0))
    pair = spec((1, rows, CH), lambda j, *_: (jnp.maximum(j - 2, 0), 0, 0))
    return call(
        grad_heads_body,
        "grad_heads",
        4,
        info,
        (*normed, *ct, *att, *dq, *dkv),
        [whole(rows, D)] * 4 + [whole(rows, CH)] * 4 + [pair] * 2,
        (shaped((2, 4, CH, CH)),) * 2 + (shaped((4, 1, CH), f32),),
        [message, message, spec((1, 1, CH), lambda j, *_: (j, 0, 0))],
        4 * rows * D * 4 * CH,
    )


def ring(array, step):
    return lax.ppermute(array, "tp", [(i, (i + step) % N_TP) for i in range(N_TP)])


def gather_tp(own):
    behind = ring(own, 1)
    ahead = ring(own, -1)
    return own, behind, ahead, ring(behind, 1)


def scatter_tp(chunks):
    far = ring(chunks[2], 1)
    back = ring(chunks[3], -1)
    both = (chunks[1].astype(f32) + far.astype(f32)).astype(bf16)
    near = ring(both, 1)
    return chunks[0].astype(f32) + back.astype(f32) + near.astype(f32)


def reduce_grads(kept, given, c, two):
    got = swap(given, "dp", 1, N_DP)
    across = (kept[1].astype(f32) + got[1].astype(f32)).astype(bf16)
    moved = swap(across, "dp", 2, N_DP)
    total = (kept[0].astype(f32) + got[0].astype(f32) + moved.astype(f32)).astype(bf16)
    if not two:
        return lax.psum(total, "ctx").astype(f32)
    half = total.shape[0] // 2
    mine = lax.dynamic_slice_in_dim(total, c * half, half, 0)
    theirs = lax.dynamic_slice_in_dim(total, (1 - c) * half, half, 0)
    received = swap(theirs, "ctx", 1, 2)
    mine = (mine.astype(f32) + received.astype(f32)).astype(bf16)
    other = swap(mine, "ctx", 1, 2)
    low = jnp.where(c == 0, mine, other)
    high = jnp.where(c == 0, other, mine)
    return jnp.concatenate([low, high], axis=0).astype(f32)


def body(
    block_in,
    doc_starts,
    query_weight,
    key_weight,
    value_weight,
    output_weight,
    up_weight,
    down_weight,
    query_bias,
    key_bias,
    value_bias,
    up_bias,
    output_bias,
    norm_gain,
    norm_shift,
    cotangent,
):
    seqs, rows, _ = block_in.shape
    d, c, t = lax.axis_index("dp"), lax.axis_index("ctx"), lax.axis_index("tp")
    n_ctx = lax.axis_size("ctx")
    two = n_ctx == 2
    info = jnp.stack([t, c, d]).astype(jnp.int32)

    x_parts = [gather_tp(block_in[s]) for s in range(seqs)]

    small = jnp.concatenate(
        [query_bias, key_bias, value_bias, up_bias, output_bias, norm_gain, norm_shift]
    )
    small_all = lax.all_gather(small, ("tp", "dp"), axis=0, tiled=False)
    small_all = small_all.reshape(N_TP, N_DP, -1)
    small_here = lax.dynamic_index_in_dim(small_all, t, 0, keepdims=False)
    sizes = [query_bias.size] * 3 + [up_bias.size] + [output_bias.size] * 3
    offsets = [sum(sizes[:n]) for n in range(len(sizes) + 1)]

    def small_of(table, n):
        return table[..., offsets[n] : offsets[n + 1]].reshape(1, -1)

    qkv_bias = jnp.concatenate([small_of(small_here, n) for n in range(3)], axis=1)
    up_shift = small_of(small_here, 3)
    output_shift = small_of(small_here, 4)
    gain, shift = small_of(small_all, 5), small_of(small_all, 6)
    gain_here = small_of(small_here, 5).astype(f32)

    wq = gather_shards(
        jnp.concatenate([query_weight, key_weight, value_weight], axis=1), 0, d, c, two, "place_qkv"
    )
    wu = gather_shards(up_weight, 0, d, c, two, "place_up")
    wo = gather_shards(
        jnp.concatenate([output_weight, down_weight], axis=0), 1, d, c, two, "place_out"
    )

    ct_parts = [gather_tp(cotangent[s]) for s in range(seqs)]

    here = c * rows + jnp.arange(rows, dtype=jnp.int32)
    tables, opening = rotary_tables(doc_starts, here)
    blocks = 1 if two else n_ctx
    before, _ = rotary_tables(doc_starts, jnp.arange(blocks * rows, dtype=jnp.int32))
    before = [a.reshape(seqs, blocks, rows, 128) for a in before]

    xf, normed, avg, inv, q, kv, kvp = [], [], [], [], [], [], []
    for s in range(seqs):
        one = norm_qkv(info, x_parts[s], gain, shift, wq, qkv_bias, [a[s] for a in tables])
        for target, value in zip((xf, normed, avg, inv, q, kv), one):
            target.append(value)
        if two:
            kvp.append(lax.ppermute(kv[s], "ctx", [(0, 1)])[None])
        else:
            kvp.append(lax.all_gather(kv[s], "ctx", axis=0, tiled=False))
    h0, h1, g0, g1 = mlp_up(info, normed, wu, up_shift)
    hidden, slope = (h0, h1), (g0, g1)

    cf, out_bias_sum, datt, dup = [], [], [], []
    att, dq, dkv = [], [], []
    out_sum = []
    for s in range(seqs):
        one = back_out(info, ct_parts[s], wo, slope[s])
        for target, value in zip((cf, out_bias_sum, datt, dup), one):
            target.append(value)
    up_kept, up_given, up_sum = grad_up(info, normed, dup)
    down_kept, down_given = grad_down(info, hidden, cf)
    for s in range(seqs):
        a, b, own, sent = attention(
            info,
            opening[s][None],
            q[s],
            kv[s],
            kvp[s],
            datt[s],
            [x[s] for x in tables],
            [x[s] for x in before],
        )
        att.append(a)
        dq.append(b)
        if two:
            back = lax.ppermute(sent[0], "ctx", [(1, 0)])
        else:
            back = lax.psum_scatter(sent, "ctx", scatter_dimension=0, tiled=False)
        dkv.append((own.astype(f32) + back.astype(f32)).astype(bf16))
        out_sum.append(scatter_tp(project_out(info, att[s], hidden[s], wo)))
    block_out = jnp.stack(out_sum)
    block_out = (block_in.astype(f32) + block_out + output_shift.astype(f32)).astype(bf16)

    normed_grad, row_sums, column_sums = [], [], []
    for s in range(seqs):
        *chunks, row_sum, column_sum = back_in(
            info, dq[s], dkv[s], dup[s], wq, wu, xf[s], gain, avg[s], inv[s]
        )
        normed_grad.append(scatter_tp(chunks))
        row_sums.append(row_sum)
        column_sums.append(column_sum)
    head_kept, head_given, head_sum = grad_heads(info, normed, cf, att, dq, dkv)

    up_wg = reduce_grads(up_kept, up_given, c, two)
    down_wg = reduce_grads(down_kept, down_given, c, two)
    head_wg = reduce_grads(head_kept, head_given, c, two)
    up_wg = up_wg.transpose(1, 0, 2).reshape(CH, -1)
    down_wg = down_wg.reshape(-1, CH)

    row_sums = lax.psum(jnp.stack(row_sums), "tp")
    total_plain, total_cross = row_sums[..., 0:1], row_sums[..., 1:2]
    root = jnp.stack(inv)
    standard = (block_in.astype(f32) - jnp.stack(avg)) * root
    scaled = jnp.stack(normed_grad) * gain_here
    in_grad = cotangent.astype(f32) + root * (
        scaled - total_plain / D - standard * total_cross / D
    )

    local = jnp.concatenate(
        [head_sum[1:].reshape(-1), up_sum.reshape(-1), sum(out_bias_sum).reshape(-1)]
    )
    both = sum(column_sums)
    both = lax.psum_scatter(both, "tp", scatter_dimension=0, tiled=False).reshape(-1)
    summed = lax.psum(jnp.concatenate([local, both]), ("dp", "ctx"))
    at = 0
    small_grads = []
    for size in (CH, CH, CH, up_sum.size, CH, CH, CH):
        part = summed[at : at + size]
        at += size
        share = size // N_DP
        small_grads.append(lax.dynamic_slice_in_dim(part, d * share, share, 0))
    query_bg, key_bg, value_bg, up_bg, output_bg, gain_g, shift_g = small_grads
    return (
        block_out,
        in_grad,
        head_wg[1],
        head_wg[2],
        head_wg[3],
        head_wg[0],
        up_wg,
        down_wg,
        query_bg,
        key_bg,
        value_bg,
        up_bg,
        output_bg,
        gain_g,
        shift_g,
    )


def solution(mesh):
    return jax.shard_map(
        body,
        mesh=mesh,
        in_specs=(
            P("dp", "ctx", "tp"),
            P("dp", None),
            P("dp", "tp"),
            P("dp", "tp"),
            P("dp", "tp"),
            P("tp", "dp"),
            P("dp", "tp"),
            P("tp", "dp"),
        )
        + (P(("tp", "dp")),) * 7
        + (P("dp", "ctx", "tp"),),
        out_specs=(
            P("dp", "ctx", "tp"),
            P("dp", "ctx", "tp"),
            P("dp", "tp"),
            P("dp", "tp"),
            P("dp", "tp"),
            P("tp", "dp"),
            P("dp", "tp"),
            P("tp", "dp"),
        )
        + (P(("tp", "dp")),) * 7,
        check_vma=False,
    )
```

```python
import functools
import math

import jax
import jax.numpy as jnp
from jax import lax
from jax.experimental import pallas as pl
from jax.experimental.pallas import tpu as pltpu
from jax.sharding import PartitionSpec as P

HEAD_DIM = 64
ROT = 32
D = 2048
N_DP = 4
N_TP = 4
CH = D // N_TP
EPS = 1e-05
NEG = -1e30
VMEM = 56 * 2**20
COST = 0.3

bf16 = jnp.bfloat16
f32 = jnp.float32


def dot_nn(a, b):
    return lax.dot_general(a, b, (((1,), (0,)), ((), ())), preferred_element_type=f32)


def dot_nt(a, b):
    return lax.dot_general(a, b, (((1,), (1,)), ((), ())), preferred_element_type=f32)


def dot_tn(a, b):
    return lax.dot_general(a, b, (((0,), (0,)), ((), ())), preferred_element_type=f32)


def spec(block, index):
    return pl.BlockSpec(block, index)


def whole(*block):
    zeros = (0,) * len(block)
    return pl.BlockSpec(block, lambda g, *_: zeros)


def shaped(shape, dtype=bf16):
    return jax.ShapeDtypeStruct(tuple(shape), dtype)


def call(body, name, grid, info, ins, in_specs, outs, out_specs, flops, scratch=()):
    moved = sum(math.prod(a.shape) * a.dtype.itemsize for a in (*ins, *jax.tree.leaves(outs)))
    return pl.pallas_call(
        body,
        grid_spec=pltpu.PrefetchScalarGridSpec(
            num_scalar_prefetch=1,
            grid=(grid,),
            in_specs=in_specs,
            out_specs=out_specs,
            scratch_shapes=list(scratch),
        ),
        out_shape=outs,
        compiler_params=pltpu.CompilerParams(vmem_limit_bytes=VMEM),
        cost_estimate=pl.CostEstimate(
            flops=int(flops * COST), bytes_accessed=int(moved * COST), transcendentals=0
        ),
        name=name,
    )(info, *ins)


def columns(index, width=CH):
    return pl.ds(pl.multiple_of(index * width, width), width)


def place(pieces, axis, shape, name):
    step = 256
    places, steps = [], []
    for array, at in pieces:
        count = array.shape[axis] // step
        steps.append((len(places), count))
        places += [at // step + n for n in range(count)]
    where = jnp.stack([jnp.asarray(at, jnp.int32) for at in places])

    def body(where_ref, *refs):
        *sources, out = refs
        g = pl.program_id(0)
        for source, (first, count) in zip(sources, steps):

            @pl.when((g >= first) & (g < first + count))
            def _(source=source):
                out[...] = source[...]

    block = (step, shape[1]) if axis == 0 else (shape[0], step)

    def at(index):
        return (index, 0) if axis == 0 else (0, index)

    def source_spec(first, count):
        return spec(block, lambda g, _: at(jnp.clip(g - first, 0, count - 1)))

    return call(
        body,
        name,
        len(places),
        where,
        [a for a, _ in pieces],
        [source_spec(*pair) for pair in steps],
        shaped(shape),
        spec(block, lambda g, where_ref: at(where_ref[g])),
        0,
    )


def after(value, *others):
    return lax.optimization_barrier((value, others))[0]


def swap(array, axis, bit, size):
    return lax.ppermute(array, axis, [(i, i ^ bit) for i in range(size)])


def gather_shards(own, axis, d, c, two):
    size = own.shape[axis]
    if two:
        half = size // 2
        mine = lax.dynamic_slice_in_dim(own, c * half, half, axis)
        first = swap(mine, "dp", 2, N_DP)
        second = swap(first, "ctx", 1, 2)
        near = swap(own, "dp", 1, N_DP)
        far = [(first, c * half), (second, (1 - c) * half)]
        pieces = [(own, d * size), (near, (d ^ 1) * size)]
        pieces += [(a, (d ^ 2) * size + at) for a, at in far]
        pieces += [(swap(a, "dp", 1, N_DP), (d ^ 3) * size + at) for a, at in far]
    else:
        near = swap(own, "dp", 1, N_DP)
        across = swap(own, "dp", 2, N_DP)
        pieces = [
            (own, d * size),
            (near, (d ^ 1) * size),
            (across, (d ^ 2) * size),
            (swap(across, "dp", 1, N_DP), (d ^ 3) * size),
        ]
    return pieces


def rotary_tables(starts, positions):
    before = starts[:, None, :] <= positions[None, :, None]
    opening = jnp.max(jnp.where(before, starts[:, None, :], 0), axis=2)
    relative = (positions[None, :] - opening).astype(f32)
    half = ROT // 2
    frequency = jnp.exp(jnp.arange(half, dtype=f32) * (-math.log(10000.0) / half))
    angles = relative[:, :, None] * frequency
    cosine, sine = jnp.cos(angles), jnp.sin(angles)
    ones = jnp.ones(cosine.shape[:2] + (HEAD_DIM - ROT,), f32)
    none = jnp.zeros_like(ones)
    gap = jnp.zeros_like(sine)

    def lanes(*parts):
        return jnp.concatenate(parts * 2, axis=2)

    return (
        lanes(cosine, cosine, ones),
        lanes(-sine, gap, none),
        lanes(gap, sine, none),
    ), opening


def turn(x, own, up, down):
    return x * own + pltpu.roll(x, 112, 1) * up + pltpu.roll(x, 16, 1) * down


def turn_back(x, own, up, down):
    return x * own - pltpu.roll(x, 112, 1) * up - pltpu.roll(x, 16, 1) * down


def norm_qkv_body(
    info, x0, xa, xc, xb, gain, shift, w, bias, own, up, down, xf, normed, avg, inv, q, kv
):
    j = pl.program_id(0)
    t = info[0]
    rows = x0.shape[0]

    @pl.when(j == 0)
    def _():
        for part, step in ((x0, 0), (xa, 3), (xc, 1), (xb, 2)):
            xf[:, columns((t + step) % N_TP)] = part[...]

        tile = 128

        def rows_of(i, carry):
            window = pl.ds(pl.multiple_of(i * tile, tile), tile)
            x = xf[window, :].astype(f32)
            average = jnp.sum(x, axis=1, keepdims=True) * (1.0 / D)
            centred = x - average
            variance = jnp.sum(centred * centred, axis=1, keepdims=True) * (1.0 / D)
            root = lax.rsqrt(variance + EPS)
            avg[window, :] = average
            inv[window, :] = root
            normed[window, :] = (
                centred * root * gain[...].astype(f32) + shift[...].astype(f32)
            ).astype(bf16)
            return carry

        lax.fori_loop(0, rows // tile, rows_of, 0)

    y = dot_nn(normed[...], w[...]) + bias[...].astype(f32)

    def rotated():
        parts = [
            turn(y[:, 128 * n : 128 * n + 128], own[...], up[...], down[...])
            for n in range(CH // 128)
        ]
        return jnp.concatenate(parts, axis=1).astype(bf16)

    @pl.when(j == 0)
    def _():
        q[...] = rotated()

    @pl.when(j == 1)
    def _():
        kv[0] = rotated()

    @pl.when(j == 2)
    def _():
        kv[0] = y.astype(bf16)


def norm_qkv(info, parts, gain, shift, w, bias, tables):
    rows = parts[0].shape[0]
    outs = (
        shaped((rows, D)),
        shaped((rows, D)),
        shaped((rows, 1), f32),
        shaped((rows, 1), f32),
        shaped((rows, CH)),
        shaped((2, rows, CH)),
    )
    return call(
        norm_qkv_body,
        "norm_qkv",
        3,
        info,
        (*parts, gain, shift, w, bias, *tables),
        [whole(rows, CH)] * 4
        + [whole(1, D)] * 2
        + [spec((D, CH), lambda j, *_: (0, j)), spec((1, CH), lambda j, *_: (0, j))]
        + [whole(rows, 128)] * 3,
        outs,
        [
            whole(rows, D),
            whole(rows, D),
            whole(rows, 1),
            whole(rows, 1),
            whole(rows, CH),
            spec((1, rows, CH), lambda j, *_: (jnp.maximum(j - 1, 0), 0, 0)),
        ],
        2 * rows * D * 3 * CH,
    )


def mlp_up_body(info, n0, n1, w, bias, h0, h1, g0, g1):
    root = math.sqrt(2.0 / math.pi)
    for n, h, g in ((n0, h0, g0), (n1, h1, g1)):
        u = dot_nn(n[...], w[...]) + bias[...].astype(f32)
        square = u * u
        t = jnp.tanh(root * u * (1.0 + 0.044715 * square))
        h[...] = (0.5 * u * (1.0 + t)).astype(bf16)
        slope = root * (1.0 + 3 * 0.044715 * square)
        g[...] = (0.5 * (1.0 + t) + 0.5 * u * (1.0 - t * t) * slope).astype(bf16)


def mlp_up(info, normed, w, bias):
    rows, units = normed[0].shape[0], w.shape[1]
    block = spec((rows, CH), lambda j, *_: (0, j))
    return call(
        mlp_up_body,
        "mlp_up",
        units // CH,
        info,
        (*normed, w, bias),
        [whole(rows, D)] * 2
        + [spec((D, CH), lambda j, *_: (0, j)), spec((1, CH), lambda j, *_: (0, j))],
        (shaped((rows, units)),) * 4,
        [block] * 4,
        4 * rows * D * units,
    )


def back_out_body(info, c0, ca, cc, cb, w, slope, cf, bias_grad, datt, dup):
    j = pl.program_id(0)
    t = info[0]

    @pl.when(j == 0)
    def _():
        for part, step in ((c0, 0), (ca, 3), (cc, 1), (cb, 2)):
            cf[:, columns((t + step) % N_TP)] = part[...]
        bias_grad[...] = jnp.sum(c0[...].astype(f32), axis=0, keepdims=True)

    y = dot_nt(cf[...], w[...])

    @pl.when(j == 0)
    def _():
        datt[...] = y.astype(bf16)

    @pl.when(j > 0)
    def _():
        dup[...] = (y * slope[...].astype(f32)).astype(bf16)


def back_out(info, parts, w, slope):
    rows, units = slope.shape
    later = spec((rows, CH), lambda j, *_: (0, jnp.maximum(j - 1, 0)))
    return call(
        back_out_body,
        "back_out",
        w.shape[0] // CH,
        info,
        (*parts, w, slope),
        [whole(rows, CH)] * 4 + [spec((CH, D), lambda j, *_: (j, 0)), later],
        (
            shaped((rows, D)),
            shaped((1, CH), f32),
            shaped((rows, CH)),
            shaped((rows, units)),
        ),
        [whole(rows, D), whole(1, CH), whole(rows, CH), later],
        2 * rows * D * w.shape[0],
    )


def attention_body(
    blocks, info, low, q, kv, kvp, do, own, up, down, ownp, upp, downp,
    att, dq, dkv, dkvp, scores, probs,
):
    rows = q.shape[0]
    before, start = info[1], info[1] * rows
    lane = lax.broadcasted_iota(jnp.int32, (rows, 128), 1)
    key_row = lax.broadcasted_iota(jnp.int32, (rows, 1), 0)
    query_at = start + lax.broadcasted_iota(jnp.int32, (1, rows), 1)
    first = low[0]
    do_t = do[...].astype(f32).T
    nothing = jnp.zeros((), bf16)
    outputs = []
    for head in range(2):
        mine = (lane < HEAD_DIM) if head == 0 else (lane >= HEAD_DIM)
        half = slice(HEAD_DIM * head, HEAD_DIM * (head + 1))
        qh = jnp.where(mine, q[...] * jnp.asarray(HEAD_DIM**-0.5, bf16), nothing)
        dh = jnp.where(mine, do[...], nothing)

        key_at = start + key_row
        s = dot_nt(kv[0], qh)
        s = jnp.where((key_at >= first) & (key_at <= query_at), s, NEG)
        scores[blocks] = s
        peak = jnp.max(s, axis=0, keepdims=True)

        def score(n, peak):
            s = dot_nt(kvp[n, 0], qh)
            s = jnp.where(n * rows + key_row >= first, s, NEG)
            scores[n] = s
            return jnp.maximum(peak, jnp.max(s, axis=0, keepdims=True))

        peak = lax.fori_loop(0, before, score, peak)

        def expo(n, total):
            e = jnp.exp(scores[n] - peak)
            scores[n] = e
            return total + jnp.sum(e, axis=0, keepdims=True)

        total = expo(blocks, jnp.zeros((1, rows), f32))
        total = lax.fori_loop(0, before, expo, total)
        scale = 1.0 / total

        def weigh(n, values):
            p = (scores[n] * scale).astype(bf16)
            probs[n] = p
            return dot_tn(values, p)

        out_t = weigh(blocks, kv[1])
        out_t = lax.fori_loop(0, before, lambda n, acc: acc + weigh(n, kvp[n, 1]), out_t)
        delta = jnp.sum(out_t[half] * do_t[half], axis=0, keepdims=True)

        def back(n, keys, values):
            dp = dot_nt(values, dh)
            ds = ((scores[n] * scale) * (dp - delta)).astype(bf16)
            return dot_nn(ds, qh), dot_nn(probs[n], dh), dot_tn(keys, ds)

        dk, dv, dq_t = back(blocks, kv[0], kv[1])
        if head == 0:
            dk_sum, dv_sum = dk, dv
        else:
            dk_sum, dv_sum = dk_sum + dk, dv_sum + dv

        def back_before(n, acc):
            dk, dv, more = back(n, kvp[n, 0], kvp[n, 1])
            dk = turn_back(dk, ownp[n], upp[n], downp[n])
            if head == 0:
                dkvp[n, 0] = dk.astype(bf16)
                dkvp[n, 1] = dv.astype(bf16)
            else:
                dkvp[n, 0] = (dkvp[n, 0].astype(f32) + dk).astype(bf16)
                dkvp[n, 1] = (dkvp[n, 1].astype(f32) + dv).astype(bf16)
            return acc + more

        dq_t = lax.fori_loop(0, before, back_before, dq_t)
        outputs.append((out_t[half], dq_t[half]))

    def clear(n, carry):
        dkvp[n] = jnp.zeros(dkvp.shape[1:], bf16)
        return carry

    lax.fori_loop(before, blocks, clear, 0)
    att[...] = jnp.concatenate([outputs[0][0], outputs[1][0]], axis=0).T.astype(bf16)
    grad = jnp.concatenate([outputs[0][1], outputs[1][1]], axis=0).T * HEAD_DIM**-0.5
    dq[...] = turn_back(grad, own[...], up[...], down[...]).astype(bf16)
    dkv[0] = turn_back(dk_sum, own[...], up[...], down[...]).astype(bf16)
    dkv[1] = dv_sum.astype(bf16)


def attention(info, low, q, kv, kvp, do, tables, tables_before):
    rows, width = q.shape
    blocks = kvp.shape[0]
    token = spec((rows, 128), lambda g, *_: (0, g))
    pair = spec((2, rows, 128), lambda g, *_: (0, 0, g))
    pairs = spec((blocks, 2, rows, 128), lambda g, *_: (0, 0, 0, g))
    return call(
        functools.partial(attention_body, blocks),
        "attention",
        width // 128,
        info,
        (low, q, kv, kvp, do, *tables, *tables_before),
        [whole(1, rows), token, pair, pairs, token]
        + [whole(rows, 128)] * 3
        + [whole(blocks, rows, 128)] * 3,
        (
            shaped((rows, width)),
            shaped((rows, width)),
            shaped((2, rows, width)),
            shaped((blocks, 2, rows, width)),
        ),
        [token, token, pair, pairs],
        48 * rows * rows * width,
        [
            pltpu.VMEM((blocks + 1, rows, rows), f32),
            pltpu.VMEM((blocks + 1, rows, rows), bf16),
        ],
    )


TAIL = 16
ORDER = (2, 3, 1, 0)


def relative(step):
    return jnp.where(step < 2, step + 2, 3 - step)


def out_body(info, att, hidden, w, *outs):
    j = pl.program_id(0)
    y = dot_nn(att[...], w[:CH, :]) + dot_nn(hidden[...], w[CH:, :])
    y = y.astype(bf16)
    for step, r in enumerate(ORDER):

        @pl.when(j == step)
        def _(r=r):
            outs[r][...] = y


def project_out(info, att, hidden, w):
    rows, units = hidden.shape
    return call(
        out_body,
        "project_out",
        N_TP,
        info,
        (att, hidden, w),
        [
            whole(rows, CH),
            whole(rows, units),
            spec((CH + units, CH), lambda j, info: (0, (info[0] + relative(j)) % N_TP)),
        ],
        (shaped((rows, CH)),) * N_TP,
        [whole(rows, CH)] * N_TP,
        2 * rows * D * (CH + units),
    )


def back_in_body(info, dq, dkv, dup, wq, wu, xf, gain, avg, inv, *outs):
    j = pl.program_id(0)
    *chunks, column_sums, row_sums = outs
    rows = dq.shape[0]
    y = dot_nt(dup[...], wu[...])
    y = y + dot_nt(dq[...], wq[:, :CH])
    y = y + dot_nt(dkv[0], wq[:, CH : 2 * CH])
    y = y + dot_nt(dkv[1], wq[:, 2 * CH :])
    yb = y.astype(bf16)
    for step, r in enumerate(ORDER):

        @pl.when(j == step)
        def _(r=r):
            chunks[r][:rows, :] = yb

    standard = (xf[...].astype(f32) - avg[...]) * inv[...]
    cross = y * standard
    weight = gain[...].astype(f32)
    column_sums[0, 0:1, :] = jnp.sum(cross, axis=0, keepdims=True)
    column_sums[0, 1:2, :] = jnp.sum(y, axis=0, keepdims=True)

    @pl.when(j == 0)
    def _():
        row_sums[...] = jnp.zeros(row_sums.shape, f32)

    row_sums[:, 0:1] += jnp.sum(y * weight, axis=1, keepdims=True)
    row_sums[:, 1:2] += jnp.sum(cross * weight, axis=1, keepdims=True)

    @pl.when(j == N_TP - 1)
    def _():
        turned = row_sums[...].T[:TAIL].astype(bf16)
        for chunk in chunks:
            chunk[rows:, :] = turned


def back_in(info, dq, dkv, dup, wq, wu, xf, gain, avg, inv):
    rows, units = dup.shape

    def chunk(j, info):
        return (info[0] + relative(j)) % N_TP

    return call(
        back_in_body,
        "back_in",
        N_TP,
        info,
        (dq, dkv, dup, wq, wu, xf, gain, avg, inv),
        [
            whole(rows, CH),
            whole(2, rows, CH),
            whole(rows, units),
            spec((CH, 3 * CH), lambda j, info: (chunk(j, info), 0)),
            spec((CH, units), lambda j, info: (chunk(j, info), 0)),
            spec((rows, CH), lambda j, info: (0, chunk(j, info))),
            spec((1, CH), lambda j, info: (0, chunk(j, info))),
            whole(rows, 1),
            whole(rows, 1),
        ],
        (shaped((rows + TAIL, CH)),) * N_TP + (shaped((N_TP, 2, CH), f32),),
        [whole(rows + TAIL, CH)] * N_TP
        + [spec((1, 2, CH), lambda j, _: (relative(j), 0, 0))],
        2 * rows * D * (3 * CH + units),
        [pltpu.VMEM((rows, 128), f32)],
    )


KEPT = ((0, 0), (2, 1))
GIVEN = ((1, 0), (3, 1))


def grad_up_body(info, n0, n1, g0, g1, kept, given, sums):
    d = info[2]
    left, right = g0[...], g1[...]
    for target, which in ((given, GIVEN), (kept, KEPT)):
        for r, at in which:
            rows = columns(d ^ r)
            target[at, 0] = (dot_tn(n0[:, rows], left) + dot_tn(n1[:, rows], right)).astype(bf16)
    sums[...] = jnp.sum(left.astype(f32), axis=0, keepdims=True) + jnp.sum(
        right.astype(f32), axis=0, keepdims=True
    )


def grad_up(info, normed, dup):
    rows, units = dup[0].shape
    count = units // CH
    block = spec((rows, CH), lambda j, *_: (0, j))
    message = spec((2, 1, CH, CH), lambda j, *_: (0, j, 0, 0))
    return call(
        grad_up_body,
        "grad_up",
        count,
        info,
        (*normed, *dup),
        [whole(rows, D)] * 2 + [block] * 2,
        (shaped((2, count, CH, CH)),) * 2 + (shaped((1, units), f32),),
        [message, message, spec((1, CH), lambda j, *_: (0, j))],
        4 * rows * D * units,
    )


def grad_down_body(info, h0, h1, c0, c1, kept, given):
    j = pl.program_id(0)
    y = (dot_tn(h0[...], c0[...]) + dot_tn(h1[...], c1[...])).astype(bf16)

    def store(target):
        for n in range(target.shape[1]):
            target[0, n] = y[CH * n : CH * (n + 1), :]

    @pl.when(j < 2)
    def _():
        store(given)

    @pl.when(j >= 2)
    def _():
        store(kept)


def grad_down(info, hidden, ct):
    rows, units = hidden[0].shape
    count = units // CH
    block = spec(
        (rows, CH),
        lambda j, info: (0, info[2] ^ jnp.where(j < 2, 2 * j + 1, 2 * j - 4)),
    )
    return call(
        grad_down_body,
        "grad_down",
        N_DP,
        info,
        (*hidden, *ct),
        [whole(rows, units)] * 2 + [block] * 2,
        (shaped((2, count, CH, CH)),) * 2,
        [
            spec((1, count, CH, CH), lambda j, *_: (jnp.maximum(j - 2, 0), 0, 0, 0)),
            spec((1, count, CH, CH), lambda j, *_: (jnp.minimum(j, 1), 0, 0, 0)),
        ],
        4 * rows * D * units,
    )


def grad_heads_body(
    info, n0, n1, c0, c1, a0, a1, q0, q1, kv0, kv1, kept, given, sums
):
    j = pl.program_id(0)
    d = info[2]

    def store(lefts, rights, of_rows):
        for target, which in ((given, GIVEN), (kept, KEPT)):
            for r, at in which:
                window = columns(d ^ r)
                if of_rows:
                    y = sum(dot_tn(a[:, window], b) for a, b in zip(lefts, rights))
                else:
                    y = sum(dot_tn(b, a[:, window]) for a, b in zip(lefts, rights))
                target[at, 0] = y.astype(bf16)

    def add_up(rights):
        sums[0] = sum(jnp.sum(b.astype(f32), axis=0, keepdims=True) for b in rights)

    @pl.when(j == 0)
    def _():
        rights = (a0[...], a1[...])
        store((c0, c1), rights, False)
        add_up(rights)

    @pl.when(j == 1)
    def _():
        rights = (q0[...], q1[...])
        store((n0, n1), rights, True)
        add_up(rights)

    @pl.when(j > 1)
    def _():
        rights = (kv0[0], kv1[0])
        store((n0, n1), rights, True)
        add_up(rights)


def grad_heads(info, normed, ct, att, dq, dkv):
    rows = normed[0].shape[0]
    message = spec((2, 1, CH, CH), lambda j, *_: (0, j, 0, 0))
    pair = spec((1, rows, CH), lambda j, *_: (jnp.maximum(j - 2, 0), 0, 0))
    return call(
        grad_heads_body,
        "grad_heads",
        4,
        info,
        (*normed, *ct, *att, *dq, *dkv),
        [whole(rows, D)] * 4 + [whole(rows, CH)] * 4 + [pair] * 2,
        (shaped((2, 4, CH, CH)),) * 2 + (shaped((4, 1, CH), f32),),
        [message, message, spec((1, 1, CH), lambda j, *_: (j, 0, 0))],
        4 * rows * D * 4 * CH,
    )


def ring(array, step):
    return lax.ppermute(array, "tp", [(i, (i + step) % N_TP) for i in range(N_TP)])


def gather_tp(own):
    behind = ring(own, 1)
    ahead = ring(own, -1)
    return own, behind, ahead, ring(behind, 1)


def scatter_tp(chunks):
    far = ring(chunks[2], 1)
    back = ring(chunks[3], -1)
    both = (chunks[1].astype(f32) + far.astype(f32)).astype(bf16)
    near = ring(both, 1)
    return chunks[0].astype(f32) + back.astype(f32) + near.astype(f32)


class Reduction:
    def __init__(self, kept, given, c, two):
        self.kept, self.c, self.two = kept, c, two
        self.got = swap(given, "dp", 1, N_DP)

    def over_x(self):
        self.across = (self.kept[1].astype(f32) + self.got[1].astype(f32)).astype(bf16)
        self.moved = swap(self.across, "dp", 2, N_DP)
        return self.across

    def over_y(self):
        parts = (self.kept[0], self.got[0], self.moved)
        total = sum(a.astype(f32) for a in parts).astype(bf16)
        if not self.two:
            self.total = lax.psum(total, "ctx")
            return total
        half = total.shape[0] // 2
        self.mine = lax.dynamic_slice_in_dim(total, self.c * half, half, 0)
        theirs = lax.dynamic_slice_in_dim(total, (1 - self.c) * half, half, 0)
        self.received = swap(theirs, "ctx", 1, 2)
        return theirs

    def back_y(self):
        if self.two:
            self.mine = (self.mine.astype(f32) + self.received.astype(f32)).astype(bf16)
            self.other = swap(self.mine, "ctx", 1, 2)
            return self.mine
        return self.total

    def result(self):
        if not self.two:
            return [a.astype(f32) for a in self.total]
        low = jnp.where(self.c == 0, self.mine, self.other).astype(f32)
        high = jnp.where(self.c == 0, self.other, self.mine).astype(f32)
        return [*low, *high]


def body(
    block_in,
    doc_starts,
    query_weight,
    key_weight,
    value_weight,
    output_weight,
    up_weight,
    down_weight,
    query_bias,
    key_bias,
    value_bias,
    up_bias,
    output_bias,
    norm_gain,
    norm_shift,
    cotangent,
):
    seqs, rows, _ = block_in.shape
    d, c, t = lax.axis_index("dp"), lax.axis_index("ctx"), lax.axis_index("tp")
    n_ctx = lax.axis_size("ctx")
    two = n_ctx == 2
    info = jnp.stack([t, c, d]).astype(jnp.int32)

    small = jnp.concatenate(
        [query_bias, key_bias, value_bias, up_bias, output_bias, norm_gain, norm_shift]
    )
    small_all = lax.all_gather(small, ("tp", "dp"), axis=0, tiled=False)
    big = (block_in, query_weight, key_weight, value_weight, output_weight, up_weight, down_weight)
    big, small_all = lax.optimization_barrier((big, small_all))
    block_in, query_weight, key_weight, value_weight, output_weight, up_weight, down_weight = big

    x_parts = [gather_tp(block_in[0])]
    x_parts.append(gather_tp(after(block_in[1], x_parts[0][1])))

    wq_shard = jnp.concatenate([query_weight, key_weight, value_weight], axis=1)
    wo_shard = jnp.concatenate([output_weight, down_weight], axis=0)
    wq_pieces = gather_shards(wq_shard, 0, d, c, two)
    wu_pieces = gather_shards(after(up_weight, wq_pieces[2][0]), 0, d, c, two)
    wo_pieces = gather_shards(after(wo_shard, wu_pieces[2][0]), 1, d, c, two)

    ct_parts = [gather_tp(after(cotangent[0], x_parts[1][1]))]
    ct_parts.append(gather_tp(after(cotangent[1], ct_parts[0][1])))

    small_all = small_all.reshape(N_TP, N_DP, -1)
    small_here = lax.dynamic_index_in_dim(small_all, t, 0, keepdims=False)
    sizes = [query_bias.size] * 3 + [up_bias.size] + [output_bias.size] * 3
    offsets = [sum(sizes[:n]) for n in range(len(sizes) + 1)]

    def small_of(table, n):
        return table[..., offsets[n] : offsets[n + 1]].reshape(1, -1)

    qkv_bias = jnp.concatenate([small_of(small_here, n) for n in range(3)], axis=1)
    up_shift = small_of(small_here, 3)
    output_shift = small_of(small_here, 4)
    gain, shift = small_of(small_all, 5), small_of(small_all, 6)
    gain_here = small_of(small_here, 5).astype(f32)

    here = c * rows + jnp.arange(rows, dtype=jnp.int32)
    tables, opening = rotary_tables(doc_starts, here)
    blocks = 1 if two else n_ctx
    before, _ = rotary_tables(doc_starts, jnp.arange(blocks * rows, dtype=jnp.int32))
    before = [a.reshape(seqs, blocks, rows, 128) for a in before]

    xf, normed, avg, inv, q, kv, kvp = [], [], [], [], [], [], []
    hidden, slope = [], []
    cf, out_bias_sum, datt, dup = [], [], [], []
    att, dq, dkv_own, dkv_sent, dkv = [], [], [], [], []
    out_sum, normed_grad, column_sums = [], [], []

    def norm_step(s, info):
        one = norm_qkv(info, x_parts[s], gain, shift, wq, qkv_bias, [a[s] for a in tables])
        for target, value in zip((xf, normed, avg, inv, q, kv), one):
            target.append(value)
        if two:
            kvp.append(lax.ppermute(kv[s], "ctx", [(0, 1)])[None])
        else:
            kvp.append(lax.all_gather(kv[s], "ctx", axis=0, tiled=False))

    def back_out_step(s, info):
        one = back_out(info, ct_parts[s], wo, slope[s])
        for target, value in zip((cf, out_bias_sum, datt, dup), one):
            target.append(value)

    def attention_step(s, info):
        one = attention(
            info,
            opening[s][None],
            q[s],
            kv[s],
            kvp[s],
            datt[s],
            [x[s] for x in tables],
            [x[s] for x in before],
        )
        for target, value in zip((att, dq, dkv_own, dkv_sent), one):
            target.append(value)
        if two:
            back = lax.ppermute(dkv_sent[s][0], "ctx", [(1, 0)])
        else:
            back = lax.psum_scatter(dkv_sent[s], "ctx", scatter_dimension=0, tiled=False)
        dkv.append((dkv_own[s].astype(f32) + back.astype(f32)).astype(bf16))

    def out_step(s, info):
        chunks = project_out(info, att[s], hidden[s], wo)
        out_sum.append(scatter_tp(chunks))
        return chunks

    def back_in_step(s, info):
        *chunks, sums = back_in(info, dq[s], dkv[s], dup[s], wq, wu, xf[s], gain, avg[s], inv[s])
        normed_grad.append(scatter_tp(chunks))
        column_sums.append(sums)
        return chunks

    wq = place(wq_pieces, 0, (D, 3 * CH), "place_qkv")
    norm_step(0, info)
    norm_step(1, after(info, kv[0]))
    wu = place(wu_pieces, 0, (D, up_weight.shape[1]), "place_up")
    h0, h1, g0, g1 = mlp_up(after(info, kv[1]), normed, wu, up_shift)
    hidden, slope = (h0, h1), (g0, g1)
    wo = place(wo_pieces, 1, (wo_shard.shape[0], D), "place_out")
    back_out_step(0, after(info, h1))
    attention_step(0, after(info, dup[0]))
    chunks = out_step(0, after(info, att[0]))
    back_out_step(1, after(info, chunks))
    up_kept, up_given, up_sum = grad_up(after(info, dup[1]), normed, dup)
    up = Reduction(up_kept, up_given, c, two)
    down_kept, down_given = grad_down(after(info, up_kept), hidden, cf)
    down = Reduction(down_kept, down_given, c, two)
    attention_step(1, after(info, down_kept, up.over_x()))
    head_kept, head_given, head_sum = grad_heads(
        after(info, att[1], down.over_x()), normed, cf, att, dq, dkv
    )
    head = Reduction(head_kept, head_given, c, two)
    chunks = back_in_step(0, after(info, head_kept))
    chunks = out_step(1, after(info, chunks, head.over_x(), up.over_y()))
    chunks = back_in_step(1, after(info, chunks, up.back_y()))
    down.over_y()
    down.back_y()
    head.over_y()
    head.back_y()

    block_out = jnp.stack(out_sum)
    block_out = (block_in.astype(f32) + block_out + output_shift.astype(f32)).astype(bf16)
    up_wg = jnp.concatenate(up.result(), axis=1)
    down_wg = jnp.concatenate(down.result(), axis=0)
    output_wg, query_wg, key_wg, value_wg = head.result()

    def input_gradient(s):
        total = normed_grad[s]
        plain, cross = total[rows][:, None], total[rows + 1][:, None]
        standard = (block_in[s].astype(f32) - avg[s]) * inv[s]
        scaled = total[:rows] * gain_here
        return cotangent[s].astype(f32) + inv[s] * (scaled - plain / D - standard * cross / D)

    in_grad = jnp.stack([input_gradient(s) for s in range(seqs)])

    sums = sum(column_sums)
    both = sums[0] + sum(ring(sums[r], r) for r in range(1, N_TP))
    summed = jnp.concatenate(
        [
            head_sum[1:].reshape(-1),
            up_sum.reshape(-1),
            sum(out_bias_sum).reshape(-1),
            both.reshape(-1),
        ]
    )
    summed = summed + swap(summed, "dp", 1, N_DP)
    summed = summed + swap(summed, "dp", 2, N_DP)
    summed = summed + swap(summed, "ctx", 1, 2) if two else lax.psum(summed, "ctx")
    at = 0
    small_grads = []
    for size in (CH, CH, CH, up_sum.size, CH, CH, CH):
        part = summed[at : at + size]
        at += size
        share = size // N_DP
        small_grads.append(lax.dynamic_slice_in_dim(part, d * share, share, 0))
    query_bg, key_bg, value_bg, up_bg, output_bg, gain_g, shift_g = small_grads
    return (
        block_out,
        in_grad,
        query_wg,
        key_wg,
        value_wg,
        output_wg,
        up_wg,
        down_wg,
        query_bg,
        key_bg,
        value_bg,
        up_bg,
        output_bg,
        gain_g,
        shift_g,
    )


def solution(mesh):
    return jax.shard_map(
        body,
        mesh=mesh,
        in_specs=(
            P("dp", "ctx", "tp"),
            P("dp", None),
            P("dp", "tp"),
            P("dp", "tp"),
            P("dp", "tp"),
            P("tp", "dp"),
            P("dp", "tp"),
            P("tp", "dp"),
        )
        + (P(("tp", "dp")),) * 7
        + (P("dp", "ctx", "tp"),),
        out_specs=(
            P("dp", "ctx", "tp"),
            P("dp", "ctx", "tp"),
            P("dp", "tp"),
            P("dp", "tp"),
            P("dp", "tp"),
            P("tp", "dp"),
            P("dp", "tp"),
            P("tp", "dp"),
        )
        + (P(("tp", "dp")),) * 7,
        check_vma=False,
    )
```

```python
import functools
import math

import jax
import jax.numpy as jnp
from jax import lax
from jax.experimental import pallas as pl
from jax.experimental.pallas import tpu as pltpu
from jax.sharding import PartitionSpec as P

HEAD_DIM = 64
ROT = 32
D = 2048
N_DP = 4
N_TP = 4
CH = D // N_TP
EPS = 1e-05
NEG = -1e30
VMEM = 56 * 2**20
COST = 0.02

bf16 = jnp.bfloat16
f32 = jnp.float32


def dot_nn(a, b):
    return lax.dot_general(a, b, (((1,), (0,)), ((), ())), preferred_element_type=f32)


def dot_nt(a, b):
    return lax.dot_general(a, b, (((1,), (1,)), ((), ())), preferred_element_type=f32)


def dot_tn(a, b):
    return lax.dot_general(a, b, (((0,), (0,)), ((), ())), preferred_element_type=f32)


def spec(block, index):
    return pl.BlockSpec(block, index)


def whole(*block):
    zeros = (0,) * len(block)
    return pl.BlockSpec(block, lambda g, *_: zeros)


def one_of(s, *block):
    zeros = (0,) * len(block)
    return pl.BlockSpec((None, *block), lambda g, *_: (s, *zeros))


def shaped(shape, dtype=bf16):
    return jax.ShapeDtypeStruct(tuple(shape), dtype)


HBM = pl.BlockSpec(memory_space=pltpu.HBM)


def call(body, name, grid, info, ins, in_specs, outs, out_specs, flops, scratch=(), deps=()):
    moved = sum(math.prod(a.shape) * a.dtype.itemsize for a in (*ins, *jax.tree.leaves(outs)))
    first, last = 1 + len(ins), 1 + len(ins) + len(deps)

    def without_deps(*refs):
        body(*refs[:first], *refs[last:])

    return pl.pallas_call(
        without_deps,
        grid_spec=pltpu.PrefetchScalarGridSpec(
            num_scalar_prefetch=1,
            grid=(grid,),
            in_specs=[*in_specs, *[HBM] * len(deps)],
            out_specs=out_specs,
            scratch_shapes=list(scratch),
        ),
        out_shape=outs,
        compiler_params=pltpu.CompilerParams(vmem_limit_bytes=VMEM),
        cost_estimate=pl.CostEstimate(
            flops=int(flops * COST), bytes_accessed=int(moved * COST), transcendentals=0
        ),
        name=name,
    )(info, *ins, *deps)


def tie(value, *deps):
    def nothing(*refs):
        del refs

    return pl.pallas_call(
        nothing,
        in_specs=[HBM] * (1 + len(deps)),
        out_specs=HBM,
        out_shape=shaped(value.shape, value.dtype),
        input_output_aliases={0: 0},
        cost_estimate=pl.CostEstimate(flops=0, bytes_accessed=0, transcendentals=0),
        name="tie",
    )(value, *deps)


def columns(index, width=CH):
    return pl.ds(pl.multiple_of(index * width, width), width)


def layout_of(two):
    if two:
        halves = [("c", CH // 2), ("other", CH // 2)]
    else:
        halves = [("", CH)]
    return [(0, "", CH), (1, "", CH)] + [(r, *half) for r in (2, 3) for half in halves]


def piece_offset(info, half):
    return {"": 0, "c": info[1], "other": 1 - info[1]}[half] * (CH // 2)


def piece_window(info, piece):
    r, half, size = piece
    start = (info[2] ^ r) * CH + piece_offset(info, half)
    return pl.ds(pl.multiple_of(start, size), size)


class Clock:
    def __init__(self):
        self.marks = ()

    def go(self, value):
        return tie(value, *self.marks) if self.marks else value

    def sync(self, *arrays):
        def nothing(*refs):
            del refs

        self.marks = (
            pl.pallas_call(
                nothing,
                in_specs=[HBM] * (len(arrays) + len(self.marks)),
                out_specs=HBM,
                out_shape=shaped((8, 128), f32),
                cost_estimate=pl.CostEstimate(flops=0, bytes_accessed=0, transcendentals=0),
                name="sync",
            )(*arrays, *self.marks),
        )


def swap(array, axis, bit, size):
    return lax.ppermute(array, axis, [(i, i ^ bit) for i in range(size)])


class Shards:
    def __init__(self, own, axis, d, c, two, made=True):
        self.own, self.two, self.made = own, two, made
        size = own.shape[axis] // 2
        self.part = lax.dynamic_slice_in_dim(own, c * size, size, axis) if two else own

    def near_core(self, clock):
        self.own = clock.go(self.own) if self.made else self.own
        self.near = swap(self.own, "dp", 1, N_DP)

    def over_x(self, clock):
        self.first = swap(clock.go(self.part), "dp", 2, N_DP)

    def over_y(self, clock):
        self.first = clock.go(self.first)
        self.second = swap(self.first, "ctx", 1, 2) if self.two else self.first

    def far_core(self, clock):
        self.first = clock.go(self.first)
        far = [self.first]
        if self.two:
            self.second = clock.go(self.second)
            far.append(self.second)
        self.far_near = [swap(a, "dp", 1, N_DP) for a in far]
        self.pieces = [self.own, self.near, *far, *self.far_near]


def rotary_tables(starts, positions):
    before = starts[:, None, :] <= positions[None, :, None]
    opening = jnp.max(jnp.where(before, starts[:, None, :], 0), axis=2)
    relative = (positions[None, :] - opening).astype(f32)
    half = ROT // 2
    lane = jnp.arange(128, dtype=jnp.int32) % HEAD_DIM
    frequency = jnp.exp((lane % half).astype(f32) * (-math.log(10000.0) / half))
    angles = relative[:, :, None] * jnp.where(lane < ROT, frequency, 0.0)
    sine = jnp.sin(angles)
    return (
        jnp.cos(angles),
        jnp.where(lane < half, -sine, 0.0),
        jnp.where(lane >= half, sine, 0.0),
    ), opening


def turn(x, own, up, down):
    return x * own + pltpu.roll(x, 112, 1) * up + pltpu.roll(x, 16, 1) * down


def turn_back(x, own, up, down):
    return x * own - pltpu.roll(x, 112, 1) * up - pltpu.roll(x, 16, 1) * down


def stream_pieces(layout, info, sources, held, sems, axis, blocks):
    j = pl.program_id(0)

    def copies(block):
        cut = pl.ds(pl.multiple_of(block * CH, CH), CH)
        for n, (piece, source) in enumerate(zip(layout, sources)):
            window = piece_window(info, piece)
            if axis == 0:
                pair = source.at[:, cut], held.at[window, cut]
            else:
                pair = source.at[cut, :], held.at[cut, window]
            yield pltpu.make_async_copy(*pair, sems.at[block, n])

    @pl.when(j == 0)
    def _():
        for block in range(blocks):
            for copy in copies(block):
                copy.start()

    for copy in copies(j):
        copy.wait()


def norm_qkv_body(layout, info, x0, xa, xc, xb, gain, shift, bias, own, up, down, *refs):
    *w, normed, avg, inv, q, kv0, kv1, held, sems = refs
    j = pl.program_id(0)
    t = info[0]
    seqs, rows, _ = x0.shape
    stream_pieces(layout, info, w, held, sems, 0, 3)

    @pl.when(j == 0)
    def _():
        parts = [(x0, t), (xa, (t + 3) % N_TP), (xc, (t + 1) % N_TP), (xb, (t + 2) % N_TP)]
        tile = 128

        def rows_of(i, carry):
            s = i // (rows // tile)
            window = pl.ds(pl.multiple_of((i % (rows // tile)) * tile, tile), tile)
            x = [part[s, window, :].astype(f32) for part, _ in parts]
            average = sum(jnp.sum(a, axis=1, keepdims=True) for a in x) * (1.0 / D)
            x = [a - average for a in x]
            variance = sum(jnp.sum(a * a, axis=1, keepdims=True) for a in x) * (1.0 / D)
            root = lax.rsqrt(variance + EPS)
            avg[s, window, :] = average
            inv[s, window, :] = root
            for a, (_, index) in zip(x, parts):
                at = columns(index)
                y = a * root * gain[:, at].astype(f32) + shift[:, at].astype(f32)
                normed[s, window, at] = y.astype(bf16)
            return carry

        lax.fori_loop(0, seqs * rows // tile, rows_of, 0)

    for s, kv in ((0, kv0), (1, kv1)):
        y = dot_nn(normed[s], held[:, columns(j)]) + bias[...].astype(f32)

        def rotated(s=s, y=y):
            parts = [
                turn(y[:, 128 * n : 128 * n + 128], own[s], up[s], down[s])
                for n in range(CH // 128)
            ]
            return jnp.concatenate(parts, axis=1).astype(bf16)

        @pl.when(j == 0)
        def _(s=s, rotated=rotated):
            q[s] = rotated()

        @pl.when(j == 1)
        def _(kv=kv, rotated=rotated):
            kv[0] = rotated()

        @pl.when(j == 2)
        def _(kv=kv, y=y):
            kv[0] = y.astype(bf16)


def norm_qkv(layout, info, parts, gain, shift, w, bias, tables, deps=()):
    seqs, rows, _ = parts[0].shape
    outs = (
        shaped((seqs, rows, D)),
        shaped((seqs, rows, 1), f32),
        shaped((seqs, rows, 1), f32),
        shaped((seqs, rows, CH)),
        shaped((2, rows, CH)),
        shaped((2, rows, CH)),
    )
    pair = spec((1, rows, CH), lambda j, *_: (jnp.maximum(j - 1, 0), 0, 0))
    return call(
        functools.partial(norm_qkv_body, layout),
        "norm_qkv",
        3,
        info,
        (*parts, gain, shift, bias, *tables, *w),
        [whole(seqs, rows, CH)] * 4
        + [whole(1, D)] * 2
        + [spec((1, CH), lambda j, *_: (0, j))]
        + [whole(seqs, rows, 128)] * 3
        + [HBM] * len(w),
        outs,
        [
            whole(seqs, rows, D),
            whole(seqs, rows, 1),
            whole(seqs, rows, 1),
            whole(seqs, rows, CH),
            pair,
            pair,
        ],
        2 * seqs * rows * D * 3 * CH,
        [pltpu.VMEM((D, 3 * CH), bf16), pltpu.SemaphoreType.DMA((3, len(w)))],
        deps=deps,
    )


def mlp_up_body(layout, info, normed, bias, *refs):
    *w, hidden, grad, held, sems = refs
    j = pl.program_id(0)
    stream_pieces(layout, info, w, held, sems, 0, held.shape[1] // CH)
    root = math.sqrt(2.0 / math.pi)
    for s in range(normed.shape[0]):
        u = dot_nn(normed[s], held[:, columns(j)]) + bias[...].astype(f32)
        square = u * u
        t = jnp.tanh(u * (root + (root * 0.044715) * square))
        half = 0.5 + 0.5 * t
        hidden[s] = (u * half).astype(bf16)
        slope = root + (3 * 0.044715 * root) * square
        grad[s] = (half + (0.5 * u) * (1.0 - t * t) * slope).astype(bf16)


def mlp_up(layout, info, normed, w, bias, deps=()):
    seqs, rows, _ = normed.shape
    units = w[0].shape[1]
    block = spec((seqs, rows, CH), lambda j, *_: (0, 0, j))
    return call(
        functools.partial(mlp_up_body, layout),
        "mlp_up",
        units // CH,
        info,
        (normed, bias, *w),
        [whole(seqs, rows, D), spec((1, CH), lambda j, *_: (0, j))] + [HBM] * len(w),
        (shaped((seqs, rows, units)),) * 2,
        [block] * 2,
        2 * seqs * rows * D * units,
        [pltpu.VMEM((D, units), bf16), pltpu.SemaphoreType.DMA((units // CH, len(w)))],
        deps=deps,
    )


def back_out_body(layout, info, c0, ca, cc, cb, slope, *refs):
    *w, cf, bias_grad, datt, dup, held, sems = refs
    j = pl.program_id(0)
    t = info[0]
    stream_pieces(layout, info, w, held, sems, 1, held.shape[0] // CH)

    @pl.when(j == 0)
    def _():
        for part, step in ((c0, 0), (ca, 3), (cc, 1), (cb, 2)):
            cf[:, columns((t + step) % N_TP)] = part[...]
        bias_grad[...] = jnp.sum(c0[...].astype(f32), axis=0, keepdims=True)

    y = dot_nt(cf[...], held[columns(j), :])

    @pl.when(j == 0)
    def _():
        datt[...] = y.astype(bf16)

    @pl.when(j > 0)
    def _():
        dup[...] = (y * slope[...].astype(f32)).astype(bf16)


def back_out(layout, info, s, parts, w, slope, deps=()):
    _, rows, units = slope.shape
    later = spec((rows, CH), lambda j, *_: (0, jnp.maximum(j - 1, 0)))
    slopes = spec((None, rows, CH), lambda j, *_: (s, 0, jnp.maximum(j - 1, 0)))
    return call(
        functools.partial(back_out_body, layout),
        "back_out",
        1 + units // CH,
        info,
        (*parts, slope, *w),
        [whole(rows, CH)] * 4 + [slopes] + [HBM] * len(w),
        (
            shaped((rows, D)),
            shaped((1, CH), f32),
            shaped((rows, CH)),
            shaped((rows, units)),
        ),
        [whole(rows, D), whole(1, CH), whole(rows, CH), later],
        2 * rows * D * (CH + units),
        [
            pltpu.VMEM((CH + units, D), bf16),
            pltpu.SemaphoreType.DMA((1 + units // CH, len(w))),
        ],
        deps=deps,
    )


def attention_body(
    blocks, info, low, q, kv, kvp, do, own, up, down, ownp, upp, downp,
    att, dq, dkv, dkvp, scores, probs,
):
    rows = q.shape[0]
    before, start = info[1], info[1] * rows
    lane = lax.broadcasted_iota(jnp.int32, (rows, 128), 1)
    key_row = lax.broadcasted_iota(jnp.int32, (rows, 1), 0)
    query_at = start + lax.broadcasted_iota(jnp.int32, (1, rows), 1)
    first = low[0]
    do_t = do[...].astype(f32).T
    nothing = jnp.zeros((), bf16)
    outputs = []
    for head in range(2):
        mine = (lane < HEAD_DIM) if head == 0 else (lane >= HEAD_DIM)
        half = slice(HEAD_DIM * head, HEAD_DIM * (head + 1))
        qh = jnp.where(mine, q[...] * jnp.asarray(HEAD_DIM**-0.5, bf16), nothing)
        dh = jnp.where(mine, do[...], nothing)

        key_at = start + key_row
        s = dot_nt(kv[0], qh)
        s = jnp.where((key_at >= first) & (key_at <= query_at), s, NEG)
        scores[blocks] = s
        peak = jnp.max(s, axis=0, keepdims=True)

        def score(n, peak):
            s = dot_nt(kvp[n, 0], qh)
            s = jnp.where(n * rows + key_row >= first, s, NEG)
            scores[n] = s
            return jnp.maximum(peak, jnp.max(s, axis=0, keepdims=True))

        peak = lax.fori_loop(0, before, score, peak)

        def expo(n, total):
            e = jnp.exp(scores[n] - peak)
            scores[n] = e
            return total + jnp.sum(e, axis=0, keepdims=True)

        total = expo(blocks, jnp.zeros((1, rows), f32))
        total = lax.fori_loop(0, before, expo, total)
        scale = 1.0 / total

        def weigh(n, values):
            p = (scores[n] * scale).astype(bf16)
            probs[n] = p
            return dot_tn(values, p)

        out_t = weigh(blocks, kv[1])
        out_t = lax.fori_loop(0, before, lambda n, acc: acc + weigh(n, kvp[n, 1]), out_t)
        delta = jnp.sum(out_t[half] * do_t[half], axis=0, keepdims=True)

        def back(n, keys, values):
            dp = dot_nt(values, dh)
            ds = ((scores[n] * scale) * (dp - delta)).astype(bf16)
            return dot_nn(ds, qh), dot_nn(probs[n], dh), dot_tn(keys, ds)

        dk, dv, dq_t = back(blocks, kv[0], kv[1])
        if head == 0:
            dk_sum, dv_sum = dk, dv
        else:
            dk_sum, dv_sum = dk_sum + dk, dv_sum + dv

        def back_before(n, acc):
            dk, dv, more = back(n, kvp[n, 0], kvp[n, 1])
            dk = turn_back(dk, ownp[n], upp[n], downp[n])
            if head == 0:
                dkvp[n, 0] = dk.astype(bf16)
                dkvp[n, 1] = dv.astype(bf16)
            else:
                dkvp[n, 0] = (dkvp[n, 0].astype(f32) + dk).astype(bf16)
                dkvp[n, 1] = (dkvp[n, 1].astype(f32) + dv).astype(bf16)
            return acc + more

        dq_t = lax.fori_loop(0, before, back_before, dq_t)
        outputs.append((out_t[half], dq_t[half]))

    def clear(n, carry):
        dkvp[n] = jnp.zeros(dkvp.shape[1:], bf16)
        return carry

    lax.fori_loop(before, blocks, clear, 0)
    att[...] = jnp.concatenate([outputs[0][0], outputs[1][0]], axis=0).T.astype(bf16)
    grad = jnp.concatenate([outputs[0][1], outputs[1][1]], axis=0).T * HEAD_DIM**-0.5
    dq[...] = turn_back(grad, own[...], up[...], down[...]).astype(bf16)
    dkv[0] = turn_back(dk_sum, own[...], up[...], down[...]).astype(bf16)
    dkv[1] = dv_sum.astype(bf16)


def attention_two_body(
    info, low, q, kv, kvp, do, own, up, down, ownp, upp, downp, att, dq, dkv, dkvp
):
    rows = q.shape[0]
    part = rows // 2
    before, start = info[1], info[1] * rows

    def tail(x, skipped):
        return x[:, skipped:] if skipped else x

    def merge(acc, x, skipped, op):
        if acc is None:
            return x
        if not skipped:
            return op(acc, x)
        return jnp.concatenate([acc[:, :skipped], op(acc[:, skipped:], x)], axis=1)

    def run(with_before):
        lane = lax.broadcasted_iota(jnp.int32, (rows, 128), 1)
        key_row = lax.broadcasted_iota(jnp.int32, (part, 1), 0)
        query_at = start + lax.broadcasted_iota(jnp.int32, (1, rows), 1)
        first = low[...]
        do_t = do[...].astype(f32).T
        nothing = jnp.zeros((), bf16)
        blocks = []
        for n in range(2):
            if with_before:
                blocks.append((kvp.at[0], n * part, 0, False))
        for n in range(2):
            blocks.append((kv, n * part, n * part, True))
        outputs = []
        dk_sum, dv_sum = [0.0] * len(blocks), [0.0] * len(blocks)
        for head in range(2):
            mine = (lane < HEAD_DIM) if head == 0 else (lane >= HEAD_DIM)
            half = slice(HEAD_DIM * head, HEAD_DIM * (head + 1))
            qh = jnp.where(mine, q[...] * jnp.asarray(HEAD_DIM**-0.5, bf16), nothing)
            dh = jnp.where(mine, do[...], nothing)
            scores, peak = [], None
            for ref, row, skip, here in blocks:
                s = dot_nt(ref[0, row : row + part], qh[skip:])
                key_at = (start if here else start - rows) + row + key_row
                allowed = key_at >= tail(first, skip)
                if here:
                    allowed = allowed & (key_at <= tail(query_at, skip))
                s = jnp.where(allowed, s, NEG)
                scores.append(s)
                peak = merge(peak, jnp.max(s, axis=0, keepdims=True), skip, jnp.maximum)
            terms, total = [], None
            for s, (_, _, skip, _) in zip(scores, blocks):
                e = jnp.exp(s - tail(peak, skip))
                terms.append(e)
                total = merge(total, jnp.sum(e, axis=0, keepdims=True), skip, jnp.add)
            scale = 1.0 / total
            probs, rounded, out_t = [], [], None
            for e, (ref, row, skip, _) in zip(terms, blocks):
                p = e * tail(scale, skip)
                pb = p.astype(bf16)
                probs.append(p)
                rounded.append(pb)
                out_t = merge(out_t, dot_tn(ref[1, row : row + part], pb), skip, jnp.add)
            delta = jnp.sum(out_t[half] * do_t[half], axis=0, keepdims=True)
            dq_t = None
            for n, (ref, row, skip, _) in enumerate(blocks):
                dp = dot_nt(ref[1, row : row + part], dh[skip:])
                ds = (probs[n] * (dp - tail(delta, skip))).astype(bf16)
                dv_sum[n] = dv_sum[n] + dot_nn(rounded[n], dh[skip:])
                dk_sum[n] = dk_sum[n] + dot_nn(ds, qh[skip:])
                dq_t = merge(dq_t, dot_tn(ref[0, row : row + part], ds), skip, jnp.add)
            outputs.append((out_t[half], dq_t[half]))
        att[...] = jnp.concatenate([outputs[0][0], outputs[1][0]], axis=0).T.astype(bf16)
        grad = jnp.concatenate([outputs[0][1], outputs[1][1]], axis=0).T * HEAD_DIM**-0.5
        dq[...] = turn_back(grad, own[...], up[...], down[...]).astype(bf16)
        dk = jnp.concatenate(dk_sum[-2:], axis=0)
        dkv[0] = turn_back(dk, own[...], up[...], down[...]).astype(bf16)
        dkv[1] = jnp.concatenate(dv_sum[-2:], axis=0).astype(bf16)
        if with_before:
            dk = jnp.concatenate(dk_sum[:2], axis=0)
            dkvp[0, 0] = turn_back(dk, ownp[0], upp[0], downp[0]).astype(bf16)
            dkvp[0, 1] = jnp.concatenate(dv_sum[:2], axis=0).astype(bf16)
        else:
            dkvp[...] = jnp.zeros(dkvp.shape, bf16)

    @pl.when(before == 0)
    def _():
        run(False)

    @pl.when(before > 0)
    def _():
        run(True)


def attention(info, s, low, q, kv, kvp, do, tables, tables_before, deps=()):
    _, rows, width = q.shape
    blocks = kvp.shape[0]
    token = spec((rows, 128), lambda g, *_: (0, g))
    query = spec((None, rows, 128), lambda g, *_: (s, 0, g))
    pair = spec((2, rows, 128), lambda g, *_: (0, 0, g))
    pairs = spec((blocks, 2, rows, 128), lambda g, *_: (0, 0, 0, g))
    return call(
        attention_two_body if blocks == 1 else functools.partial(attention_body, blocks),
        "attention",
        width // 128,
        info,
        (low, q, kv, kvp, do, *tables, *tables_before),
        [one_of(s, 1, rows), query, pair, pairs, token]
        + [one_of(s, rows, 128)] * 3
        + [one_of(s, blocks, rows, 128)] * 3,
        (
            shaped((rows, width)),
            shaped((rows, width)),
            shaped((2, rows, width)),
            shaped((blocks, 2, rows, width)),
        ),
        [token, token, pair, pairs],
        48 * rows * rows * width,
        []
        if blocks == 1
        else [
            pltpu.VMEM((blocks + 1, rows, rows), f32),
            pltpu.VMEM((blocks + 1, rows, rows), bf16),
        ],
        deps=deps,
    )


TAIL = 16


def fetch_pieces(layout, sources, targets, sems, axis):
    copies = [[] for _ in range(N_DP)]
    at = [r * CH for r in range(N_DP)]
    n = 0
    for group, target in zip(sources, targets):
        at = [r * CH for r in range(N_DP)]
        for (r, _, size), source in zip(layout, group):
            window = pl.ds(at[r], size)
            place = target.at[window, :] if axis == 0 else target.at[:, window]
            copies[r].append(pltpu.make_async_copy(source, place, sems.at[n]))
            at[r] += size
            n += 1
    return copies


def with_chunk(layout, info, copies, work):
    j = pl.program_id(0)

    @pl.when(j == 0)
    def _():
        for group in copies:
            for copy in group:
                copy.start()

    for r in range(N_DP):

        @pl.when(j == r)
        def _(r=r):
            for copy in copies[r]:
                copy.wait()
            at = r * CH
            for s, half, size in layout:
                if s == r:
                    offset = pl.multiple_of(piece_offset(info, half), size)
                    work(pl.ds(at, size), pl.ds(offset, size))
                    at += size


def chunk_now(info):
    return ((info[2] ^ pl.program_id(0)) + N_TP - info[0]) % N_TP


def out_body(layout, info, att, hidden, *refs):
    count = len(layout)
    w, outs = refs[:count], refs[count : count + N_TP]
    held, y, sems = refs[count + N_TP :]

    def work(place, window):
        part = dot_nn(att[...], held[:CH, place]) + dot_nn(hidden[...], held[CH:, place])
        y[:, window] = part.astype(bf16)

    with_chunk(layout, info, fetch_pieces(layout, [w], [held], sems, 1), work)
    for r in range(N_TP):

        @pl.when(chunk_now(info) == r)
        def _(r=r):
            outs[r][...] = y[...]


def project_out(layout, info, s, att, hidden, w, deps=()):
    _, rows, units = hidden.shape
    return call(
        functools.partial(out_body, layout),
        "project_out",
        N_TP,
        info,
        (att, hidden, *w),
        [whole(rows, CH), one_of(s, rows, units)] + [HBM] * len(w),
        (shaped((rows, CH)),) * N_TP,
        [whole(rows, CH)] * N_TP,
        2 * rows * D * (CH + units),
        [
            pltpu.VMEM((CH + units, D), bf16),
            pltpu.VMEM((rows, CH), bf16),
            pltpu.SemaphoreType.DMA((len(w),)),
        ],
        deps=deps,
    )


def back_in_body(layout, info, x0, xa, xc, xb, dq, dkv, dup, gain, avg, inv, *refs):
    count = len(layout)
    wq, wu = refs[:count], refs[count : 2 * count]
    *chunks, held_q, held_u, y, xs, row_sums, column_sums, sems = refs[2 * count :]
    j = pl.program_id(0)
    rows = dq.shape[0]

    def work(place, window):
        part = dot_nt(dup[...], held_u[place, :])
        part = part + dot_nt(dq[...], held_q[place, :CH])
        part = part + dot_nt(dkv[0], held_q[place, CH : 2 * CH])
        y[:, window] = part + dot_nt(dkv[1], held_q[place, 2 * CH :])

    copies = fetch_pieces(layout, [wq, wu], [held_q, held_u], sems, 0)
    with_chunk(layout, info, copies, work)
    for r, part in enumerate((x0, xc, xb, xa)):

        @pl.when(chunk_now(info) == r)
        def _(r=r, part=part):
            chunks[r][:rows, :] = y[...].astype(bf16)
            xs[...] = part[...]

    total = y[...]
    standard = (xs[...].astype(f32) - avg[...]) * inv[...]
    cross = total * standard
    weight = gain[...].astype(f32)

    @pl.when(j == 0)
    def _():
        row_sums[...] = jnp.zeros(row_sums.shape, f32)
        column_sums[...] = jnp.zeros(column_sums.shape, f32)

    both = jnp.concatenate(
        [jnp.sum(cross, axis=0, keepdims=True), jnp.sum(total, axis=0, keepdims=True)], axis=0
    )
    column_sums[chunk_now(info), 0:2, :] = both
    row_sums[:, 0:1] += jnp.sum(total * weight, axis=1, keepdims=True)
    row_sums[:, 1:2] += jnp.sum(cross * weight, axis=1, keepdims=True)

    @pl.when(j == N_TP - 1)
    def _():
        turned = row_sums[...].T[: TAIL // 2]
        for r, chunk in enumerate(chunks):
            chunk[rows:, :] = jnp.concatenate([turned, column_sums[r]], axis=0).astype(bf16)


def back_in(layout, info, s, parts, dq, dkv, dup, wq, wu, gain, avg, inv, deps=()):
    rows, units = dup.shape
    return call(
        functools.partial(back_in_body, layout),
        "back_in",
        N_TP,
        info,
        (*parts, dq, dkv, dup, gain, avg, inv, *wq, *wu),
        [one_of(s, rows, CH)] * 4
        + [
            whole(rows, CH),
            whole(2, rows, CH),
            whole(rows, units),
            spec((1, CH), lambda j, info: (0, info[2] ^ j)),
            one_of(s, rows, 1),
            one_of(s, rows, 1),
        ]
        + [HBM] * (2 * len(wq)),
        (shaped((rows + TAIL, CH)),) * N_TP,
        [whole(rows + TAIL, CH)] * N_TP,
        2 * rows * D * (3 * CH + units),
        [
            pltpu.VMEM((D, 3 * CH), bf16),
            pltpu.VMEM((D, units), bf16),
            pltpu.VMEM((rows, CH), f32),
            pltpu.VMEM((rows, CH), bf16),
            pltpu.VMEM((rows, 128), f32),
            pltpu.VMEM((N_TP, TAIL // 2, CH), f32),
            pltpu.SemaphoreType.DMA((2 * len(wq),)),
        ],
        deps=deps,
    )


KEPT = ((0, 0), (2, 1))
GIVEN = ((1, 0), (3, 1))


def grad_up_body(info, normed, g0, g1, kept, given, sums):
    d = info[2]
    rights = (g0[...], g1[...])
    store_by_rows(d, normed, rights, kept, given)
    sums[...] = sum(jnp.sum(b.astype(f32), axis=0, keepdims=True) for b in rights)


def grad_up(info, normed, dup, n, deps=()):
    rows = dup[0].shape[0]
    block = spec((rows, CH), lambda j, *_: (0, 2 * n + j))
    message = spec((2, 1, CH, CH), lambda j, *_: (0, j, 0, 0))
    return call(
        grad_up_body,
        "grad_up",
        2,
        info,
        (normed, *dup),
        [whole(2, rows, D)] + [block] * 2,
        (shaped((2, 2, CH, CH)),) * 2 + (shaped((1, 2 * CH), f32),),
        [message, message, spec((1, CH), lambda j, *_: (0, j))],
        8 * rows * D * CH,
        deps=deps,
    )


def grad_down_body(info, hidden, c0, c1, kept, given):
    j = pl.program_id(0)
    y = (dot_tn(hidden[0], c0[...]) + dot_tn(hidden[1], c1[...])).astype(bf16)

    def store(target):
        for n in range(target.shape[1]):
            target[0, n] = y[CH * n : CH * (n + 1), :]

    @pl.when(j < 2)
    def _():
        store(given)

    @pl.when(j >= 2)
    def _():
        store(kept)


def grad_down(info, hidden, ct, deps=()):
    _, rows, units = hidden.shape
    count = units // CH
    block = spec(
        (rows, CH),
        lambda j, info: (0, info[2] ^ jnp.where(j < 2, 2 * j + 1, 2 * j - 4)),
    )
    return call(
        grad_down_body,
        "grad_down",
        N_DP,
        info,
        (hidden, *ct),
        [whole(2, rows, units)] + [block] * 2,
        (shaped((2, count, CH, CH)),) * 2,
        [
            spec((1, count, CH, CH), lambda j, *_: (jnp.maximum(j - 2, 0), 0, 0, 0)),
            spec((1, count, CH, CH), lambda j, *_: (jnp.minimum(j, 1), 0, 0, 0)),
        ],
        4 * rows * D * units,
        deps=deps,
    )


def store_by_rows(d, lefts, rights, kept, given):
    for target, which in ((given, GIVEN), (kept, KEPT)):
        for r, at in which:
            window = columns(d ^ r)
            y = sum(dot_tn(lefts[s, :, window], b) for s, b in enumerate(rights))
            target[at, 0] = y.astype(bf16)


def grad_out_query_body(info, normed, c0, c1, a0, a1, q0, q1, kept, given, sums):
    j = pl.program_id(0)
    d = info[2]

    @pl.when(j == 0)
    def _():
        lefts = (a0[...], a1[...])
        for target, which in ((given, GIVEN), (kept, KEPT)):
            for r, at in which:
                window = columns(d ^ r)
                y = sum(dot_tn(a, b[:, window]) for a, b in zip(lefts, (c0, c1)))
                target[at, 0] = y.astype(bf16)

    @pl.when(j == 1)
    def _():
        rights = (q0[...], q1[...])
        store_by_rows(d, normed, rights, kept, given)
        sums[...] = sum(jnp.sum(b.astype(f32), axis=0, keepdims=True) for b in rights)


def grad_out_query(info, normed, ct, att, dq, deps=()):
    rows = normed.shape[1]
    message = spec((2, 1, CH, CH), lambda j, *_: (0, j, 0, 0))
    return call(
        grad_out_query_body,
        "grad_out_query",
        2,
        info,
        (normed, *ct, *att, *dq),
        [whole(2, rows, D)] + [whole(rows, D)] * 2 + [whole(rows, CH)] * 4,
        (shaped((2, 2, CH, CH)),) * 2 + (shaped((1, CH), f32),),
        [message, message, whole(1, CH)],
        4 * rows * D * 2 * CH,
        deps=deps,
    )


def grad_key_value_body(info, normed, kv0, kv1, kept, given, sums):
    rights = (kv0[0], kv1[0])
    store_by_rows(info[2], normed, rights, kept, given)
    sums[0] = sum(jnp.sum(b.astype(f32), axis=0, keepdims=True) for b in rights)


def grad_key_value(info, normed, dkv, deps=()):
    rows = normed.shape[1]
    message = spec((2, 1, CH, CH), lambda j, *_: (0, j, 0, 0))
    pair = spec((1, rows, CH), lambda j, *_: (j, 0, 0))
    return call(
        grad_key_value_body,
        "grad_key_value",
        2,
        info,
        (normed, *dkv),
        [whole(2, rows, D)] + [pair] * 2,
        (shaped((2, 2, CH, CH)),) * 2 + (shaped((2, 1, CH), f32),),
        [message, message, spec((1, 1, CH), lambda j, *_: (j, 0, 0))],
        4 * rows * D * 2 * CH,
        deps=deps,
    )


def ring(array, step):
    return lax.ppermute(array, "tp", [(i, (i + step) % N_TP) for i in range(N_TP)])


class Gather:
    def __init__(self, own):
        self.own = own

    def forth(self, clock):
        self.own = clock.go(self.own)
        self.behind = ring(self.own, 1)

    def back(self):
        self.ahead = ring(self.own, -1)

    def sides(self, clock):
        self.forth(clock)
        self.ahead = ring(self.own, -1)

    def onward(self, clock):
        self.behind = clock.go(self.behind)
        self.far = ring(self.behind, 1)
        self.parts = (self.own, self.behind, self.ahead, self.far)


class Scatter:
    def __init__(self, chunks, clock):
        self.own, self.share, far, self.given = chunks
        self.far = ring(clock.go(far), 1)

    def backward(self, clock):
        self.back = ring(clock.go(self.given), -1)

    def onward(self, clock):
        both = (self.share.astype(f32) + self.far.astype(f32)).astype(bf16)
        self.near = ring(clock.go(both), 1)

    def total(self, clock):
        return self.own.astype(f32) + self.back.astype(f32) + clock.go(self.near).astype(f32)


class Reduction:
    def __init__(self, kept, given, clock, two):
        self.kept, self.two = kept, two
        self.got = swap(clock.go(given), "dp", 1, N_DP)
        self.moved, self.here, self.there = {}, {}, {}

    def add(self):
        total = (self.kept[1].astype(f32) + self.got[1].astype(f32)).astype(bf16)
        self.across = [total[n : n + 2] for n in range(0, total.shape[0], 2)]

    def over_x(self, n, clock):
        self.moved[n] = swap(clock.go(self.across[n]), "dp", 2, N_DP)

    def over_y(self, n, clock):
        at = slice(2 * n, 2 * n + 2)
        parts = (self.kept[0, at], self.got[0, at], clock.go(self.moved[n]))
        here = sum(a.astype(f32) for a in parts).astype(bf16)
        self.here[n] = here
        self.there[n] = swap(here, "ctx", 1, 2) if self.two else lax.psum(here, "ctx")

    def result(self, clock):
        blocks = []
        for n in sorted(self.here):
            total = clock.go(self.there[n]).astype(f32)
            if self.two:
                total = total + self.here[n].astype(f32)
            blocks += [*total]
        return blocks


def body(
    block_in,
    doc_starts,
    query_weight,
    key_weight,
    value_weight,
    output_weight,
    up_weight,
    down_weight,
    query_bias,
    key_bias,
    value_bias,
    up_bias,
    output_bias,
    norm_gain,
    norm_shift,
    cotangent,
):
    seqs, rows, _ = block_in.shape
    d, c, t = lax.axis_index("dp"), lax.axis_index("ctx"), lax.axis_index("tp")
    n_ctx = lax.axis_size("ctx")
    two = n_ctx == 2
    info = jnp.stack([t, c, d]).astype(jnp.int32)

    clock = Clock()

    x = Gather(block_in)
    x.forth(clock)
    small = jnp.concatenate(
        [query_bias, key_bias, value_bias, up_bias, output_bias, norm_gain, norm_shift]
    )
    size = small.size
    near = swap(small, "dp", 1, N_DP)
    flip = (d & 1) == 1
    pair = jnp.concatenate([jnp.where(flip, near, small), jnp.where(flip, small, near)])
    across = swap(pair, "dp", 2, N_DP)
    flip = (d & 2) == 2
    small_here = jnp.concatenate([jnp.where(flip, across, pair), jnp.where(flip, pair, across)])
    small_here = small_here.reshape(N_DP, size)

    def small_of(first, length):
        return small_here[:, first : first + length].reshape(1, -1)

    share = query_bias.size
    share_units = up_bias.size
    qkv_bias = jnp.concatenate([small_of(n * share, share) for n in range(3)], axis=1)
    up_shift = small_of(3 * share, share_units)
    output_shift = small_of(3 * share + share_units, share)
    gain_here = small_of(4 * share + share_units, share)
    shift_here = small_of(5 * share + share_units, share)
    both = jnp.concatenate([gain_here, shift_here], axis=0)
    others = [ring(both, -r) for r in range(1, N_TP)]
    wq_shard = jnp.concatenate([query_weight, key_weight, value_weight], axis=1)
    shards_q = Shards(tie(wq_shard, across), 0, d, c, two)
    shards_q.over_x(clock)
    shards_u = Shards(up_weight, 0, d, c, two, made=False)
    wo_shard = jnp.concatenate([output_weight, down_weight], axis=0)
    shards_o = Shards(wo_shard, 1, d, c, two)
    clock.sync(x.behind, shards_q.first, *others)

    x.back()
    x.onward(clock)
    shards_q.over_y(clock)
    shards_u.over_x(clock)
    gain_here = gain_here.astype(f32)
    circle = jnp.concatenate([both, *others] * 2, axis=1)
    gain_shift = lax.dynamic_slice_in_dim(circle, (N_TP - t) % N_TP * CH, D, 1)
    gain, shift = gain_shift[0:1], gain_shift[1:2]

    here = c * rows + jnp.arange(rows, dtype=jnp.int32)
    tables, opening = rotary_tables(doc_starts, here)
    blocks = 1 if two else n_ctx
    before, _ = rotary_tables(doc_starts, jnp.arange(blocks * rows, dtype=jnp.int32))
    before = [a.reshape(seqs, blocks, rows, 128) for a in before]

    clock.sync(shards_q.second, shards_u.first, x.ahead)

    shards_q.near_core(clock)
    shards_q.far_core(clock)
    shards_u.near_core(clock)
    clock.sync(shards_q.near, *shards_q.far_near, shards_u.near)

    shards_u.over_y(clock)
    shards_o.over_x(clock)
    ct = [Gather(cotangent[s]) for s in range(seqs)]
    clock.sync(x.far, shards_u.second, shards_o.first, *before, *(g.own for g in ct))

    def send_keys(s):
        kv[s] = clock.go(kv[s])
        if two:
            kvp[s] = lax.ppermute(kv[s], "ctx", [(0, 1)])[None]
        else:
            kvp[s] = lax.all_gather(kv[s], "ctx", axis=0, tiled=False)

    def back_out_step(s):
        return back_out(layout, info, s, ct[s].parts, shards_o.pieces, slope, deps=clock.marks)

    def attention_step(s):
        return attention(
            info,
            s,
            opening[:, None],
            q,
            kv[s],
            kvp[s],
            datt[s],
            tables,
            before,
            deps=clock.marks,
        )

    def returned(sent):
        if two:
            return lax.ppermute(clock.go(sent[0]), "ctx", [(1, 0)])
        return lax.psum_scatter(clock.go(sent), "ctx", scatter_dimension=0, tiled=False)

    def out_step(s):
        return project_out(
            layout, info, s, att[s], hidden, shards_o.pieces, deps=clock.marks
        )

    def back_in_step(s):
        return back_in(
            layout,
            info,
            s,
            x.parts,
            dq[s],
            dkv[s],
            dup[s],
            shards_q.pieces,
            shards_u.pieces,
            gain,
            avg,
            inv,
            deps=clock.marks,
        )

    layout = layout_of(two)
    kvp, datt, att, dq, dkv, dup, cf, out_bias_sum = ([None] * seqs for _ in range(8))

    shards_o.over_y(clock)
    shards_u.far_core(clock)
    ct[0].sides(clock)
    normed, avg, inv, q, *kv = norm_qkv(
        layout, info, x.parts, gain, shift, shards_q.pieces, qkv_bias, tables, deps=clock.marks
    )
    clock.sync(normed, *shards_u.far_near, ct[0].behind, ct[0].ahead)

    ct[0].onward(clock)
    ct[1].sides(clock)
    send_keys(0)
    hidden, slope = mlp_up(layout, info, normed, shards_u.pieces, up_shift, deps=clock.marks)
    clock.sync(hidden, ct[0].far, ct[1].behind, shards_o.second)

    shards_o.near_core(clock)
    shards_o.far_core(clock)
    clock.sync(shards_o.near, *shards_o.far_near)
    ct[1].onward(clock)
    send_keys(1)
    cf[0], out_bias_sum[0], datt[0], dup[0] = back_out_step(0)
    clock.sync(datt[0], kvp[0])

    att[0], dq[0], dkv_0, sent_0 = attention_step(0)
    clock.sync(att[0], ct[1].ahead, ct[1].far)

    sent_0 = returned(sent_0)
    cf[1], out_bias_sum[1], datt[1], dup[1] = back_out_step(1)
    clock.sync(datt[1], kvp[1])

    def grad_up_step(n):
        kept, given, sums = grad_up(info, normed, dup, n, deps=clock.marks)
        up_sums.append(sums)
        clock.sync(kept)
        return Reduction(kept, given, clock, two)

    up, up_sums = [], []
    up.append(grad_up_step(0))
    clock.sync(sent_0)
    dkv[0] = (dkv_0.astype(f32) + sent_0.astype(f32)).astype(bf16)
    up.append(grad_up_step(1))
    clock.sync(up[0].got)

    up[0].add()
    up[0].over_x(0, clock)
    down_kept, down_given = grad_down(info, hidden, cf, deps=clock.marks)
    clock.sync(down_kept, up[1].got)

    down = Reduction(down_kept, down_given, clock, two)
    up[1].add()
    up[1].over_x(0, clock)
    chunks_0 = out_step(0)
    clock.sync(chunks_0[0], up[0].moved[0], down.got)

    up[0].over_y(0, clock)
    down.add()
    down.over_x(0, clock)
    out_0 = Scatter(chunks_0, clock)
    out_0.backward(clock)
    att[1], dq[1], dkv_1, sent_1 = attention_step(1)
    clock.sync(att[1], up[1].moved[0], out_0.far, out_0.back)

    sent_1 = returned(sent_1)
    up[1].over_y(0, clock)
    out_0.onward(clock)
    head_kept, head_given, query_sum = grad_out_query(
        info, normed, cf, att, dq, deps=clock.marks
    )
    clock.sync(head_kept, out_0.near, up[0].there[0])

    head = Reduction(head_kept, head_given, clock, two)
    down.over_x(1, clock)
    chunks_0 = back_in_step(0)
    clock.sync(chunks_0[0], head.got, sent_1, down.moved[0])

    head.add()
    head.over_x(0, clock)
    down.over_y(0, clock)
    in_0 = Scatter(chunks_0, clock)
    in_0.backward(clock)
    dkv[1] = (dkv_1.astype(f32) + sent_1.astype(f32)).astype(bf16)
    pair_kept, pair_given, pair_sum = grad_key_value(info, normed, dkv, deps=clock.marks)
    clock.sync(pair_kept, up[1].there[0], down.moved[1])

    pair = Reduction(pair_kept, pair_given, clock, two)
    chunks_1 = out_step(1)
    clock.sync(chunks_1[0], pair.got, in_0.far, in_0.back, head.moved[0])

    pair.add()
    pair.over_x(0, clock)
    down.over_y(1, clock)
    in_0.onward(clock)
    out_1 = Scatter(chunks_1, clock)
    chunks_1 = back_in_step(1)
    clock.sync(chunks_1[0], in_0.near, down.there[0], pair.moved[0], out_1.far)

    in_1 = Scatter(chunks_1, clock)
    in_1.backward(clock)
    head.over_y(0, clock)
    out_1.backward(clock)
    clock.sync(in_1.far, in_1.back, down.there[1])

    in_1.onward(clock)
    out_1.onward(clock)
    pair.over_y(0, clock)
    clock.sync(in_1.near, out_1.near)

    block_out = jnp.stack([out_0.total(clock), out_1.total(clock)])
    normed_grad = [in_0.total(clock), in_1.total(clock)]
    block_out = (block_in.astype(f32) + block_out + output_shift.astype(f32)).astype(bf16)
    up_wg = jnp.concatenate(up[0].result(clock) + up[1].result(clock), axis=1)
    down_wg = jnp.concatenate(down.result(clock), axis=0)
    output_wg, query_wg = head.result(clock)
    key_wg, value_wg = pair.result(clock)

    def input_gradient(s):
        total = normed_grad[s]
        plain, cross = total[rows][:, None], total[rows + 1][:, None]
        standard = (block_in[s].astype(f32) - avg[s]) * inv[s]
        scaled = total[:rows] * gain_here
        return cotangent[s].astype(f32) + inv[s] * (scaled - plain / D - standard * cross / D)

    in_grad = jnp.stack([input_gradient(s) for s in range(seqs)])

    summed = jnp.concatenate(
        [
            query_sum.reshape(-1),
            pair_sum.reshape(-1),
            *(a.reshape(-1) for a in up_sums),
            sum(out_bias_sum).reshape(-1),
            sum(a[rows + 8 : rows + 10] for a in normed_grad).reshape(-1),
        ]
    )
    summed = summed + swap(summed, "dp", 1, N_DP)
    summed = summed + swap(summed, "dp", 2, N_DP)
    summed = summed + swap(summed, "ctx", 1, 2) if two else lax.psum(summed, "ctx")
    at = 0
    small_grads = []
    for size in (CH, CH, CH, N_DP * share_units, CH, CH, CH):
        part = summed[at : at + size]
        at += size
        share = size // N_DP
        small_grads.append(lax.dynamic_slice_in_dim(part, d * share, share, 0))
    query_bg, key_bg, value_bg, up_bg, output_bg, gain_g, shift_g = small_grads
    return (
        block_out,
        in_grad,
        query_wg,
        key_wg,
        value_wg,
        output_wg,
        up_wg,
        down_wg,
        query_bg,
        key_bg,
        value_bg,
        up_bg,
        output_bg,
        gain_g,
        shift_g,
    )


def solution(mesh):
    return jax.shard_map(
        body,
        mesh=mesh,
        in_specs=(
            P("dp", "ctx", "tp"),
            P("dp", None),
            P("dp", "tp"),
            P("dp", "tp"),
            P("dp", "tp"),
            P("tp", "dp"),
            P("dp", "tp"),
            P("tp", "dp"),
        )
        + (P(("tp", "dp")),) * 7
        + (P("dp", "ctx", "tp"),),
        out_specs=(
            P("dp", "ctx", "tp"),
            P("dp", "ctx", "tp"),
            P("dp", "tp"),
            P("dp", "tp"),
            P("dp", "tp"),
            P("tp", "dp"),
            P("dp", "tp"),
            P("tp", "dp"),
        )
        + (P(("tp", "dp")),) * 7,
        check_vma=False,
    )
```

```python
import functools
import math

import jax
import jax.numpy as jnp
from jax import lax
from jax.experimental import pallas as pl
from jax.experimental.pallas import tpu as pltpu
from jax.sharding import PartitionSpec as P

HEAD_DIM = 64
ROT = 32
D = 2048
N_DP = 4
N_TP = 4
CH = D // N_TP
EPS = 1e-05
NEG = -1e30
VMEM = 56 * 2**20
COST = 0.02

bf16 = jnp.bfloat16
f32 = jnp.float32


def dot_nn(a, b):
    return lax.dot_general(a, b, (((1,), (0,)), ((), ())), preferred_element_type=f32)


def dot_nt(a, b):
    return lax.dot_general(a, b, (((1,), (1,)), ((), ())), preferred_element_type=f32)


def dot_tn(a, b):
    return lax.dot_general(a, b, (((0,), (0,)), ((), ())), preferred_element_type=f32)


def spec(block, index):
    return pl.BlockSpec(block, index)


def whole(*block):
    zeros = (0,) * len(block)
    return pl.BlockSpec(block, lambda g, *_: zeros)


def one_of(s, *block):
    zeros = (0,) * len(block)
    return pl.BlockSpec((None, *block), lambda g, *_: (s, *zeros))


def shaped(shape, dtype=bf16):
    return jax.ShapeDtypeStruct(tuple(shape), dtype)


ANYWHERE = pl.BlockSpec(memory_space=pl.ANY)


def call(body, name, grid, info, ins, in_specs, outs, out_specs, flops, scratch=(), deps=()):
    moved = sum(math.prod(a.shape) * a.dtype.itemsize for a in (*ins, *jax.tree.leaves(outs)))
    first, last = 1 + len(ins), 1 + len(ins) + len(deps)

    def without_deps(*refs):
        body(*refs[:first], *refs[last:])

    return pl.pallas_call(
        without_deps,
        grid_spec=pltpu.PrefetchScalarGridSpec(
            num_scalar_prefetch=1,
            grid=(grid,),
            in_specs=[*in_specs, *[ANYWHERE] * len(deps)],
            out_specs=out_specs,
            scratch_shapes=list(scratch),
        ),
        out_shape=outs,
        compiler_params=pltpu.CompilerParams(vmem_limit_bytes=VMEM),
        cost_estimate=pl.CostEstimate(
            flops=int(flops * COST), bytes_accessed=int(moved * COST), transcendentals=0
        ),
        name=name,
    )(info, *ins, *deps)


def tie(value, *deps):
    def nothing(*refs):
        del refs

    return pl.pallas_call(
        nothing,
        in_specs=[ANYWHERE] * (1 + len(deps)),
        out_specs=ANYWHERE,
        out_shape=shaped(value.shape, value.dtype),
        input_output_aliases={0: 0},
        cost_estimate=pl.CostEstimate(flops=0, bytes_accessed=0, transcendentals=0),
        name="tie",
    )(value, *deps)


def columns(index, width=CH):
    return pl.ds(pl.multiple_of(index * width, width), width)


def layout_of(two):
    if two:
        halves = [("c", CH // 2), ("other", CH // 2)]
    else:
        halves = [("", CH)]
    return [(0, "", CH), (1, "", CH)] + [(r, *half) for r in (2, 3) for half in halves]


def piece_offset(info, half):
    return {"": 0, "c": info[1], "other": 1 - info[1]}[half] * (CH // 2)


def piece_window(info, piece):
    r, half, size = piece
    start = (info[2] ^ r) * CH + piece_offset(info, half)
    return pl.ds(pl.multiple_of(start, size), size)


class Clock:
    def __init__(self):
        self.marks = ()

    def go(self, value):
        return tie(value, *self.marks) if self.marks else value

    def sync(self, *arrays):
        def nothing(*refs):
            del refs

        self.marks = (
            pl.pallas_call(
                nothing,
                in_specs=[ANYWHERE] * (len(arrays) + len(self.marks)),
                out_specs=ANYWHERE,
                out_shape=shaped((8, 128), f32),
                cost_estimate=pl.CostEstimate(flops=0, bytes_accessed=0, transcendentals=0),
                name="sync",
            )(*arrays, *self.marks),
        )


def swap(array, axis, bit, size):
    return lax.ppermute(array, axis, [(i, i ^ bit) for i in range(size)])


class Shards:
    def __init__(self, own, axis, d, c, two, made=True):
        self.own, self.two, self.made = own, two, made
        size = own.shape[axis] // 2
        self.part = lax.dynamic_slice_in_dim(own, c * size, size, axis) if two else own

    def near_core(self, clock):
        self.own = clock.go(self.own) if self.made else self.own
        self.near = swap(self.own, "dp", 1, N_DP)

    def over_x(self, clock):
        self.first = swap(clock.go(self.part), "dp", 2, N_DP)

    def over_y(self, clock):
        self.first = clock.go(self.first)
        self.second = swap(self.first, "ctx", 1, 2) if self.two else self.first

    def far_core(self, clock):
        self.first = clock.go(self.first)
        far = [self.first]
        if self.two:
            self.second = clock.go(self.second)
            far.append(self.second)
        self.far_near = [swap(a, "dp", 1, N_DP) for a in far]
        self.pieces = [self.own, self.near, *far, *self.far_near]


def rotary_tables(starts, positions):
    before = starts[:, None, :] <= positions[None, :, None]
    opening = jnp.max(jnp.where(before, starts[:, None, :], 0), axis=2)
    relative = (positions[None, :] - opening).astype(f32)
    half = ROT // 2
    lane = jnp.arange(128, dtype=jnp.int32) % HEAD_DIM
    frequency = jnp.exp((lane % half).astype(f32) * (-math.log(10000.0) / half))
    angles = relative[:, :, None] * jnp.where(lane < ROT, frequency, 0.0)
    sine = jnp.sin(angles)
    return (
        jnp.cos(angles),
        jnp.where(lane < half, -sine, 0.0),
        jnp.where(lane >= half, sine, 0.0),
    ), opening


def add_rounded(a, b):
    return (a.astype(f32) + b.astype(f32)).astype(bf16)


def turn(x, own, up, down):
    return x * own + pltpu.roll(x, 112, 1) * up + pltpu.roll(x, 16, 1) * down


def turn_back(x, own, up, down):
    return x * own - pltpu.roll(x, 112, 1) * up - pltpu.roll(x, 16, 1) * down


def stream_pieces(layout, info, sources, held, sems, axis, blocks):
    j = pl.program_id(0)

    def copies(block):
        cut = pl.ds(pl.multiple_of(block * CH, CH), CH)
        for n, (piece, source) in enumerate(zip(layout, sources)):
            window = piece_window(info, piece)
            if axis == 0:
                pair = source.at[:, cut], held.at[window, cut]
            else:
                pair = source.at[cut, :], held.at[cut, window]
            yield pltpu.make_async_copy(*pair, sems.at[block, n])

    @pl.when(j == 0)
    def _():
        for block in range(blocks):
            for copy in copies(block):
                copy.start()

    for copy in copies(j):
        copy.wait()


def norm_qkv_body(layout, info, x0, xa, xc, xb, gain, shift, bias, own, up, down, *refs):
    *w, normed, stats, q, kv0, kv1, columns_held, held, sems = refs
    j = pl.program_id(0)
    t = info[0]
    seqs, rows, _ = x0.shape
    stream_pieces(layout, info, w, held, sems, 0, 3)

    @pl.when(j == 0)
    def _():
        parts = [(x0, t), (xa, (t + 3) % N_TP), (xc, (t + 1) % N_TP), (xb, (t + 2) % N_TP)]
        tile = 128

        def rows_of(i, carry):
            s = i // (rows // tile)
            window = pl.ds(pl.multiple_of((i % (rows // tile)) * tile, tile), tile)
            x = [part[s, window, :].astype(f32) for part, _ in parts]
            average = sum(jnp.sum(a, axis=1, keepdims=True) for a in x) * (1.0 / D)
            x = [a - average for a in x]
            variance = sum(jnp.sum(a * a, axis=1, keepdims=True) for a in x) * (1.0 / D)
            root = lax.rsqrt(variance + EPS)
            columns_held[s, window, 0:1] = average
            columns_held[s, window, 1:2] = root
            for a, (_, index) in zip(x, parts):
                at = columns(index)
                y = a * root * gain[:, at].astype(f32) + shift[:, at].astype(f32)
                normed[s, window, at] = y.astype(bf16)
            return carry

        columns_held[...] = jnp.zeros(columns_held.shape, f32)
        lax.fori_loop(0, seqs * rows // tile, rows_of, 0)
        for s in range(seqs):
            stats[s] = columns_held[s].T[: stats.shape[1]]

    for s, kv in ((0, kv0), (1, kv1)):
        y = dot_nn(normed[s], held[:, columns(j)]) + bias[...].astype(f32)

        def rotated(s=s, y=y):
            parts = [
                turn(y[:, 128 * n : 128 * n + 128], own[s], up[s], down[s])
                for n in range(CH // 128)
            ]
            return jnp.concatenate(parts, axis=1).astype(bf16)

        @pl.when(j == 0)
        def _(s=s, rotated=rotated):
            q[s] = rotated()

        @pl.when(j == 1)
        def _(kv=kv, rotated=rotated):
            kv[0] = rotated()

        @pl.when(j == 2)
        def _(kv=kv, y=y):
            kv[0] = y.astype(bf16)


def norm_qkv(layout, info, parts, gain, shift, w, bias, tables, deps=()):
    seqs, rows, _ = parts[0].shape
    outs = (
        shaped((seqs, rows, D)),
        shaped((seqs, 8, rows), f32),
        shaped((seqs, rows, CH)),
        shaped((2, rows, CH)),
        shaped((2, rows, CH)),
    )
    pair = spec((1, rows, CH), lambda j, *_: (jnp.maximum(j - 1, 0), 0, 0))
    return call(
        functools.partial(norm_qkv_body, layout),
        "norm_qkv",
        3,
        info,
        (*parts, gain, shift, bias, *tables, *w),
        [whole(seqs, rows, CH)] * 4
        + [whole(1, D)] * 2
        + [spec((1, CH), lambda j, *_: (0, j))]
        + [whole(seqs, rows, 128)] * 3
        + [ANYWHERE] * len(w),
        outs,
        [
            whole(seqs, rows, D),
            whole(seqs, 8, rows),
            whole(seqs, rows, CH),
            pair,
            pair,
        ],
        2 * seqs * rows * D * 3 * CH,
        [
            pltpu.VMEM((seqs, rows, 128), f32),
            pltpu.VMEM((D, 3 * CH), bf16),
            pltpu.SemaphoreType.DMA((3, len(w))),
        ],
        deps=deps,
    )


def mlp_up_body(layout, info, normed, bias, *refs):
    *w, hidden, grad, held, sems = refs
    j = pl.program_id(0)
    stream_pieces(layout, info, w, held, sems, 0, held.shape[1] // CH)
    root = math.sqrt(2.0 / math.pi)
    for s in range(normed.shape[0]):
        u = dot_nn(normed[s], held[:, columns(j)]) + bias[...].astype(f32)
        square = u * u
        t = jnp.tanh(u * (root + (root * 0.044715) * square))
        half = 0.5 + 0.5 * t
        hidden[s] = (u * half).astype(bf16)
        slope = root + (3 * 0.044715 * root) * square
        grad[s] = (half + (0.5 * u) * (1.0 - t * t) * slope).astype(bf16)


def mlp_up(layout, info, normed, w, bias, deps=()):
    seqs, rows, _ = normed.shape
    units = w[0].shape[1]
    block = spec((seqs, rows, CH), lambda j, *_: (0, 0, j))
    return call(
        functools.partial(mlp_up_body, layout),
        "mlp_up",
        units // CH,
        info,
        (normed, bias, *w),
        [whole(seqs, rows, D), spec((1, CH), lambda j, *_: (0, j))] + [ANYWHERE] * len(w),
        (shaped((seqs, rows, units)),) * 2,
        [block] * 2,
        2 * seqs * rows * D * units,
        [pltpu.VMEM((D, units), bf16), pltpu.SemaphoreType.DMA((units // CH, len(w)))],
        deps=deps,
    )


def back_out_body(layout, info, c0, ca, cc, cb, slope, *refs):
    *w, cf, bias_grad, datt, dup, held, sems = refs
    j = pl.program_id(0)
    t = info[0]
    seqs = c0.shape[0]
    stream_pieces(layout, info, w, held, sems, 1, held.shape[0] // CH)

    @pl.when(j == 0)
    def _():
        for part, step in ((c0, 0), (ca, 3), (cc, 1), (cb, 2)):
            cf[:, :, columns((t + step) % N_TP)] = part[...]
        bias_grad[...] = sum(
            jnp.sum(c0[s].astype(f32), axis=0, keepdims=True) for s in range(seqs)
        )

    for s in range(seqs):
        y = dot_nt(cf[s], held[columns(j), :])

        @pl.when(j == 0)
        def _(s=s, y=y):
            datt[s] = y.astype(bf16)

        @pl.when(j > 0)
        def _(s=s, y=y):
            dup[s] = (y * slope[s].astype(f32)).astype(bf16)


def back_out(layout, info, parts, w, slope, deps=()):
    seqs, rows, units = slope.shape
    later = spec((seqs, rows, CH), lambda j, *_: (0, 0, jnp.maximum(j - 1, 0)))
    return call(
        functools.partial(back_out_body, layout),
        "back_out",
        1 + units // CH,
        info,
        (*parts, slope, *w),
        [whole(seqs, rows, CH)] * 4 + [later] + [ANYWHERE] * len(w),
        (
            shaped((seqs, rows, D)),
            shaped((1, CH), f32),
            shaped((seqs, rows, CH)),
            shaped((seqs, rows, units)),
        ),
        [whole(seqs, rows, D), whole(1, CH), whole(seqs, rows, CH), later],
        2 * seqs * rows * D * (CH + units),
        [
            pltpu.VMEM((CH + units, D), bf16),
            pltpu.SemaphoreType.DMA((1 + units // CH, len(w))),
        ],
        deps=deps,
    )


def attention_body(
    blocks, info, low, q, kv, kvp, do, own, up, down, ownp, upp, downp,
    att, dq, dkv, dkvp, scores, probs,
):
    rows = q.shape[0]
    before, start = info[1], info[1] * rows
    lane = lax.broadcasted_iota(jnp.int32, (rows, 128), 1)
    key_row = lax.broadcasted_iota(jnp.int32, (rows, 1), 0)
    query_at = start + lax.broadcasted_iota(jnp.int32, (1, rows), 1)
    first = low[0]
    do_t = do[...].astype(f32).T
    nothing = jnp.zeros((), bf16)
    outputs = []
    for head in range(2):
        mine = (lane < HEAD_DIM) if head == 0 else (lane >= HEAD_DIM)
        half = slice(HEAD_DIM * head, HEAD_DIM * (head + 1))
        qh = jnp.where(mine, q[...] * jnp.asarray(HEAD_DIM**-0.5, bf16), nothing)
        dh = jnp.where(mine, do[...], nothing)

        key_at = start + key_row
        s = dot_nt(kv[0], qh)
        s = jnp.where((key_at >= first) & (key_at <= query_at), s, NEG)
        scores[blocks] = s
        peak = jnp.max(s, axis=0, keepdims=True)

        def score(n, peak):
            s = dot_nt(kvp[n, 0], qh)
            s = jnp.where(n * rows + key_row >= first, s, NEG)
            scores[n] = s
            return jnp.maximum(peak, jnp.max(s, axis=0, keepdims=True))

        peak = lax.fori_loop(0, before, score, peak)

        def expo(n, total):
            e = jnp.exp(scores[n] - peak)
            scores[n] = e
            return total + jnp.sum(e, axis=0, keepdims=True)

        total = expo(blocks, jnp.zeros((1, rows), f32))
        total = lax.fori_loop(0, before, expo, total)
        scale = 1.0 / total

        def weigh(n, values):
            p = (scores[n] * scale).astype(bf16)
            probs[n] = p
            return dot_tn(values, p)

        out_t = weigh(blocks, kv[1])
        out_t = lax.fori_loop(0, before, lambda n, acc: acc + weigh(n, kvp[n, 1]), out_t)
        delta = jnp.sum(out_t[half] * do_t[half], axis=0, keepdims=True)

        def back(n, keys, values):
            dp = dot_nt(values, dh)
            ds = ((scores[n] * scale) * (dp - delta)).astype(bf16)
            return dot_nn(ds, qh), dot_nn(probs[n], dh), dot_tn(keys, ds)

        dk, dv, dq_t = back(blocks, kv[0], kv[1])
        if head == 0:
            dk_sum, dv_sum = dk, dv
        else:
            dk_sum, dv_sum = dk_sum + dk, dv_sum + dv

        def back_before(n, acc):
            dk, dv, more = back(n, kvp[n, 0], kvp[n, 1])
            dk = turn_back(dk, ownp[n], upp[n], downp[n])
            if head == 0:
                dkvp[n, 0] = dk.astype(bf16)
                dkvp[n, 1] = dv.astype(bf16)
            else:
                dkvp[n, 0] = (dkvp[n, 0].astype(f32) + dk).astype(bf16)
                dkvp[n, 1] = (dkvp[n, 1].astype(f32) + dv).astype(bf16)
            return acc + more

        dq_t = lax.fori_loop(0, before, back_before, dq_t)
        outputs.append((out_t[half], dq_t[half]))

    def clear(n, carry):
        dkvp[n] = jnp.zeros(dkvp.shape[1:], bf16)
        return carry

    lax.fori_loop(before, blocks, clear, 0)
    att[...] = jnp.concatenate([outputs[0][0], outputs[1][0]], axis=0).T.astype(bf16)
    grad = jnp.concatenate([outputs[0][1], outputs[1][1]], axis=0).T * HEAD_DIM**-0.5
    dq[...] = turn_back(grad, own[...], up[...], down[...]).astype(bf16)
    dkv[0] = turn_back(dk_sum, own[...], up[...], down[...]).astype(bf16)
    dkv[1] = dv_sum.astype(bf16)


def attention_two_body(
    info, low, q, kv, kvp, do, own, up, down, ownp, upp, downp, att, dq, dkv, dkvp
):
    rows = q.shape[0]
    part = rows // 2
    before, start = info[1], info[1] * rows

    def tail(x, skipped):
        return x[:, skipped:] if skipped else x

    def merge(acc, x, skipped, op):
        if acc is None:
            return x
        if not skipped:
            return op(acc, x)
        return jnp.concatenate([acc[:, :skipped], op(acc[:, skipped:], x)], axis=1)

    def run(with_before):
        lane = lax.broadcasted_iota(jnp.int32, (rows, 128), 1)
        key_row = lax.broadcasted_iota(jnp.int32, (part, 1), 0)
        query_at = start + lax.broadcasted_iota(jnp.int32, (1, rows), 1)
        first = low[...]
        do_t = do[...].astype(f32).T
        nothing = jnp.zeros((), bf16)
        blocks = []
        for n in range(2):
            if with_before:
                blocks.append((kvp.at[0], n * part, 0, False))
        for n in range(2):
            blocks.append((kv, n * part, n * part, True))
        outputs = []
        dk_sum, dv_sum = [0.0] * len(blocks), [0.0] * len(blocks)
        for head in range(2):
            mine = (lane < HEAD_DIM) if head == 0 else (lane >= HEAD_DIM)
            half = slice(HEAD_DIM * head, HEAD_DIM * (head + 1))
            qh = jnp.where(mine, q[...] * jnp.asarray(HEAD_DIM**-0.5, bf16), nothing)
            dh = jnp.where(mine, do[...], nothing)
            scores, peak = [], None
            for ref, row, skip, here in blocks:
                s = dot_nt(ref[0, row : row + part], qh[skip:])
                key_at = (start if here else start - rows) + row + key_row
                allowed = key_at >= tail(first, skip)
                if here:
                    allowed = allowed & (key_at <= tail(query_at, skip))
                s = jnp.where(allowed, s, NEG)
                scores.append(s)
                peak = merge(peak, jnp.max(s, axis=0, keepdims=True), skip, jnp.maximum)
            terms, total = [], None
            for s, (_, _, skip, _) in zip(scores, blocks):
                e = jnp.exp(s - tail(peak, skip))
                terms.append(e)
                total = merge(total, jnp.sum(e, axis=0, keepdims=True), skip, jnp.add)
            scale = 1.0 / total
            probs, rounded, out_t = [], [], None
            for e, (ref, row, skip, _) in zip(terms, blocks):
                p = e * tail(scale, skip)
                pb = p.astype(bf16)
                probs.append(p)
                rounded.append(pb)
                out_t = merge(out_t, dot_tn(ref[1, row : row + part], pb), skip, jnp.add)
            delta = jnp.sum(out_t[half] * do_t[half], axis=0, keepdims=True)
            dq_t = None
            for n, (ref, row, skip, _) in enumerate(blocks):
                dp = dot_nt(ref[1, row : row + part], dh[skip:])
                ds = (probs[n] * (dp - tail(delta, skip))).astype(bf16)
                dv_sum[n] = dv_sum[n] + dot_nn(rounded[n], dh[skip:])
                dk_sum[n] = dk_sum[n] + dot_nn(ds, qh[skip:])
                dq_t = merge(dq_t, dot_tn(ref[0, row : row + part], ds), skip, jnp.add)
            outputs.append((out_t[half], dq_t[half]))
        att[...] = jnp.concatenate([outputs[0][0], outputs[1][0]], axis=0).T.astype(bf16)
        grad = jnp.concatenate([outputs[0][1], outputs[1][1]], axis=0).T * HEAD_DIM**-0.5
        dq[...] = turn_back(grad, own[...], up[...], down[...]).astype(bf16)
        dk = jnp.concatenate(dk_sum[-2:], axis=0)
        dkv[0] = turn_back(dk, own[...], up[...], down[...]).astype(bf16)
        dkv[1] = jnp.concatenate(dv_sum[-2:], axis=0).astype(bf16)
        if with_before:
            dk = jnp.concatenate(dk_sum[:2], axis=0)
            dkvp[0, 0] = turn_back(dk, ownp[0], upp[0], downp[0]).astype(bf16)
            dkvp[0, 1] = jnp.concatenate(dv_sum[:2], axis=0).astype(bf16)
        else:
            dkvp[...] = jnp.zeros(dkvp.shape, bf16)

    @pl.when(before == 0)
    def _():
        run(False)

    @pl.when(before > 0)
    def _():
        run(True)


def attention(info, s, low, q, kv, kvp, do, tables, tables_before, deps=()):
    _, rows, width = q.shape
    blocks = kvp.shape[0]
    token = spec((rows, 128), lambda g, *_: (0, g))
    query = spec((None, rows, 128), lambda g, *_: (s, 0, g))
    pair = spec((2, rows, 128), lambda g, *_: (0, 0, g))
    pairs = spec((blocks, 2, rows, 128), lambda g, *_: (0, 0, 0, g))
    return call(
        attention_two_body if blocks == 1 else functools.partial(attention_body, blocks),
        "attention",
        width // 128,
        info,
        (low, q, kv, kvp, do, *tables, *tables_before),
        [one_of(s, 1, rows), query, pair, pairs, query]
        + [one_of(s, rows, 128)] * 3
        + [one_of(s, blocks, rows, 128)] * 3,
        (
            shaped((rows, width)),
            shaped((rows, width)),
            shaped((2, rows, width)),
            shaped((blocks, 2, rows, width)),
        ),
        [token, token, pair, pairs],
        48 * rows * rows * width,
        []
        if blocks == 1
        else [
            pltpu.VMEM((blocks + 1, rows, rows), f32),
            pltpu.VMEM((blocks + 1, rows, rows), bf16),
        ],
        deps=deps,
    )


TAIL = 16


def fetch_pieces(layout, sources, targets, sems, axis):
    copies = [[] for _ in range(N_DP)]
    at = [r * CH for r in range(N_DP)]
    n = 0
    for group, target in zip(sources, targets):
        at = [r * CH for r in range(N_DP)]
        for (r, _, size), source in zip(layout, group):
            window = pl.ds(at[r], size)
            place = target.at[window, :] if axis == 0 else target.at[:, window]
            copies[r].append(pltpu.make_async_copy(source, place, sems.at[n]))
            at[r] += size
            n += 1
    return copies


def with_chunk(layout, info, copies, work):
    j = pl.program_id(0)

    @pl.when(j == 0)
    def _():
        for group in copies:
            for copy in group:
                copy.start()

    for r in range(N_DP):

        @pl.when(j == r)
        def _(r=r):
            for copy in copies[r]:
                copy.wait()
            at = r * CH
            for s, half, size in layout:
                if s == r:
                    offset = pl.multiple_of(piece_offset(info, half), size)
                    work(pl.ds(at, size), pl.ds(offset, size))
                    at += size


def chunk_now(info):
    return ((info[2] ^ pl.program_id(0)) + N_TP - info[0]) % N_TP


def out_body(layout, info, att, hidden, *refs):
    count = len(layout)
    w, outs = refs[:count], refs[count : count + N_TP]
    held, y, sems = refs[count + N_TP :]

    def work(place, window):
        part = dot_nn(att[...], held[:CH, place]) + dot_nn(hidden[...], held[CH:, place])
        y[:, window] = part.astype(bf16)

    with_chunk(layout, info, fetch_pieces(layout, [w], [held], sems, 1), work)
    for r in range(N_TP):

        @pl.when(chunk_now(info) == r)
        def _(r=r):
            outs[r][...] = y[...]


def project_out(layout, info, s, att, hidden, w, deps=()):
    _, rows, units = hidden.shape
    return call(
        functools.partial(out_body, layout),
        "project_out",
        N_TP,
        info,
        (att, hidden, *w),
        [whole(rows, CH), one_of(s, rows, units)] + [ANYWHERE] * len(w),
        (shaped((rows, CH)),) * N_TP,
        [whole(rows, CH)] * N_TP,
        2 * rows * D * (CH + units),
        [
            pltpu.VMEM((CH + units, D), bf16),
            pltpu.VMEM((rows, CH), bf16),
            pltpu.SemaphoreType.DMA((len(w),)),
        ],
        deps=deps,
    )


def back_in_body(layout, info, x0, xa, xc, xb, dq, dkv, back, dup, gain, stats, *refs):
    count = len(layout)
    wq, wu = refs[:count], refs[count : 2 * count]
    *chunks, held_q, held_u, y, xs, row_sums, column_sums, both, sems = refs[2 * count :]
    j = pl.program_id(0)
    rows = dq.shape[0]

    @pl.when(j == 0)
    def _():
        both[...] = add_rounded(dkv[...], back[...])


    def work(place, window):
        part = dot_nt(dup[...], held_u[place, :])
        part = part + dot_nt(dq[...], held_q[place, :CH])
        part = part + dot_nt(both[0], held_q[place, CH : 2 * CH])
        y[:, window] = part + dot_nt(both[1], held_q[place, 2 * CH :])

    copies = fetch_pieces(layout, [wq, wu], [held_q, held_u], sems, 0)
    with_chunk(layout, info, copies, work)
    for r, part in enumerate((x0, xc, xb, xa)):

        @pl.when(chunk_now(info) == r)
        def _(r=r, part=part):
            chunks[r][:rows, :] = y[...].astype(bf16)
            xs[...] = part[...]

    total = y[...]
    turned = stats[...].T
    standard = (xs[...].astype(f32) - turned[:, 0:1]) * turned[:, 1:2]
    cross = total * standard
    weight = gain[...].astype(f32)

    @pl.when(j == 0)
    def _():
        row_sums[...] = jnp.zeros(row_sums.shape, f32)
        column_sums[...] = jnp.zeros(column_sums.shape, f32)

    both = jnp.concatenate(
        [jnp.sum(cross, axis=0, keepdims=True), jnp.sum(total, axis=0, keepdims=True)], axis=0
    )
    column_sums[chunk_now(info), 0:2, :] = both
    row_sums[:, 0:1] += jnp.sum(total * weight, axis=1, keepdims=True)
    row_sums[:, 1:2] += jnp.sum(cross * weight, axis=1, keepdims=True)

    @pl.when(j == N_TP - 1)
    def _():
        turned = row_sums[...].T[: TAIL // 2]
        for r, chunk in enumerate(chunks):
            chunk[rows:, :] = jnp.concatenate([turned, column_sums[r]], axis=0).astype(bf16)


def back_in(layout, info, s, parts, dq, dkv, back, dup, wq, wu, gain, stats, deps=()):
    _, rows, units = dup.shape
    return call(
        functools.partial(back_in_body, layout),
        "back_in",
        N_TP,
        info,
        (*parts, dq, dkv, back, dup, gain, stats, *wq, *wu),
        [one_of(s, rows, CH)] * 4
        + [
            whole(rows, CH),
            whole(2, rows, CH),
            whole(2, rows, CH),
            one_of(s, rows, units),
            spec((1, CH), lambda j, info: (0, info[2] ^ j)),
            one_of(s, 8, rows),
        ]
        + [ANYWHERE] * (2 * len(wq)),
        (shaped((rows + TAIL, CH)),) * N_TP,
        [whole(rows + TAIL, CH)] * N_TP,
        2 * rows * D * (3 * CH + units),
        [
            pltpu.VMEM((D, 3 * CH), bf16),
            pltpu.VMEM((D, units), bf16),
            pltpu.VMEM((rows, CH), f32),
            pltpu.VMEM((rows, CH), bf16),
            pltpu.VMEM((rows, 128), f32),
            pltpu.VMEM((N_TP, TAIL // 2, CH), f32),
            pltpu.VMEM((2, rows, CH), bf16),
            pltpu.SemaphoreType.DMA((2 * len(wq),)),
        ],
        deps=deps,
    )


KEPT = ((0, 0), (2, 1))
GIVEN = ((1, 0), (3, 1))


def grad_up_body(info, normed, dup, kept, given, sums):
    d = info[2]
    rights = (dup[0], dup[1])
    store_by_rows(d, normed, rights, kept, given)
    sums[...] = sum(jnp.sum(b.astype(f32), axis=0, keepdims=True) for b in rights)


def grad_up(info, normed, dup, n, deps=()):
    rows = dup.shape[1]
    block = spec((2, rows, CH), lambda j, *_: (0, 0, 2 * n + j))
    message = spec((2, 1, CH, CH), lambda j, *_: (0, j, 0, 0))
    return call(
        grad_up_body,
        "grad_up",
        2,
        info,
        (normed, dup),
        [whole(2, rows, D), block],
        (shaped((2, 2, CH, CH)),) * 2 + (shaped((1, 2 * CH), f32),),
        [message, message, spec((1, CH), lambda j, *_: (0, j))],
        8 * rows * D * CH,
        deps=deps,
    )


def grad_down_body(info, hidden, ct, kept, given):
    j = pl.program_id(0)
    y = (dot_tn(hidden[0], ct[0]) + dot_tn(hidden[1], ct[1])).astype(bf16)

    def store(target):
        for n in range(target.shape[1]):
            target[0, n] = y[CH * n : CH * (n + 1), :]

    @pl.when(j < 2)
    def _():
        store(given)

    @pl.when(j >= 2)
    def _():
        store(kept)


def grad_down(info, hidden, ct, deps=()):
    _, rows, units = hidden.shape
    count = units // CH
    block = spec(
        (2, rows, CH),
        lambda j, info: (0, 0, info[2] ^ jnp.where(j < 2, 2 * j + 1, 2 * j - 4)),
    )
    return call(
        grad_down_body,
        "grad_down",
        N_DP,
        info,
        (hidden, ct),
        [whole(2, rows, units), block],
        (shaped((2, count, CH, CH)),) * 2,
        [
            spec((1, count, CH, CH), lambda j, *_: (jnp.maximum(j - 2, 0), 0, 0, 0)),
            spec((1, count, CH, CH), lambda j, *_: (jnp.minimum(j, 1), 0, 0, 0)),
        ],
        4 * rows * D * units,
        deps=deps,
    )


def store_by_rows(d, lefts, rights, kept, given):
    for target, which in ((given, GIVEN), (kept, KEPT)):
        for r, at in which:
            window = columns(d ^ r)
            y = sum(dot_tn(lefts[s, :, window], b) for s, b in enumerate(rights))
            target[at, 0] = y.astype(bf16)


def grad_out_query_body(info, normed, ct, a0, a1, q0, q1, kept, given, sums):
    j = pl.program_id(0)
    d = info[2]

    @pl.when(j == 0)
    def _():
        lefts = (a0[...], a1[...])
        for target, which in ((given, GIVEN), (kept, KEPT)):
            for r, at in which:
                window = columns(d ^ r)
                y = sum(dot_tn(a, ct[s, :, window]) for s, a in enumerate(lefts))
                target[at, 0] = y.astype(bf16)

    @pl.when(j == 1)
    def _():
        rights = (q0[...], q1[...])
        store_by_rows(d, normed, rights, kept, given)
        sums[...] = sum(jnp.sum(b.astype(f32), axis=0, keepdims=True) for b in rights)


def grad_out_query(info, normed, ct, att, dq, deps=()):
    rows = normed.shape[1]
    message = spec((2, 1, CH, CH), lambda j, *_: (0, j, 0, 0))
    return call(
        grad_out_query_body,
        "grad_out_query",
        2,
        info,
        (normed, ct, *att, *dq),
        [whole(2, rows, D)] * 2 + [whole(rows, CH)] * 4,
        (shaped((2, 2, CH, CH)),) * 2 + (shaped((1, CH), f32),),
        [message, message, whole(1, CH)],
        4 * rows * D * 2 * CH,
        deps=deps,
    )


def grad_key_value_body(info, normed, kv0, back0, kv1, back1, kept, given, sums):
    rights = (add_rounded(kv0[0], back0[0]), add_rounded(kv1[0], back1[0]))
    store_by_rows(info[2], normed, rights, kept, given)
    sums[0] = sum(jnp.sum(b.astype(f32), axis=0, keepdims=True) for b in rights)


def grad_key_value(info, normed, dkv, sent, deps=()):
    rows = normed.shape[1]
    message = spec((2, 1, CH, CH), lambda j, *_: (0, j, 0, 0))
    pair = spec((1, rows, CH), lambda j, *_: (j, 0, 0))
    return call(
        grad_key_value_body,
        "grad_key_value",
        2,
        info,
        (normed, dkv[0], sent[0], dkv[1], sent[1]),
        [whole(2, rows, D)] + [pair] * 4,
        (shaped((2, 2, CH, CH)),) * 2 + (shaped((2, 1, CH), f32),),
        [message, message, spec((1, 1, CH), lambda j, *_: (j, 0, 0))],
        4 * rows * D * 2 * CH,
        deps=deps,
    )


def finish_blocks_body(info, *refs):
    *sums, out = refs
    j = pl.program_id(0)
    for n in range(len(sums) // 2):
        here, there = sums[2 * n : 2 * n + 2]

        @pl.when((j >= 2 * n) & (j < 2 * n + 2))
        def _(here=here, there=there):
            out[...] = here[0].astype(f32) + there[0].astype(f32)


def finish_blocks(info, sums, axis, deps=()):
    count = len(sums)
    arrays = [a for pair in sums for a in pair]
    blocks = [
        spec((1, CH, CH), lambda j, _, n=n: (jnp.clip(j - 2 * n, 0, 1), 0, 0))
        for n in range(count)
        for _ in range(2)
    ]
    return call(
        finish_blocks_body,
        "finish_blocks",
        2 * count,
        info,
        arrays,
        blocks,
        shaped((2 * count * CH, CH) if axis == 0 else (CH, 2 * count * CH), f32),
        spec((CH, CH), lambda j, _: (j, 0) if axis == 0 else (0, j)),
        0,
        deps=deps,
    )


def finish_pair_body(info, here, there, *outs):
    for n, out in enumerate(outs):
        out[...] = here[n].astype(f32) + there[n].astype(f32)


def finish_pair(info, here, there, deps=()):
    part = CH // 2
    return call(
        finish_pair_body,
        "finish_pair",
        2,
        info,
        (here, there),
        [spec((2, part, CH), lambda j, _: (0, j, 0))] * 2,
        (shaped((CH, CH), f32),) * 2,
        [spec((part, CH), lambda j, _: (j, 0))] * 2,
        0,
        deps=deps,
    )


def finish_out_body(info, *refs):
    *shares, x, shift, out = refs
    for s in range(2):
        own, back, near = shares[3 * s : 3 * s + 3]
        total = own[...].astype(f32) + back[...].astype(f32) + near[...].astype(f32)
        out[s] = (x[s].astype(f32) + total + shift[...].astype(f32)).astype(bf16)


def finish_out(info, shares, x, shift, deps=()):
    seqs, rows, _ = x.shape
    part = rows // 2
    both = spec((seqs, part, CH), lambda j, _: (0, j, 0))
    return call(
        finish_out_body,
        "finish_out",
        2,
        info,
        (*shares, x, shift),
        [spec((part, CH), lambda j, _: (j, 0))] * 6 + [both, whole(1, CH)],
        shaped(x.shape),
        both,
        0,
        deps=deps,
    )


def finish_in_body(info, *refs):
    shares, tails, wide = refs[:6], refs[6:12], refs[12:18]
    x, ct, stats, gain, out, sums = refs[18:]
    weight = gain[...].astype(f32)
    for s in range(2):
        at = slice(3 * s, 3 * s + 3)
        total = sum(a[...].astype(f32) for a in shares[at])
        tail = sum(a[...].astype(f32) for a in tails[at])
        column = jnp.concatenate([tail[:8], stats[s]], axis=0).T
        plain, cross = column[:, 0:1], column[:, 1:2]
        average, root = column[:, 8:9], column[:, 9:10]
        standard = (x[s].astype(f32) - average) * root
        scaled = total * weight - plain * (1.0 / D) - standard * (cross * (1.0 / D))
        out[s] = ct[s].astype(f32) + root * scaled

    @pl.when(pl.program_id(0) == 0)
    def _():
        sums[...] = sum(a[...].astype(f32)[8:] for a in wide)


def finish_in(info, shares, x, ct, stats, gain, deps=()):
    seqs, rows, _ = x.shape
    part = rows // 2
    both = spec((seqs, part, CH), lambda j, _: (0, j, 0))
    last = rows // TAIL
    return call(
        finish_in_body,
        "finish_in",
        2,
        info,
        (*shares, *shares, *shares, x, ct, stats, gain),
        [spec((part, CH), lambda j, _: (j, 0))] * 6
        + [spec((TAIL, part), lambda j, _: (last, j))] * 6
        + [spec((TAIL, CH), lambda j, _: (last, 0))] * 6
        + [both, both, spec((seqs, 8, part), lambda j, _: (0, 0, j)), whole(1, CH)],
        (shaped(x.shape, f32), shaped((TAIL // 2, CH), f32)),
        [both, whole(TAIL // 2, CH)],
        0,
        deps=deps,
    )


SMALL = 16


def small_table_body(info, query, pair, up0, up1, out, last, table):
    table[...] = jnp.zeros(table.shape, f32)
    table[0:1, :] = query[...]
    table[1:2, :] = pair[0]
    table[2:3, :] = pair[1]
    for n in range(2):
        table[3 + n : 4 + n, :] = up0[:, CH * n : CH * (n + 1)]
        table[5 + n : 6 + n, :] = up1[:, CH * n : CH * (n + 1)]
    table[7:8, :] = out[...]
    table[8:10, :] = last[0:2, :]


def small_table(info, arrays):
    return call(
        small_table_body,
        "small_table",
        1,
        info,
        arrays,
        [whole(*a.shape) for a in arrays],
        shaped((SMALL, CH), f32),
        whole(SMALL, CH),
        0,
    )


def ring(array, step):
    return lax.ppermute(array, "tp", [(i, (i + step) % N_TP) for i in range(N_TP)])


class Gather:
    def __init__(self, own):
        self.own = own

    def forth(self, clock):
        self.own = clock.go(self.own)
        self.behind = ring(self.own, 1)

    def back(self):
        self.ahead = ring(self.own, -1)

    def sides(self, clock):
        self.forth(clock)
        self.ahead = ring(self.own, -1)

    def onward(self, clock):
        self.behind = clock.go(self.behind)
        self.far = ring(self.behind, 1)
        self.parts = (self.own, self.behind, self.ahead, self.far)


class Scatter:
    def __init__(self, chunks, clock):
        self.own, self.share, far, self.given = chunks
        self.far = ring(clock.go(far), 1)

    def backward(self, clock):
        self.back = ring(clock.go(self.given), -1)

    def onward(self, clock):
        both = (self.share.astype(f32) + self.far.astype(f32)).astype(bf16)
        self.near = ring(clock.go(both), 1)

    def shares(self):
        return self.own, self.back, self.near


class Reduction:
    def __init__(self, kept, given, clock, two):
        self.kept, self.two = kept, two
        self.got = swap(clock.go(given), "dp", 1, N_DP)
        self.moved, self.here, self.there = {}, {}, {}

    def add(self):
        total = (self.kept[1].astype(f32) + self.got[1].astype(f32)).astype(bf16)
        self.across = [total[n : n + 2] for n in range(0, total.shape[0], 2)]

    def over_x(self, n, clock):
        self.moved[n] = swap(clock.go(self.across[n]), "dp", 2, N_DP)

    def over_y(self, n, clock):
        at = slice(2 * n, 2 * n + 2)
        parts = (self.kept[0, at], self.got[0, at], clock.go(self.moved[n]))
        here = sum(a.astype(f32) for a in parts).astype(bf16)
        self.here[n] = here
        self.there[n] = swap(here, "ctx", 1, 2) if self.two else lax.psum(here, "ctx")

    def sums(self, n):
        if self.two:
            return self.here[n], self.there[n]
        return self.there[n], jnp.zeros_like(self.there[n])


def body(
    block_in,
    doc_starts,
    query_weight,
    key_weight,
    value_weight,
    output_weight,
    up_weight,
    down_weight,
    query_bias,
    key_bias,
    value_bias,
    up_bias,
    output_bias,
    norm_gain,
    norm_shift,
    cotangent,
):
    seqs, rows, _ = block_in.shape
    d, c, t = lax.axis_index("dp"), lax.axis_index("ctx"), lax.axis_index("tp")
    n_ctx = lax.axis_size("ctx")
    two = n_ctx == 2
    info = jnp.stack([t, c, d]).astype(jnp.int32)

    clock = Clock()

    x = Gather(block_in)
    x.forth(clock)
    small = jnp.concatenate(
        [query_bias, key_bias, value_bias, up_bias, output_bias, norm_gain, norm_shift]
    )
    size = small.size
    near = swap(small, "dp", 1, N_DP)
    flip = (d & 1) == 1
    pair = jnp.concatenate([jnp.where(flip, near, small), jnp.where(flip, small, near)])
    across = swap(pair, "dp", 2, N_DP)
    flip = (d & 2) == 2
    small_here = jnp.concatenate([jnp.where(flip, across, pair), jnp.where(flip, pair, across)])
    small_here = small_here.reshape(N_DP, size)

    def small_of(first, length):
        return small_here[:, first : first + length].reshape(1, -1)

    share = query_bias.size
    share_units = up_bias.size
    qkv_bias = jnp.concatenate([small_of(n * share, share) for n in range(3)], axis=1)
    up_shift = small_of(3 * share, share_units)
    output_shift = small_of(3 * share + share_units, share)
    gain_here = small_of(4 * share + share_units, share)
    shift_here = small_of(5 * share + share_units, share)
    both = jnp.concatenate([gain_here, shift_here], axis=0)
    others = [ring(both, -r) for r in range(1, N_TP)]
    wq_shard = jnp.concatenate([query_weight, key_weight, value_weight], axis=1)
    shards_q = Shards(tie(wq_shard, across), 0, d, c, two)
    shards_q.over_x(clock)
    shards_u = Shards(up_weight, 0, d, c, two, made=False)
    wo_shard = jnp.concatenate([output_weight, down_weight], axis=0)
    shards_o = Shards(wo_shard, 1, d, c, two)
    clock.sync(x.behind, shards_q.first, *others, shards_u.part)

    x.back()
    shards_q.over_y(clock)
    shards_u.over_x(clock)
    shards_q.near_core(clock)
    circle = jnp.concatenate([both, *others] * 2, axis=1)
    gain_shift = lax.dynamic_slice_in_dim(circle, (N_TP - t) % N_TP * CH, D, 1)
    gain, shift = gain_shift[0:1], gain_shift[1:2]

    here = c * rows + jnp.arange(rows, dtype=jnp.int32)
    tables, opening = rotary_tables(doc_starts, here)
    blocks = 1 if two else n_ctx
    before, _ = rotary_tables(doc_starts, jnp.arange(blocks * rows, dtype=jnp.int32))
    before = [a.reshape(seqs, blocks, rows, 128) for a in before]

    clock.sync(shards_q.second, shards_u.first, x.ahead, shards_q.near, shards_o.part)
    shards_u.near_core(clock)

    x.onward(clock)
    shards_u.over_y(clock)
    shards_o.over_x(clock)
    shards_q.far_core(clock)
    clock.sync(
        x.far,
        *shards_q.far_near,
        shards_u.second,
        shards_o.first,
        *before,
    )

    def send_keys(s):
        kv[s] = clock.go(kv[s])
        if two:
            kvp[s] = lax.ppermute(kv[s], "ctx", [(0, 1)])[None]
        else:
            kvp[s] = lax.all_gather(kv[s], "ctx", axis=0, tiled=False)

    def attention_step(s):
        return attention(
            info,
            s,
            opening[:, None],
            q,
            kv[s],
            kvp[s],
            datt,
            tables,
            before,
            deps=clock.marks,
        )

    def returned(sent):
        if two:
            return lax.ppermute(clock.go(sent[0]), "ctx", [(1, 0)])
        return lax.psum_scatter(clock.go(sent), "ctx", scatter_dimension=0, tiled=False)

    def out_step(s):
        return project_out(
            layout, info, s, att[s], hidden, shards_o.pieces, deps=clock.marks
        )

    def back_in_step(s):
        return back_in(
            layout,
            info,
            s,
            x.parts,
            dq[s],
            dkv[s],
            sent[s],
            dup,
            shards_q.pieces,
            shards_u.pieces,
            gain,
            stats,
            deps=clock.marks,
        )

    layout = layout_of(two)
    kvp, att, dq, dkv, sent = ([None] * seqs for _ in range(5))

    shards_o.over_y(clock)
    shards_u.far_core(clock)
    ct = Gather(cotangent)
    ct.behind, ct.ahead = ring(ct.own, 1), ring(ct.own, -1)
    normed, stats, q, *kv = norm_qkv(
        layout, info, x.parts, gain, shift, shards_q.pieces, qkv_bias, tables, deps=clock.marks
    )
    clock.sync(normed, *shards_u.far_near, shards_u.near, ct.behind)

    shards_o.near_core(clock)
    ct.onward(clock)
    hidden, slope = mlp_up(layout, info, normed, shards_u.pieces, up_shift, deps=clock.marks)
    clock.sync(hidden, shards_o.second, ct.ahead, ct.far, shards_o.near)

    shards_o.far_core(clock)
    send_keys(0)
    send_keys(1)
    clock.sync(*shards_o.far_near)

    cf, out_bias_sum, datt, dup = back_out(
        layout, info, ct.parts, shards_o.pieces, slope, deps=clock.marks
    )
    clock.sync(datt, kvp[0])

    def grad_up_step(n):
        kept, given, sums = grad_up(info, normed, dup, n, deps=clock.marks)
        up_sums.append(sums)
        clock.sync(kept)
        return Reduction(kept, given, clock, two)

    up, up_sums = [], []
    up.append(grad_up_step(0))
    up.append(grad_up_step(1))
    clock.sync(up[0].got)

    up[0].add()
    up[0].over_x(0, clock)
    att[0], dq[0], dkv[0], sent[0] = attention_step(0)
    clock.sync(att[0], up[0].moved[0], up[1].got, kvp[1])

    sent[0] = returned(sent[0])
    up[1].add()
    up[1].over_x(0, clock)
    att[1], dq[1], dkv[1], sent[1] = attention_step(1)
    clock.sync(att[1], sent[0], up[1].moved[0])

    sent[1] = returned(sent[1])
    chunks_0 = out_step(0)
    clock.sync(chunks_0[0], *clock.marks)
    down_kept, down_given = grad_down(info, hidden, cf, deps=clock.marks)
    clock.sync(down_kept, sent[1])

    up[0].over_y(0, clock)
    down = Reduction(down_kept, down_given, clock, two)
    out_0 = Scatter(chunks_0, clock)
    out_0.backward(clock)
    chunks_0 = back_in_step(0)
    clock.sync(chunks_0[0], up[0].there[0], down.got, out_0.far, out_0.back)

    up[1].over_y(0, clock)
    down.add()
    down.over_x(0, clock)
    in_0 = Scatter(chunks_0, clock)
    in_0.backward(clock)
    head_kept, head_given, query_sum = grad_out_query(
        info, normed, cf, att, dq, deps=clock.marks
    )
    clock.sync(head_kept, *clock.marks)
    pair_kept, pair_given, pair_sum = grad_key_value(info, normed, dkv, sent, deps=clock.marks)
    clock.sync(pair_kept, up[1].there[0], down.moved[0], in_0.far, in_0.back)

    down.over_y(0, clock)
    down.over_x(1, clock)
    head = Reduction(head_kept, head_given, clock, two)
    out_0.onward(clock)
    in_0.onward(clock)
    chunks_1 = out_step(1)
    clock.sync(chunks_1[0], down.there[0], down.moved[1], head.got, out_0.near, in_0.near)

    down.over_y(1, clock)
    head.add()
    head.over_x(0, clock)
    pair = Reduction(pair_kept, pair_given, clock, two)
    out_1 = Scatter(chunks_1, clock)
    out_1.backward(clock)
    chunks_1 = back_in_step(1)
    clock.sync(chunks_1[0], down.there[1], head.moved[0], pair.got, out_1.far, out_1.back)

    in_1 = Scatter(chunks_1, clock)
    in_1.backward(clock)
    head.over_y(0, clock)
    pair.add()
    pair.over_x(0, clock)
    up_wg = finish_blocks(info, [up[0].sums(0), up[1].sums(0)], 1, deps=clock.marks)
    down_wg = finish_blocks(info, [down.sums(0), down.sums(1)], 0, deps=clock.marks)
    clock.sync(in_1.far, in_1.back, head.there[0], pair.moved[0], up_wg, down_wg)

    in_1.onward(clock)
    pair.over_y(0, clock)
    output_wg, query_wg = finish_pair(info, *head.sums(0), deps=clock.marks)
    clock.sync(in_1.near, output_wg)

    out_1.onward(clock)
    in_grad, last = finish_in(
        info,
        (*in_0.shares(), *in_1.shares()),
        block_in,
        cotangent,
        stats,
        gain_here,
        deps=clock.marks,
    )
    table = small_table(info, (query_sum, pair_sum, *up_sums, out_bias_sum, last))
    table = table + swap(table, "dp", 1, N_DP)
    table = table + swap(table, "dp", 2, N_DP)
    table = table + swap(table, "ctx", 1, 2) if two else lax.psum(table, "ctx")
    block_out = finish_out(info, (*out_0.shares(), *out_1.shares()), block_in, output_shift)
    key_wg, value_wg = finish_pair(info, *pair.sums(0))

    share = CH // N_DP
    mine = lax.dynamic_slice_in_dim(table, d * share, share, 1)
    query_bg, key_bg, value_bg = mine[0], mine[1], mine[2]
    output_bg, gain_g, shift_g = mine[7], mine[8], mine[9]
    up_bg = lax.dynamic_slice_in_dim(table, 3 + d, 1, 0).reshape(-1)
    return (
        block_out,
        in_grad,
        query_wg,
        key_wg,
        value_wg,
        output_wg,
        up_wg,
        down_wg,
        query_bg,
        key_bg,
        value_bg,
        up_bg,
        output_bg,
        gain_g,
        shift_g,
    )


def solution(mesh):
    return jax.shard_map(
        body,
        mesh=mesh,
        in_specs=(
            P("dp", "ctx", "tp"),
            P("dp", None),
            P("dp", "tp"),
            P("dp", "tp"),
            P("dp", "tp"),
            P("tp", "dp"),
            P("dp", "tp"),
            P("tp", "dp"),
        )
        + (P(("tp", "dp")),) * 7
        + (P("dp", "ctx", "tp"),),
        out_specs=(
            P("dp", "ctx", "tp"),
            P("dp", "ctx", "tp"),
            P("dp", "tp"),
            P("dp", "tp"),
            P("dp", "tp"),
            P("tp", "dp"),
            P("dp", "tp"),
            P("tp", "dp"),
        )
        + (P(("tp", "dp")),) * 7,
        check_vma=False,
    )
```

```python
import functools
import math

import jax
import jax.numpy as jnp
from jax import lax
from jax.experimental import pallas as pl
from jax.experimental.pallas import tpu as pltpu
from jax.sharding import PartitionSpec as P

HEAD_DIM = 64
ROT = 32
D = 2048
N_DP = 4
N_TP = 4
CH = D // N_TP
EPS = 1e-05
NEG = -1e30
VMEM = 127 * 2**19
COST = 0.02

bf16 = jnp.bfloat16
f32 = jnp.float32


def dot_nn(a, b):
    return lax.dot_general(a, b, (((1,), (0,)), ((), ())), preferred_element_type=f32)


def dot_nt(a, b):
    return lax.dot_general(a, b, (((1,), (1,)), ((), ())), preferred_element_type=f32)


def dot_tn(a, b):
    return lax.dot_general(a, b, (((0,), (0,)), ((), ())), preferred_element_type=f32)


def spec(block, index):
    return pl.BlockSpec(block, index)


def whole(*block):
    zeros = (0,) * len(block)
    return pl.BlockSpec(block, lambda g, *_: zeros)


def once(*block):
    zeros = (0,) * len(block)
    return pl.BlockSpec(block, lambda g, *_: zeros, pipeline_mode=pl.Buffered(1))


def one_of(s, *block):
    zeros = (0,) * len(block)
    return pl.BlockSpec((None, *block), lambda g, *_: (s, *zeros))


def shaped(shape, dtype=bf16):
    return jax.ShapeDtypeStruct(tuple(shape), dtype)


ANYWHERE = pl.BlockSpec(memory_space=pl.ANY)


def call(body, name, grid, info, ins, in_specs, outs, out_specs, flops, scratch=(), deps=()):
    moved = sum(math.prod(a.shape) * a.dtype.itemsize for a in (*ins, *jax.tree.leaves(outs)))
    first, last = 1 + len(ins), 1 + len(ins) + len(deps)

    def without_deps(*refs):
        body(*refs[:first], *refs[last:])

    return pl.pallas_call(
        without_deps,
        grid_spec=pltpu.PrefetchScalarGridSpec(
            num_scalar_prefetch=1,
            grid=(grid,),
            in_specs=[*in_specs, *[ANYWHERE] * len(deps)],
            out_specs=out_specs,
            scratch_shapes=list(scratch),
        ),
        out_shape=outs,
        compiler_params=pltpu.CompilerParams(vmem_limit_bytes=VMEM),
        cost_estimate=pl.CostEstimate(
            flops=int(flops * COST), bytes_accessed=int(moved * COST), transcendentals=0
        ),
        name=name,
    )(info, *ins, *deps)


def tie(value, *deps):
    def nothing(*refs):
        del refs

    return pl.pallas_call(
        nothing,
        in_specs=[ANYWHERE] * (1 + len(deps)),
        out_specs=ANYWHERE,
        out_shape=shaped(value.shape, value.dtype),
        input_output_aliases={0: 0},
        compiler_params=pltpu.CompilerParams(vmem_limit_bytes=VMEM),
        cost_estimate=pl.CostEstimate(flops=0, bytes_accessed=0, transcendentals=0),
        name="tie",
    )(value, *deps)


def columns(index, width=CH):
    return pl.ds(pl.multiple_of(index * width, width), width)


def layout_of(two):
    if two:
        halves = [("c", CH // 2), ("other", CH // 2)]
    else:
        halves = [("", CH)]
    return [(0, "", CH), (1, "", CH)] + [(r, *half) for r in (2, 3) for half in halves]


def piece_offset(info, half):
    return {"": 0, "c": info[1], "other": 1 - info[1]}[half] * (CH // 2)


def piece_window(info, piece):
    r, half, size = piece
    start = (info[2] ^ r) * CH + piece_offset(info, half)
    return pl.ds(pl.multiple_of(start, size), size)


class Clock:
    def __init__(self):
        self.marks = ()

    def go(self, value):
        return tie(value, *self.marks) if self.marks else value

    def sync(self, *arrays):
        def nothing(*refs):
            del refs

        self.marks = (
            pl.pallas_call(
                nothing,
                in_specs=[ANYWHERE] * (len(arrays) + len(self.marks)),
                out_specs=ANYWHERE,
                out_shape=shaped((8, 128), f32),
                compiler_params=pltpu.CompilerParams(vmem_limit_bytes=VMEM),
                cost_estimate=pl.CostEstimate(flops=0, bytes_accessed=0, transcendentals=0),
                name="sync",
            )(*arrays, *self.marks),
        )


def swap(array, axis, bit, size):
    return lax.ppermute(array, axis, [(i, i ^ bit) for i in range(size)])


class Shards:
    def __init__(self, own, axis, d, c, two, made=True):
        self.own, self.two, self.made = own, two, made
        size = own.shape[axis] // 2
        self.part = lax.dynamic_slice_in_dim(own, c * size, size, axis) if two else own

    def near_core(self, clock):
        self.own = clock.go(self.own) if self.made else self.own
        self.near = swap(self.own, "dp", 1, N_DP)

    def over_x(self, clock):
        self.first = swap(clock.go(self.part), "dp", 2, N_DP)

    def over_y(self, clock):
        self.first = clock.go(self.first)
        self.second = swap(self.first, "ctx", 1, 2) if self.two else self.first

    def far_core(self, clock):
        self.first = clock.go(self.first)
        far = [self.first]
        if self.two:
            self.second = clock.go(self.second)
            far.append(self.second)
        self.far_near = [swap(a, "dp", 1, N_DP) for a in far]
        self.pieces = [self.own, self.near, *far, *self.far_near]


def rotary_tables(starts, positions):
    before = starts[:, None, :] <= positions[None, :, None]
    opening = jnp.max(jnp.where(before, starts[:, None, :], 0), axis=2)
    relative = (positions[None, :] - opening).astype(f32)
    half = ROT // 2
    lane = jnp.arange(128, dtype=jnp.int32) % HEAD_DIM
    frequency = jnp.exp((lane % half).astype(f32) * (-math.log(10000.0) / half))
    angles = relative[:, :, None] * jnp.where(lane < ROT, frequency, 0.0)
    sine = jnp.sin(angles)
    return (
        jnp.cos(angles),
        jnp.where(lane < half, -sine, 0.0),
        jnp.where(lane >= half, sine, 0.0),
    ), opening


def add_rounded(a, b):
    return (a.astype(f32) + b.astype(f32)).astype(bf16)


def turn(x, own, up, down):
    return x * own + pltpu.roll(x, 112, 1) * up + pltpu.roll(x, 16, 1) * down


def turn_back(x, own, up, down):
    return x * own - pltpu.roll(x, 112, 1) * up - pltpu.roll(x, 16, 1) * down


def stream_pieces(layout, info, sources, held, sems, axis, blocks):
    j = pl.program_id(0)

    def copies(block):
        cut = pl.ds(pl.multiple_of(block * CH, CH), CH)
        for n, (piece, source) in enumerate(zip(layout, sources)):
            window = piece_window(info, piece)
            if axis == 0:
                pair = source.at[:, cut], held.at[window, cut]
            else:
                pair = source.at[cut, :], held.at[cut, window]
            yield pltpu.make_async_copy(*pair, sems.at[block, n])

    @pl.when(j == 0)
    def _():
        for block in range(blocks):
            for copy in copies(block):
                copy.start()

    for copy in copies(j):
        copy.wait()


def norm_qkv_body(layout, info, x0, xa, xc, xb, gain, shift, bias, own, up, down, *refs):
    *w, normed, stats, q, kv0, kv1, columns_held, held, sems = refs
    j = pl.program_id(0)
    t = info[0]
    seqs, rows, _ = x0.shape
    stream_pieces(layout, info, w, held, sems, 0, 3)

    @pl.when(j == 0)
    def _():
        parts = [(x0, t), (xa, (t + 3) % N_TP), (xc, (t + 1) % N_TP), (xb, (t + 2) % N_TP)]
        tile = 128

        def rows_of(i, carry):
            s = i // (rows // tile)
            window = pl.ds(pl.multiple_of((i % (rows // tile)) * tile, tile), tile)
            x = [part[s, window, :].astype(f32) for part, _ in parts]
            average = sum(jnp.sum(a, axis=1, keepdims=True) for a in x) * (1.0 / D)
            x = [a - average for a in x]
            variance = sum(jnp.sum(a * a, axis=1, keepdims=True) for a in x) * (1.0 / D)
            root = lax.rsqrt(variance + EPS)
            columns_held[s, window, 0:1] = average
            columns_held[s, window, 1:2] = root
            for a, (_, index) in zip(x, parts):
                at = columns(index)
                y = a * root * gain[:, at].astype(f32) + shift[:, at].astype(f32)
                normed[s, window, at] = y.astype(bf16)
            return carry

        columns_held[...] = jnp.zeros(columns_held.shape, f32)
        lax.fori_loop(0, seqs * rows // tile, rows_of, 0)
        for s in range(seqs):
            stats[s] = columns_held[s].T[: stats.shape[1]]

    for s, kv in ((0, kv0), (1, kv1)):
        y = dot_nn(normed[s], held[:, columns(j)]) + bias[...].astype(f32)

        def rotated(s=s, y=y):
            parts = [
                turn(y[:, 128 * n : 128 * n + 128], own[s], up[s], down[s])
                for n in range(CH // 128)
            ]
            return jnp.concatenate(parts, axis=1).astype(bf16)

        @pl.when(j == 0)
        def _(s=s, rotated=rotated):
            q[s] = rotated()

        @pl.when(j == 1)
        def _(kv=kv, rotated=rotated):
            kv[0] = rotated()

        @pl.when(j == 2)
        def _(kv=kv, y=y):
            kv[0] = y.astype(bf16)


def norm_qkv(layout, info, parts, gain, shift, w, bias, tables, deps=()):
    seqs, rows, _ = parts[0].shape
    outs = (
        shaped((seqs, rows, D)),
        shaped((seqs, 8, rows), f32),
        shaped((seqs, rows, CH)),
        shaped((2, rows, CH)),
        shaped((2, rows, CH)),
    )
    pair = spec((1, rows, CH), lambda j, *_: (jnp.maximum(j - 1, 0), 0, 0))
    return call(
        functools.partial(norm_qkv_body, layout),
        "norm_qkv",
        3,
        info,
        (*parts, gain, shift, bias, *tables, *w),
        [whole(seqs, rows, CH)] * 4
        + [whole(1, D)] * 2
        + [spec((1, CH), lambda j, *_: (0, j))]
        + [whole(seqs, rows, 128)] * 3
        + [ANYWHERE] * len(w),
        outs,
        [
            whole(seqs, rows, D),
            whole(seqs, 8, rows),
            whole(seqs, rows, CH),
            pair,
            pair,
        ],
        2 * seqs * rows * D * 3 * CH,
        [
            pltpu.VMEM((seqs, rows, 128), f32),
            pltpu.VMEM((D, 3 * CH), bf16),
            pltpu.SemaphoreType.DMA((3, len(w))),
        ],
        deps=deps,
    )


def mlp_up_body(layout, info, normed, bias, *refs):
    *w, hidden, grad, held, sems = refs
    j = pl.program_id(0)
    stream_pieces(layout, info, w, held, sems, 0, held.shape[1] // CH)
    root = math.sqrt(2.0 / math.pi)
    for s in range(normed.shape[0]):
        u = dot_nn(normed[s], held[:, columns(j)]) + bias[...].astype(f32)
        square = u * u
        t = jnp.tanh(u * (root + (root * 0.044715) * square))
        half = 0.5 + 0.5 * t
        hidden[s] = (u * half).astype(bf16)
        slope = root + (3 * 0.044715 * root) * square
        grad[s] = (half + (0.5 * u) * (1.0 - t * t) * slope).astype(bf16)


def mlp_up(layout, info, normed, w, bias, deps=()):
    seqs, rows, _ = normed.shape
    units = w[0].shape[1]
    block = spec((seqs, rows, CH), lambda j, *_: (0, 0, j))
    return call(
        functools.partial(mlp_up_body, layout),
        "mlp_up",
        units // CH,
        info,
        (normed, bias, *w),
        [whole(seqs, rows, D), spec((1, CH), lambda j, *_: (0, j))] + [ANYWHERE] * len(w),
        (shaped((seqs, rows, units)),) * 2,
        [block] * 2,
        2 * seqs * rows * D * units,
        [pltpu.VMEM((D, units), bf16), pltpu.SemaphoreType.DMA((units // CH, len(w)))],
        deps=deps,
    )


def back_out_body(layout, info, c0, ca, cc, cb, slope, *refs):
    *w, cf, bias_grad, datt, dup, held, sems = refs
    j = pl.program_id(0)
    t = info[0]
    seqs = c0.shape[0]
    stream_pieces(layout, info, w, held, sems, 1, held.shape[0] // CH)

    @pl.when(j == 0)
    def _():
        for part, step in ((c0, 0), (ca, 3), (cc, 1), (cb, 2)):
            cf[:, :, columns((t + step) % N_TP)] = part[...]
        bias_grad[...] = sum(
            jnp.sum(c0[s].astype(f32), axis=0, keepdims=True) for s in range(seqs)
        )

    for s in range(seqs):
        y = dot_nt(cf[s], held[columns(j), :])

        @pl.when(j == 0)
        def _(s=s, y=y):
            datt[s] = y.astype(bf16)

        @pl.when(j > 0)
        def _(s=s, y=y):
            dup[s] = (y * slope[s].astype(f32)).astype(bf16)


def back_out(layout, info, parts, w, slope, deps=()):
    seqs, rows, units = slope.shape
    later = spec((seqs, rows, CH), lambda j, *_: (0, 0, jnp.maximum(j - 1, 0)))
    return call(
        functools.partial(back_out_body, layout),
        "back_out",
        1 + units // CH,
        info,
        (*parts, slope, *w),
        [whole(seqs, rows, CH)] * 4 + [later] + [ANYWHERE] * len(w),
        (
            shaped((seqs, rows, D)),
            shaped((1, CH), f32),
            shaped((seqs, rows, CH)),
            shaped((seqs, rows, units)),
        ),
        [whole(seqs, rows, D), whole(1, CH), whole(seqs, rows, CH), later],
        2 * seqs * rows * D * (CH + units),
        [
            pltpu.VMEM((CH + units, D), bf16),
            pltpu.SemaphoreType.DMA((1 + units // CH, len(w))),
        ],
        deps=deps,
    )


def attention_body(
    blocks, info, low, q, kv, kvp, do, own, up, down, ownp, upp, downp,
    att, dq, dkv, dkvp, scores, probs,
):
    rows = q.shape[0]
    before, start = info[1], info[1] * rows
    lane = lax.broadcasted_iota(jnp.int32, (rows, 128), 1)
    key_row = lax.broadcasted_iota(jnp.int32, (rows, 1), 0)
    query_at = start + lax.broadcasted_iota(jnp.int32, (1, rows), 1)
    first = low[0]
    do_t = do[...].astype(f32).T
    nothing = jnp.zeros((), bf16)
    outputs = []
    for head in range(2):
        mine = (lane < HEAD_DIM) if head == 0 else (lane >= HEAD_DIM)
        half = slice(HEAD_DIM * head, HEAD_DIM * (head + 1))
        qh = jnp.where(mine, q[...] * jnp.asarray(HEAD_DIM**-0.5, bf16), nothing)
        dh = jnp.where(mine, do[...], nothing)

        key_at = start + key_row
        s = dot_nt(kv[0], qh)
        s = jnp.where((key_at >= first) & (key_at <= query_at), s, NEG)
        scores[blocks] = s
        peak = jnp.max(s, axis=0, keepdims=True)

        def score(n, peak):
            s = dot_nt(kvp[n, 0], qh)
            s = jnp.where(n * rows + key_row >= first, s, NEG)
            scores[n] = s
            return jnp.maximum(peak, jnp.max(s, axis=0, keepdims=True))

        peak = lax.fori_loop(0, before, score, peak)

        def expo(n, total):
            e = jnp.exp(scores[n] - peak)
            scores[n] = e
            return total + jnp.sum(e, axis=0, keepdims=True)

        total = expo(blocks, jnp.zeros((1, rows), f32))
        total = lax.fori_loop(0, before, expo, total)
        scale = 1.0 / total

        def weigh(n, values):
            p = (scores[n] * scale).astype(bf16)
            probs[n] = p
            return dot_tn(values, p)

        out_t = weigh(blocks, kv[1])
        out_t = lax.fori_loop(0, before, lambda n, acc: acc + weigh(n, kvp[n, 1]), out_t)
        delta = jnp.sum(out_t[half] * do_t[half], axis=0, keepdims=True)

        def back(n, keys, values):
            dp = dot_nt(values, dh)
            ds = ((scores[n] * scale) * (dp - delta)).astype(bf16)
            return dot_nn(ds, qh), dot_nn(probs[n], dh), dot_tn(keys, ds)

        dk, dv, dq_t = back(blocks, kv[0], kv[1])
        if head == 0:
            dk_sum, dv_sum = dk, dv
        else:
            dk_sum, dv_sum = dk_sum + dk, dv_sum + dv

        def back_before(n, acc):
            dk, dv, more = back(n, kvp[n, 0], kvp[n, 1])
            dk = turn_back(dk, ownp[n], upp[n], downp[n])
            if head == 0:
                dkvp[n, 0] = dk.astype(bf16)
                dkvp[n, 1] = dv.astype(bf16)
            else:
                dkvp[n, 0] = (dkvp[n, 0].astype(f32) + dk).astype(bf16)
                dkvp[n, 1] = (dkvp[n, 1].astype(f32) + dv).astype(bf16)
            return acc + more

        dq_t = lax.fori_loop(0, before, back_before, dq_t)
        outputs.append((out_t[half], dq_t[half]))

    def clear(n, carry):
        dkvp[n] = jnp.zeros(dkvp.shape[1:], bf16)
        return carry

    lax.fori_loop(before, blocks, clear, 0)
    att[...] = jnp.concatenate([outputs[0][0], outputs[1][0]], axis=0).T.astype(bf16)
    grad = jnp.concatenate([outputs[0][1], outputs[1][1]], axis=0).T * HEAD_DIM**-0.5
    dq[...] = turn_back(grad, own[...], up[...], down[...]).astype(bf16)
    dkv[0] = turn_back(dk_sum, own[...], up[...], down[...]).astype(bf16)
    dkv[1] = dv_sum.astype(bf16)


def attention_two_body(
    info, low, q, kv, kvp, do, own, up, down, ownp, upp, downp, att, dq, dkv, dkvp
):
    rows = q.shape[0]
    part = rows // 2
    before, start = info[1], info[1] * rows

    def tail(x, skipped):
        return x[:, skipped:] if skipped else x

    def merge(acc, x, skipped, op):
        if acc is None:
            return x
        if not skipped:
            return op(acc, x)
        return jnp.concatenate([acc[:, :skipped], op(acc[:, skipped:], x)], axis=1)

    def run(with_before):
        lane = lax.broadcasted_iota(jnp.int32, (rows, 128), 1)
        key_row = lax.broadcasted_iota(jnp.int32, (part, 1), 0)
        query_at = start + lax.broadcasted_iota(jnp.int32, (1, rows), 1)
        first = low[...]
        do_t = do[...].astype(f32).T
        nothing = jnp.zeros((), bf16)
        blocks = []
        for n in range(2):
            if with_before:
                blocks.append((kvp.at[0], n * part, 0, False))
        for n in range(2):
            blocks.append((kv, n * part, n * part, True))
        outputs = []
        dk_sum, dv_sum = [0.0] * len(blocks), [0.0] * len(blocks)
        for head in range(2):
            mine = (lane < HEAD_DIM) if head == 0 else (lane >= HEAD_DIM)
            half = slice(HEAD_DIM * head, HEAD_DIM * (head + 1))
            qh = jnp.where(mine, q[...] * jnp.asarray(HEAD_DIM**-0.5, bf16), nothing)
            dh = jnp.where(mine, do[...], nothing)
            scores, peak = [], None
            for ref, row, skip, here in blocks:
                s = dot_nt(ref[0, row : row + part], qh[skip:])
                key_at = (start if here else start - rows) + row + key_row
                allowed = key_at >= tail(first, skip)
                if here:
                    allowed = allowed & (key_at <= tail(query_at, skip))
                s = jnp.where(allowed, s, NEG)
                scores.append(s)
                peak = merge(peak, jnp.max(s, axis=0, keepdims=True), skip, jnp.maximum)
            terms, total = [], None
            for s, (_, _, skip, _) in zip(scores, blocks):
                e = jnp.exp(s - tail(peak, skip))
                terms.append(e)
                total = merge(total, jnp.sum(e, axis=0, keepdims=True), skip, jnp.add)
            scale = 1.0 / total
            probs, rounded, out_t = [], [], None
            for e, (ref, row, skip, _) in zip(terms, blocks):
                p = e * tail(scale, skip)
                pb = p.astype(bf16)
                probs.append(p)
                rounded.append(pb)
                out_t = merge(out_t, dot_tn(ref[1, row : row + part], pb), skip, jnp.add)
            delta = jnp.sum(out_t[half] * do_t[half], axis=0, keepdims=True)
            dq_t = None
            for n, (ref, row, skip, _) in enumerate(blocks):
                dp = dot_nt(ref[1, row : row + part], dh[skip:])
                ds = (probs[n] * (dp - tail(delta, skip))).astype(bf16)
                dv_sum[n] = dv_sum[n] + dot_nn(rounded[n], dh[skip:])
                dk_sum[n] = dk_sum[n] + dot_nn(ds, qh[skip:])
                dq_t = merge(dq_t, dot_tn(ref[0, row : row + part], ds), skip, jnp.add)
            outputs.append((out_t[half], dq_t[half]))
        att[...] = jnp.concatenate([outputs[0][0], outputs[1][0]], axis=0).T.astype(bf16)
        grad = jnp.concatenate([outputs[0][1], outputs[1][1]], axis=0).T * HEAD_DIM**-0.5
        dq[...] = turn_back(grad, own[...], up[...], down[...]).astype(bf16)
        dk = jnp.concatenate(dk_sum[-2:], axis=0)
        dkv[0] = turn_back(dk, own[...], up[...], down[...]).astype(bf16)
        dkv[1] = jnp.concatenate(dv_sum[-2:], axis=0).astype(bf16)
        if with_before:
            dk = jnp.concatenate(dk_sum[:2], axis=0)
            dkvp[0, 0] = turn_back(dk, ownp[0], upp[0], downp[0]).astype(bf16)
            dkvp[0, 1] = jnp.concatenate(dv_sum[:2], axis=0).astype(bf16)
        else:
            dkvp[...] = jnp.zeros(dkvp.shape, bf16)

    @pl.when(before == 0)
    def _():
        run(False)

    @pl.when(before > 0)
    def _():
        run(True)


def attention(info, s, low, q, kv, kvp, do, tables, tables_before, deps=()):
    _, rows, width = q.shape
    blocks = kvp.shape[0]
    token = spec((rows, 128), lambda g, *_: (0, g))
    query = spec((None, rows, 128), lambda g, *_: (s, 0, g))
    pair = spec((2, rows, 128), lambda g, *_: (0, 0, g))
    pairs = spec((blocks, 2, rows, 128), lambda g, *_: (0, 0, 0, g))
    return call(
        attention_two_body if blocks == 1 else functools.partial(attention_body, blocks),
        "attention",
        width // 128,
        info,
        (low, q, kv, kvp, do, *tables, *tables_before),
        [one_of(s, 1, rows), query, pair, pairs, query]
        + [one_of(s, rows, 128)] * 3
        + [one_of(s, blocks, rows, 128)] * 3,
        (
            shaped((rows, width)),
            shaped((rows, width)),
            shaped((2, rows, width)),
            shaped((blocks, 2, rows, width)),
        ),
        [token, token, pair, pairs],
        48 * rows * rows * width,
        []
        if blocks == 1
        else [
            pltpu.VMEM((blocks + 1, rows, rows), f32),
            pltpu.VMEM((blocks + 1, rows, rows), bf16),
        ],
        deps=deps,
    )


TAIL = 16


def fetch_pieces(layout, sources, targets, sems, axis):
    copies = [[] for _ in range(N_DP)]
    at = [r * CH for r in range(N_DP)]
    n = 0
    for group, target in zip(sources, targets):
        at = [r * CH for r in range(N_DP)]
        for (r, _, size), source in zip(layout, group):
            window = pl.ds(at[r], size)
            place = target.at[window, :] if axis == 0 else target.at[:, window]
            copies[r].append(pltpu.make_async_copy(source, place, sems.at[n]))
            at[r] += size
            n += 1
    return copies


def with_chunk(layout, info, copies, work):
    j = pl.program_id(0)

    @pl.when(j == 0)
    def _():
        for group in copies:
            for copy in group:
                copy.start()

    for r in range(N_DP):

        @pl.when(j == r)
        def _(r=r):
            for copy in copies[r]:
                copy.wait()
            at = r * CH
            for s, half, size in layout:
                if s == r:
                    offset = pl.multiple_of(piece_offset(info, half), size)
                    work(pl.ds(at, size), pl.ds(offset, size))
                    at += size


def chunk_now(info):
    return ((info[2] ^ pl.program_id(0)) + N_TP - info[0]) % N_TP


def out_hidden_body(layout, info, hidden, *refs):
    count = len(layout)
    w, outs = refs[:count], refs[count : count + N_TP]
    held, y, sems = refs[count + N_TP :]

    def work(place, window):
        for s in range(hidden.shape[0]):
            y[s, :, window] = dot_nn(hidden[s], held[:, place]).astype(bf16)

    lower = [a.at[pl.ds(CH, held.shape[0]), :] for a in w]
    with_chunk(layout, info, fetch_pieces(layout, [lower], [held], sems, 1), work)
    for r in range(N_TP):

        @pl.when(chunk_now(info) == r)
        def _(r=r):
            outs[r][...] = y[...]


def out_hidden(layout, info, hidden, w, deps=()):
    seqs, rows, units = hidden.shape
    return call(
        functools.partial(out_hidden_body, layout),
        "out_hidden",
        N_TP,
        info,
        (hidden, *w),
        [once(seqs, rows, units)] + [ANYWHERE] * len(w),
        (shaped((seqs, rows, CH)),) * N_TP,
        [whole(seqs, rows, CH)] * N_TP,
        2 * seqs * rows * D * units,
        [
            pltpu.VMEM((units, D), bf16),
            pltpu.VMEM((seqs, rows, CH), bf16),
            pltpu.SemaphoreType.DMA((len(w),)),
        ],
        deps=deps,
    )


def out_heads_body(layout, info, a0, a1, p0, p1, p2, p3, *refs):
    count = len(layout)
    w, outs = refs[:count], refs[count : count + N_TP]
    held, y, sems = refs[count + N_TP :]

    def work(place, window):
        for s, att in ((0, a0), (1, a1)):
            y[s, :, window] = dot_nn(att[...], held[:, place])

    upper = [a.at[pl.ds(0, CH), :] for a in w]
    with_chunk(layout, info, fetch_pieces(layout, [upper], [held], sems, 1), work)
    for r, part in enumerate((p0, p1, p2, p3)):

        @pl.when(chunk_now(info) == r)
        def _(r=r, part=part):
            outs[r][...] = (y[...] + part[...].astype(f32)).astype(bf16)


def out_heads(layout, info, att, parts, w, deps=()):
    seqs, rows, _ = parts[0].shape
    return call(
        functools.partial(out_heads_body, layout),
        "out_heads",
        N_TP,
        info,
        (*att, *parts, *w),
        [once(rows, CH)] * 2 + [once(seqs, rows, CH)] * N_TP + [ANYWHERE] * len(w),
        (shaped((seqs, rows, CH)),) * N_TP,
        [whole(seqs, rows, CH)] * N_TP,
        2 * seqs * rows * D * CH,
        [
            pltpu.VMEM((CH, D), bf16),
            pltpu.VMEM((seqs, rows, CH), f32),
            pltpu.SemaphoreType.DMA((len(w),)),
        ],
        deps=deps,
    )


def back_in_body(layout, info, x0, xa, xc, xb, dq, dkv, back, dup, gain, stats, *refs):
    count = len(layout)
    wq, wu = refs[:count], refs[count : 2 * count]
    *chunks, held_q, held_u, y, xs, row_sums, column_sums, both, sems = refs[2 * count :]
    j = pl.program_id(0)
    rows = dq.shape[0]

    @pl.when(j == 0)
    def _():
        both[...] = add_rounded(dkv[...], back[...])


    def work(place, window):
        part = dot_nt(dup[...], held_u[place, :])
        part = part + dot_nt(dq[...], held_q[place, :CH])
        part = part + dot_nt(both[0], held_q[place, CH : 2 * CH])
        y[:, window] = part + dot_nt(both[1], held_q[place, 2 * CH :])

    copies = fetch_pieces(layout, [wq, wu], [held_q, held_u], sems, 0)
    with_chunk(layout, info, copies, work)
    for r, part in enumerate((x0, xc, xb, xa)):

        @pl.when(chunk_now(info) == r)
        def _(r=r, part=part):
            chunks[r][:rows, :] = y[...].astype(bf16)
            xs[...] = part[...]

    total = y[...]
    turned = stats[...].T
    standard = (xs[...].astype(f32) - turned[:, 0:1]) * turned[:, 1:2]
    cross = total * standard
    weight = gain[...].astype(f32)

    @pl.when(j == 0)
    def _():
        row_sums[...] = jnp.zeros(row_sums.shape, f32)
        column_sums[...] = jnp.zeros(column_sums.shape, f32)

    both = jnp.concatenate(
        [jnp.sum(cross, axis=0, keepdims=True), jnp.sum(total, axis=0, keepdims=True)], axis=0
    )
    column_sums[chunk_now(info), 0:2, :] = both
    row_sums[:, 0:1] += jnp.sum(total * weight, axis=1, keepdims=True)
    row_sums[:, 1:2] += jnp.sum(cross * weight, axis=1, keepdims=True)

    @pl.when(j == N_TP - 1)
    def _():
        turned = row_sums[...].T[: TAIL // 2]
        for r, chunk in enumerate(chunks):
            chunk[rows:, :] = jnp.concatenate([turned, column_sums[r]], axis=0).astype(bf16)


def back_in(layout, info, s, parts, dq, dkv, back, dup, wq, wu, gain, stats, deps=()):
    _, rows, units = dup.shape
    return call(
        functools.partial(back_in_body, layout),
        "back_in",
        N_TP,
        info,
        (*parts, dq, dkv, back, dup, gain, stats, *wq, *wu),
        [one_of(s, rows, CH)] * 4
        + [
            whole(rows, CH),
            whole(2, rows, CH),
            whole(2, rows, CH),
            one_of(s, rows, units),
            spec((1, CH), lambda j, info: (0, info[2] ^ j)),
            one_of(s, 8, rows),
        ]
        + [ANYWHERE] * (2 * len(wq)),
        (shaped((rows + TAIL, CH)),) * N_TP,
        [whole(rows + TAIL, CH)] * N_TP,
        2 * rows * D * (3 * CH + units),
        [
            pltpu.VMEM((D, 3 * CH), bf16),
            pltpu.VMEM((D, units), bf16),
            pltpu.VMEM((rows, CH), f32),
            pltpu.VMEM((rows, CH), bf16),
            pltpu.VMEM((rows, 128), f32),
            pltpu.VMEM((N_TP, TAIL // 2, CH), f32),
            pltpu.VMEM((2, rows, CH), bf16),
            pltpu.SemaphoreType.DMA((2 * len(wq),)),
        ],
        deps=deps,
    )


KEPT = ((0, 0), (2, 1))
GIVEN = ((1, 0), (3, 1))


def grad_up_body(info, normed, dup, kept, given, sums):
    d = info[2]
    rights = (dup[0], dup[1])
    store_by_rows(d, normed, rights, kept, given)
    sums[...] = sum(jnp.sum(b.astype(f32), axis=0, keepdims=True) for b in rights)


def grad_up(info, normed, dup, deps=()):
    _, rows, units = dup.shape
    count = units // CH
    message = spec((2, 1, CH, CH), lambda j, *_: (0, j, 0, 0))
    return call(
        grad_up_body,
        "grad_up",
        count,
        info,
        (normed, dup),
        [whole(2, rows, D), spec((2, rows, CH), lambda j, *_: (0, 0, j))],
        (shaped((2, count, CH, CH)),) * 2 + (shaped((1, units), f32),),
        [message, message, spec((1, CH), lambda j, *_: (0, j))],
        4 * rows * D * units,
        deps=deps,
    )


def grad_down_body(info, hidden, ct, kept, given):
    j = pl.program_id(0)
    y = (dot_tn(hidden[0], ct[0]) + dot_tn(hidden[1], ct[1])).astype(bf16)

    def store(target):
        for n in range(target.shape[1]):
            target[0, n] = y[CH * n : CH * (n + 1), :]

    @pl.when(j < 2)
    def _():
        store(given)

    @pl.when(j >= 2)
    def _():
        store(kept)


def grad_down(info, hidden, ct, deps=()):
    _, rows, units = hidden.shape
    count = units // CH
    block = spec(
        (2, rows, CH),
        lambda j, info: (0, 0, info[2] ^ jnp.where(j < 2, 2 * j + 1, 2 * j - 4)),
    )
    return call(
        grad_down_body,
        "grad_down",
        N_DP,
        info,
        (hidden, ct),
        [whole(2, rows, units), block],
        (shaped((2, count, CH, CH)),) * 2,
        [
            spec((1, count, CH, CH), lambda j, *_: (jnp.maximum(j - 2, 0), 0, 0, 0)),
            spec((1, count, CH, CH), lambda j, *_: (jnp.minimum(j, 1), 0, 0, 0)),
        ],
        4 * rows * D * units,
        deps=deps,
    )


def store_by_rows(d, lefts, rights, kept, given):
    for target, which in ((given, GIVEN), (kept, KEPT)):
        for r, at in which:
            window = columns(d ^ r)
            y = sum(dot_tn(lefts[s, :, window], b) for s, b in enumerate(rights))
            target[at, 0] = y.astype(bf16)


def grad_out_query_body(info, normed, ct, a0, a1, q0, q1, kept, given, sums):
    j = pl.program_id(0)
    d = info[2]

    @pl.when(j == 0)
    def _():
        lefts = (a0[...], a1[...])
        for target, which in ((given, GIVEN), (kept, KEPT)):
            for r, at in which:
                window = columns(d ^ r)
                y = sum(dot_tn(a, ct[s, :, window]) for s, a in enumerate(lefts))
                target[at, 0] = y.astype(bf16)

    @pl.when(j == 1)
    def _():
        rights = (q0[...], q1[...])
        store_by_rows(d, normed, rights, kept, given)
        sums[...] = sum(jnp.sum(b.astype(f32), axis=0, keepdims=True) for b in rights)


def grad_out_query(info, normed, ct, att, dq, deps=()):
    rows = normed.shape[1]
    message = spec((2, 1, CH, CH), lambda j, *_: (0, j, 0, 0))
    return call(
        grad_out_query_body,
        "grad_out_query",
        2,
        info,
        (normed, ct, *att, *dq),
        [whole(2, rows, D)] * 2 + [whole(rows, CH)] * 4,
        (shaped((2, 2, CH, CH)),) * 2 + (shaped((1, CH), f32),),
        [message, message, whole(1, CH)],
        4 * rows * D * 2 * CH,
        deps=deps,
    )


def grad_key_value_body(info, normed, kv0, back0, kv1, back1, kept, given, sums):
    rights = (add_rounded(kv0[0], back0[0]), add_rounded(kv1[0], back1[0]))
    store_by_rows(info[2], normed, rights, kept, given)
    sums[0] = sum(jnp.sum(b.astype(f32), axis=0, keepdims=True) for b in rights)


def grad_key_value(info, normed, dkv, sent, deps=()):
    rows = normed.shape[1]
    message = spec((2, 1, CH, CH), lambda j, *_: (0, j, 0, 0))
    pair = spec((1, rows, CH), lambda j, *_: (j, 0, 0))
    return call(
        grad_key_value_body,
        "grad_key_value",
        2,
        info,
        (normed, dkv[0], sent[0], dkv[1], sent[1]),
        [whole(2, rows, D)] + [pair] * 4,
        (shaped((2, 2, CH, CH)),) * 2 + (shaped((2, 1, CH), f32),),
        [message, message, spec((1, 1, CH), lambda j, *_: (j, 0, 0))],
        4 * rows * D * 2 * CH,
        deps=deps,
    )


def combine_body(counts, info, *refs):
    ins, outs = refs[: sum(counts)], refs[sum(counts) :]
    at = 0
    for count, out in zip(counts, outs):
        terms = ins[at : at + count]
        at += count

        def add(terms=terms, out=out):
            out[...] = sum(a[...].astype(f32) for a in terms).astype(bf16)

        if len(out.shape) == 3:
            add()
        else:
            pl.when(pl.program_id(0) == 0)(add)


def combine(info, big, small, deps=()):
    steps = 2
    part = 2 * CH // steps
    ins, in_specs, outs, out_specs = [], [], [], []
    for job in big:
        for array, row in job:
            ins.append(array.reshape(-1, part, CH))
            in_specs.append(spec((1, part, CH), lambda j, _, at=row // part: (at + j, 0, 0)))
        outs.append(shaped((steps, part, CH)))
        out_specs.append(spec((1, part, CH), lambda j, _: (j, 0, 0)))
    for job in small:
        ins += job
        in_specs += [whole(*a.shape) for a in job]
        outs.append(shaped(job[0].shape))
        out_specs.append(whole(*job[0].shape))
    results = call(
        functools.partial(combine_body, [len(job) for job in (*big, *small)]),
        "combine",
        steps,
        info,
        ins,
        in_specs,
        outs,
        out_specs,
        0,
        deps=deps,
    )
    count = len(big)
    return [a.reshape(2, CH, CH) for a in results[:count]] + list(results[count:])


def finish_blocks_body(info, *refs):
    *sums, out = refs
    j = pl.program_id(0)
    for n in range(len(sums) // 2):
        here, there = sums[2 * n : 2 * n + 2]

        @pl.when((j >= 2 * n) & (j < 2 * n + 2))
        def _(here=here, there=there):
            out[...] = here[0].astype(f32) + there[0].astype(f32)


def finish_blocks(info, sums, axis, deps=()):
    count = len(sums)
    arrays = [a for pair in sums for a in pair]
    blocks = [
        spec((1, CH, CH), lambda j, _, n=n: (jnp.clip(j - 2 * n, 0, 1), 0, 0))
        for n in range(count)
        for _ in range(2)
    ]
    return call(
        finish_blocks_body,
        "finish_blocks",
        2 * count,
        info,
        arrays,
        blocks,
        shaped((2 * count * CH, CH) if axis == 0 else (CH, 2 * count * CH), f32),
        spec((CH, CH), lambda j, _: (j, 0) if axis == 0 else (0, j)),
        0,
        deps=deps,
    )


def finish_pair_body(info, here, there, *outs):
    for n, out in enumerate(outs):
        out[...] = here[n].astype(f32) + there[n].astype(f32)


def finish_pair(info, here, there, deps=()):
    part = CH // 2
    return call(
        finish_pair_body,
        "finish_pair",
        2,
        info,
        (here, there),
        [spec((2, part, CH), lambda j, _: (0, j, 0))] * 2,
        (shaped((CH, CH), f32),) * 2,
        [spec((part, CH), lambda j, _: (j, 0))] * 2,
        0,
        deps=deps,
    )


def finish_out_body(info, own, back, near, x, shift, out):
    total = own[...].astype(f32) + back[...].astype(f32) + near[...].astype(f32)
    out[...] = (x[...].astype(f32) + total + shift[...].astype(f32)).astype(bf16)


def finish_out(info, shares, x, shift, deps=()):
    seqs, rows, _ = x.shape
    both = spec((seqs, rows // 2, CH), lambda j, _: (0, j, 0))
    return call(
        finish_out_body,
        "finish_out",
        2,
        info,
        (*shares, x, shift),
        [both] * 4 + [whole(1, CH)],
        shaped(x.shape),
        both,
        0,
        deps=deps,
    )


def finish_in_body(info, *refs):
    shares, tails, wide = refs[:6], refs[6:12], refs[12:18]
    x, ct, stats, gain, out, sums = refs[18:]
    weight = gain[...].astype(f32)
    for s in range(2):
        at = slice(3 * s, 3 * s + 3)
        total = sum(a[...].astype(f32) for a in shares[at])
        tail = sum(a[...].astype(f32) for a in tails[at])
        column = jnp.concatenate([tail[:8], stats[s]], axis=0).T
        plain, cross = column[:, 0:1], column[:, 1:2]
        average, root = column[:, 8:9], column[:, 9:10]
        standard = (x[s].astype(f32) - average) * root
        scaled = total * weight - plain * (1.0 / D) - standard * (cross * (1.0 / D))
        out[s] = ct[s].astype(f32) + root * scaled

    @pl.when(pl.program_id(0) == 0)
    def _():
        sums[...] = sum(a[...].astype(f32)[8:] for a in wide)


def finish_in(info, shares, x, ct, stats, gain, deps=()):
    seqs, rows, _ = x.shape
    part = rows // 2
    both = spec((seqs, part, CH), lambda j, _: (0, j, 0))
    last = rows // TAIL
    return call(
        finish_in_body,
        "finish_in",
        2,
        info,
        (*shares, *shares, *shares, x, ct, stats, gain),
        [spec((part, CH), lambda j, _: (j, 0))] * 6
        + [spec((TAIL, part), lambda j, _: (last, j))] * 6
        + [spec((TAIL, CH), lambda j, _: (last, 0))] * 6
        + [both, both, spec((seqs, 8, part), lambda j, _: (0, 0, j)), whole(1, CH)],
        (shaped(x.shape, f32), shaped((TAIL // 2, CH), f32)),
        [both, whole(TAIL // 2, CH)],
        0,
        deps=deps,
    )


SMALL = 16


def small_table_body(info, query, pair, up, out, last, table):
    table[...] = jnp.zeros(table.shape, f32)
    table[0:1, :] = query[...]
    table[1:2, :] = pair[0]
    table[2:3, :] = pair[1]
    for n in range(4):
        table[3 + n : 4 + n, :] = up[:, CH * n : CH * (n + 1)]
    table[7:8, :] = out[...]
    table[8:10, :] = last[0:2, :]


def small_table(info, arrays):
    return call(
        small_table_body,
        "small_table",
        1,
        info,
        arrays,
        [whole(*a.shape) for a in arrays],
        shaped((SMALL, CH), f32),
        whole(SMALL, CH),
        0,
    )


def ring(array, step):
    return lax.ppermute(array, "tp", [(i, (i + step) % N_TP) for i in range(N_TP)])


class Gather:
    def __init__(self, own):
        self.own = own

    def forth(self, clock):
        self.own = clock.go(self.own)
        self.behind = ring(self.own, 1)

    def back(self):
        self.ahead = ring(self.own, -1)

    def sides(self, clock):
        self.forth(clock)
        self.ahead = ring(self.own, -1)

    def onward(self, clock):
        self.behind = clock.go(self.behind)
        self.far = ring(self.behind, 1)
        self.parts = (self.own, self.behind, self.ahead, self.far)


class Scatter:
    def __init__(self, chunks):
        self.own, self.share, self.first, self.given = chunks

    def forward(self, clock):
        self.far = ring(clock.go(self.first), 1)

    def backward(self, clock):
        self.back = ring(clock.go(self.given), -1)

    def both(self):
        return [self.share, self.far]

    def onward(self, both):
        self.near = ring(both, 1)

    def shares(self):
        return self.own, self.back, self.near


class Reduction:
    def __init__(self, kept, given, clock, two):
        self.kept, self.two = kept, two
        self.got = swap(clock.go(given), "dp", 1, N_DP)
        self.moved, self.here, self.there = {}, {}, {}

    def across(self, n):
        row = (self.kept.shape[1] + 2 * n) * CH
        return [(self.kept, row), (self.got, row)]

    def here_sum(self, n):
        row = 2 * n * CH
        return [(self.kept, row), (self.got, row), (self.moved[n], 0)]

    def over_x(self, n, across):
        self.moved[n] = swap(across, "dp", 2, N_DP)

    def over_y(self, n, here):
        self.here[n] = here
        self.there[n] = swap(here, "ctx", 1, 2) if self.two else lax.psum(here, "ctx")

    def sums(self, n):
        if self.two:
            return self.here[n], self.there[n]
        return self.there[n], jnp.zeros_like(self.there[n])


def body(
    block_in,
    doc_starts,
    query_weight,
    key_weight,
    value_weight,
    output_weight,
    up_weight,
    down_weight,
    query_bias,
    key_bias,
    value_bias,
    up_bias,
    output_bias,
    norm_gain,
    norm_shift,
    cotangent,
):
    seqs, rows, _ = block_in.shape
    d, c, t = lax.axis_index("dp"), lax.axis_index("ctx"), lax.axis_index("tp")
    n_ctx = lax.axis_size("ctx")
    two = n_ctx == 2
    info = jnp.stack([t, c, d]).astype(jnp.int32)

    clock = Clock()

    x = Gather(block_in)
    x.forth(clock)
    small = jnp.concatenate(
        [query_bias, key_bias, value_bias, up_bias, output_bias, norm_gain, norm_shift]
    )
    size = small.size
    near = swap(small, "dp", 1, N_DP)
    flip = (d & 1) == 1
    pair = jnp.concatenate([jnp.where(flip, near, small), jnp.where(flip, small, near)])
    across = swap(pair, "dp", 2, N_DP)
    flip = (d & 2) == 2
    small_here = jnp.concatenate([jnp.where(flip, across, pair), jnp.where(flip, pair, across)])
    small_here = small_here.reshape(N_DP, size)

    def small_of(first, length):
        return small_here[:, first : first + length].reshape(1, -1)

    share = query_bias.size
    share_units = up_bias.size
    qkv_bias = jnp.concatenate([small_of(n * share, share) for n in range(3)], axis=1)
    up_shift = small_of(3 * share, share_units)
    output_shift = small_of(3 * share + share_units, share)
    gain_here = small_of(4 * share + share_units, share)
    shift_here = small_of(5 * share + share_units, share)
    both = jnp.concatenate([gain_here, shift_here], axis=0)
    others = [ring(both, -r) for r in range(1, N_TP)]
    wq_shard = jnp.concatenate([query_weight, key_weight, value_weight], axis=1)
    shards_q = Shards(tie(wq_shard, across), 0, d, c, two)
    shards_q.over_x(clock)
    shards_u = Shards(up_weight, 0, d, c, two, made=False)
    wo_shard = jnp.concatenate([output_weight, down_weight], axis=0)
    shards_o = Shards(wo_shard, 1, d, c, two)
    clock.sync(x.behind, shards_q.first, *others, shards_u.part)

    x.back()
    shards_q.over_y(clock)
    shards_u.over_x(clock)
    shards_q.near_core(clock)
    circle = jnp.concatenate([both, *others] * 2, axis=1)
    gain_shift = lax.dynamic_slice_in_dim(circle, (N_TP - t) % N_TP * CH, D, 1)
    gain, shift = gain_shift[0:1], gain_shift[1:2]

    here = c * rows + jnp.arange(rows, dtype=jnp.int32)
    tables, opening = rotary_tables(doc_starts, here)
    blocks = 1 if two else n_ctx
    before, _ = rotary_tables(doc_starts, jnp.arange(blocks * rows, dtype=jnp.int32))
    before = [a.reshape(seqs, blocks, rows, 128) for a in before]

    clock.sync(shards_q.second, shards_u.first, x.ahead, shards_q.near, shards_o.part)
    shards_u.near_core(clock)

    x.onward(clock)
    shards_u.over_y(clock)
    shards_o.over_x(clock)
    shards_q.far_core(clock)
    clock.sync(
        x.far,
        *shards_q.far_near,
        shards_u.second,
        shards_o.first,
        *before,
    )

    def send_keys(s):
        kv[s] = clock.go(kv[s])
        if two:
            kvp[s] = lax.ppermute(kv[s], "ctx", [(0, 1)])[None]
        else:
            kvp[s] = lax.all_gather(kv[s], "ctx", axis=0, tiled=False)

    def attention_step(s):
        return attention(
            info,
            s,
            opening[:, None],
            q,
            kv[s],
            kvp[s],
            datt,
            tables,
            before,
            deps=clock.marks,
        )

    def returned(sent):
        if two:
            return lax.ppermute(clock.go(sent[0]), "ctx", [(1, 0)])
        return lax.psum_scatter(clock.go(sent), "ctx", scatter_dimension=0, tiled=False)

    def back_in_step(s):
        return back_in(
            layout,
            info,
            s,
            x.parts,
            dq[s],
            dkv[s],
            sent[s],
            dup,
            shards_q.pieces,
            shards_u.pieces,
            gain,
            stats,
            deps=clock.marks,
        )

    layout = layout_of(two)
    kvp, att, dq, dkv, sent = ([None] * seqs for _ in range(5))

    shards_o.over_y(clock)
    shards_u.far_core(clock)
    ct = Gather(cotangent)
    ct.behind, ct.ahead = ring(ct.own, 1), ring(ct.own, -1)
    normed, stats, q, *kv = norm_qkv(
        layout, info, x.parts, gain, shift, shards_q.pieces, qkv_bias, tables, deps=clock.marks
    )
    clock.sync(normed, *shards_u.far_near, shards_u.near, ct.behind)

    shards_o.near_core(clock)
    ct.onward(clock)
    hidden, slope = mlp_up(layout, info, normed, shards_u.pieces, up_shift, deps=clock.marks)
    clock.sync(hidden, shards_o.second, ct.ahead, shards_o.near)

    shards_o.far_core(clock)
    send_keys(0)
    send_keys(1)
    clock.sync(*shards_o.far_near)
    out_parts = out_hidden(layout, info, hidden, shards_o.pieces, deps=clock.marks)
    clock.sync(out_parts[0], ct.far)

    cf, out_bias_sum, datt, dup = back_out(
        layout, info, ct.parts, shards_o.pieces, slope, deps=clock.marks
    )
    clock.sync(datt, kvp[0], kvp[1])

    def added(big, small=()):
        return combine(info, big, list(small), deps=clock.marks)

    up_kept, up_given, up_sum = grad_up(info, normed, dup, deps=clock.marks)
    clock.sync(up_kept)
    up = Reduction(up_kept, up_given, clock, two)
    att[0], dq[0], dkv[0], sent[0] = attention_step(0)
    clock.sync(att[0], up.got)

    sent[0] = returned(sent[0])
    across, across_1 = added([up.across(0), up.across(1)])
    up.over_x(0, across)
    clock.sync(across)
    down_kept, down_given = grad_down(info, hidden, cf, deps=clock.marks)
    clock.sync(down_kept, *clock.marks)
    att[1], dq[1], dkv[1], sent[1] = attention_step(1)
    clock.sync(att[1], sent[0], up.moved[0])

    sent[1] = returned(sent[1])
    up.over_x(1, clock.go(across_1))
    down = Reduction(down_kept, down_given, clock, two)
    (here,) = added([up.here_sum(0)])
    clock.sync(here)
    out = Scatter(out_heads(layout, info, att, out_parts, shards_o.pieces, deps=clock.marks))
    clock.sync(out.own, *clock.marks)
    head_kept, head_given, query_sum = grad_out_query(
        info, normed, cf, att, dq, deps=clock.marks
    )
    clock.sync(head_kept, down.got)
    across, across_1 = added([down.across(0), down.across(1)])
    clock.sync(across, sent[1])
    clock.sync(up.moved[1])

    out.forward(clock)
    up.over_y(0, clock.go(here))
    down.over_x(0, clock.go(across))
    head = Reduction(head_kept, head_given, clock, two)
    (here,) = added([up.here_sum(1)])
    clock.sync(here)
    back_0 = Scatter(back_in_step(0))
    clock.sync(back_0.own, out.far)
    clock.sync(up.there[0])
    clock.sync(down.moved[0], head.got)

    back_0.forward(clock)
    back_0.backward(clock)
    up.over_y(1, clock.go(here))
    down.over_x(1, clock.go(across_1))
    here, across, out_both = added([down.here_sum(0), head.across(0)], [out.both()])
    clock.sync(here)
    pair_kept, pair_given, pair_sum = grad_key_value(info, normed, dkv, sent, deps=clock.marks)
    clock.sync(pair_kept, back_0.far, back_0.back)
    clock.sync(up.there[1])
    clock.sync(down.moved[1])

    out.backward(clock)
    down.over_y(0, clock.go(here))
    head.over_x(0, clock.go(across))
    pair = Reduction(pair_kept, pair_given, clock, two)
    here, both_0 = added([down.here_sum(1)], [back_0.both()])
    clock.sync(here)
    back_1 = Scatter(back_in_step(1))
    clock.sync(back_1.own, out.back)
    clock.sync(down.there[0])
    clock.sync(head.moved[0], pair.got)

    back_1.forward(clock)
    back_1.backward(clock)
    down.over_y(1, clock.go(here))
    across, here = added([pair.across(0), head.here_sum(0)])
    pair.over_x(0, across)
    clock.sync(across)
    up_wg = finish_blocks(info, [up.sums(0), up.sums(1)], 1, deps=clock.marks)
    clock.sync(up_wg, back_1.far, back_1.back)
    clock.sync(down.there[1])
    clock.sync(pair.moved[0])

    back_0.onward(clock.go(both_0))
    head.over_y(0, clock.go(here))
    here, both_1 = added([pair.here_sum(0)], [back_1.both()])
    back_1.onward(both_1)
    clock.sync(here)
    down_wg = finish_blocks(info, [down.sums(0), down.sums(1)], 0, deps=clock.marks)
    clock.sync(down_wg, back_0.near, back_1.near)
    clock.sync(head.there[0])

    out.onward(clock.go(out_both))
    pair.over_y(0, clock.go(here))
    in_grad, last = finish_in(
        info,
        (*back_0.shares(), *back_1.shares()),
        block_in,
        cotangent,
        stats,
        gain_here,
        deps=clock.marks,
    )
    clock.sync(in_grad)
    table = small_table(info, (query_sum, pair_sum, up_sum, out_bias_sum, last))
    output_wg, query_wg = finish_pair(info, *head.sums(0), deps=clock.marks)
    table = table + swap(table, "dp", 1, N_DP)
    table = table + swap(table, "dp", 2, N_DP)
    table = table + swap(table, "ctx", 1, 2) if two else lax.psum(table, "ctx")
    block_out = finish_out(info, out.shares(), block_in, output_shift)
    key_wg, value_wg = finish_pair(info, *pair.sums(0))

    share = CH // N_DP
    mine = lax.dynamic_slice_in_dim(table, d * share, share, 1)
    query_bg, key_bg, value_bg = mine[0], mine[1], mine[2]
    output_bg, gain_g, shift_g = mine[7], mine[8], mine[9]
    up_bg = lax.dynamic_slice_in_dim(table, 3 + d, 1, 0).reshape(-1)
    return (
        block_out,
        in_grad,
        query_wg,
        key_wg,
        value_wg,
        output_wg,
        up_wg,
        down_wg,
        query_bg,
        key_bg,
        value_bg,
        up_bg,
        output_bg,
        gain_g,
        shift_g,
    )


def solution(mesh):
    return jax.shard_map(
        body,
        mesh=mesh,
        in_specs=(
            P("dp", "ctx", "tp"),
            P("dp", None),
            P("dp", "tp"),
            P("dp", "tp"),
            P("dp", "tp"),
            P("tp", "dp"),
            P("dp", "tp"),
            P("tp", "dp"),
        )
        + (P(("tp", "dp")),) * 7
        + (P("dp", "ctx", "tp"),),
        out_specs=(
            P("dp", "ctx", "tp"),
            P("dp", "ctx", "tp"),
            P("dp", "tp"),
            P("dp", "tp"),
            P("dp", "tp"),
            P("tp", "dp"),
            P("dp", "tp"),
            P("tp", "dp"),
        )
        + (P(("tp", "dp")),) * 7,
        check_vma=False,
    )
```

```python
import functools
import math

import jax
import jax.numpy as jnp
from jax import lax
from jax.experimental import pallas as pl
from jax.experimental.pallas import tpu as pltpu
from jax.sharding import PartitionSpec as P

HEAD_DIM = 64
ROT = 32
D = 2048
N_DP = 4
N_TP = 4
CH = D // N_TP
EPS = 1e-05
NEG = -1e30
VMEM = 127 * 2**19
COST = 0.02

bf16 = jnp.bfloat16
f32 = jnp.float32


def dot_nn(a, b):
    return lax.dot_general(a, b, (((1,), (0,)), ((), ())), preferred_element_type=f32)


def dot_nt(a, b):
    return lax.dot_general(a, b, (((1,), (1,)), ((), ())), preferred_element_type=f32)


def dot_tn(a, b):
    return lax.dot_general(a, b, (((0,), (0,)), ((), ())), preferred_element_type=f32)


def spec(block, index):
    return pl.BlockSpec(block, index)


def whole(*block):
    zeros = (0,) * len(block)
    return pl.BlockSpec(block, lambda g, *_: zeros)


def once(*block):
    zeros = (0,) * len(block)
    return pl.BlockSpec(block, lambda g, *_: zeros, pipeline_mode=pl.Buffered(1))


def one_of(s, *block):
    zeros = (0,) * len(block)
    return pl.BlockSpec((None, *block), lambda g, *_: (s, *zeros))


def shaped(shape, dtype=bf16):
    return jax.ShapeDtypeStruct(tuple(shape), dtype)


ANYWHERE = pl.BlockSpec(memory_space=pl.ANY)


def call(body, name, grid, info, ins, in_specs, outs, out_specs, flops, scratch=(), deps=()):
    moved = sum(math.prod(a.shape) * a.dtype.itemsize for a in (*ins, *jax.tree.leaves(outs)))
    first, last = 1 + len(ins), 1 + len(ins) + len(deps)

    def without_deps(*refs):
        body(*refs[:first], *refs[last:])

    return pl.pallas_call(
        without_deps,
        grid_spec=pltpu.PrefetchScalarGridSpec(
            num_scalar_prefetch=1,
            grid=(grid,),
            in_specs=[*in_specs, *[ANYWHERE] * len(deps)],
            out_specs=out_specs,
            scratch_shapes=list(scratch),
        ),
        out_shape=outs,
        compiler_params=pltpu.CompilerParams(vmem_limit_bytes=VMEM),
        cost_estimate=pl.CostEstimate(
            flops=int(flops * COST), bytes_accessed=int(moved * COST), transcendentals=0
        ),
        name=name,
    )(info, *ins, *deps)


def tie(value, *deps):
    def nothing(*refs):
        del refs

    return pl.pallas_call(
        nothing,
        in_specs=[ANYWHERE] * (1 + len(deps)),
        out_specs=ANYWHERE,
        out_shape=shaped(value.shape, value.dtype),
        input_output_aliases={0: 0},
        compiler_params=pltpu.CompilerParams(vmem_limit_bytes=VMEM),
        cost_estimate=pl.CostEstimate(flops=0, bytes_accessed=0, transcendentals=0),
        name="tie",
    )(value, *deps)


def columns(index, width=CH):
    return pl.ds(pl.multiple_of(index * width, width), width)


def layout_of(two):
    if two:
        halves = [("c", CH // 2), ("other", CH // 2)]
    else:
        halves = [("", CH)]
    return [(0, "", CH), (1, "", CH)] + [(r, *half) for r in (2, 3) for half in halves]


def piece_offset(info, half):
    return {"": 0, "c": info[1], "other": 1 - info[1]}[half] * (CH // 2)


def piece_window(info, piece):
    r, half, size = piece
    start = (info[2] ^ r) * CH + piece_offset(info, half)
    return pl.ds(pl.multiple_of(start, size), size)


class Clock:
    def __init__(self):
        self.marks = ()

    def go(self, value):
        return tie(value, *self.marks) if self.marks else value

    def sync(self, *arrays):
        def nothing(*refs):
            del refs

        self.marks = (
            pl.pallas_call(
                nothing,
                in_specs=[ANYWHERE] * (len(arrays) + len(self.marks)),
                out_specs=ANYWHERE,
                out_shape=shaped((8, 128), f32),
                compiler_params=pltpu.CompilerParams(vmem_limit_bytes=VMEM),
                cost_estimate=pl.CostEstimate(flops=0, bytes_accessed=0, transcendentals=0),
                name="sync",
            )(*arrays, *self.marks),
        )


def swap(array, axis, bit, size):
    return lax.ppermute(array, axis, [(i, i ^ bit) for i in range(size)])


class Shards:
    def __init__(self, own, axis, d, c, two, made=True):
        self.own, self.two, self.made = own, two, made
        size = own.shape[axis] // 2
        self.part = lax.dynamic_slice_in_dim(own, c * size, size, axis) if two else own

    def near_core(self, clock):
        self.own = clock.go(self.own) if self.made else self.own
        self.near = swap(self.own, "dp", 1, N_DP)

    def over_x(self, clock):
        self.first = swap(clock.go(self.part), "dp", 2, N_DP)

    def over_y(self, clock):
        self.first = clock.go(self.first)
        self.second = swap(self.first, "ctx", 1, 2) if self.two else self.first

    def far_core(self, clock):
        self.first = clock.go(self.first)
        far = [self.first]
        if self.two:
            self.second = clock.go(self.second)
            far.append(self.second)
        self.far_near = [swap(a, "dp", 1, N_DP) for a in far]
        self.pieces = [self.own, self.near, *far, *self.far_near]


def rotary_tables(starts, positions):
    before = starts[:, None, :] <= positions[None, :, None]
    opening = jnp.max(jnp.where(before, starts[:, None, :], 0), axis=2)
    relative = (positions[None, :] - opening).astype(f32)
    half = ROT // 2
    lane = jnp.arange(128, dtype=jnp.int32) % HEAD_DIM
    frequency = jnp.exp((lane % half).astype(f32) * (-math.log(10000.0) / half))
    angles = relative[:, :, None] * jnp.where(lane < ROT, frequency, 0.0)
    sine = jnp.sin(angles)
    return (
        jnp.cos(angles),
        jnp.where(lane < half, -sine, 0.0),
        jnp.where(lane >= half, sine, 0.0),
    ), opening


def add_rounded(a, b):
    return (a.astype(f32) + b.astype(f32)).astype(bf16)


def turn(x, own, up, down):
    return x * own + pltpu.roll(x, 112, 1) * up + pltpu.roll(x, 16, 1) * down


def turn_back(x, own, up, down):
    return x * own - pltpu.roll(x, 112, 1) * up - pltpu.roll(x, 16, 1) * down


def stream_pieces(layout, info, sources, held, sems, axis, blocks):
    j = pl.program_id(0)

    def copies(block):
        cut = pl.ds(pl.multiple_of(block * CH, CH), CH)
        for n, (piece, source) in enumerate(zip(layout, sources)):
            window = piece_window(info, piece)
            if axis == 0:
                pair = source.at[:, cut], held.at[window, cut]
            else:
                pair = source.at[cut, :], held.at[cut, window]
            yield pltpu.make_async_copy(*pair, sems.at[block, n])

    @pl.when(j == 0)
    def _():
        for block in range(blocks):
            for copy in copies(block):
                copy.start()

    for copy in copies(j):
        copy.wait()


def norm_qkv_body(layout, info, x0, xa, xc, xb, gain, shift, bias, own, up, down, *refs):
    *w, normed, stats, q, kv0, kv1, columns_held, held, sems = refs
    j = pl.program_id(0)
    t = info[0]
    seqs, rows, _ = x0.shape
    stream_pieces(layout, info, w, held, sems, 0, 3)

    @pl.when(j == 0)
    def _():
        parts = [(x0, t), (xa, (t + 3) % N_TP), (xc, (t + 1) % N_TP), (xb, (t + 2) % N_TP)]
        tile = 128

        def rows_of(i, carry):
            s = i // (rows // tile)
            window = pl.ds(pl.multiple_of((i % (rows // tile)) * tile, tile), tile)
            x = [part[s, window, :].astype(f32) for part, _ in parts]
            average = sum(jnp.sum(a, axis=1, keepdims=True) for a in x) * (1.0 / D)
            x = [a - average for a in x]
            variance = sum(jnp.sum(a * a, axis=1, keepdims=True) for a in x) * (1.0 / D)
            root = lax.rsqrt(variance + EPS)
            columns_held[s, window, 0:1] = average
            columns_held[s, window, 1:2] = root
            for a, (_, index) in zip(x, parts):
                at = columns(index)
                y = a * root * gain[:, at].astype(f32) + shift[:, at].astype(f32)
                normed[s, window, at] = y.astype(bf16)
            return carry

        columns_held[...] = jnp.zeros(columns_held.shape, f32)
        lax.fori_loop(0, seqs * rows // tile, rows_of, 0)
        for s in range(seqs):
            stats[s] = columns_held[s].T[: stats.shape[1]]

    for s, kv in ((0, kv0), (1, kv1)):
        y = dot_nn(normed[s], held[:, columns(j)]) + bias[...].astype(f32)

        def rotated(s=s, y=y):
            parts = [
                turn(y[:, 128 * n : 128 * n + 128], own[s], up[s], down[s])
                for n in range(CH // 128)
            ]
            return jnp.concatenate(parts, axis=1).astype(bf16)

        @pl.when(j == 0)
        def _(s=s, rotated=rotated):
            q[s] = rotated()

        @pl.when(j == 1)
        def _(kv=kv, rotated=rotated):
            kv[0] = rotated()

        @pl.when(j == 2)
        def _(kv=kv, y=y):
            kv[0] = y.astype(bf16)


def norm_qkv(layout, info, parts, gain, shift, w, bias, tables, deps=()):
    seqs, rows, _ = parts[0].shape
    outs = (
        shaped((seqs, rows, D)),
        shaped((seqs, 8, rows), f32),
        shaped((seqs, rows, CH)),
        shaped((2, rows, CH)),
        shaped((2, rows, CH)),
    )
    pair = spec((1, rows, CH), lambda j, *_: (jnp.maximum(j - 1, 0), 0, 0))
    return call(
        functools.partial(norm_qkv_body, layout),
        "norm_qkv",
        3,
        info,
        (*parts, gain, shift, bias, *tables, *w),
        [whole(seqs, rows, CH)] * 4
        + [whole(1, D)] * 2
        + [spec((1, CH), lambda j, *_: (0, j))]
        + [whole(seqs, rows, 128)] * 3
        + [ANYWHERE] * len(w),
        outs,
        [
            whole(seqs, rows, D),
            whole(seqs, 8, rows),
            whole(seqs, rows, CH),
            pair,
            pair,
        ],
        2 * seqs * rows * D * 3 * CH,
        [
            pltpu.VMEM((seqs, rows, 128), f32),
            pltpu.VMEM((D, 3 * CH), bf16),
            pltpu.SemaphoreType.DMA((3, len(w))),
        ],
        deps=deps,
    )


def mlp_up_body(layout, info, normed, bias, *refs):
    *w, hidden, grad, held, sems = refs
    j = pl.program_id(0)
    stream_pieces(layout, info, w, held, sems, 0, held.shape[1] // CH)
    root = math.sqrt(2.0 / math.pi)
    for s in range(normed.shape[0]):
        u = dot_nn(normed[s], held[:, columns(j)]) + bias[...].astype(f32)
        square = u * u
        t = jnp.tanh(u * (root + (root * 0.044715) * square))
        half = 0.5 + 0.5 * t
        hidden[s] = (u * half).astype(bf16)
        slope = root + (3 * 0.044715 * root) * square
        grad[s] = (half + (0.5 * u) * (1.0 - t * t) * slope).astype(bf16)


def mlp_up(layout, info, normed, w, bias, deps=()):
    seqs, rows, _ = normed.shape
    units = w[0].shape[1]
    block = spec((seqs, rows, CH), lambda j, *_: (0, 0, j))
    return call(
        functools.partial(mlp_up_body, layout),
        "mlp_up",
        units // CH,
        info,
        (normed, bias, *w),
        [whole(seqs, rows, D), spec((1, CH), lambda j, *_: (0, j))] + [ANYWHERE] * len(w),
        (shaped((seqs, rows, units)),) * 2,
        [block] * 2,
        2 * seqs * rows * D * units,
        [pltpu.VMEM((D, units), bf16), pltpu.SemaphoreType.DMA((units // CH, len(w)))],
        deps=deps,
    )


def back_out_body(layout, info, c0, ca, cc, cb, slope, *refs):
    *w, cf, bias_grad, datt, dup, held, sems, cf_sems = refs
    j = pl.program_id(0)
    t = info[0]
    seqs = c0.shape[0]
    parts = [(c0, t), (ca, (t + 3) % N_TP), (cc, (t + 1) % N_TP), (cb, (t + 2) % N_TP)]
    stream_pieces(layout, info, w, held, sems, 1, held.shape[0] // CH)
    copies = [
        pltpu.make_async_copy(part, cf.at[:, :, columns(index)], cf_sems.at[n])
        for n, (part, index) in enumerate(parts)
    ]

    @pl.when(j == 0)
    def _():
        for copy in copies:
            copy.start()
        bias_grad[...] = sum(
            jnp.sum(c0[s].astype(f32), axis=0, keepdims=True) for s in range(seqs)
        )

    for s in range(seqs):
        y = sum(dot_nt(part[s], held[columns(j), columns(index)]) for part, index in parts)

        @pl.when(j == 0)
        def _(s=s, y=y):
            datt[s] = y.astype(bf16)

        @pl.when(j > 0)
        def _(s=s, y=y):
            dup[s] = (y * slope[s].astype(f32)).astype(bf16)

    @pl.when(j == pl.num_programs(0) - 1)
    def _():
        for copy in copies:
            copy.wait()


def back_out(layout, info, parts, w, slope, deps=()):
    seqs, rows, units = slope.shape
    later = spec((seqs, rows, CH), lambda j, *_: (0, 0, jnp.maximum(j - 1, 0)))
    return call(
        functools.partial(back_out_body, layout),
        "back_out",
        1 + units // CH,
        info,
        (*parts, slope, *w),
        [once(seqs, rows, CH)] * 4 + [later] + [ANYWHERE] * len(w),
        (
            shaped((seqs, rows, D)),
            shaped((1, CH), f32),
            shaped((seqs, rows, CH)),
            shaped((seqs, rows, units)),
        ),
        [ANYWHERE, whole(1, CH), whole(seqs, rows, CH), later],
        2 * seqs * rows * D * (CH + units),
        [
            pltpu.VMEM((CH + units, D), bf16),
            pltpu.SemaphoreType.DMA((1 + units // CH, len(w))),
            pltpu.SemaphoreType.DMA((len(parts),)),
        ],
        deps=deps,
    )


def attention_body(
    blocks, info, low, q, kv, kvp, do, own, up, down, ownp, upp, downp,
    att, dq, dkv, dkvp, scores, probs,
):
    rows = q.shape[0]
    before, start = info[1], info[1] * rows
    lane = lax.broadcasted_iota(jnp.int32, (rows, 128), 1)
    key_row = lax.broadcasted_iota(jnp.int32, (rows, 1), 0)
    query_at = start + lax.broadcasted_iota(jnp.int32, (1, rows), 1)
    first = low[0]
    do_t = do[...].astype(f32).T
    nothing = jnp.zeros((), bf16)
    outputs = []
    for head in range(2):
        mine = (lane < HEAD_DIM) if head == 0 else (lane >= HEAD_DIM)
        half = slice(HEAD_DIM * head, HEAD_DIM * (head + 1))
        qh = jnp.where(mine, q[...] * jnp.asarray(HEAD_DIM**-0.5, bf16), nothing)
        dh = jnp.where(mine, do[...], nothing)

        key_at = start + key_row
        s = dot_nt(kv[0], qh)
        s = jnp.where((key_at >= first) & (key_at <= query_at), s, NEG)
        scores[blocks] = s
        peak = jnp.max(s, axis=0, keepdims=True)

        def score(n, peak):
            s = dot_nt(kvp[n, 0], qh)
            s = jnp.where(n * rows + key_row >= first, s, NEG)
            scores[n] = s
            return jnp.maximum(peak, jnp.max(s, axis=0, keepdims=True))

        peak = lax.fori_loop(0, before, score, peak)

        def expo(n, total):
            e = jnp.exp(scores[n] - peak)
            scores[n] = e
            return total + jnp.sum(e, axis=0, keepdims=True)

        total = expo(blocks, jnp.zeros((1, rows), f32))
        total = lax.fori_loop(0, before, expo, total)
        scale = 1.0 / total

        def weigh(n, values):
            p = (scores[n] * scale).astype(bf16)
            probs[n] = p
            return dot_tn(values, p)

        out_t = weigh(blocks, kv[1])
        out_t = lax.fori_loop(0, before, lambda n, acc: acc + weigh(n, kvp[n, 1]), out_t)
        delta = jnp.sum(out_t[half] * do_t[half], axis=0, keepdims=True)

        def back(n, keys, values):
            dp = dot_nt(values, dh)
            ds = ((scores[n] * scale) * (dp - delta)).astype(bf16)
            return dot_nn(ds, qh), dot_nn(probs[n], dh), dot_tn(keys, ds)

        dk, dv, dq_t = back(blocks, kv[0], kv[1])
        if head == 0:
            dk_sum, dv_sum = dk, dv
        else:
            dk_sum, dv_sum = dk_sum + dk, dv_sum + dv

        def back_before(n, acc):
            dk, dv, more = back(n, kvp[n, 0], kvp[n, 1])
            dk = turn_back(dk, ownp[n], upp[n], downp[n])
            if head == 0:
                dkvp[n, 0] = dk.astype(bf16)
                dkvp[n, 1] = dv.astype(bf16)
            else:
                dkvp[n, 0] = (dkvp[n, 0].astype(f32) + dk).astype(bf16)
                dkvp[n, 1] = (dkvp[n, 1].astype(f32) + dv).astype(bf16)
            return acc + more

        dq_t = lax.fori_loop(0, before, back_before, dq_t)
        outputs.append((out_t[half], dq_t[half]))

    def clear(n, carry):
        dkvp[n] = jnp.zeros(dkvp.shape[1:], bf16)
        return carry

    lax.fori_loop(before, blocks, clear, 0)
    att[...] = jnp.concatenate([outputs[0][0], outputs[1][0]], axis=0).T.astype(bf16)
    grad = jnp.concatenate([outputs[0][1], outputs[1][1]], axis=0).T * HEAD_DIM**-0.5
    dq[...] = turn_back(grad, own[...], up[...], down[...]).astype(bf16)
    dkv[0] = turn_back(dk_sum, own[...], up[...], down[...]).astype(bf16)
    dkv[1] = dv_sum.astype(bf16)


def attention_two_body(
    info, low, q, kv, kvp, do, own, up, down, ownp, upp, downp, att, dq, dkv, dkvp
):
    rows = q.shape[0]
    part = rows // 2
    before, start = info[1], info[1] * rows

    def tail(x, skipped):
        return x[:, skipped:] if skipped else x

    def merge(acc, x, skipped, op):
        if acc is None:
            return x
        if not skipped:
            return op(acc, x)
        return jnp.concatenate([acc[:, :skipped], op(acc[:, skipped:], x)], axis=1)

    def run(with_before):
        lane = lax.broadcasted_iota(jnp.int32, (rows, 128), 1)
        key_row = lax.broadcasted_iota(jnp.int32, (part, 1), 0)
        query_at = start + lax.broadcasted_iota(jnp.int32, (1, rows), 1)
        first = low[...]
        do_t = do[...].astype(f32).T
        nothing = jnp.zeros((), bf16)
        blocks = []
        for n in range(2):
            if with_before:
                blocks.append((kvp.at[0], n * part, 0, False))
        for n in range(2):
            blocks.append((kv, n * part, n * part, True))
        dk_sum, dv_sum = [0.0] * len(blocks), [0.0] * len(blocks)
        heads = []
        for head in range(2):
            mine = (lane < HEAD_DIM) if head == 0 else (lane >= HEAD_DIM)
            qh = jnp.where(mine, q[...] * jnp.asarray(HEAD_DIM**-0.5, bf16), nothing)
            dh = jnp.where(mine, do[...], nothing)
            heads.append((qh, dh, slice(HEAD_DIM * head, HEAD_DIM * (head + 1))))

        def score(head):
            qh = heads[head][0]
            scores, peak = [], None
            for ref, row, skip, here in blocks:
                s = dot_nt(ref[0, row : row + part], qh[skip:])
                key_at = (start if here else start - rows) + row + key_row
                allowed = key_at >= tail(first, skip)
                if here:
                    allowed = allowed & (key_at <= tail(query_at, skip))
                s = jnp.where(allowed, s, NEG)
                scores.append(s)
                peak = merge(peak, jnp.max(s, axis=0, keepdims=True), skip, jnp.maximum)
            return scores, peak

        def grads(head):
            dh = heads[head][1]
            return [
                dot_nt(ref[1, row : row + part], dh[skip:]) for ref, row, skip, _ in blocks
            ]

        def soften(scores, peak):
            terms, total = [], None
            for s, (_, _, skip, _) in zip(scores, blocks):
                e = jnp.exp(s - tail(peak, skip))
                terms.append(e)
                total = merge(total, jnp.sum(e, axis=0, keepdims=True), skip, jnp.add)
            scale = 1.0 / total
            probs = [e * tail(scale, skip) for e, (_, _, skip, _) in zip(terms, blocks)]
            return probs, [p.astype(bf16) for p in probs]

        def weigh(head, rounded):
            out_t = None
            for n, (ref, row, skip, _) in enumerate(blocks):
                out_t = merge(
                    out_t, dot_tn(ref[1, row : row + part], rounded[n]), skip, jnp.add
                )
                dv_sum[n] = dv_sum[n] + dot_nn(rounded[n], heads[head][1][skip:])
            half = heads[head][2]
            return out_t[half], jnp.sum(out_t[half] * do_t[half], axis=0, keepdims=True)

        def differ(probs, dps, delta):
            return [
                (p * (dp - tail(delta, skip))).astype(bf16)
                for p, dp, (_, _, skip, _) in zip(probs, dps, blocks)
            ]

        def back(head, dss):
            dq_t = None
            for n, (ref, row, skip, _) in enumerate(blocks):
                dk_sum[n] = dk_sum[n] + dot_nn(dss[n], heads[head][0][skip:])
                dq_t = merge(dq_t, dot_tn(ref[0, row : row + part], dss[n]), skip, jnp.add)
            return dq_t[heads[head][2]]

        scores_0 = score(0)
        scores_1 = score(1)
        probs_0, rounded_0 = soften(*scores_0)
        out_0, delta_0 = weigh(0, rounded_0)
        probs_1, rounded_1 = soften(*scores_1)
        dss_0 = differ(probs_0, grads(0), delta_0)
        out_1, delta_1 = weigh(1, rounded_1)
        dq_0 = back(0, dss_0)
        dss_1 = differ(probs_1, grads(1), delta_1)
        dq_1 = back(1, dss_1)
        outputs = [(out_0, dq_0), (out_1, dq_1)]

        att[...] = jnp.concatenate([outputs[0][0], outputs[1][0]], axis=0).T.astype(bf16)
        grad = jnp.concatenate([outputs[0][1], outputs[1][1]], axis=0).T * HEAD_DIM**-0.5
        dq[...] = turn_back(grad, own[...], up[...], down[...]).astype(bf16)
        dk = jnp.concatenate(dk_sum[-2:], axis=0)
        dkv[0] = turn_back(dk, own[...], up[...], down[...]).astype(bf16)
        dkv[1] = jnp.concatenate(dv_sum[-2:], axis=0).astype(bf16)
        if with_before:
            dk = jnp.concatenate(dk_sum[:2], axis=0)
            dkvp[0, 0] = turn_back(dk, ownp[0], upp[0], downp[0]).astype(bf16)
            dkvp[0, 1] = jnp.concatenate(dv_sum[:2], axis=0).astype(bf16)
        else:
            dkvp[...] = jnp.zeros(dkvp.shape, bf16)

    @pl.when(before == 0)
    def _():
        run(False)

    @pl.when(before > 0)
    def _():
        run(True)


def attention(info, s, low, q, kv, kvp, do, tables, tables_before, deps=()):
    _, rows, width = q.shape
    blocks = kvp.shape[0]
    token = spec((rows, 128), lambda g, *_: (0, g))
    query = spec((None, rows, 128), lambda g, *_: (s, 0, g))
    pair = spec((2, rows, 128), lambda g, *_: (0, 0, g))
    pairs = spec((blocks, 2, rows, 128), lambda g, *_: (0, 0, 0, g))
    return call(
        attention_two_body if blocks == 1 else functools.partial(attention_body, blocks),
        "attention",
        width // 128,
        info,
        (low, q, kv, kvp, do, *tables, *tables_before),
        [one_of(s, 1, rows), query, pair, pairs, query]
        + [one_of(s, rows, 128)] * 3
        + [one_of(s, blocks, rows, 128)] * 3,
        (
            shaped((rows, width)),
            shaped((rows, width)),
            shaped((2, rows, width)),
            shaped((blocks, 2, rows, width)),
        ),
        [token, token, pair, pairs],
        48 * rows * rows * width,
        []
        if blocks == 1
        else [
            pltpu.VMEM((blocks + 1, rows, rows), f32),
            pltpu.VMEM((blocks + 1, rows, rows), bf16),
        ],
        deps=deps,
    )


TAIL = 16


def fetch_pieces(layout, sources, targets, sems, axis):
    copies = [[] for _ in range(N_DP)]
    at = [r * CH for r in range(N_DP)]
    n = 0
    for group, target in zip(sources, targets):
        at = [r * CH for r in range(N_DP)]
        for (r, _, size), source in zip(layout, group):
            window = pl.ds(at[r], size)
            place = target.at[window, :] if axis == 0 else target.at[:, window]
            copies[r].append(pltpu.make_async_copy(source, place, sems.at[n]))
            at[r] += size
            n += 1
    return copies


def with_chunk(layout, info, copies, work):
    j = pl.program_id(0)

    @pl.when(j == 0)
    def _():
        for group in copies:
            for copy in group:
                copy.start()

    for r in range(N_DP):

        @pl.when(j == r)
        def _(r=r):
            for copy in copies[r]:
                copy.wait()
            at = r * CH
            for s, half, size in layout:
                if s == r:
                    offset = pl.multiple_of(piece_offset(info, half), size)
                    work(pl.ds(at, size), pl.ds(offset, size))
                    at += size


def chunk_now(info):
    return ((info[2] ^ pl.program_id(0)) + N_TP - info[0]) % N_TP


def out_hidden_body(layout, info, hidden, *refs):
    *w, out, held, sems = refs

    def work(place, window):
        for s in range(hidden.shape[0]):
            out[0, s, :, window] = dot_nn(hidden[s], held[:, place]).astype(bf16)

    lower = [a.at[pl.ds(CH, held.shape[0]), :] for a in w]
    with_chunk(layout, info, fetch_pieces(layout, [lower], [held], sems, 1), work)


def out_hidden(layout, info, hidden, w, deps=()):
    seqs, rows, units = hidden.shape
    return call(
        functools.partial(out_hidden_body, layout),
        "out_hidden",
        N_DP,
        info,
        (hidden, *w),
        [once(seqs, rows, units)] + [ANYWHERE] * len(w),
        shaped((N_DP, seqs, rows, CH)),
        spec((1, seqs, rows, CH), lambda j, *_: (j, 0, 0, 0)),
        2 * seqs * rows * D * units,
        [pltpu.VMEM((units, D), bf16), pltpu.SemaphoreType.DMA((len(w),))],
        deps=deps,
    )


def out_heads_body(layout, info, a0, a1, part, *refs):
    count = len(layout)
    w, outs = refs[:count], refs[count : count + N_TP]
    held, y, sems, out_sems = refs[count + N_TP :]
    j = pl.program_id(0)

    def work(place, window):
        for s, att in ((0, a0), (1, a1)):
            total = dot_nn(att[...], held[:, place]) + part[0, s, :, window].astype(f32)
            y[j, s, :, window] = total.astype(bf16)

    upper = [a.at[pl.ds(0, CH), :] for a in w]
    with_chunk(layout, info, fetch_pieces(layout, [upper], [held], sems, 1), work)
    for r in range(N_TP):

        @pl.when(chunk_now(info) == r)
        def _(r=r):
            pltpu.make_async_copy(y.at[j], outs[r], out_sems.at[r]).start()

    @pl.when(j == N_TP - 1)
    def _():
        for r in range(N_TP):
            pltpu.make_async_copy(y.at[r], outs[r], out_sems.at[r]).wait()


def out_heads(layout, info, att, parts, w, deps=()):
    _, seqs, rows, _ = parts.shape
    return call(
        functools.partial(out_heads_body, layout),
        "out_heads",
        N_TP,
        info,
        (*att, parts, *w),
        [once(rows, CH)] * 2
        + [spec((1, seqs, rows, CH), lambda j, *_: (j, 0, 0, 0))]
        + [ANYWHERE] * len(w),
        (shaped((seqs, rows, CH)),) * N_TP,
        [ANYWHERE] * N_TP,
        2 * seqs * rows * D * CH,
        [
            pltpu.VMEM((CH, D), bf16),
            pltpu.VMEM((N_TP, seqs, rows, CH), bf16),
            pltpu.SemaphoreType.DMA((len(w),)),
            pltpu.SemaphoreType.DMA((N_TP,)),
        ],
        deps=deps,
    )


def back_in_body(layout, info, x0, xa, xc, xb, dq, dkv, back, dup, gain, stats, *refs):
    count = len(layout)
    wq, wu = refs[:count], refs[count : 2 * count]
    *chunks, held_q, held_u, y, xs, row_sums, column_sums, both, sems = refs[2 * count :]
    j = pl.program_id(0)
    rows = dq.shape[0]

    @pl.when(j == 0)
    def _():
        both[...] = add_rounded(dkv[...], back[...])


    def work(place, window):
        part = dot_nt(dup[...], held_u[place, :])
        part = part + dot_nt(dq[...], held_q[place, :CH])
        part = part + dot_nt(both[0], held_q[place, CH : 2 * CH])
        y[:, window] = part + dot_nt(both[1], held_q[place, 2 * CH :])

    copies = fetch_pieces(layout, [wq, wu], [held_q, held_u], sems, 0)
    with_chunk(layout, info, copies, work)
    for r, part in enumerate((x0, xc, xb, xa)):

        @pl.when(chunk_now(info) == r)
        def _(r=r, part=part):
            chunks[r][:rows, :] = y[...].astype(bf16)
            xs[...] = part[...]

    total = y[...]
    turned = stats[...].T
    standard = (xs[...].astype(f32) - turned[:, 0:1]) * turned[:, 1:2]
    cross = total * standard
    weight = gain[...].astype(f32)

    @pl.when(j == 0)
    def _():
        row_sums[...] = jnp.zeros(row_sums.shape, f32)
        column_sums[...] = jnp.zeros(column_sums.shape, f32)

    both = jnp.concatenate(
        [jnp.sum(cross, axis=0, keepdims=True), jnp.sum(total, axis=0, keepdims=True)], axis=0
    )
    column_sums[chunk_now(info), 0:2, :] = both
    row_sums[:, 0:1] += jnp.sum(total * weight, axis=1, keepdims=True)
    row_sums[:, 1:2] += jnp.sum(cross * weight, axis=1, keepdims=True)

    @pl.when(j == N_TP - 1)
    def _():
        turned = row_sums[...].T[: TAIL // 2]
        for r, chunk in enumerate(chunks):
            chunk[rows:, :] = jnp.concatenate([turned, column_sums[r]], axis=0).astype(bf16)


def back_in(layout, info, s, parts, dq, dkv, back, dup, wq, wu, gain, stats, deps=()):
    _, rows, units = dup.shape
    return call(
        functools.partial(back_in_body, layout),
        "back_in",
        N_TP,
        info,
        (*parts, dq, dkv, back, dup, gain, stats, *wq, *wu),
        [one_of(s, rows, CH)] * 4
        + [
            whole(rows, CH),
            whole(2, rows, CH),
            whole(2, rows, CH),
            one_of(s, rows, units),
            spec((1, CH), lambda j, info: (0, info[2] ^ j)),
            one_of(s, 8, rows),
        ]
        + [ANYWHERE] * (2 * len(wq)),
        (shaped((rows + TAIL, CH)),) * N_TP,
        [whole(rows + TAIL, CH)] * N_TP,
        2 * rows * D * (3 * CH + units),
        [
            pltpu.VMEM((D, 3 * CH), bf16),
            pltpu.VMEM((D, units), bf16),
            pltpu.VMEM((rows, CH), f32),
            pltpu.VMEM((rows, CH), bf16),
            pltpu.VMEM((rows, 128), f32),
            pltpu.VMEM((N_TP, TAIL // 2, CH), f32),
            pltpu.VMEM((2, rows, CH), bf16),
            pltpu.SemaphoreType.DMA((2 * len(wq),)),
        ],
        deps=deps,
    )


KEPT = ((0, 0), (2, 1))
GIVEN = ((1, 0), (3, 1))


def grad_up_body(info, normed, dup, kept, given, sums):
    d = info[2]
    rights = (dup[0], dup[1])
    store_by_rows(d, normed, rights, kept, given)
    sums[...] = sum(jnp.sum(b.astype(f32), axis=0, keepdims=True) for b in rights)


def grad_up(info, normed, dup, deps=()):
    _, rows, units = dup.shape
    count = units // CH
    message = spec((2, 1, CH, CH), lambda j, *_: (0, j, 0, 0))
    return call(
        grad_up_body,
        "grad_up",
        count,
        info,
        (normed, dup),
        [whole(2, rows, D), spec((2, rows, CH), lambda j, *_: (0, 0, j))],
        (shaped((2, count, CH, CH)),) * 2 + (shaped((1, units), f32),),
        [message, message, spec((1, CH), lambda j, *_: (0, j))],
        4 * rows * D * units,
        deps=deps,
    )


def grad_down_body(info, hidden, ct, kept, given):
    d = info[2]
    for target, which in ((given, GIVEN), (kept, KEPT)):
        for r, at in which:
            window = columns(d ^ r)
            y = dot_tn(hidden[0], ct[0, :, window]) + dot_tn(hidden[1], ct[1, :, window])
            target[at, 0] = y.astype(bf16)


def grad_down(info, hidden, ct, deps=()):
    _, rows, units = hidden.shape
    count = units // CH
    message = spec((2, 1, CH, CH), lambda j, *_: (0, j, 0, 0))
    return call(
        grad_down_body,
        "grad_down",
        count,
        info,
        (hidden, ct),
        [spec((2, rows, CH), lambda j, *_: (0, 0, j)), once(2, rows, D)],
        (shaped((2, count, CH, CH)),) * 2,
        [message, message],
        4 * rows * D * units,
        deps=deps,
    )


def store_by_rows(d, lefts, rights, kept, given):
    for target, which in ((given, GIVEN), (kept, KEPT)):
        for r, at in which:
            window = columns(d ^ r)
            y = sum(dot_tn(lefts[s, :, window], b) for s, b in enumerate(rights))
            target[at, 0] = y.astype(bf16)


def grad_out_query_body(info, normed, ct, a0, a1, q0, q1, kept, given, sums):
    j = pl.program_id(0)
    d = info[2]

    @pl.when(j == 0)
    def _():
        lefts = (a0[...], a1[...])
        for target, which in ((given, GIVEN), (kept, KEPT)):
            for r, at in which:
                window = columns(d ^ r)
                y = sum(dot_tn(a, ct[s, :, window]) for s, a in enumerate(lefts))
                target[at, 0] = y.astype(bf16)

    @pl.when(j == 1)
    def _():
        rights = (q0[...], q1[...])
        store_by_rows(d, normed, rights, kept, given)
        sums[...] = sum(jnp.sum(b.astype(f32), axis=0, keepdims=True) for b in rights)


def grad_out_query(info, normed, ct, att, dq, deps=()):
    rows = normed.shape[1]
    message = spec((2, 1, CH, CH), lambda j, *_: (0, j, 0, 0))
    return call(
        grad_out_query_body,
        "grad_out_query",
        2,
        info,
        (normed, ct, *att, *dq),
        [whole(2, rows, D)] * 2 + [whole(rows, CH)] * 4,
        (shaped((2, 2, CH, CH)),) * 2 + (shaped((1, CH), f32),),
        [message, message, whole(1, CH)],
        4 * rows * D * 2 * CH,
        deps=deps,
    )


def grad_key_value_body(info, normed, kv0, back0, kv1, back1, kept, given, sums):
    rights = (add_rounded(kv0[0], back0[0]), add_rounded(kv1[0], back1[0]))
    store_by_rows(info[2], normed, rights, kept, given)
    sums[0] = sum(jnp.sum(b.astype(f32), axis=0, keepdims=True) for b in rights)


def grad_key_value(info, normed, dkv, sent, deps=()):
    rows = normed.shape[1]
    message = spec((2, 1, CH, CH), lambda j, *_: (0, j, 0, 0))
    pair = spec((1, rows, CH), lambda j, *_: (j, 0, 0))
    return call(
        grad_key_value_body,
        "grad_key_value",
        2,
        info,
        (normed, dkv[0], sent[0], dkv[1], sent[1]),
        [whole(2, rows, D)] + [pair] * 4,
        (shaped((2, 2, CH, CH)),) * 2 + (shaped((2, 1, CH), f32),),
        [message, message, spec((1, 1, CH), lambda j, *_: (j, 0, 0))],
        4 * rows * D * 2 * CH,
        deps=deps,
    )


def combine_body(counts, info, *refs):
    ins, outs = refs[: sum(counts)], refs[sum(counts) :]
    at = 0
    for count, out in zip(counts, outs):
        terms = ins[at : at + count]
        at += count

        def add(terms=terms, out=out):
            out[...] = sum(a[...].astype(f32) for a in terms).astype(bf16)

        if len(out.shape) == 3:
            add()
        else:
            pl.when(pl.program_id(0) == 0)(add)


def combine(info, big, small, deps=()):
    steps = 2
    part = 2 * CH // steps
    ins, in_specs, outs, out_specs = [], [], [], []
    for job in big:
        for array, row in job:
            ins.append(array.reshape(-1, part, CH))
            in_specs.append(spec((1, part, CH), lambda j, _, at=row // part: (at + j, 0, 0)))
        outs.append(shaped((steps, part, CH)))
        out_specs.append(spec((1, part, CH), lambda j, _: (j, 0, 0)))
    for job in small:
        ins += job
        in_specs += [whole(*a.shape) for a in job]
        outs.append(shaped(job[0].shape))
        out_specs.append(whole(*job[0].shape))
    results = call(
        functools.partial(combine_body, [len(job) for job in (*big, *small)]),
        "combine",
        steps,
        info,
        ins,
        in_specs,
        outs,
        out_specs,
        0,
        deps=deps,
    )
    count = len(big)
    return [a.reshape(2, CH, CH) for a in results[:count]] + list(results[count:])


def finish_blocks_body(info, *refs):
    *sums, out = refs
    j = pl.program_id(0)
    for n in range(len(sums) // 2):
        here, there = sums[2 * n : 2 * n + 2]

        @pl.when((j >= 2 * n) & (j < 2 * n + 2))
        def _(here=here, there=there):
            out[...] = here[0].astype(f32) + there[0].astype(f32)


def finish_blocks(info, sums, axis, deps=()):
    count = len(sums)
    arrays = [a for pair in sums for a in pair]
    blocks = [
        spec((1, CH, CH), lambda j, _, n=n: (jnp.clip(j - 2 * n, 0, 1), 0, 0))
        for n in range(count)
        for _ in range(2)
    ]
    return call(
        finish_blocks_body,
        "finish_blocks",
        2 * count,
        info,
        arrays,
        blocks,
        shaped((2 * count * CH, CH) if axis == 0 else (CH, 2 * count * CH), f32),
        spec((CH, CH), lambda j, _: (j, 0) if axis == 0 else (0, j)),
        0,
        deps=deps,
    )


def finish_pair_body(info, here, there, *outs):
    for n, out in enumerate(outs):
        out[...] = here[n].astype(f32) + there[n].astype(f32)


def finish_pair(info, here, there, deps=()):
    part = CH // 2
    return call(
        finish_pair_body,
        "finish_pair",
        2,
        info,
        (here, there),
        [spec((2, part, CH), lambda j, _: (0, j, 0))] * 2,
        (shaped((CH, CH), f32),) * 2,
        [spec((part, CH), lambda j, _: (j, 0))] * 2,
        0,
        deps=deps,
    )


def finish_last_body(info, own, back, near, x, shift, here, there, out, first, second):
    total = own[...].astype(f32) + back[...].astype(f32) + near[...].astype(f32)
    out[...] = (x[...].astype(f32) + total + shift[...].astype(f32)).astype(bf16)
    finish_pair_body(info, here, there, first, second)


def finish_last(info, shares, x, shift, here, there, deps=()):
    seqs, rows, _ = x.shape
    both = spec((seqs, rows // 2, CH), lambda j, _: (0, j, 0))
    pair = spec((2, CH // 2, CH), lambda j, _: (0, j, 0))
    half = spec((CH // 2, CH), lambda j, _: (j, 0))
    return call(
        finish_last_body,
        "finish_last",
        2,
        info,
        (*shares, x, shift, here, there),
        [both] * 4 + [whole(1, CH), pair, pair],
        (shaped(x.shape), shaped((CH, CH), f32), shaped((CH, CH), f32)),
        [both, half, half],
        0,
        deps=deps,
    )


def finish_in_body(info, *refs):
    shares, tails, wide = refs[:6], refs[6:12], refs[12:18]
    x, ct, stats, gain, out, sums = refs[18:]
    weight = gain[...].astype(f32)
    for s in range(2):
        at = slice(3 * s, 3 * s + 3)
        total = sum(a[...].astype(f32) for a in shares[at])
        tail = sum(a[...].astype(f32) for a in tails[at])
        column = jnp.concatenate([tail[:8], stats[s]], axis=0).T
        plain, cross = column[:, 0:1], column[:, 1:2]
        average, root = column[:, 8:9], column[:, 9:10]
        standard = (x[s].astype(f32) - average) * root
        scaled = total * weight - plain * (1.0 / D) - standard * (cross * (1.0 / D))
        out[s] = ct[s].astype(f32) + root * scaled

    @pl.when(pl.program_id(0) == 0)
    def _():
        sums[...] = sum(a[...].astype(f32)[8:] for a in wide)


def finish_in(info, shares, x, ct, stats, gain, deps=()):
    seqs, rows, _ = x.shape
    part = rows // 2
    both = spec((seqs, part, CH), lambda j, _: (0, j, 0))
    last = rows // TAIL
    return call(
        finish_in_body,
        "finish_in",
        2,
        info,
        (*shares, *shares, *shares, x, ct, stats, gain),
        [spec((part, CH), lambda j, _: (j, 0))] * 6
        + [spec((TAIL, part), lambda j, _: (last, j))] * 6
        + [spec((TAIL, CH), lambda j, _: (last, 0))] * 6
        + [both, both, spec((seqs, 8, part), lambda j, _: (0, 0, j)), whole(1, CH)],
        (shaped(x.shape, f32), shaped((TAIL // 2, CH), f32)),
        [both, whole(TAIL // 2, CH)],
        0,
        deps=deps,
    )


SMALL = 16


def small_table_body(info, query, pair, up, out, last, table):
    table[...] = jnp.zeros(table.shape, f32)
    table[0:1, :] = query[...]
    table[1:2, :] = pair[0]
    table[2:3, :] = pair[1]
    for n in range(4):
        table[3 + n : 4 + n, :] = up[:, CH * n : CH * (n + 1)]
    table[7:8, :] = out[...]
    table[8:10, :] = last[0:2, :]


def small_table(info, arrays):
    return call(
        small_table_body,
        "small_table",
        1,
        info,
        arrays,
        [whole(*a.shape) for a in arrays],
        shaped((SMALL, CH), f32),
        whole(SMALL, CH),
        0,
    )


def ring(array, step):
    return lax.ppermute(array, "tp", [(i, (i + step) % N_TP) for i in range(N_TP)])


class Gather:
    def __init__(self, own):
        self.own = own

    def forth(self, clock):
        self.own = clock.go(self.own)
        self.behind = ring(self.own, 1)

    def back(self):
        self.ahead = ring(self.own, -1)

    def sides(self, clock):
        self.forth(clock)
        self.ahead = ring(self.own, -1)

    def onward(self, clock):
        self.behind = clock.go(self.behind)
        self.far = ring(self.behind, 1)
        self.parts = (self.own, self.behind, self.ahead, self.far)


class Scatter:
    def __init__(self, chunks):
        self.own, self.share, self.first, self.given = chunks

    def forward(self, clock):
        self.far = ring(clock.go(self.first), 1)

    def backward(self, clock):
        self.back = ring(clock.go(self.given), -1)

    def both(self):
        return [self.share, self.far]

    def onward(self, both):
        self.near = ring(both, 1)

    def shares(self):
        return self.own, self.back, self.near


class Reduction:
    def __init__(self, kept, given, clock, two):
        self.kept, self.two = kept, two
        self.got = swap(clock.go(given), "dp", 1, N_DP)
        self.moved, self.here, self.there = {}, {}, {}

    def across(self, n):
        row = (self.kept.shape[1] + 2 * n) * CH
        return [(self.kept, row), (self.got, row)]

    def here_sum(self, n):
        row = 2 * n * CH
        return [(self.kept, row), (self.got, row), (self.moved[n], 0)]

    def over_x(self, n, across):
        self.moved[n] = swap(across, "dp", 2, N_DP)

    def over_y(self, n, here):
        self.here[n] = here
        self.there[n] = swap(here, "ctx", 1, 2) if self.two else lax.psum(here, "ctx")

    def sums(self, n):
        if self.two:
            return self.here[n], self.there[n]
        return self.there[n], jnp.zeros_like(self.there[n])


def body(
    block_in,
    doc_starts,
    query_weight,
    key_weight,
    value_weight,
    output_weight,
    up_weight,
    down_weight,
    query_bias,
    key_bias,
    value_bias,
    up_bias,
    output_bias,
    norm_gain,
    norm_shift,
    cotangent,
):
    seqs, rows, _ = block_in.shape
    d, c, t = lax.axis_index("dp"), lax.axis_index("ctx"), lax.axis_index("tp")
    n_ctx = lax.axis_size("ctx")
    two = n_ctx == 2
    info = jnp.stack([t, c, d]).astype(jnp.int32)

    clock = Clock()

    x = Gather(block_in)
    x.forth(clock)
    small = jnp.concatenate(
        [query_bias, key_bias, value_bias, up_bias, output_bias, norm_gain, norm_shift]
    )
    size = small.size
    near = swap(small, "dp", 1, N_DP)
    flip = (d & 1) == 1
    pair = jnp.concatenate([jnp.where(flip, near, small), jnp.where(flip, small, near)])
    across = swap(pair, "dp", 2, N_DP)
    flip = (d & 2) == 2
    small_here = jnp.concatenate([jnp.where(flip, across, pair), jnp.where(flip, pair, across)])
    small_here = small_here.reshape(N_DP, size)

    def small_of(first, length):
        return small_here[:, first : first + length].reshape(1, -1)

    share = query_bias.size
    share_units = up_bias.size
    qkv_bias = jnp.concatenate([small_of(n * share, share) for n in range(3)], axis=1)
    up_shift = small_of(3 * share, share_units)
    output_shift = small_of(3 * share + share_units, share)
    gain_here = small_of(4 * share + share_units, share)
    shift_here = small_of(5 * share + share_units, share)
    both = jnp.concatenate([gain_here, shift_here], axis=0)
    others = [ring(both, -r) for r in range(1, N_TP)]
    wq_shard = jnp.concatenate([query_weight, key_weight, value_weight], axis=1)
    shards_q = Shards(tie(wq_shard, across), 0, d, c, two)
    shards_q.over_x(clock)
    shards_u = Shards(up_weight, 0, d, c, two, made=False)
    wo_shard = jnp.concatenate([output_weight, down_weight], axis=0)
    shards_o = Shards(wo_shard, 1, d, c, two)
    clock.sync(x.behind, shards_q.first, *others, shards_u.part)

    x.back()
    shards_q.over_y(clock)
    shards_u.over_x(clock)
    shards_q.near_core(clock)
    circle = jnp.concatenate([both, *others] * 2, axis=1)
    gain_shift = lax.dynamic_slice_in_dim(circle, (N_TP - t) % N_TP * CH, D, 1)
    gain, shift = gain_shift[0:1], gain_shift[1:2]

    here = c * rows + jnp.arange(rows, dtype=jnp.int32)
    tables, opening = rotary_tables(doc_starts, here)
    blocks = 1 if two else n_ctx
    before, _ = rotary_tables(doc_starts, jnp.arange(blocks * rows, dtype=jnp.int32))
    before = [a.reshape(seqs, blocks, rows, 128) for a in before]

    clock.sync(shards_q.second, shards_u.first, x.ahead, shards_q.near, shards_o.part)
    shards_u.near_core(clock)

    x.onward(clock)
    shards_u.over_y(clock)
    shards_o.over_x(clock)
    shards_q.far_core(clock)
    clock.sync(
        x.far,
        *shards_q.far_near,
        shards_u.second,
        shards_o.first,
        *before,
    )

    def send_keys(s):
        kv[s] = clock.go(kv[s])
        if two:
            kvp[s] = lax.ppermute(kv[s], "ctx", [(0, 1)])[None]
        else:
            kvp[s] = lax.all_gather(kv[s], "ctx", axis=0, tiled=False)

    def attention_step(s):
        return attention(
            info,
            s,
            opening[:, None],
            q,
            kv[s],
            kvp[s],
            datt,
            tables,
            before,
            deps=clock.marks,
        )

    def returned(sent):
        if two:
            return lax.ppermute(clock.go(sent[0]), "ctx", [(1, 0)])
        return lax.psum_scatter(clock.go(sent), "ctx", scatter_dimension=0, tiled=False)

    def back_in_step(s):
        return back_in(
            layout,
            info,
            s,
            x.parts,
            dq[s],
            dkv[s],
            sent[s],
            dup,
            shards_q.pieces,
            shards_u.pieces,
            gain,
            stats,
            deps=clock.marks,
        )

    layout = layout_of(two)
    kvp, att, dq, dkv, sent = ([None] * seqs for _ in range(5))

    shards_o.over_y(clock)
    shards_u.far_core(clock)
    ct = Gather(cotangent)
    ct.behind, ct.ahead = ring(ct.own, 1), ring(ct.own, -1)
    normed, stats, q, *kv = norm_qkv(
        layout, info, x.parts, gain, shift, shards_q.pieces, qkv_bias, tables, deps=clock.marks
    )
    clock.sync(normed, *shards_u.far_near, shards_u.near, ct.behind, shards_o.second)

    shards_o.near_core(clock)
    shards_o.far_core(clock)
    ct.onward(clock)
    hidden, slope = mlp_up(layout, info, normed, shards_u.pieces, up_shift, deps=clock.marks)
    clock.sync(hidden, shards_o.near, *shards_o.far_near)

    send_keys(0)
    send_keys(1)
    out_parts = out_hidden(layout, info, hidden, shards_o.pieces, deps=clock.marks)
    clock.sync(out_parts, ct.ahead, ct.far)

    cf, out_bias_sum, datt, dup = back_out(
        layout, info, ct.parts, shards_o.pieces, slope, deps=clock.marks
    )
    clock.sync(datt, kvp[0])

    def added(big, small=()):
        return combine(info, big, list(small), deps=clock.marks)

    up_kept, up_given, up_sum = grad_up(info, normed, dup, deps=clock.marks)
    clock.sync(up_kept, kvp[1])
    up = Reduction(up_kept, up_given, clock, two)
    att[0], dq[0], dkv[0], sent[0] = attention_step(0)
    clock.sync(att[0], up.got)

    sent[0] = returned(sent[0])
    across, across_1 = added([up.across(0), up.across(1)])
    up.over_x(0, across)
    clock.sync(across)
    down_kept, down_given = grad_down(info, hidden, cf, deps=clock.marks)
    clock.sync(down_kept, *clock.marks)
    att[1], dq[1], dkv[1], sent[1] = attention_step(1)
    clock.sync(att[1], sent[0], up.moved[0])

    sent[1] = returned(sent[1])
    up.over_x(1, clock.go(across_1))
    down = Reduction(down_kept, down_given, clock, two)
    out = Scatter(out_heads(layout, info, att, out_parts, shards_o.pieces, deps=clock.marks))
    clock.sync(out.own, *clock.marks)
    head_kept, head_given, query_sum = grad_out_query(
        info, normed, cf, att, dq, deps=clock.marks
    )
    clock.sync(head_kept, down.got)
    across, across_1, here = added([down.across(0), down.across(1), up.here_sum(0)])
    clock.sync(across, sent[1])

    up.over_y(0, clock.go(here))
    out.forward(clock)
    clock.sync(up.moved[1])
    down.over_x(0, clock.go(across))
    head = Reduction(head_kept, head_given, clock, two)
    (here,) = added([up.here_sum(1)])
    clock.sync(here)
    back_0 = Scatter(back_in_step(0))
    clock.sync(back_0.own)
    clock.sync(up.there[0])

    up.over_y(1, clock.go(here))
    clock.sync(out.far)
    back_0.forward(clock)
    back_0.backward(clock)
    clock.sync(down.moved[0], head.got)
    down.over_x(1, clock.go(across_1))
    here, across, out_both = added([down.here_sum(0), head.across(0)], [out.both()])
    clock.sync(here)
    pair_kept, pair_given, pair_sum = grad_key_value(info, normed, dkv, sent, deps=clock.marks)
    clock.sync(pair_kept)
    clock.sync(up.there[1])

    down.over_y(0, clock.go(here))
    clock.sync(back_0.far, back_0.back)
    out.backward(clock)
    clock.sync(down.moved[1])
    head.over_x(0, clock.go(across))
    pair = Reduction(pair_kept, pair_given, clock, two)
    here, both_0 = added([down.here_sum(1)], [back_0.both()])
    clock.sync(here)
    back_1 = Scatter(back_in_step(1))
    clock.sync(back_1.own)
    clock.sync(down.there[0])

    down.over_y(1, clock.go(here))
    clock.sync(out.back)
    back_1.forward(clock)
    back_1.backward(clock)
    clock.sync(head.moved[0], pair.got)
    (across,) = added([pair.across(0)])
    pair.over_x(0, across)
    clock.sync(across)
    (here,) = added([head.here_sum(0)])
    clock.sync(here)
    up_wg = finish_blocks(info, [up.sums(0), up.sums(1)], 1, deps=clock.marks)
    clock.sync(up_wg)
    clock.sync(down.there[1])

    head.over_y(0, clock.go(here))
    back_0.onward(clock.go(both_0))
    clock.sync(back_1.far, back_1.back)
    (both_1,) = added([], [back_1.both()])
    back_1.onward(both_1)
    clock.sync(pair.moved[0])
    (here,) = added([pair.here_sum(0)])
    clock.sync(here)
    down_wg = finish_blocks(info, [down.sums(0), down.sums(1)], 0, deps=clock.marks)
    clock.sync(down_wg)
    clock.sync(head.there[0])

    pair.over_y(0, clock.go(here))
    clock.sync(back_0.near, back_1.near)
    out.onward(clock.go(out_both))
    in_grad, last = finish_in(
        info,
        (*back_0.shares(), *back_1.shares()),
        block_in,
        cotangent,
        stats,
        gain_here,
        deps=clock.marks,
    )
    clock.sync(in_grad)
    table = small_table(info, (query_sum, pair_sum, up_sum, out_bias_sum, last))
    output_wg, query_wg = finish_pair(info, *head.sums(0), deps=clock.marks)
    table = table + swap(table, "dp", 1, N_DP)
    table = table + swap(table, "dp", 2, N_DP)
    table = table + swap(table, "ctx", 1, 2) if two else lax.psum(table, "ctx")
    block_out, key_wg, value_wg = finish_last(
        info, out.shares(), block_in, output_shift, *pair.sums(0)
    )

    share = CH // N_DP
    mine = lax.dynamic_slice_in_dim(table, d * share, share, 1)
    query_bg, key_bg, value_bg = mine[0], mine[1], mine[2]
    output_bg, gain_g, shift_g = mine[7], mine[8], mine[9]
    up_bg = lax.dynamic_slice_in_dim(table, 3 + d, 1, 0).reshape(-1)
    return (
        block_out,
        in_grad,
        query_wg,
        key_wg,
        value_wg,
        output_wg,
        up_wg,
        down_wg,
        query_bg,
        key_bg,
        value_bg,
        up_bg,
        output_bg,
        gain_g,
        shift_g,
    )


def solution(mesh):
    return jax.shard_map(
        body,
        mesh=mesh,
        in_specs=(
            P("dp", "ctx", "tp"),
            P("dp", None),
            P("dp", "tp"),
            P("dp", "tp"),
            P("dp", "tp"),
            P("tp", "dp"),
            P("dp", "tp"),
            P("tp", "dp"),
        )
        + (P(("tp", "dp")),) * 7
        + (P("dp", "ctx", "tp"),),
        out_specs=(
            P("dp", "ctx", "tp"),
            P("dp", "ctx", "tp"),
            P("dp", "tp"),
            P("dp", "tp"),
            P("dp", "tp"),
            P("tp", "dp"),
            P("dp", "tp"),
            P("tp", "dp"),
        )
        + (P(("tp", "dp")),) * 7,
        check_vma=False,
    )
```

```python
import functools
import math

import jax
import jax.numpy as jnp
from jax import lax
from jax.experimental import pallas as pl
from jax.experimental.pallas import tpu as pltpu
from jax.sharding import PartitionSpec as P

HEAD_DIM = 64
ROT = 32
D = 2048
N_DP = 4
N_TP = 4
CH = D // N_TP
EPS = 1e-05
NEG = -1e30
VMEM = 127 * 2**19
COST = 0.02

bf16 = jnp.bfloat16
f32 = jnp.float32


def dot_nn(a, b):
    return lax.dot_general(a, b, (((1,), (0,)), ((), ())), preferred_element_type=f32)


def dot_nt(a, b):
    return lax.dot_general(a, b, (((1,), (1,)), ((), ())), preferred_element_type=f32)


def dot_tn(a, b):
    return lax.dot_general(a, b, (((0,), (0,)), ((), ())), preferred_element_type=f32)


def spec(block, index):
    return pl.BlockSpec(block, index)


def whole(*block):
    zeros = (0,) * len(block)
    return pl.BlockSpec(block, lambda g, *_: zeros)


def once(*block):
    zeros = (0,) * len(block)
    return pl.BlockSpec(block, lambda g, *_: zeros, pipeline_mode=pl.Buffered(1))


def one_of(s, *block):
    zeros = (0,) * len(block)
    return pl.BlockSpec((None, *block), lambda g, *_: (s, *zeros))


def shaped(shape, dtype=bf16):
    return jax.ShapeDtypeStruct(tuple(shape), dtype)


ANYWHERE = pl.BlockSpec(memory_space=pl.ANY)


def call(
    body, name, grid, info, ins, in_specs, outs, out_specs, flops, scratch=(), deps=(), aliases=()
):
    moved = sum(math.prod(a.shape) * a.dtype.itemsize for a in (*ins, *jax.tree.leaves(outs)))
    first, last = 1 + len(ins), 1 + len(ins) + len(deps)

    def without_deps(*refs):
        body(*refs[:first], *refs[last:])

    return pl.pallas_call(
        without_deps,
        grid_spec=pltpu.PrefetchScalarGridSpec(
            num_scalar_prefetch=1,
            grid=(grid,),
            in_specs=[*in_specs, *[ANYWHERE] * len(deps)],
            out_specs=out_specs,
            scratch_shapes=list(scratch),
        ),
        out_shape=outs,
        input_output_aliases={1 + n: m for n, m in aliases},
        compiler_params=pltpu.CompilerParams(vmem_limit_bytes=VMEM),
        cost_estimate=pl.CostEstimate(
            flops=int(flops * COST), bytes_accessed=int(moved * COST), transcendentals=0
        ),
        name=name,
    )(info, *ins, *deps)


def tie(value, *deps):
    def nothing(*refs):
        del refs

    return pl.pallas_call(
        nothing,
        in_specs=[ANYWHERE] * (1 + len(deps)),
        out_specs=ANYWHERE,
        out_shape=shaped(value.shape, value.dtype),
        input_output_aliases={0: 0},
        compiler_params=pltpu.CompilerParams(vmem_limit_bytes=VMEM),
        cost_estimate=pl.CostEstimate(flops=0, bytes_accessed=0, transcendentals=0),
        name="tie",
    )(value, *deps)


def columns(index, width=CH):
    return pl.ds(pl.multiple_of(index * width, width), width)


def layout_of(two):
    if two:
        halves = [("c", CH // 2), ("other", CH // 2)]
    else:
        halves = [("", CH)]
    return [(0, "", CH), (1, "", CH)] + [(r, *half) for r in (2, 3) for half in halves]


def piece_offset(info, half):
    return {"": 0, "c": info[1], "other": 1 - info[1]}[half] * (CH // 2)


def piece_window(info, piece):
    r, half, size = piece
    start = (info[2] ^ r) * CH + piece_offset(info, half)
    return pl.ds(pl.multiple_of(start, size), size)


class Clock:
    def __init__(self):
        self.marks = ()

    def go(self, value):
        return tie(value, *self.marks) if self.marks else value

    def sync(self, *arrays):
        def nothing(*refs):
            del refs

        self.marks = (
            pl.pallas_call(
                nothing,
                in_specs=[ANYWHERE] * (len(arrays) + len(self.marks)),
                out_specs=ANYWHERE,
                out_shape=shaped((8, 128), f32),
                compiler_params=pltpu.CompilerParams(vmem_limit_bytes=VMEM),
                cost_estimate=pl.CostEstimate(flops=0, bytes_accessed=0, transcendentals=0),
                name="sync",
            )(*arrays, *self.marks),
        )


def swap(array, axis, bit, size):
    return lax.ppermute(array, axis, [(i, i ^ bit) for i in range(size)])


class Shards:
    def __init__(self, own, axis, d, c, two, made=True):
        self.own, self.two, self.made = own, two, made
        size = own.shape[axis] // 2
        self.part = lax.dynamic_slice_in_dim(own, c * size, size, axis) if two else own

    def near_core(self, clock):
        self.own = clock.go(self.own) if self.made else self.own
        self.near = swap(self.own, "dp", 1, N_DP)

    def over_x(self, clock):
        self.first = swap(clock.go(self.part), "dp", 2, N_DP)

    def over_y(self, clock):
        self.first = clock.go(self.first)
        self.second = swap(self.first, "ctx", 1, 2) if self.two else self.first

    def far_core(self, clock):
        self.first = clock.go(self.first)
        far = [self.first]
        if self.two:
            self.second = clock.go(self.second)
            far.append(self.second)
        self.far_near = [swap(a, "dp", 1, N_DP) for a in far]
        self.pieces = [self.own, self.near, *far, *self.far_near]


def rotary_tables(starts, positions):
    before = starts[:, None, :] <= positions[None, :, None]
    opening = jnp.max(jnp.where(before, starts[:, None, :], 0), axis=2)
    relative = (positions[None, :] - opening).astype(f32)
    half = ROT // 2
    lane = jnp.arange(128, dtype=jnp.int32) % HEAD_DIM
    frequency = jnp.exp((lane % half).astype(f32) * (-math.log(10000.0) / half))
    angles = relative[:, :, None] * jnp.where(lane < ROT, frequency, 0.0)
    sine = jnp.sin(angles)
    return (
        jnp.cos(angles),
        jnp.where(lane < half, -sine, 0.0),
        jnp.where(lane >= half, sine, 0.0),
    ), opening


def add_rounded(a, b):
    return (a.astype(f32) + b.astype(f32)).astype(bf16)


def turn(x, own, up, down):
    return x * own + pltpu.roll(x, 112, 1) * up + pltpu.roll(x, 16, 1) * down


def turn_back(x, own, up, down):
    return x * own - pltpu.roll(x, 112, 1) * up - pltpu.roll(x, 16, 1) * down


def stream_pieces(layout, info, sources, held, sems, axis, blocks):
    j = pl.program_id(0)

    def copies(block):
        cut = pl.ds(pl.multiple_of(block * CH, CH), CH)
        for n, (piece, source) in enumerate(zip(layout, sources)):
            window = piece_window(info, piece)
            if axis == 0:
                pair = source.at[:, cut], held.at[window, cut]
            else:
                pair = source.at[cut, :], held.at[cut, window]
            yield pltpu.make_async_copy(*pair, sems.at[block, n])

    @pl.when(j == 0)
    def _():
        for block in range(blocks):
            for copy in copies(block):
                copy.start()

    for copy in copies(j):
        copy.wait()


def norm_qkv_body(layout, info, x0, xa, xc, xb, gain, shift, bias, own, up, down, *refs):
    *w, normed, stats, q, kv0, kv1, columns_held, held, sems = refs
    j = pl.program_id(0)
    t = info[0]
    seqs, rows, _ = x0.shape
    stream_pieces(layout, info, w, held, sems, 0, 3)

    @pl.when(j == 0)
    def _():
        parts = [(x0, t), (xa, (t + 3) % N_TP), (xc, (t + 1) % N_TP), (xb, (t + 2) % N_TP)]
        tile = 128

        def rows_of(i, carry):
            s = i // (rows // tile)
            window = pl.ds(pl.multiple_of((i % (rows // tile)) * tile, tile), tile)
            x = [part[s, window, :].astype(f32) for part, _ in parts]
            average = sum(jnp.sum(a, axis=1, keepdims=True) for a in x) * (1.0 / D)
            x = [a - average for a in x]
            variance = sum(jnp.sum(a * a, axis=1, keepdims=True) for a in x) * (1.0 / D)
            root = lax.rsqrt(variance + EPS)
            columns_held[s, window, 0:1] = average
            columns_held[s, window, 1:2] = root
            for a, (_, index) in zip(x, parts):
                at = columns(index)
                y = a * root * gain[:, at].astype(f32) + shift[:, at].astype(f32)
                normed[s, window, at] = y.astype(bf16)
            return carry

        columns_held[...] = jnp.zeros(columns_held.shape, f32)
        lax.fori_loop(0, seqs * rows // tile, rows_of, 0)
        for s in range(seqs):
            stats[s] = columns_held[s].T[: stats.shape[1]]

    for s, kv in ((0, kv0), (1, kv1)):
        y = dot_nn(normed[s], held[:, columns(j)]) + bias[...].astype(f32)

        def rotated(s=s, y=y):
            parts = [
                turn(y[:, 128 * n : 128 * n + 128], own[s], up[s], down[s])
                for n in range(CH // 128)
            ]
            return jnp.concatenate(parts, axis=1).astype(bf16)

        @pl.when(j == 0)
        def _(s=s, rotated=rotated):
            q[s] = rotated()

        @pl.when(j == 1)
        def _(kv=kv, rotated=rotated):
            kv[0] = rotated()

        @pl.when(j == 2)
        def _(kv=kv, y=y):
            kv[0] = y.astype(bf16)


def norm_qkv(layout, info, parts, gain, shift, w, bias, tables, deps=()):
    seqs, rows, _ = parts[0].shape
    outs = (
        shaped((seqs, rows, D)),
        shaped((seqs, 8, rows), f32),
        shaped((seqs, rows, CH)),
        shaped((2, rows, CH)),
        shaped((2, rows, CH)),
    )
    pair = spec((1, rows, CH), lambda j, *_: (jnp.maximum(j - 1, 0), 0, 0))
    return call(
        functools.partial(norm_qkv_body, layout),
        "norm_qkv",
        3,
        info,
        (*parts, gain, shift, bias, *tables, *w),
        [whole(seqs, rows, CH)] * 4
        + [whole(1, D)] * 2
        + [spec((1, CH), lambda j, *_: (0, j))]
        + [whole(seqs, rows, 128)] * 3
        + [ANYWHERE] * len(w),
        outs,
        [
            whole(seqs, rows, D),
            whole(seqs, 8, rows),
            whole(seqs, rows, CH),
            pair,
            pair,
        ],
        2 * seqs * rows * D * 3 * CH,
        [
            pltpu.VMEM((seqs, rows, 128), f32),
            pltpu.VMEM((D, 3 * CH), bf16),
            pltpu.SemaphoreType.DMA((3, len(w))),
        ],
        deps=deps,
    )


def mlp_up_body(layout, info, normed, bias, *refs):
    *w, hidden, grad, held, sems = refs
    j = pl.program_id(0)
    stream_pieces(layout, info, w, held, sems, 0, held.shape[1] // CH)
    root = math.sqrt(2.0 / math.pi)
    for s in range(normed.shape[0]):
        u = dot_nn(normed[s], held[:, columns(j)]) + bias[...].astype(f32)
        square = u * u
        t = jnp.tanh(u * (root + (root * 0.044715) * square))
        half = 0.5 + 0.5 * t
        hidden[s] = (u * half).astype(bf16)
        slope = root + (3 * 0.044715 * root) * square
        grad[s] = (half + (0.5 * u) * (1.0 - t * t) * slope).astype(bf16)


def mlp_up(layout, info, normed, w, bias, deps=()):
    seqs, rows, _ = normed.shape
    units = w[0].shape[1]
    block = spec((seqs, rows, CH), lambda j, *_: (0, 0, j))
    return call(
        functools.partial(mlp_up_body, layout),
        "mlp_up",
        units // CH,
        info,
        (normed, bias, *w),
        [whole(seqs, rows, D), spec((1, CH), lambda j, *_: (0, j))] + [ANYWHERE] * len(w),
        (shaped((seqs, rows, units)),) * 2,
        [block] * 2,
        2 * seqs * rows * D * units,
        [pltpu.VMEM((D, units), bf16), pltpu.SemaphoreType.DMA((units // CH, len(w)))],
        deps=deps,
    )


def back_out_body(layout, info, c0, ca, cc, cb, slope, *refs):
    *w, cf, bias_grad, datt, dup, held, sems, cf_sems = refs
    j = pl.program_id(0)
    t = info[0]
    seqs = c0.shape[0]
    parts = [(c0, t), (ca, (t + 3) % N_TP), (cc, (t + 1) % N_TP), (cb, (t + 2) % N_TP)]
    stream_pieces(layout, info, w, held, sems, 1, held.shape[0] // CH)
    copies = [
        pltpu.make_async_copy(part, cf.at[:, :, columns(index)], cf_sems.at[n])
        for n, (part, index) in enumerate(parts)
    ]

    @pl.when(j == 0)
    def _():
        for copy in copies:
            copy.start()
        bias_grad[...] = sum(
            jnp.sum(c0[s].astype(f32), axis=0, keepdims=True) for s in range(seqs)
        )

    for s in range(seqs):
        y = sum(dot_nt(part[s], held[columns(j), columns(index)]) for part, index in parts)

        @pl.when(j == 0)
        def _(s=s, y=y):
            datt[s] = y.astype(bf16)

        @pl.when(j > 0)
        def _(s=s, y=y):
            dup[s] = (y * slope[s].astype(f32)).astype(bf16)

    @pl.when(j == pl.num_programs(0) - 1)
    def _():
        for copy in copies:
            copy.wait()


def back_out(layout, info, parts, w, slope, deps=()):
    seqs, rows, units = slope.shape
    later = spec((seqs, rows, CH), lambda j, *_: (0, 0, jnp.maximum(j - 1, 0)))
    return call(
        functools.partial(back_out_body, layout),
        "back_out",
        1 + units // CH,
        info,
        (*parts, slope, *w),
        [once(seqs, rows, CH)] * 4 + [later] + [ANYWHERE] * len(w),
        (
            shaped((seqs, rows, D)),
            shaped((1, CH), f32),
            shaped((seqs, rows, CH)),
            shaped((seqs, rows, units)),
        ),
        [ANYWHERE, whole(1, CH), whole(seqs, rows, CH), later],
        2 * seqs * rows * D * (CH + units),
        [
            pltpu.VMEM((CH + units, D), bf16),
            pltpu.SemaphoreType.DMA((1 + units // CH, len(w))),
            pltpu.SemaphoreType.DMA((len(parts),)),
        ],
        deps=deps,
    )


def attention_body(
    blocks, info, low, q, kv, kvp, do, own, up, down, ownp, upp, downp,
    att, dq, dkv, dkvp, scores, probs,
):
    rows = q.shape[0]
    before, start = info[1], info[1] * rows
    lane = lax.broadcasted_iota(jnp.int32, (rows, 128), 1)
    key_row = lax.broadcasted_iota(jnp.int32, (rows, 1), 0)
    query_at = start + lax.broadcasted_iota(jnp.int32, (1, rows), 1)
    first = low[0]
    do_t = do[...].astype(f32).T
    nothing = jnp.zeros((), bf16)
    outputs = []
    for head in range(2):
        mine = (lane < HEAD_DIM) if head == 0 else (lane >= HEAD_DIM)
        half = slice(HEAD_DIM * head, HEAD_DIM * (head + 1))
        qh = jnp.where(mine, q[...] * jnp.asarray(HEAD_DIM**-0.5, bf16), nothing)
        dh = jnp.where(mine, do[...], nothing)

        key_at = start + key_row
        s = dot_nt(kv[0], qh)
        s = jnp.where((key_at >= first) & (key_at <= query_at), s, NEG)
        scores[blocks] = s
        peak = jnp.max(s, axis=0, keepdims=True)

        def score(n, peak):
            s = dot_nt(kvp[n, 0], qh)
            s = jnp.where(n * rows + key_row >= first, s, NEG)
            scores[n] = s
            return jnp.maximum(peak, jnp.max(s, axis=0, keepdims=True))

        peak = lax.fori_loop(0, before, score, peak)

        def expo(n, total):
            e = jnp.exp(scores[n] - peak)
            scores[n] = e
            return total + jnp.sum(e, axis=0, keepdims=True)

        total = expo(blocks, jnp.zeros((1, rows), f32))
        total = lax.fori_loop(0, before, expo, total)
        scale = 1.0 / total

        def weigh(n, values):
            p = (scores[n] * scale).astype(bf16)
            probs[n] = p
            return dot_tn(values, p)

        out_t = weigh(blocks, kv[1])
        out_t = lax.fori_loop(0, before, lambda n, acc: acc + weigh(n, kvp[n, 1]), out_t)
        delta = jnp.sum(out_t[half] * do_t[half], axis=0, keepdims=True)

        def back(n, keys, values):
            dp = dot_nt(values, dh)
            ds = ((scores[n] * scale) * (dp - delta)).astype(bf16)
            return dot_nn(ds, qh), dot_nn(probs[n], dh), dot_tn(keys, ds)

        dk, dv, dq_t = back(blocks, kv[0], kv[1])
        if head == 0:
            dk_sum, dv_sum = dk, dv
        else:
            dk_sum, dv_sum = dk_sum + dk, dv_sum + dv

        def back_before(n, acc):
            dk, dv, more = back(n, kvp[n, 0], kvp[n, 1])
            dk = turn_back(dk, ownp[n], upp[n], downp[n])
            if head == 0:
                dkvp[n, 0] = dk.astype(bf16)
                dkvp[n, 1] = dv.astype(bf16)
            else:
                dkvp[n, 0] = (dkvp[n, 0].astype(f32) + dk).astype(bf16)
                dkvp[n, 1] = (dkvp[n, 1].astype(f32) + dv).astype(bf16)
            return acc + more

        dq_t = lax.fori_loop(0, before, back_before, dq_t)
        outputs.append((out_t[half], dq_t[half]))

    def clear(n, carry):
        dkvp[n] = jnp.zeros(dkvp.shape[1:], bf16)
        return carry

    lax.fori_loop(before, blocks, clear, 0)
    att[...] = jnp.concatenate([outputs[0][0], outputs[1][0]], axis=0).T.astype(bf16)
    grad = jnp.concatenate([outputs[0][1], outputs[1][1]], axis=0).T * HEAD_DIM**-0.5
    dq[...] = turn_back(grad, own[...], up[...], down[...]).astype(bf16)
    dkv[0] = turn_back(dk_sum, own[...], up[...], down[...]).astype(bf16)
    dkv[1] = dv_sum.astype(bf16)


def attention_two_body(
    info, low, q, kv, kvp, do, own, up, down, ownp, upp, downp, att, dq, dkv, dkvp
):
    rows = q.shape[0]
    part = rows // 2
    before, start = info[1], info[1] * rows

    def tail(x, skipped):
        return x[:, skipped:] if skipped else x

    def merge(acc, x, skipped, op):
        if acc is None:
            return x
        if not skipped:
            return op(acc, x)
        return jnp.concatenate([acc[:, :skipped], op(acc[:, skipped:], x)], axis=1)

    def run(with_before):
        lane = lax.broadcasted_iota(jnp.int32, (rows, 128), 1)
        key_row = lax.broadcasted_iota(jnp.int32, (part, 1), 0)
        query_at = start + lax.broadcasted_iota(jnp.int32, (1, rows), 1)
        first = low[...]
        do_t = do[...].astype(f32).T
        nothing = jnp.zeros((), bf16)
        blocks = []
        for n in range(2):
            if with_before:
                blocks.append((kvp.at[0], n * part, 0, False))
        for n in range(2):
            blocks.append((kv, n * part, n * part, True))
        dk_sum, dv_sum = [0.0] * len(blocks), [0.0] * len(blocks)
        heads = []
        for head in range(2):
            mine = (lane < HEAD_DIM) if head == 0 else (lane >= HEAD_DIM)
            qh = jnp.where(mine, q[...] * jnp.asarray(HEAD_DIM**-0.5, bf16), nothing)
            dh = jnp.where(mine, do[...], nothing)
            heads.append((qh, dh, slice(HEAD_DIM * head, HEAD_DIM * (head + 1))))

        def score(head):
            qh = heads[head][0]
            scores, peak = [], None
            for ref, row, skip, here in blocks:
                s = dot_nt(ref[0, row : row + part], qh[skip:])
                key_at = (start if here else start - rows) + row + key_row
                allowed = key_at >= tail(first, skip)
                if here:
                    allowed = allowed & (key_at <= tail(query_at, skip))
                s = jnp.where(allowed, s, NEG)
                scores.append(s)
                peak = merge(peak, jnp.max(s, axis=0, keepdims=True), skip, jnp.maximum)
            return scores, peak

        def grads(head):
            dh = heads[head][1]
            return [
                dot_nt(ref[1, row : row + part], dh[skip:]) for ref, row, skip, _ in blocks
            ]

        def soften(scores, peak):
            terms, total = [], None
            for s, (_, _, skip, _) in zip(scores, blocks):
                e = jnp.exp(s - tail(peak, skip))
                terms.append(e)
                total = merge(total, jnp.sum(e, axis=0, keepdims=True), skip, jnp.add)
            scale = 1.0 / total
            probs = [e * tail(scale, skip) for e, (_, _, skip, _) in zip(terms, blocks)]
            return probs, [p.astype(bf16) for p in probs]

        def weigh(head, rounded):
            out_t = None
            for n, (ref, row, skip, _) in enumerate(blocks):
                out_t = merge(
                    out_t, dot_tn(ref[1, row : row + part], rounded[n]), skip, jnp.add
                )
                dv_sum[n] = dv_sum[n] + dot_nn(rounded[n], heads[head][1][skip:])
            half = heads[head][2]
            return out_t[half], jnp.sum(out_t[half] * do_t[half], axis=0, keepdims=True)

        def differ(probs, dps, delta):
            return [
                (p * (dp - tail(delta, skip))).astype(bf16)
                for p, dp, (_, _, skip, _) in zip(probs, dps, blocks)
            ]

        def back(head, dss):
            dq_t = None
            for n, (ref, row, skip, _) in enumerate(blocks):
                dk_sum[n] = dk_sum[n] + dot_nn(dss[n], heads[head][0][skip:])
                dq_t = merge(dq_t, dot_tn(ref[0, row : row + part], dss[n]), skip, jnp.add)
            return dq_t[heads[head][2]]

        scores_0 = score(0)
        scores_1 = score(1)
        probs_0, rounded_0 = soften(*scores_0)
        out_0, delta_0 = weigh(0, rounded_0)
        dss_0 = differ(probs_0, grads(0), delta_0)
        probs_1, rounded_1 = soften(*scores_1)
        dq_0 = back(0, dss_0)
        out_1, delta_1 = weigh(1, rounded_1)
        dss_1 = differ(probs_1, grads(1), delta_1)
        dq_1 = back(1, dss_1)
        outputs = [(out_0, dq_0), (out_1, dq_1)]

        att[...] = jnp.concatenate([outputs[0][0], outputs[1][0]], axis=0).T.astype(bf16)
        grad = jnp.concatenate([outputs[0][1], outputs[1][1]], axis=0).T * HEAD_DIM**-0.5
        dq[...] = turn_back(grad, own[...], up[...], down[...]).astype(bf16)
        dk = jnp.concatenate(dk_sum[-2:], axis=0)
        dkv[0] = turn_back(dk, own[...], up[...], down[...]).astype(bf16)
        dkv[1] = jnp.concatenate(dv_sum[-2:], axis=0).astype(bf16)
        if with_before:
            dk = jnp.concatenate(dk_sum[:2], axis=0)
            dkvp[0, 0] = turn_back(dk, ownp[0], upp[0], downp[0]).astype(bf16)
            dkvp[0, 1] = jnp.concatenate(dv_sum[:2], axis=0).astype(bf16)
        else:
            dkvp[...] = jnp.zeros(dkvp.shape, bf16)

    @pl.when(before == 0)
    def _():
        run(False)

    @pl.when(before > 0)
    def _():
        run(True)


def attention(info, s, low, q, kv, kvp, do, tables, tables_before, deps=()):
    _, rows, width = q.shape
    blocks = kvp.shape[0]
    token = spec((rows, 128), lambda g, *_: (0, g))
    query = spec((None, rows, 128), lambda g, *_: (s, 0, g))
    pair = spec((2, rows, 128), lambda g, *_: (0, 0, g))
    pairs = spec((blocks, 2, rows, 128), lambda g, *_: (0, 0, 0, g))
    return call(
        attention_two_body if blocks == 1 else functools.partial(attention_body, blocks),
        "attention",
        width // 128,
        info,
        (low, q, kv, kvp, do, *tables, *tables_before),
        [one_of(s, 1, rows), query, pair, pairs, query]
        + [one_of(s, rows, 128)] * 3
        + [one_of(s, blocks, rows, 128)] * 3,
        (
            shaped((rows, width)),
            shaped((rows, width)),
            shaped((2, rows, width)),
            shaped((blocks, 2, rows, width)),
        ),
        [token, token, pair, pairs],
        48 * rows * rows * width,
        []
        if blocks == 1
        else [
            pltpu.VMEM((blocks + 1, rows, rows), f32),
            pltpu.VMEM((blocks + 1, rows, rows), bf16),
        ],
        deps=deps,
    )


TAIL = 16


def fetch_pieces(layout, sources, targets, sems, axis):
    copies = [[] for _ in range(N_DP)]
    at = [r * CH for r in range(N_DP)]
    n = 0
    for group, target in zip(sources, targets):
        at = [r * CH for r in range(N_DP)]
        for (r, _, size), source in zip(layout, group):
            window = pl.ds(at[r], size)
            place = target.at[window, :] if axis == 0 else target.at[:, window]
            copies[r].append(pltpu.make_async_copy(source, place, sems.at[n]))
            at[r] += size
            n += 1
    return copies


def with_chunk(layout, info, copies, work):
    j = pl.program_id(0)

    @pl.when(j == 0)
    def _():
        for group in copies:
            for copy in group:
                copy.start()

    for r in range(N_DP):

        @pl.when(j == r)
        def _(r=r):
            for copy in copies[r]:
                copy.wait()
            at = r * CH
            for s, half, size in layout:
                if s == r:
                    offset = pl.multiple_of(piece_offset(info, half), size)
                    work(pl.ds(at, size), pl.ds(offset, size))
                    at += size


def chunk_now(info):
    return ((info[2] ^ pl.program_id(0)) + N_TP - info[0]) % N_TP


def out_hidden_body(layout, info, hidden, *refs):
    *w, out, held, sems = refs

    def work(place, window):
        for s in range(hidden.shape[0]):
            out[0, s, :, window] = dot_nn(hidden[s], held[:, place]).astype(bf16)

    lower = [a.at[pl.ds(CH, held.shape[0]), :] for a in w]
    with_chunk(layout, info, fetch_pieces(layout, [lower], [held], sems, 1), work)


def out_hidden(layout, info, hidden, w, deps=()):
    seqs, rows, units = hidden.shape
    return call(
        functools.partial(out_hidden_body, layout),
        "out_hidden",
        N_DP,
        info,
        (hidden, *w),
        [once(seqs, rows, units)] + [ANYWHERE] * len(w),
        shaped((N_DP, seqs, rows, CH)),
        spec((1, seqs, rows, CH), lambda j, *_: (j, 0, 0, 0)),
        2 * seqs * rows * D * units,
        [pltpu.VMEM((units, D), bf16), pltpu.SemaphoreType.DMA((len(w),))],
        deps=deps,
    )


def out_heads_body(layout, info, a0, a1, part, *refs):
    count = len(layout)
    w, outs = refs[:count], refs[count : count + N_TP]
    held, y, sems, out_sems = refs[count + N_TP :]
    j = pl.program_id(0)

    def work(place, window):
        for s, att in ((0, a0), (1, a1)):
            total = dot_nn(att[...], held[:, place]) + part[0, s, :, window].astype(f32)
            y[j, s, :, window] = total.astype(bf16)

    upper = [a.at[pl.ds(0, CH), :] for a in w]
    with_chunk(layout, info, fetch_pieces(layout, [upper], [held], sems, 1), work)
    for r in range(N_TP):

        @pl.when(chunk_now(info) == r)
        def _(r=r):
            pltpu.make_async_copy(y.at[j], outs[r], out_sems.at[r]).start()

    @pl.when(j == N_TP - 1)
    def _():
        for r in range(N_TP):
            pltpu.make_async_copy(y.at[r], outs[r], out_sems.at[r]).wait()


def out_heads(layout, info, att, parts, w, deps=()):
    _, seqs, rows, _ = parts.shape
    return call(
        functools.partial(out_heads_body, layout),
        "out_heads",
        N_TP,
        info,
        (*att, parts, *w),
        [once(rows, CH)] * 2
        + [spec((1, seqs, rows, CH), lambda j, *_: (j, 0, 0, 0))]
        + [ANYWHERE] * len(w),
        (shaped((seqs, rows, CH)),) * N_TP,
        [ANYWHERE] * N_TP,
        2 * seqs * rows * D * CH,
        [
            pltpu.VMEM((CH, D), bf16),
            pltpu.VMEM((N_TP, seqs, rows, CH), bf16),
            pltpu.SemaphoreType.DMA((len(w),)),
            pltpu.SemaphoreType.DMA((N_TP,)),
        ],
        deps=deps,
    )


def back_in_body(layout, info, x0, xa, xc, xb, dq, dkv, back, dup, gain, stats, *refs):
    count = len(layout)
    wq, wu = refs[:count], refs[count : 2 * count]
    *chunks, held_q, held_u, y, xs, row_sums, column_sums, both, sems = refs[2 * count :]
    j = pl.program_id(0)
    rows = dq.shape[0]

    @pl.when(j == 0)
    def _():
        both[...] = add_rounded(dkv[...], back[...])


    def work(place, window):
        part = dot_nt(dup[...], held_u[place, :])
        part = part + dot_nt(dq[...], held_q[place, :CH])
        part = part + dot_nt(both[0], held_q[place, CH : 2 * CH])
        y[:, window] = part + dot_nt(both[1], held_q[place, 2 * CH :])

    copies = fetch_pieces(layout, [wq, wu], [held_q, held_u], sems, 0)
    with_chunk(layout, info, copies, work)
    for r, part in enumerate((x0, xc, xb, xa)):

        @pl.when(chunk_now(info) == r)
        def _(r=r, part=part):
            chunks[r][:rows, :] = y[...].astype(bf16)
            xs[...] = part[...]

    total = y[...]
    turned = stats[...].T
    standard = (xs[...].astype(f32) - turned[:, 0:1]) * turned[:, 1:2]
    cross = total * standard
    weight = gain[...].astype(f32)

    @pl.when(j == 0)
    def _():
        row_sums[...] = jnp.zeros(row_sums.shape, f32)
        column_sums[...] = jnp.zeros(column_sums.shape, f32)

    both = jnp.concatenate(
        [jnp.sum(cross, axis=0, keepdims=True), jnp.sum(total, axis=0, keepdims=True)], axis=0
    )
    column_sums[chunk_now(info), 0:2, :] = both
    row_sums[:, 0:1] += jnp.sum(total * weight, axis=1, keepdims=True)
    row_sums[:, 1:2] += jnp.sum(cross * weight, axis=1, keepdims=True)

    @pl.when(j == N_TP - 1)
    def _():
        turned = row_sums[...].T[: TAIL // 2]
        for r, chunk in enumerate(chunks):
            chunk[rows:, :] = jnp.concatenate([turned, column_sums[r]], axis=0).astype(bf16)


def back_in(layout, info, s, parts, dq, dkv, back, dup, wq, wu, gain, stats, deps=()):
    _, rows, units = dup.shape
    return call(
        functools.partial(back_in_body, layout),
        "back_in",
        N_TP,
        info,
        (*parts, dq, dkv, back, dup, gain, stats, *wq, *wu),
        [one_of(s, rows, CH)] * 4
        + [
            whole(rows, CH),
            whole(2, rows, CH),
            whole(2, rows, CH),
            one_of(s, rows, units),
            spec((1, CH), lambda j, info: (0, info[2] ^ j)),
            one_of(s, 8, rows),
        ]
        + [ANYWHERE] * (2 * len(wq)),
        (shaped((rows + TAIL, CH)),) * N_TP,
        [whole(rows + TAIL, CH)] * N_TP,
        2 * rows * D * (3 * CH + units),
        [
            pltpu.VMEM((D, 3 * CH), bf16),
            pltpu.VMEM((D, units), bf16),
            pltpu.VMEM((rows, CH), f32),
            pltpu.VMEM((rows, CH), bf16),
            pltpu.VMEM((rows, 128), f32),
            pltpu.VMEM((N_TP, TAIL // 2, CH), f32),
            pltpu.VMEM((2, rows, CH), bf16),
            pltpu.SemaphoreType.DMA((2 * len(wq),)),
        ],
        deps=deps,
    )


KEPT = ((0, 0), (2, 1))
GIVEN = ((1, 0), (3, 1))


def grad_up_body(info, normed, dup, kept, given, sums):
    d = info[2]
    rights = (dup[0], dup[1])
    store_by_rows(d, normed, rights, kept, given)
    sums[...] = sum(jnp.sum(b.astype(f32), axis=0, keepdims=True) for b in rights)


def grad_up(info, normed, dup, deps=()):
    _, rows, units = dup.shape
    count = units // CH
    message = spec((2, 1, CH, CH), lambda j, *_: (0, j, 0, 0))
    return call(
        grad_up_body,
        "grad_up",
        count,
        info,
        (normed, dup),
        [whole(2, rows, D), spec((2, rows, CH), lambda j, *_: (0, 0, j))],
        (shaped((2, count, CH, CH)),) * 2 + (shaped((1, units), f32),),
        [message, message, spec((1, CH), lambda j, *_: (0, j))],
        4 * rows * D * units,
        deps=deps,
    )


def grad_down_body(offsets, info, hidden, *refs):
    parts = refs[: len(offsets)]
    kept, given, tiles, sems = refs[-4:]
    n = pl.program_id(0)
    for i, (part, offset) in enumerate(zip(parts, offsets)):
        tiles[n, i] = (dot_tn(hidden[0], part[0]) + dot_tn(hidden[1], part[1])).astype(bf16)
        r = ((info[0] + offset) % N_TP) ^ info[2]
        for odd, target in ((0, kept), (1, given)):

            @pl.when(r % 2 == odd)
            def _(i=i, r=r, target=target):
                place = target.at[r // 2, n]
                pltpu.make_async_copy(tiles.at[n, i], place, sems.at[n, i]).start()

    @pl.when(n == tiles.shape[0] - 1)
    def _():
        for m in range(tiles.shape[0]):
            for i in range(len(offsets)):
                pltpu.make_async_copy(tiles.at[m, i], kept.at[0, 0], sems.at[m, i]).wait()


def grad_down(info, hidden, parts, offsets, begun=(), deps=()):
    _, rows, units = hidden.shape
    count = units // CH
    at = 1 + len(parts)
    return call(
        functools.partial(grad_down_body, offsets),
        "grad_down",
        count,
        info,
        (hidden, *parts, *begun),
        [spec((2, rows, CH), lambda j, *_: (0, 0, j))]
        + [once(2, rows, CH)] * len(parts)
        + [ANYWHERE] * len(begun),
        (shaped((2, count, CH, CH)),) * 2,
        [ANYWHERE] * 2,
        4 * rows * CH * units * len(parts),
        [
            pltpu.VMEM((count, len(parts), CH, CH), bf16),
            pltpu.SemaphoreType.DMA((count, len(parts))),
        ],
        deps=deps,
        aliases=[(at + n, n) for n in range(len(begun))],
    )


def store_by_rows(d, lefts, rights, kept, given):
    for target, which in ((given, GIVEN), (kept, KEPT)):
        for r, at in which:
            window = columns(d ^ r)
            y = sum(dot_tn(lefts[s, :, window], b) for s, b in enumerate(rights))
            target[at, 0] = y.astype(bf16)


def grad_out_query_body(info, normed, ct, a0, a1, q0, q1, kept, given, sums):
    j = pl.program_id(0)
    d = info[2]

    @pl.when(j == 0)
    def _():
        lefts = (a0[...], a1[...])
        for target, which in ((given, GIVEN), (kept, KEPT)):
            for r, at in which:
                window = columns(d ^ r)
                y = sum(dot_tn(a, ct[s, :, window]) for s, a in enumerate(lefts))
                target[at, 0] = y.astype(bf16)

    @pl.when(j == 1)
    def _():
        rights = (q0[...], q1[...])
        store_by_rows(d, normed, rights, kept, given)
        sums[...] = sum(jnp.sum(b.astype(f32), axis=0, keepdims=True) for b in rights)


def grad_out_query(info, normed, ct, att, dq, deps=()):
    rows = normed.shape[1]
    message = spec((2, 1, CH, CH), lambda j, *_: (0, j, 0, 0))
    return call(
        grad_out_query_body,
        "grad_out_query",
        2,
        info,
        (normed, ct, *att, *dq),
        [whole(2, rows, D)] * 2 + [whole(rows, CH)] * 4,
        (shaped((2, 2, CH, CH)),) * 2 + (shaped((1, CH), f32),),
        [message, message, whole(1, CH)],
        4 * rows * D * 2 * CH,
        deps=deps,
    )


def grad_key_value_body(info, normed, kv0, back0, kv1, back1, kept, given, sums):
    rights = (add_rounded(kv0[0], back0[0]), add_rounded(kv1[0], back1[0]))
    store_by_rows(info[2], normed, rights, kept, given)
    sums[0] = sum(jnp.sum(b.astype(f32), axis=0, keepdims=True) for b in rights)


def grad_key_value(info, normed, dkv, sent, deps=()):
    rows = normed.shape[1]
    message = spec((2, 1, CH, CH), lambda j, *_: (0, j, 0, 0))
    pair = spec((1, rows, CH), lambda j, *_: (j, 0, 0))
    return call(
        grad_key_value_body,
        "grad_key_value",
        2,
        info,
        (normed, dkv[0], sent[0], dkv[1], sent[1]),
        [whole(2, rows, D)] + [pair] * 4,
        (shaped((2, 2, CH, CH)),) * 2 + (shaped((2, 1, CH), f32),),
        [message, message, spec((1, 1, CH), lambda j, *_: (j, 0, 0))],
        4 * rows * D * 2 * CH,
        deps=deps,
    )


def combine_body(counts, info, *refs):
    ins, outs = refs[: sum(counts)], refs[sum(counts) :]
    at = 0
    for count, out in zip(counts, outs):
        terms = ins[at : at + count]
        at += count

        def add(terms=terms, out=out):
            out[...] = sum(a[...].astype(f32) for a in terms).astype(bf16)

        if len(out.shape) == 3:
            add()
        else:
            pl.when(pl.program_id(0) == 0)(add)


def combine(info, big, small, deps=()):
    steps = 2
    part = 2 * CH // steps
    ins, in_specs, outs, out_specs = [], [], [], []
    for job in big:
        for array, row in job:
            ins.append(array.reshape(-1, part, CH))
            in_specs.append(spec((1, part, CH), lambda j, _, at=row // part: (at + j, 0, 0)))
        outs.append(shaped((steps, part, CH)))
        out_specs.append(spec((1, part, CH), lambda j, _: (j, 0, 0)))
    for job in small:
        ins += job
        in_specs += [whole(*a.shape) for a in job]
        outs.append(shaped(job[0].shape))
        out_specs.append(whole(*job[0].shape))
    results = call(
        functools.partial(combine_body, [len(job) for job in (*big, *small)]),
        "combine",
        steps,
        info,
        ins,
        in_specs,
        outs,
        out_specs,
        0,
        deps=deps,
    )
    count = len(big)
    return [a.reshape(2, CH, CH) for a in results[:count]] + list(results[count:])


def finish_blocks_body(info, *refs):
    *sums, out = refs
    j = pl.program_id(0)
    for n in range(len(sums) // 2):
        here, there = sums[2 * n : 2 * n + 2]

        @pl.when((j >= 2 * n) & (j < 2 * n + 2))
        def _(here=here, there=there):
            out[...] = here[0].astype(f32) + there[0].astype(f32)


def finish_blocks(info, sums, axis, deps=()):
    count = len(sums)
    arrays = [a for pair in sums for a in pair]
    blocks = [
        spec((1, CH, CH), lambda j, _, n=n: (jnp.clip(j - 2 * n, 0, 1), 0, 0))
        for n in range(count)
        for _ in range(2)
    ]
    return call(
        finish_blocks_body,
        "finish_blocks",
        2 * count,
        info,
        arrays,
        blocks,
        shaped((2 * count * CH, CH) if axis == 0 else (CH, 2 * count * CH), f32),
        spec((CH, CH), lambda j, _: (j, 0) if axis == 0 else (0, j)),
        0,
        deps=deps,
    )


def finish_pair_body(info, here, there, *outs):
    for n, out in enumerate(outs):
        out[...] = here[n].astype(f32) + there[n].astype(f32)


def finish_pair(info, here, there, deps=()):
    part = CH // 2
    return call(
        finish_pair_body,
        "finish_pair",
        2,
        info,
        (here, there),
        [spec((2, part, CH), lambda j, _: (0, j, 0))] * 2,
        (shaped((CH, CH), f32),) * 2,
        [spec((part, CH), lambda j, _: (j, 0))] * 2,
        0,
        deps=deps,
    )


def finish_last_body(info, own, back, near, x, shift, here, there, out, first, second):
    total = own[...].astype(f32) + back[...].astype(f32) + near[...].astype(f32)
    out[...] = (x[...].astype(f32) + total + shift[...].astype(f32)).astype(bf16)
    finish_pair_body(info, here, there, first, second)


def finish_last(info, shares, x, shift, here, there, deps=()):
    seqs, rows, _ = x.shape
    both = spec((seqs, rows // 2, CH), lambda j, _: (0, j, 0))
    pair = spec((2, CH // 2, CH), lambda j, _: (0, j, 0))
    half = spec((CH // 2, CH), lambda j, _: (j, 0))
    return call(
        finish_last_body,
        "finish_last",
        2,
        info,
        (*shares, x, shift, here, there),
        [both] * 4 + [whole(1, CH), pair, pair],
        (shaped(x.shape), shaped((CH, CH), f32), shaped((CH, CH), f32)),
        [both, half, half],
        0,
        deps=deps,
    )


def finish_in_body(info, *refs):
    shares, tails, wide = refs[:6], refs[6:12], refs[12:18]
    x, ct, stats, gain, out, sums = refs[18:]
    weight = gain[...].astype(f32)
    for s in range(2):
        at = slice(3 * s, 3 * s + 3)
        total = sum(a[...].astype(f32) for a in shares[at])
        tail = sum(a[...].astype(f32) for a in tails[at])
        column = jnp.concatenate([tail[:8], stats[s]], axis=0).T
        plain, cross = column[:, 0:1], column[:, 1:2]
        average, root = column[:, 8:9], column[:, 9:10]
        standard = (x[s].astype(f32) - average) * root
        scaled = total * weight - plain * (1.0 / D) - standard * (cross * (1.0 / D))
        out[s] = ct[s].astype(f32) + root * scaled

    @pl.when(pl.program_id(0) == 0)
    def _():
        sums[...] = sum(a[...].astype(f32)[8:] for a in wide)


def finish_in(info, shares, x, ct, stats, gain, deps=()):
    seqs, rows, _ = x.shape
    part = rows // 2
    both = spec((seqs, part, CH), lambda j, _: (0, j, 0))
    last = rows // TAIL
    return call(
        finish_in_body,
        "finish_in",
        2,
        info,
        (*shares, *shares, *shares, x, ct, stats, gain),
        [spec((part, CH), lambda j, _: (j, 0))] * 6
        + [spec((TAIL, part), lambda j, _: (last, j))] * 6
        + [spec((TAIL, CH), lambda j, _: (last, 0))] * 6
        + [both, both, spec((seqs, 8, part), lambda j, _: (0, 0, j)), whole(1, CH)],
        (shaped(x.shape, f32), shaped((TAIL // 2, CH), f32)),
        [both, whole(TAIL // 2, CH)],
        0,
        deps=deps,
    )


SMALL = 16


def small_table_body(info, query, pair, up, out, last, table):
    table[...] = jnp.zeros(table.shape, f32)
    table[0:1, :] = query[...]
    table[1:2, :] = pair[0]
    table[2:3, :] = pair[1]
    for n in range(4):
        table[3 + n : 4 + n, :] = up[:, CH * n : CH * (n + 1)]
    table[7:8, :] = out[...]
    table[8:10, :] = last[0:2, :]


def small_table(info, arrays):
    return call(
        small_table_body,
        "small_table",
        1,
        info,
        arrays,
        [whole(*a.shape) for a in arrays],
        shaped((SMALL, CH), f32),
        whole(SMALL, CH),
        0,
    )


def ring(array, step):
    return lax.ppermute(array, "tp", [(i, (i + step) % N_TP) for i in range(N_TP)])


class Gather:
    def __init__(self, own):
        self.own = own

    def forth(self, clock):
        self.own = clock.go(self.own)
        self.behind = ring(self.own, 1)

    def back(self):
        self.ahead = ring(self.own, -1)

    def sides(self, clock):
        self.forth(clock)
        self.ahead = ring(self.own, -1)

    def onward(self, clock):
        self.behind = clock.go(self.behind)
        self.far = ring(self.behind, 1)
        self.parts = (self.own, self.behind, self.ahead, self.far)


class Scatter:
    def __init__(self, chunks):
        self.own, self.share, self.first, self.given = chunks

    def forward(self, clock):
        self.far = ring(clock.go(self.first), 1)

    def backward(self, clock):
        self.back = ring(clock.go(self.given), -1)

    def both(self):
        return [self.share, self.far]

    def onward(self, both):
        self.near = ring(both, 1)

    def shares(self):
        return self.own, self.back, self.near


class Reduction:
    def __init__(self, kept, given, clock, two):
        self.kept, self.two = kept, two
        self.got = swap(clock.go(given), "dp", 1, N_DP)
        self.moved, self.here, self.there = {}, {}, {}

    def across(self, n):
        row = (self.kept.shape[1] + 2 * n) * CH
        return [(self.kept, row), (self.got, row)]

    def here_sum(self, n):
        row = 2 * n * CH
        return [(self.kept, row), (self.got, row), (self.moved[n], 0)]

    def over_x(self, n, across):
        self.moved[n] = swap(across, "dp", 2, N_DP)

    def over_y(self, n, here):
        self.here[n] = here
        self.there[n] = swap(here, "ctx", 1, 2) if self.two else lax.psum(here, "ctx")

    def sums(self, n):
        if self.two:
            return self.here[n], self.there[n]
        return self.there[n], jnp.zeros_like(self.there[n])


def body(
    block_in,
    doc_starts,
    query_weight,
    key_weight,
    value_weight,
    output_weight,
    up_weight,
    down_weight,
    query_bias,
    key_bias,
    value_bias,
    up_bias,
    output_bias,
    norm_gain,
    norm_shift,
    cotangent,
):
    seqs, rows, _ = block_in.shape
    d, c, t = lax.axis_index("dp"), lax.axis_index("ctx"), lax.axis_index("tp")
    n_ctx = lax.axis_size("ctx")
    two = n_ctx == 2
    info = jnp.stack([t, c, d]).astype(jnp.int32)

    clock = Clock()

    x = Gather(block_in)
    x.forth(clock)
    small = jnp.concatenate(
        [query_bias, key_bias, value_bias, up_bias, output_bias, norm_gain, norm_shift]
    )
    size = small.size
    near = swap(small, "dp", 1, N_DP)
    flip = (d & 1) == 1
    pair = jnp.concatenate([jnp.where(flip, near, small), jnp.where(flip, small, near)])
    across = swap(pair, "dp", 2, N_DP)
    flip = (d & 2) == 2
    small_here = jnp.concatenate([jnp.where(flip, across, pair), jnp.where(flip, pair, across)])
    small_here = small_here.reshape(N_DP, size)

    def small_of(first, length):
        return small_here[:, first : first + length].reshape(1, -1)

    share = query_bias.size
    share_units = up_bias.size
    qkv_bias = jnp.concatenate([small_of(n * share, share) for n in range(3)], axis=1)
    up_shift = small_of(3 * share, share_units)
    output_shift = small_of(3 * share + share_units, share)
    gain_here = small_of(4 * share + share_units, share)
    shift_here = small_of(5 * share + share_units, share)
    both = jnp.concatenate([gain_here, shift_here], axis=0)
    others = [ring(both, -r) for r in range(1, N_TP)]
    wq_shard = jnp.concatenate([query_weight, key_weight, value_weight], axis=1)
    shards_q = Shards(tie(wq_shard, across), 0, d, c, two)
    shards_q.over_x(clock)
    shards_u = Shards(up_weight, 0, d, c, two, made=False)
    wo_shard = jnp.concatenate([output_weight, down_weight], axis=0)
    shards_o = Shards(wo_shard, 1, d, c, two)
    clock.sync(x.behind, shards_q.first, *others, shards_u.part)

    x.back()
    shards_q.over_y(clock)
    shards_u.over_x(clock)
    shards_q.near_core(clock)
    circle = jnp.concatenate([both, *others] * 2, axis=1)
    gain_shift = lax.dynamic_slice_in_dim(circle, (N_TP - t) % N_TP * CH, D, 1)
    gain, shift = gain_shift[0:1], gain_shift[1:2]

    here = c * rows + jnp.arange(rows, dtype=jnp.int32)
    tables, opening = rotary_tables(doc_starts, here)
    blocks = 1 if two else n_ctx
    before, _ = rotary_tables(doc_starts, jnp.arange(blocks * rows, dtype=jnp.int32))
    before = [a.reshape(seqs, blocks, rows, 128) for a in before]

    clock.sync(shards_q.second, shards_u.first, x.ahead, shards_q.near, shards_o.part)
    shards_u.near_core(clock)

    x.onward(clock)
    shards_u.over_y(clock)
    shards_o.over_x(clock)
    shards_q.far_core(clock)
    clock.sync(
        x.far,
        *shards_q.far_near,
        shards_u.second,
        shards_o.first,
        *before,
    )

    def send_keys(s):
        kv[s] = clock.go(kv[s])
        if two:
            kvp[s] = lax.ppermute(kv[s], "ctx", [(0, 1)])[None]
        else:
            kvp[s] = lax.all_gather(kv[s], "ctx", axis=0, tiled=False)

    def attention_step(s):
        return attention(
            info,
            s,
            opening[:, None],
            q,
            kv[s],
            kvp[s],
            datt,
            tables,
            before,
            deps=clock.marks,
        )

    def returned(sent):
        if two:
            return lax.ppermute(clock.go(sent[0]), "ctx", [(1, 0)])
        return lax.psum_scatter(clock.go(sent), "ctx", scatter_dimension=0, tiled=False)

    def back_in_step(s):
        return back_in(
            layout,
            info,
            s,
            x.parts,
            dq[s],
            dkv[s],
            sent[s],
            dup,
            shards_q.pieces,
            shards_u.pieces,
            gain,
            stats,
            deps=clock.marks,
        )

    layout = layout_of(two)
    kvp, att, dq, dkv, sent = ([None] * seqs for _ in range(5))

    shards_o.over_y(clock)
    shards_u.far_core(clock)
    ct = Gather(cotangent)
    ct.behind, ct.ahead = ring(ct.own, 1), ring(ct.own, -1)
    normed, stats, q, *kv = norm_qkv(
        layout, info, x.parts, gain, shift, shards_q.pieces, qkv_bias, tables, deps=clock.marks
    )
    clock.sync(normed, *shards_u.far_near, shards_u.near, ct.behind, shards_o.second)

    shards_o.near_core(clock)
    shards_o.far_core(clock)
    ct.onward(clock)
    hidden, slope = mlp_up(layout, info, normed, shards_u.pieces, up_shift, deps=clock.marks)
    clock.sync(hidden, shards_o.near, *shards_o.far_near)

    send_keys(0)
    send_keys(1)
    out_parts = out_hidden(layout, info, hidden, shards_o.pieces, deps=clock.marks)
    clock.sync(out_parts, ct.ahead)
    down_begun = grad_down(
        info, hidden, (ct.own, ct.behind, ct.ahead), (0, 3, 1), deps=clock.marks
    )
    clock.sync(down_begun[0], ct.far)

    cf, out_bias_sum, datt, dup = back_out(
        layout, info, ct.parts, shards_o.pieces, slope, deps=clock.marks
    )
    clock.sync(datt, kvp[0])

    def added(big, small=()):
        return combine(info, big, list(small), deps=clock.marks)

    up_kept, up_given, up_sum = grad_up(info, normed, dup, deps=clock.marks)
    clock.sync(up_kept, kvp[1])
    up = Reduction(up_kept, up_given, clock, two)
    att[0], dq[0], dkv[0], sent[0] = attention_step(0)
    clock.sync(att[0], up.got)

    sent[0] = returned(sent[0])
    across, across_1 = added([up.across(0), up.across(1)])
    up.over_x(0, across)
    clock.sync(across)
    down_kept, down_given = grad_down(
        info, hidden, (ct.far,), (2,), down_begun, deps=clock.marks
    )
    clock.sync(down_kept, *clock.marks)
    att[1], dq[1], dkv[1], sent[1] = attention_step(1)
    clock.sync(att[1], sent[0], up.moved[0])

    sent[1] = returned(sent[1])
    up.over_x(1, clock.go(across_1))
    down = Reduction(down_kept, down_given, clock, two)
    out = Scatter(out_heads(layout, info, att, out_parts, shards_o.pieces, deps=clock.marks))
    clock.sync(out.own, *clock.marks)
    head_kept, head_given, query_sum = grad_out_query(
        info, normed, cf, att, dq, deps=clock.marks
    )
    clock.sync(head_kept, down.got)
    across, across_1, here = added([down.across(0), down.across(1), up.here_sum(0)])
    clock.sync(across, sent[1])

    up.over_y(0, clock.go(here))
    out.forward(clock)
    clock.sync(up.moved[1])
    down.over_x(0, clock.go(across))
    head = Reduction(head_kept, head_given, clock, two)
    (here,) = added([up.here_sum(1)])
    clock.sync(here)
    back_0 = Scatter(back_in_step(0))
    clock.sync(back_0.own)
    clock.sync(up.there[0])

    up.over_y(1, clock.go(here))
    clock.sync(out.far)
    back_0.forward(clock)
    back_0.backward(clock)
    clock.sync(down.moved[0], head.got)
    down.over_x(1, clock.go(across_1))
    here, across, out_both = added([down.here_sum(0), head.across(0)], [out.both()])
    clock.sync(here)
    pair_kept, pair_given, pair_sum = grad_key_value(info, normed, dkv, sent, deps=clock.marks)
    clock.sync(pair_kept)
    clock.sync(up.there[1])

    down.over_y(0, clock.go(here))
    clock.sync(back_0.far, back_0.back)
    out.backward(clock)
    clock.sync(down.moved[1])
    head.over_x(0, clock.go(across))
    pair = Reduction(pair_kept, pair_given, clock, two)
    here, both_0 = added([down.here_sum(1)], [back_0.both()])
    clock.sync(here)
    back_1 = Scatter(back_in_step(1))
    clock.sync(back_1.own)
    clock.sync(down.there[0])

    down.over_y(1, clock.go(here))
    clock.sync(out.back)
    back_1.forward(clock)
    back_1.backward(clock)
    clock.sync(head.moved[0], pair.got)
    (across,) = added([pair.across(0)])
    pair.over_x(0, across)
    clock.sync(across)
    (here,) = added([head.here_sum(0)])
    clock.sync(here)
    up_wg = finish_blocks(info, [up.sums(0), up.sums(1)], 1, deps=clock.marks)
    clock.sync(up_wg)
    clock.sync(down.there[1])

    head.over_y(0, clock.go(here))
    back_0.onward(clock.go(both_0))
    clock.sync(back_1.far, back_1.back)
    (both_1,) = added([], [back_1.both()])
    back_1.onward(both_1)
    clock.sync(pair.moved[0])
    (here,) = added([pair.here_sum(0)])
    clock.sync(here)
    down_wg = finish_blocks(info, [down.sums(0), down.sums(1)], 0, deps=clock.marks)
    clock.sync(down_wg)
    clock.sync(head.there[0])

    pair.over_y(0, clock.go(here))
    clock.sync(back_0.near, back_1.near)
    out.onward(clock.go(out_both))
    in_grad, last = finish_in(
        info,
        (*back_0.shares(), *back_1.shares()),
        block_in,
        cotangent,
        stats,
        gain_here,
        deps=clock.marks,
    )
    clock.sync(in_grad)
    table = small_table(info, (query_sum, pair_sum, up_sum, out_bias_sum, last))
    output_wg, query_wg = finish_pair(info, *head.sums(0), deps=clock.marks)
    table = table + swap(table, "dp", 1, N_DP)
    table = table + swap(table, "dp", 2, N_DP)
    table = table + swap(table, "ctx", 1, 2) if two else lax.psum(table, "ctx")
    block_out, key_wg, value_wg = finish_last(
        info, out.shares(), block_in, output_shift, *pair.sums(0)
    )

    share = CH // N_DP
    mine = lax.dynamic_slice_in_dim(table, d * share, share, 1)
    query_bg, key_bg, value_bg = mine[0], mine[1], mine[2]
    output_bg, gain_g, shift_g = mine[7], mine[8], mine[9]
    up_bg = lax.dynamic_slice_in_dim(table, 3 + d, 1, 0).reshape(-1)
    return (
        block_out,
        in_grad,
        query_wg,
        key_wg,
        value_wg,
        output_wg,
        up_wg,
        down_wg,
        query_bg,
        key_bg,
        value_bg,
        up_bg,
        output_bg,
        gain_g,
        shift_g,
    )


def solution(mesh):
    return jax.shard_map(
        body,
        mesh=mesh,
        in_specs=(
            P("dp", "ctx", "tp"),
            P("dp", None),
            P("dp", "tp"),
            P("dp", "tp"),
            P("dp", "tp"),
            P("tp", "dp"),
            P("dp", "tp"),
            P("tp", "dp"),
        )
        + (P(("tp", "dp")),) * 7
        + (P("dp", "ctx", "tp"),),
        out_specs=(
            P("dp", "ctx", "tp"),
            P("dp", "ctx", "tp"),
            P("dp", "tp"),
            P("dp", "tp"),
            P("dp", "tp"),
            P("tp", "dp"),
            P("dp", "tp"),
            P("tp", "dp"),
        )
        + (P(("tp", "dp")),) * 7,
        check_vma=False,
    )
```

```python
import functools
import math

import jax
import jax.numpy as jnp
from jax import lax
from jax.experimental import pallas as pl
from jax.experimental.pallas import tpu as pltpu
from jax.sharding import PartitionSpec as P

HEAD_DIM = 64
ROT = 32
D = 2048
N_DP = 4
N_TP = 4
CH = D // N_TP
EPS = 1e-05
NEG = -1e30
VMEM = 127 * 2**19
COST = 0.02

bf16 = jnp.bfloat16
f32 = jnp.float32


def dot_nn(a, b):
    return lax.dot_general(a, b, (((1,), (0,)), ((), ())), preferred_element_type=f32)


def dot_nt(a, b):
    return lax.dot_general(a, b, (((1,), (1,)), ((), ())), preferred_element_type=f32)


def dot_tn(a, b):
    return lax.dot_general(a, b, (((0,), (0,)), ((), ())), preferred_element_type=f32)


def spec(block, index):
    return pl.BlockSpec(block, index)


def whole(*block):
    zeros = (0,) * len(block)
    return pl.BlockSpec(block, lambda g, *_: zeros)


def once(*block):
    zeros = (0,) * len(block)
    return pl.BlockSpec(block, lambda g, *_: zeros, pipeline_mode=pl.Buffered(1))


def one_of(s, *block):
    zeros = (0,) * len(block)
    return pl.BlockSpec((None, *block), lambda g, *_: (s, *zeros))


def shaped(shape, dtype=bf16):
    return jax.ShapeDtypeStruct(tuple(shape), dtype)


ANYWHERE = pl.BlockSpec(memory_space=pl.ANY)


def call(
    body, name, grid, info, ins, in_specs, outs, out_specs, flops, scratch=(), deps=(), aliases=()
):
    moved = sum(math.prod(a.shape) * a.dtype.itemsize for a in (*ins, *jax.tree.leaves(outs)))
    first, last = 1 + len(ins), 1 + len(ins) + len(deps)

    def without_deps(*refs):
        body(*refs[:first], *refs[last:])

    return pl.pallas_call(
        without_deps,
        grid_spec=pltpu.PrefetchScalarGridSpec(
            num_scalar_prefetch=1,
            grid=(grid,),
            in_specs=[*in_specs, *[ANYWHERE] * len(deps)],
            out_specs=out_specs,
            scratch_shapes=list(scratch),
        ),
        out_shape=outs,
        input_output_aliases={1 + n: m for n, m in aliases},
        compiler_params=pltpu.CompilerParams(vmem_limit_bytes=VMEM),
        cost_estimate=pl.CostEstimate(
            flops=int(flops * COST), bytes_accessed=int(moved * COST), transcendentals=0
        ),
        name=name,
    )(info, *ins, *deps)


def tie(value, *deps):
    def nothing(*refs):
        del refs

    return pl.pallas_call(
        nothing,
        in_specs=[ANYWHERE] * (1 + len(deps)),
        out_specs=ANYWHERE,
        out_shape=shaped(value.shape, value.dtype),
        input_output_aliases={0: 0},
        compiler_params=pltpu.CompilerParams(vmem_limit_bytes=VMEM),
        cost_estimate=pl.CostEstimate(flops=0, bytes_accessed=0, transcendentals=0),
        name="tie",
    )(value, *deps)


def columns(index, width=CH):
    return pl.ds(pl.multiple_of(index * width, width), width)


def layout_of(two):
    if two:
        halves = [("c", CH // 2), ("other", CH // 2)]
    else:
        halves = [("", CH)]
    return [(0, "", CH), (1, "", CH)] + [(r, *half) for r in (2, 3) for half in halves]


def piece_offset(info, half):
    return {"": 0, "c": info[1], "other": 1 - info[1]}[half] * (CH // 2)


def piece_window(info, piece):
    r, half, size = piece
    start = (info[2] ^ r) * CH + piece_offset(info, half)
    return pl.ds(pl.multiple_of(start, size), size)


class Clock:
    def __init__(self):
        self.marks = ()

    def go(self, value):
        return tie(value, *self.marks) if self.marks else value

    def sync(self, *arrays):
        def nothing(*refs):
            del refs

        self.marks = (
            pl.pallas_call(
                nothing,
                in_specs=[ANYWHERE] * (len(arrays) + len(self.marks)),
                out_specs=ANYWHERE,
                out_shape=shaped((8, 128), f32),
                compiler_params=pltpu.CompilerParams(vmem_limit_bytes=VMEM),
                cost_estimate=pl.CostEstimate(flops=0, bytes_accessed=0, transcendentals=0),
                name="sync",
            )(*arrays, *self.marks),
        )


def swap(array, axis, bit, size):
    return lax.ppermute(array, axis, [(i, i ^ bit) for i in range(size)])


class Shards:
    def __init__(self, own, axis, d, c, two, made=True):
        self.own, self.two, self.made = own, two, made
        size = own.shape[axis] // 2
        self.part = lax.dynamic_slice_in_dim(own, c * size, size, axis) if two else own

    def near_core(self, clock):
        self.own = clock.go(self.own) if self.made else self.own
        self.near = swap(self.own, "dp", 1, N_DP)

    def over_x(self, clock):
        self.first = swap(clock.go(self.part), "dp", 2, N_DP)

    def over_y(self, clock):
        self.first = clock.go(self.first)
        self.second = swap(self.first, "ctx", 1, 2) if self.two else self.first

    def far_core(self, clock):
        self.first = clock.go(self.first)
        far = [self.first]
        if self.two:
            self.second = clock.go(self.second)
            far.append(self.second)
        self.far_near = [swap(a, "dp", 1, N_DP) for a in far]
        self.pieces = [self.own, self.near, *far, *self.far_near]


def rotary_tables(starts, positions):
    before = starts[:, None, :] <= positions[None, :, None]
    opening = jnp.max(jnp.where(before, starts[:, None, :], 0), axis=2)
    relative = (positions[None, :] - opening).astype(f32)
    half = ROT // 2
    lane = jnp.arange(128, dtype=jnp.int32) % HEAD_DIM
    frequency = jnp.exp((lane % half).astype(f32) * (-math.log(10000.0) / half))
    angles = relative[:, :, None] * jnp.where(lane < ROT, frequency, 0.0)
    sine = jnp.sin(angles)
    return (
        jnp.cos(angles),
        jnp.where(lane < half, -sine, 0.0),
        jnp.where(lane >= half, sine, 0.0),
    ), opening


def add_rounded(a, b):
    return (a.astype(f32) + b.astype(f32)).astype(bf16)


def turn(x, own, up, down):
    return x * own + pltpu.roll(x, 112, 1) * up + pltpu.roll(x, 16, 1) * down


def turn_back(x, own, up, down):
    return x * own - pltpu.roll(x, 112, 1) * up - pltpu.roll(x, 16, 1) * down


def stream_pieces(layout, info, sources, held, sems, axis, blocks):
    j = pl.program_id(0)

    def copies(block):
        cut = pl.ds(pl.multiple_of(block * CH, CH), CH)
        for n, (piece, source) in enumerate(zip(layout, sources)):
            window = piece_window(info, piece)
            if axis == 0:
                pair = source.at[:, cut], held.at[window, cut]
            else:
                pair = source.at[cut, :], held.at[cut, window]
            yield pltpu.make_async_copy(*pair, sems.at[block, n])

    @pl.when(j == 0)
    def _():
        for block in range(blocks):
            for copy in copies(block):
                copy.start()

    for copy in copies(j):
        copy.wait()


def norm_qkv_body(layout, info, x0, xa, xc, xb, gain, shift, bias, own, up, down, *refs):
    *w, normed, stats, q, kv0, kv1, columns_held, held, sems = refs
    j = pl.program_id(0)
    t = info[0]
    seqs, rows, _ = x0.shape
    stream_pieces(layout, info, w, held, sems, 0, 3)

    @pl.when(j == 0)
    def _():
        parts = [(x0, t), (xa, (t + 3) % N_TP), (xc, (t + 1) % N_TP), (xb, (t + 2) % N_TP)]
        tile = 128

        def rows_of(i, carry):
            s = i // (rows // tile)
            window = pl.ds(pl.multiple_of((i % (rows // tile)) * tile, tile), tile)
            x = [part[s, window, :].astype(f32) for part, _ in parts]
            average = sum(jnp.sum(a, axis=1, keepdims=True) for a in x) * (1.0 / D)
            x = [a - average for a in x]
            variance = sum(jnp.sum(a * a, axis=1, keepdims=True) for a in x) * (1.0 / D)
            root = lax.rsqrt(variance + EPS)
            columns_held[s, window, 0:1] = average
            columns_held[s, window, 1:2] = root
            for a, (_, index) in zip(x, parts):
                at = columns(index)
                y = a * root * gain[:, at].astype(f32) + shift[:, at].astype(f32)
                normed[s, window, at] = y.astype(bf16)
            return carry

        columns_held[...] = jnp.zeros(columns_held.shape, f32)
        lax.fori_loop(0, seqs * rows // tile, rows_of, 0)
        for s in range(seqs):
            stats[s] = columns_held[s].T[: stats.shape[1]]

    for s, kv in ((0, kv0), (1, kv1)):
        y = dot_nn(normed[s], held[:, columns(j)]) + bias[...].astype(f32)

        def rotated(s=s, y=y):
            parts = [
                turn(y[:, 128 * n : 128 * n + 128], own[s], up[s], down[s])
                for n in range(CH // 128)
            ]
            return jnp.concatenate(parts, axis=1).astype(bf16)

        @pl.when(j == 0)
        def _(s=s, rotated=rotated):
            q[s] = rotated()

        @pl.when(j == 1)
        def _(kv=kv, rotated=rotated):
            kv[0] = rotated()

        @pl.when(j == 2)
        def _(kv=kv, y=y):
            kv[0] = y.astype(bf16)


def norm_qkv(layout, info, parts, gain, shift, w, bias, tables, deps=()):
    seqs, rows, _ = parts[0].shape
    outs = (
        shaped((seqs, rows, D)),
        shaped((seqs, 8, rows), f32),
        shaped((seqs, rows, CH)),
        shaped((2, rows, CH)),
        shaped((2, rows, CH)),
    )
    pair = spec((1, rows, CH), lambda j, *_: (jnp.maximum(j - 1, 0), 0, 0))
    return call(
        functools.partial(norm_qkv_body, layout),
        "norm_qkv",
        3,
        info,
        (*parts, gain, shift, bias, *tables, *w),
        [whole(seqs, rows, CH)] * 4
        + [whole(1, D)] * 2
        + [spec((1, CH), lambda j, *_: (0, j))]
        + [whole(seqs, rows, 128)] * 3
        + [ANYWHERE] * len(w),
        outs,
        [
            whole(seqs, rows, D),
            whole(seqs, 8, rows),
            whole(seqs, rows, CH),
            pair,
            pair,
        ],
        2 * seqs * rows * D * 3 * CH,
        [
            pltpu.VMEM((seqs, rows, 128), f32),
            pltpu.VMEM((D, 3 * CH), bf16),
            pltpu.SemaphoreType.DMA((3, len(w))),
        ],
        deps=deps,
    )


def mlp_up_body(layout, info, normed, bias, *refs):
    *w, hidden, grad, held, sems = refs
    j = pl.program_id(0)
    stream_pieces(layout, info, w, held, sems, 0, held.shape[1] // CH)
    root = math.sqrt(2.0 / math.pi)
    part = 512
    for s in range(normed.shape[0]):
        for row in range(0, normed.shape[1], part):
            window = slice(row, row + part)
            u = dot_nn(normed[s, window], held[:, columns(j)]) + bias[...].astype(f32)
            square = u * u
            t = jnp.tanh(u * (root + (root * 0.044715) * square))
            half = 0.5 + 0.5 * t
            value = u * half
            hidden[s, window] = value.astype(bf16)
            slope = 2 * root + (6 * 0.044715 * root) * square
            grad[s, window] = (half + value * (1.0 - half) * slope).astype(bf16)


def mlp_up(layout, info, normed, w, bias, deps=()):
    seqs, rows, _ = normed.shape
    units = w[0].shape[1]
    block = spec((seqs, rows, CH), lambda j, *_: (0, 0, j))
    return call(
        functools.partial(mlp_up_body, layout),
        "mlp_up",
        units // CH,
        info,
        (normed, bias, *w),
        [whole(seqs, rows, D), spec((1, CH), lambda j, *_: (0, j))] + [ANYWHERE] * len(w),
        (shaped((seqs, rows, units)),) * 2,
        [block] * 2,
        2 * seqs * rows * D * units,
        [pltpu.VMEM((D, units), bf16), pltpu.SemaphoreType.DMA((units // CH, len(w)))],
        deps=deps,
    )


def back_out_body(layout, info, c0, ca, cc, cb, slope, *refs):
    *w, cf, bias_grad, datt, dup, held, sems, cf_sems = refs
    j = pl.program_id(0)
    t = info[0]
    seqs = c0.shape[0]
    parts = [(c0, t), (ca, (t + 3) % N_TP), (cc, (t + 1) % N_TP), (cb, (t + 2) % N_TP)]
    stream_pieces(layout, info, w, held, sems, 1, held.shape[0] // CH)
    copies = [
        pltpu.make_async_copy(part, cf.at[:, :, columns(index)], cf_sems.at[n])
        for n, (part, index) in enumerate(parts)
    ]

    @pl.when(j == 0)
    def _():
        for copy in copies:
            copy.start()
        bias_grad[...] = sum(
            jnp.sum(c0[s].astype(f32), axis=0, keepdims=True) for s in range(seqs)
        )

    for s in range(seqs):
        y = sum(dot_nt(part[s], held[columns(j), columns(index)]) for part, index in parts)

        @pl.when(j == 0)
        def _(s=s, y=y):
            datt[s] = y.astype(bf16)

        @pl.when(j > 0)
        def _(s=s, y=y):
            dup[s] = (y * slope[s].astype(f32)).astype(bf16)

    @pl.when(j == pl.num_programs(0) - 1)
    def _():
        for copy in copies:
            copy.wait()


def back_out(layout, info, parts, w, slope, deps=()):
    seqs, rows, units = slope.shape
    later = spec((seqs, rows, CH), lambda j, *_: (0, 0, jnp.maximum(j - 1, 0)))
    return call(
        functools.partial(back_out_body, layout),
        "back_out",
        1 + units // CH,
        info,
        (*parts, slope, *w),
        [once(seqs, rows, CH)] * 4 + [later] + [ANYWHERE] * len(w),
        (
            shaped((seqs, rows, D)),
            shaped((1, CH), f32),
            shaped((seqs, rows, CH)),
            shaped((seqs, rows, units)),
        ),
        [ANYWHERE, whole(1, CH), whole(seqs, rows, CH), later],
        2 * seqs * rows * D * (CH + units),
        [
            pltpu.VMEM((CH + units, D), bf16),
            pltpu.SemaphoreType.DMA((1 + units // CH, len(w))),
            pltpu.SemaphoreType.DMA((len(parts),)),
        ],
        deps=deps,
    )


def attention_body(
    blocks, info, low, q, kv, kvp, do, own, up, down, ownp, upp, downp,
    att, dq, dkv, dkvp, scores, probs,
):
    rows = q.shape[0]
    before, start = info[1], info[1] * rows
    lane = lax.broadcasted_iota(jnp.int32, (rows, 128), 1)
    key_row = lax.broadcasted_iota(jnp.int32, (rows, 1), 0)
    query_at = start + lax.broadcasted_iota(jnp.int32, (1, rows), 1)
    first = low[0]
    do_t = do[...].astype(f32).T
    nothing = jnp.zeros((), bf16)
    outputs = []
    for head in range(2):
        mine = (lane < HEAD_DIM) if head == 0 else (lane >= HEAD_DIM)
        half = slice(HEAD_DIM * head, HEAD_DIM * (head + 1))
        qh = jnp.where(mine, q[...] * jnp.asarray(HEAD_DIM**-0.5, bf16), nothing)
        dh = jnp.where(mine, do[...], nothing)

        key_at = start + key_row
        s = dot_nt(kv[0], qh)
        s = jnp.where((key_at >= first) & (key_at <= query_at), s, NEG)
        scores[blocks] = s
        peak = jnp.max(s, axis=0, keepdims=True)

        def score(n, peak):
            s = dot_nt(kvp[n, 0], qh)
            s = jnp.where(n * rows + key_row >= first, s, NEG)
            scores[n] = s
            return jnp.maximum(peak, jnp.max(s, axis=0, keepdims=True))

        peak = lax.fori_loop(0, before, score, peak)

        def expo(n, total):
            e = jnp.exp(scores[n] - peak)
            scores[n] = e
            return total + jnp.sum(e, axis=0, keepdims=True)

        total = expo(blocks, jnp.zeros((1, rows), f32))
        total = lax.fori_loop(0, before, expo, total)
        scale = 1.0 / total

        def weigh(n, values):
            p = (scores[n] * scale).astype(bf16)
            probs[n] = p
            return dot_tn(values, p)

        out_t = weigh(blocks, kv[1])
        out_t = lax.fori_loop(0, before, lambda n, acc: acc + weigh(n, kvp[n, 1]), out_t)
        delta = jnp.sum(out_t[half] * do_t[half], axis=0, keepdims=True)

        def back(n, keys, values):
            dp = dot_nt(values, dh)
            ds = ((scores[n] * scale) * (dp - delta)).astype(bf16)
            return dot_nn(ds, qh), dot_nn(probs[n], dh), dot_tn(keys, ds)

        dk, dv, dq_t = back(blocks, kv[0], kv[1])
        if head == 0:
            dk_sum, dv_sum = dk, dv
        else:
            dk_sum, dv_sum = dk_sum + dk, dv_sum + dv

        def back_before(n, acc):
            dk, dv, more = back(n, kvp[n, 0], kvp[n, 1])
            dk = turn_back(dk, ownp[n], upp[n], downp[n])
            if head == 0:
                dkvp[n, 0] = dk.astype(bf16)
                dkvp[n, 1] = dv.astype(bf16)
            else:
                dkvp[n, 0] = (dkvp[n, 0].astype(f32) + dk).astype(bf16)
                dkvp[n, 1] = (dkvp[n, 1].astype(f32) + dv).astype(bf16)
            return acc + more

        dq_t = lax.fori_loop(0, before, back_before, dq_t)
        outputs.append((out_t[half], dq_t[half]))

    def clear(n, carry):
        dkvp[n] = jnp.zeros(dkvp.shape[1:], bf16)
        return carry

    lax.fori_loop(before, blocks, clear, 0)
    att[...] = jnp.concatenate([outputs[0][0], outputs[1][0]], axis=0).T.astype(bf16)
    grad = jnp.concatenate([outputs[0][1], outputs[1][1]], axis=0).T * HEAD_DIM**-0.5
    dq[...] = turn_back(grad, own[...], up[...], down[...]).astype(bf16)
    dkv[0] = turn_back(dk_sum, own[...], up[...], down[...]).astype(bf16)
    dkv[1] = dv_sum.astype(bf16)


def attention_two_body(
    info, low, q, kv, kvp, do, own, up, down, ownp, upp, downp, att, dq, dkv, dkvp
):
    rows = q.shape[0]
    part = rows // 2
    before, start = info[1], info[1] * rows

    def tail(x, skipped):
        return x[:, skipped:] if skipped else x

    def merge(acc, x, skipped, op):
        if acc is None:
            return x
        if not skipped:
            return op(acc, x)
        return jnp.concatenate([acc[:, :skipped], op(acc[:, skipped:], x)], axis=1)

    def run(with_before):
        lane = lax.broadcasted_iota(jnp.int32, (rows, 128), 1)
        key_row = lax.broadcasted_iota(jnp.int32, (part, 1), 0)
        query_at = start + lax.broadcasted_iota(jnp.int32, (1, rows), 1)
        first = low[...]
        do_t = do[...].astype(f32).T
        nothing = jnp.zeros((), bf16)
        blocks = []
        for n in range(2):
            if with_before:
                blocks.append((kvp.at[0], n * part, 0, False))
        for n in range(2):
            blocks.append((kv, n * part, n * part, True))
        dk_sum, dv_sum = [0.0] * len(blocks), [0.0] * len(blocks)
        heads = []
        for head in range(2):
            mine = (lane < HEAD_DIM) if head == 0 else (lane >= HEAD_DIM)
            qh = jnp.where(mine, q[...] * jnp.asarray(HEAD_DIM**-0.5, bf16), nothing)
            dh = jnp.where(mine, do[...], nothing)
            heads.append((qh, dh, slice(HEAD_DIM * head, HEAD_DIM * (head + 1))))

        def score(head):
            qh = heads[head][0]
            scores, peak = [], None
            for ref, row, skip, here in blocks:
                s = dot_nt(ref[0, row : row + part], qh[skip:])
                key_at = (start if here else start - rows) + row + key_row
                allowed = key_at >= tail(first, skip)
                if here:
                    allowed = allowed & (key_at <= tail(query_at, skip))
                s = jnp.where(allowed, s, NEG)
                scores.append(s)
                peak = merge(peak, jnp.max(s, axis=0, keepdims=True), skip, jnp.maximum)
            return scores, peak

        def grads(head):
            dh = heads[head][1]
            return [
                dot_nt(ref[1, row : row + part], dh[skip:]) for ref, row, skip, _ in blocks
            ]

        def soften(scores, peak):
            terms, total = [], None
            for s, (_, _, skip, _) in zip(scores, blocks):
                e = jnp.exp(s - tail(peak, skip))
                terms.append(e)
                total = merge(total, jnp.sum(e, axis=0, keepdims=True), skip, jnp.add)
            scale = 1.0 / total
            probs = [e * tail(scale, skip) for e, (_, _, skip, _) in zip(terms, blocks)]
            return probs, [p.astype(bf16) for p in probs]

        def weigh(head, rounded):
            out_t = None
            for n, (ref, row, skip, _) in enumerate(blocks):
                out_t = merge(
                    out_t, dot_tn(ref[1, row : row + part], rounded[n]), skip, jnp.add
                )
                dv_sum[n] = dv_sum[n] + dot_nn(rounded[n], heads[head][1][skip:])
            half = heads[head][2]
            return out_t[half], jnp.sum(out_t[half] * do_t[half], axis=0, keepdims=True)

        def differ(probs, dps, delta):
            return [
                (p * (dp - tail(delta, skip))).astype(bf16)
                for p, dp, (_, _, skip, _) in zip(probs, dps, blocks)
            ]

        def back(head, dss):
            dq_t = None
            for n, (ref, row, skip, _) in enumerate(blocks):
                dk_sum[n] = dk_sum[n] + dot_nn(dss[n], heads[head][0][skip:])
                dq_t = merge(dq_t, dot_tn(ref[0, row : row + part], dss[n]), skip, jnp.add)
            return dq_t[heads[head][2]]

        scores_0 = score(0)
        scores_1 = score(1)
        probs_0, rounded_0 = soften(*scores_0)
        out_0, delta_0 = weigh(0, rounded_0)
        dss_0 = differ(probs_0, grads(0), delta_0)
        probs_1, rounded_1 = soften(*scores_1)
        dq_0 = back(0, dss_0)
        out_1, delta_1 = weigh(1, rounded_1)
        dss_1 = differ(probs_1, grads(1), delta_1)
        dq_1 = back(1, dss_1)
        outputs = [(out_0, dq_0), (out_1, dq_1)]

        att[...] = jnp.concatenate([outputs[0][0], outputs[1][0]], axis=0).T.astype(bf16)
        grad = jnp.concatenate([outputs[0][1], outputs[1][1]], axis=0).T * HEAD_DIM**-0.5
        dq[...] = turn_back(grad, own[...], up[...], down[...]).astype(bf16)
        dk = jnp.concatenate(dk_sum[-2:], axis=0)
        dkv[0] = turn_back(dk, own[...], up[...], down[...]).astype(bf16)
        dkv[1] = jnp.concatenate(dv_sum[-2:], axis=0).astype(bf16)
        if with_before:
            dk = jnp.concatenate(dk_sum[:2], axis=0)
            dkvp[0, 0] = turn_back(dk, ownp[0], upp[0], downp[0]).astype(bf16)
            dkvp[0, 1] = jnp.concatenate(dv_sum[:2], axis=0).astype(bf16)
        else:
            dkvp[...] = jnp.zeros(dkvp.shape, bf16)

    @pl.when(before == 0)
    def _():
        run(False)

    @pl.when(before > 0)
    def _():
        run(True)


def attention(info, s, low, q, kv, kvp, do, tables, tables_before, deps=()):
    _, rows, width = q.shape
    blocks = kvp.shape[0]
    token = spec((rows, 128), lambda g, *_: (0, g))
    query = spec((None, rows, 128), lambda g, *_: (s, 0, g))
    pair = spec((2, rows, 128), lambda g, *_: (0, 0, g))
    pairs = spec((blocks, 2, rows, 128), lambda g, *_: (0, 0, 0, g))
    return call(
        attention_two_body if blocks == 1 else functools.partial(attention_body, blocks),
        "attention",
        width // 128,
        info,
        (low, q, kv, kvp, do, *tables, *tables_before),
        [one_of(s, 1, rows), query, pair, pairs, query]
        + [one_of(s, rows, 128)] * 3
        + [one_of(s, blocks, rows, 128)] * 3,
        (
            shaped((rows, width)),
            shaped((rows, width)),
            shaped((2, rows, width)),
            shaped((blocks, 2, rows, width)),
        ),
        [token, token, pair, pairs],
        48 * rows * rows * width,
        []
        if blocks == 1
        else [
            pltpu.VMEM((blocks + 1, rows, rows), f32),
            pltpu.VMEM((blocks + 1, rows, rows), bf16),
        ],
        deps=deps,
    )


TAIL = 16


def fetch_pieces(layout, sources, targets, sems, axis):
    copies = [[] for _ in range(N_DP)]
    at = [r * CH for r in range(N_DP)]
    n = 0
    for group, target in zip(sources, targets):
        at = [r * CH for r in range(N_DP)]
        for (r, _, size), source in zip(layout, group):
            window = pl.ds(at[r], size)
            place = target.at[window, :] if axis == 0 else target.at[:, window]
            copies[r].append(pltpu.make_async_copy(source, place, sems.at[n]))
            at[r] += size
            n += 1
    return copies


def with_chunk(layout, info, copies, work):
    j = pl.program_id(0)

    @pl.when(j == 0)
    def _():
        for group in copies:
            for copy in group:
                copy.start()

    for r in range(N_DP):

        @pl.when(j == r)
        def _(r=r):
            for copy in copies[r]:
                copy.wait()
            at = r * CH
            for s, half, size in layout:
                if s == r:
                    offset = pl.multiple_of(piece_offset(info, half), size)
                    work(pl.ds(at, size), pl.ds(offset, size))
                    at += size


def chunk_now(info):
    return ((info[2] ^ pl.program_id(0)) + N_TP - info[0]) % N_TP


def out_hidden_body(layout, info, hidden, *refs):
    *w, out, held, sems = refs

    def work(place, window):
        for s in range(hidden.shape[0]):
            out[0, s, :, window] = dot_nn(hidden[s], held[:, place]).astype(bf16)

    lower = [a.at[pl.ds(CH, held.shape[0]), :] for a in w]
    with_chunk(layout, info, fetch_pieces(layout, [lower], [held], sems, 1), work)


def out_hidden(layout, info, hidden, w, deps=()):
    seqs, rows, units = hidden.shape
    return call(
        functools.partial(out_hidden_body, layout),
        "out_hidden",
        N_DP,
        info,
        (hidden, *w),
        [once(seqs, rows, units)] + [ANYWHERE] * len(w),
        shaped((N_DP, seqs, rows, CH)),
        spec((1, seqs, rows, CH), lambda j, *_: (j, 0, 0, 0)),
        2 * seqs * rows * D * units,
        [pltpu.VMEM((units, D), bf16), pltpu.SemaphoreType.DMA((len(w),))],
        deps=deps,
    )


def out_heads_body(layout, info, a0, a1, part, *refs):
    count = len(layout)
    w, outs = refs[:count], refs[count : count + N_TP]
    held, y, sems, out_sems = refs[count + N_TP :]
    j = pl.program_id(0)

    def work(place, window):
        for s, att in ((0, a0), (1, a1)):
            total = dot_nn(att[...], held[:, place]) + part[0, s, :, window].astype(f32)
            y[j, s, :, window] = total.astype(bf16)

    upper = [a.at[pl.ds(0, CH), :] for a in w]
    with_chunk(layout, info, fetch_pieces(layout, [upper], [held], sems, 1), work)
    for r in range(N_TP):

        @pl.when(chunk_now(info) == r)
        def _(r=r):
            pltpu.make_async_copy(y.at[j], outs[r], out_sems.at[r]).start()

    @pl.when(j == N_TP - 1)
    def _():
        for r in range(N_TP):
            pltpu.make_async_copy(y.at[r], outs[r], out_sems.at[r]).wait()


def out_heads(layout, info, att, parts, w, deps=()):
    _, seqs, rows, _ = parts.shape
    return call(
        functools.partial(out_heads_body, layout),
        "out_heads",
        N_TP,
        info,
        (*att, parts, *w),
        [once(rows, CH)] * 2
        + [spec((1, seqs, rows, CH), lambda j, *_: (j, 0, 0, 0))]
        + [ANYWHERE] * len(w),
        (shaped((seqs, rows, CH)),) * N_TP,
        [ANYWHERE] * N_TP,
        2 * seqs * rows * D * CH,
        [
            pltpu.VMEM((CH, D), bf16),
            pltpu.VMEM((N_TP, seqs, rows, CH), bf16),
            pltpu.SemaphoreType.DMA((len(w),)),
            pltpu.SemaphoreType.DMA((N_TP,)),
        ],
        deps=deps,
    )


def back_in_body(layout, info, x0, xa, xc, xb, dq, dkv, back, dup, gain, stats, *refs):
    count = len(layout)
    wq, wu = refs[:count], refs[count : 2 * count]
    *chunks, held_q, held_u, y, xs, row_sums, column_sums, both, sems = refs[2 * count :]
    j = pl.program_id(0)
    rows = dq.shape[0]

    @pl.when(j == 0)
    def _():
        both[...] = add_rounded(dkv[...], back[...])


    def work(place, window):
        part = dot_nt(dup[...], held_u[place, :])
        part = part + dot_nt(dq[...], held_q[place, :CH])
        part = part + dot_nt(both[0], held_q[place, CH : 2 * CH])
        y[:, window] = part + dot_nt(both[1], held_q[place, 2 * CH :])

    copies = fetch_pieces(layout, [wq, wu], [held_q, held_u], sems, 0)
    with_chunk(layout, info, copies, work)
    for r, part in enumerate((x0, xc, xb, xa)):

        @pl.when(chunk_now(info) == r)
        def _(r=r, part=part):
            chunks[r][:rows, :] = y[...].astype(bf16)
            xs[...] = part[...]

    total = y[...]
    turned = stats[...].T
    standard = (xs[...].astype(f32) - turned[:, 0:1]) * turned[:, 1:2]
    cross = total * standard
    weight = gain[...].astype(f32)

    @pl.when(j == 0)
    def _():
        row_sums[...] = jnp.zeros(row_sums.shape, f32)
        column_sums[...] = jnp.zeros(column_sums.shape, f32)

    both = jnp.concatenate(
        [jnp.sum(cross, axis=0, keepdims=True), jnp.sum(total, axis=0, keepdims=True)], axis=0
    )
    column_sums[chunk_now(info), 0:2, :] = both
    row_sums[:, 0:1] += jnp.sum(total * weight, axis=1, keepdims=True)
    row_sums[:, 1:2] += jnp.sum(cross * weight, axis=1, keepdims=True)

    @pl.when(j == N_TP - 1)
    def _():
        turned = row_sums[...].T[: TAIL // 2]
        for r, chunk in enumerate(chunks):
            chunk[rows:, :] = jnp.concatenate([turned, column_sums[r]], axis=0).astype(bf16)


def back_in(layout, info, s, parts, dq, dkv, back, dup, wq, wu, gain, stats, deps=()):
    _, rows, units = dup.shape
    return call(
        functools.partial(back_in_body, layout),
        "back_in",
        N_TP,
        info,
        (*parts, dq, dkv, back, dup, gain, stats, *wq, *wu),
        [one_of(s, rows, CH)] * 4
        + [
            whole(rows, CH),
            whole(2, rows, CH),
            whole(2, rows, CH),
            one_of(s, rows, units),
            spec((1, CH), lambda j, info: (0, info[2] ^ j)),
            one_of(s, 8, rows),
        ]
        + [ANYWHERE] * (2 * len(wq)),
        (shaped((rows + TAIL, CH)),) * N_TP,
        [whole(rows + TAIL, CH)] * N_TP,
        2 * rows * D * (3 * CH + units),
        [
            pltpu.VMEM((D, 3 * CH), bf16),
            pltpu.VMEM((D, units), bf16),
            pltpu.VMEM((rows, CH), f32),
            pltpu.VMEM((rows, CH), bf16),
            pltpu.VMEM((rows, 128), f32),
            pltpu.VMEM((N_TP, TAIL // 2, CH), f32),
            pltpu.VMEM((2, rows, CH), bf16),
            pltpu.SemaphoreType.DMA((2 * len(wq),)),
        ],
        deps=deps,
    )


KEPT = ((0, 0), (2, 1))
GIVEN = ((1, 0), (3, 1))


def grad_up_body(info, normed, dup, kept, given, sums):
    d = info[2]
    rights = (dup[0], dup[1])
    store_by_rows(d, normed, rights, kept, given)
    sums[...] = sum(jnp.sum(b.astype(f32), axis=0, keepdims=True) for b in rights)


def grad_up(info, normed, dup, deps=()):
    _, rows, units = dup.shape
    count = units // CH
    message = spec((2, 1, CH, CH), lambda j, *_: (0, j, 0, 0))
    return call(
        grad_up_body,
        "grad_up",
        count,
        info,
        (normed, dup),
        [whole(2, rows, D), spec((2, rows, CH), lambda j, *_: (0, 0, j))],
        (shaped((2, count, CH, CH)),) * 2 + (shaped((1, units), f32),),
        [message, message, spec((1, CH), lambda j, *_: (0, j))],
        4 * rows * D * units,
        deps=deps,
    )


def grad_down_body(offsets, info, hidden, *refs):
    parts = refs[: len(offsets)]
    kept, given, tiles, sems = refs[-4:]
    n = pl.program_id(0)
    for i, (part, offset) in enumerate(zip(parts, offsets)):
        tiles[n, i] = (dot_tn(hidden[0], part[0]) + dot_tn(hidden[1], part[1])).astype(bf16)
        r = ((info[0] + offset) % N_TP) ^ info[2]
        for odd, target in ((0, kept), (1, given)):

            @pl.when(r % 2 == odd)
            def _(i=i, r=r, target=target):
                place = target.at[r // 2, n]
                pltpu.make_async_copy(tiles.at[n, i], place, sems.at[n, i]).start()

    @pl.when(n == tiles.shape[0] - 1)
    def _():
        for m in range(tiles.shape[0]):
            for i in range(len(offsets)):
                pltpu.make_async_copy(tiles.at[m, i], kept.at[0, 0], sems.at[m, i]).wait()


def grad_down(info, hidden, parts, offsets, begun=(), deps=()):
    _, rows, units = hidden.shape
    count = units // CH
    at = 1 + len(parts)
    return call(
        functools.partial(grad_down_body, offsets),
        "grad_down",
        count,
        info,
        (hidden, *parts, *begun),
        [spec((2, rows, CH), lambda j, *_: (0, 0, j))]
        + [once(2, rows, CH)] * len(parts)
        + [ANYWHERE] * len(begun),
        (shaped((2, count, CH, CH)),) * 2,
        [ANYWHERE] * 2,
        4 * rows * CH * units * len(parts),
        [
            pltpu.VMEM((count, len(parts), CH, CH), bf16),
            pltpu.SemaphoreType.DMA((count, len(parts))),
        ],
        deps=deps,
        aliases=[(at + n, n) for n in range(len(begun))],
    )


def store_by_rows(d, lefts, rights, kept, given):
    for target, which in ((given, GIVEN), (kept, KEPT)):
        for r, at in which:
            window = columns(d ^ r)
            y = sum(dot_tn(lefts[s, :, window], b) for s, b in enumerate(rights))
            target[at, 0] = y.astype(bf16)


def grad_out_query_body(info, normed, ct, a0, a1, q0, q1, kept, given, sums):
    j = pl.program_id(0)
    d = info[2]

    @pl.when(j == 0)
    def _():
        lefts = (a0[...], a1[...])
        for target, which in ((given, GIVEN), (kept, KEPT)):
            for r, at in which:
                window = columns(d ^ r)
                y = sum(dot_tn(a, ct[s, :, window]) for s, a in enumerate(lefts))
                target[at, 0] = y.astype(bf16)

    @pl.when(j == 1)
    def _():
        rights = (q0[...], q1[...])
        store_by_rows(d, normed, rights, kept, given)
        sums[...] = sum(jnp.sum(b.astype(f32), axis=0, keepdims=True) for b in rights)


def grad_out_query(info, normed, ct, att, dq, deps=()):
    rows = normed.shape[1]
    message = spec((2, 1, CH, CH), lambda j, *_: (0, j, 0, 0))
    return call(
        grad_out_query_body,
        "grad_out_query",
        2,
        info,
        (normed, ct, *att, *dq),
        [whole(2, rows, D)] * 2 + [whole(rows, CH)] * 4,
        (shaped((2, 2, CH, CH)),) * 2 + (shaped((1, CH), f32),),
        [message, message, whole(1, CH)],
        4 * rows * D * 2 * CH,
        deps=deps,
    )


def grad_key_value_body(info, normed, kv0, back0, kv1, back1, kept, given, sums):
    rights = (add_rounded(kv0[0], back0[0]), add_rounded(kv1[0], back1[0]))
    store_by_rows(info[2], normed, rights, kept, given)
    sums[0] = sum(jnp.sum(b.astype(f32), axis=0, keepdims=True) for b in rights)


def grad_key_value(info, normed, dkv, sent, deps=()):
    rows = normed.shape[1]
    message = spec((2, 1, CH, CH), lambda j, *_: (0, j, 0, 0))
    pair = spec((1, rows, CH), lambda j, *_: (j, 0, 0))
    return call(
        grad_key_value_body,
        "grad_key_value",
        2,
        info,
        (normed, dkv[0], sent[0], dkv[1], sent[1]),
        [whole(2, rows, D)] + [pair] * 4,
        (shaped((2, 2, CH, CH)),) * 2 + (shaped((2, 1, CH), f32),),
        [message, message, spec((1, 1, CH), lambda j, *_: (j, 0, 0))],
        4 * rows * D * 2 * CH,
        deps=deps,
    )


def combine_body(counts, info, *refs):
    ins, outs = refs[: sum(counts)], refs[sum(counts) :]
    at = 0
    for count, out in zip(counts, outs):
        terms = ins[at : at + count]
        at += count

        def add(terms=terms, out=out):
            out[...] = sum(a[...].astype(f32) for a in terms).astype(bf16)

        if len(out.shape) == 3:
            add()
        else:
            pl.when(pl.program_id(0) == 0)(add)


def combine(info, big, small, deps=()):
    steps = 2
    part = 2 * CH // steps
    ins, in_specs, outs, out_specs = [], [], [], []
    for job in big:
        for array, row in job:
            ins.append(array.reshape(-1, part, CH))
            in_specs.append(spec((1, part, CH), lambda j, _, at=row // part: (at + j, 0, 0)))
        outs.append(shaped((steps, part, CH)))
        out_specs.append(spec((1, part, CH), lambda j, _: (j, 0, 0)))
    for job in small:
        ins += job
        in_specs += [whole(*a.shape) for a in job]
        outs.append(shaped(job[0].shape))
        out_specs.append(whole(*job[0].shape))
    results = call(
        functools.partial(combine_body, [len(job) for job in (*big, *small)]),
        "combine",
        steps,
        info,
        ins,
        in_specs,
        outs,
        out_specs,
        0,
        deps=deps,
    )
    count = len(big)
    return [a.reshape(2, CH, CH) for a in results[:count]] + list(results[count:])


def finish_blocks_body(info, *refs):
    *sums, out = refs
    j = pl.program_id(0)
    for n in range(len(sums) // 2):
        here, there = sums[2 * n : 2 * n + 2]

        @pl.when((j >= 2 * n) & (j < 2 * n + 2))
        def _(here=here, there=there):
            out[...] = here[0].astype(f32) + there[0].astype(f32)


def finish_blocks(info, sums, axis, deps=()):
    count = len(sums)
    arrays = [a for pair in sums for a in pair]
    blocks = [
        spec((1, CH, CH), lambda j, _, n=n: (jnp.clip(j - 2 * n, 0, 1), 0, 0))
        for n in range(count)
        for _ in range(2)
    ]
    return call(
        finish_blocks_body,
        "finish_blocks",
        2 * count,
        info,
        arrays,
        blocks,
        shaped((2 * count * CH, CH) if axis == 0 else (CH, 2 * count * CH), f32),
        spec((CH, CH), lambda j, _: (j, 0) if axis == 0 else (0, j)),
        0,
        deps=deps,
    )


def finish_pair_body(info, here, there, *outs):
    for n, out in enumerate(outs):
        out[...] = here[n].astype(f32) + there[n].astype(f32)


def finish_pair(info, here, there, deps=()):
    part = CH // 2
    return call(
        finish_pair_body,
        "finish_pair",
        2,
        info,
        (here, there),
        [spec((2, part, CH), lambda j, _: (0, j, 0))] * 2,
        (shaped((CH, CH), f32),) * 2,
        [spec((part, CH), lambda j, _: (j, 0))] * 2,
        0,
        deps=deps,
    )


def finish_last_body(info, own, back, near, x, shift, here, there, out, first, second):
    total = own[...].astype(f32) + back[...].astype(f32) + near[...].astype(f32)
    out[...] = (x[...].astype(f32) + total + shift[...].astype(f32)).astype(bf16)
    finish_pair_body(info, here, there, first, second)


def finish_last(info, shares, x, shift, here, there, deps=()):
    seqs, rows, _ = x.shape
    both = spec((seqs, rows // 2, CH), lambda j, _: (0, j, 0))
    pair = spec((2, CH // 2, CH), lambda j, _: (0, j, 0))
    half = spec((CH // 2, CH), lambda j, _: (j, 0))
    return call(
        finish_last_body,
        "finish_last",
        2,
        info,
        (*shares, x, shift, here, there),
        [both] * 4 + [whole(1, CH), pair, pair],
        (shaped(x.shape), shaped((CH, CH), f32), shaped((CH, CH), f32)),
        [both, half, half],
        0,
        deps=deps,
    )


def finish_in_body(info, *refs):
    shares, tails, wide = refs[:6], refs[6:12], refs[12:18]
    x, ct, stats, gain, out, sums = refs[18:]
    weight = gain[...].astype(f32)
    for s in range(2):
        at = slice(3 * s, 3 * s + 3)
        total = sum(a[...].astype(f32) for a in shares[at])
        tail = sum(a[...].astype(f32) for a in tails[at])
        column = jnp.concatenate([tail[:8], stats[s]], axis=0).T
        plain, cross = column[:, 0:1], column[:, 1:2]
        average, root = column[:, 8:9], column[:, 9:10]
        standard = (x[s].astype(f32) - average) * root
        scaled = total * weight - plain * (1.0 / D) - standard * (cross * (1.0 / D))
        out[s] = ct[s].astype(f32) + root * scaled

    @pl.when(pl.program_id(0) == 0)
    def _():
        sums[...] = sum(a[...].astype(f32)[8:] for a in wide)


def finish_in(info, shares, x, ct, stats, gain, deps=()):
    seqs, rows, _ = x.shape
    part = rows // 2
    both = spec((seqs, part, CH), lambda j, _: (0, j, 0))
    last = rows // TAIL
    return call(
        finish_in_body,
        "finish_in",
        2,
        info,
        (*shares, *shares, *shares, x, ct, stats, gain),
        [spec((part, CH), lambda j, _: (j, 0))] * 6
        + [spec((TAIL, part), lambda j, _: (last, j))] * 6
        + [spec((TAIL, CH), lambda j, _: (last, 0))] * 6
        + [both, both, spec((seqs, 8, part), lambda j, _: (0, 0, j)), whole(1, CH)],
        (shaped(x.shape, f32), shaped((TAIL // 2, CH), f32)),
        [both, whole(TAIL // 2, CH)],
        0,
        deps=deps,
    )


SMALL = 16


def small_table_body(info, query, pair, up, out, last, table):
    table[...] = jnp.zeros(table.shape, f32)
    table[0:1, :] = query[...]
    table[1:2, :] = pair[0]
    table[2:3, :] = pair[1]
    for n in range(4):
        table[3 + n : 4 + n, :] = up[:, CH * n : CH * (n + 1)]
    table[7:8, :] = out[...]
    table[8:10, :] = last[0:2, :]


def small_table(info, arrays):
    return call(
        small_table_body,
        "small_table",
        1,
        info,
        arrays,
        [whole(*a.shape) for a in arrays],
        shaped((SMALL, CH), f32),
        whole(SMALL, CH),
        0,
    )


def ring(array, step):
    return lax.ppermute(array, "tp", [(i, (i + step) % N_TP) for i in range(N_TP)])


class Gather:
    def __init__(self, own):
        self.own = own

    def forth(self, clock):
        self.own = clock.go(self.own)
        self.behind = ring(self.own, 1)

    def back(self):
        self.ahead = ring(self.own, -1)

    def sides(self, clock):
        self.forth(clock)
        self.ahead = ring(self.own, -1)

    def onward(self, clock):
        self.behind = clock.go(self.behind)
        self.far = ring(self.behind, 1)
        self.parts = (self.own, self.behind, self.ahead, self.far)


class Scatter:
    def __init__(self, chunks):
        self.own, self.share, self.first, self.given = chunks

    def forward(self, clock):
        self.far = ring(clock.go(self.first), 1)

    def backward(self, clock):
        self.back = ring(clock.go(self.given), -1)

    def both(self):
        return [self.share, self.far]

    def onward(self, both):
        self.near = ring(both, 1)

    def shares(self):
        return self.own, self.back, self.near


class Reduction:
    def __init__(self, kept, given, clock, two):
        self.kept, self.two = kept, two
        self.got = swap(clock.go(given), "dp", 1, N_DP)
        self.moved, self.here, self.there = {}, {}, {}

    def across(self, n):
        row = (self.kept.shape[1] + 2 * n) * CH
        return [(self.kept, row), (self.got, row)]

    def here_sum(self, n):
        row = 2 * n * CH
        return [(self.kept, row), (self.got, row), (self.moved[n], 0)]

    def over_x(self, n, across):
        self.moved[n] = swap(across, "dp", 2, N_DP)

    def over_y(self, n, here):
        self.here[n] = here
        self.there[n] = swap(here, "ctx", 1, 2) if self.two else lax.psum(here, "ctx")

    def sums(self, n):
        if self.two:
            return self.here[n], self.there[n]
        return self.there[n], jnp.zeros_like(self.there[n])


def body(
    block_in,
    doc_starts,
    query_weight,
    key_weight,
    value_weight,
    output_weight,
    up_weight,
    down_weight,
    query_bias,
    key_bias,
    value_bias,
    up_bias,
    output_bias,
    norm_gain,
    norm_shift,
    cotangent,
):
    seqs, rows, _ = block_in.shape
    d, c, t = lax.axis_index("dp"), lax.axis_index("ctx"), lax.axis_index("tp")
    n_ctx = lax.axis_size("ctx")
    two = n_ctx == 2
    info = jnp.stack([t, c, d]).astype(jnp.int32)

    clock = Clock()

    x = Gather(block_in)
    x.forth(clock)
    small = jnp.concatenate(
        [query_bias, key_bias, value_bias, up_bias, output_bias, norm_gain, norm_shift]
    )
    size = small.size
    near = swap(small, "dp", 1, N_DP)
    flip = (d & 1) == 1
    pair = jnp.concatenate([jnp.where(flip, near, small), jnp.where(flip, small, near)])
    across = swap(pair, "dp", 2, N_DP)
    flip = (d & 2) == 2
    small_here = jnp.concatenate([jnp.where(flip, across, pair), jnp.where(flip, pair, across)])
    small_here = small_here.reshape(N_DP, size)

    def small_of(first, length):
        return small_here[:, first : first + length].reshape(1, -1)

    share = query_bias.size
    share_units = up_bias.size
    qkv_bias = jnp.concatenate([small_of(n * share, share) for n in range(3)], axis=1)
    up_shift = small_of(3 * share, share_units)
    output_shift = small_of(3 * share + share_units, share)
    gain_here = small_of(4 * share + share_units, share)
    shift_here = small_of(5 * share + share_units, share)
    both = jnp.concatenate([gain_here, shift_here], axis=0)
    others = [ring(both, -r) for r in range(1, N_TP)]
    wq_shard = jnp.concatenate([query_weight, key_weight, value_weight], axis=1)
    shards_q = Shards(tie(wq_shard, across), 0, d, c, two)
    shards_q.over_x(clock)
    shards_u = Shards(up_weight, 0, d, c, two, made=False)
    wo_shard = jnp.concatenate([output_weight, down_weight], axis=0)
    shards_o = Shards(wo_shard, 1, d, c, two)
    clock.sync(x.behind, shards_q.first, *others, shards_u.part)

    x.back()
    shards_q.over_y(clock)
    shards_u.over_x(clock)
    shards_q.near_core(clock)
    circle = jnp.concatenate([both, *others] * 2, axis=1)
    gain_shift = lax.dynamic_slice_in_dim(circle, (N_TP - t) % N_TP * CH, D, 1)
    gain, shift = gain_shift[0:1], gain_shift[1:2]

    here = c * rows + jnp.arange(rows, dtype=jnp.int32)
    tables, opening = rotary_tables(doc_starts, here)
    blocks = 1 if two else n_ctx
    before, _ = rotary_tables(doc_starts, jnp.arange(blocks * rows, dtype=jnp.int32))
    before = [a.reshape(seqs, blocks, rows, 128) for a in before]

    clock.sync(shards_q.second, shards_u.first, x.ahead, shards_q.near, shards_o.part)
    shards_u.near_core(clock)

    x.onward(clock)
    shards_u.over_y(clock)
    shards_o.over_x(clock)
    shards_q.far_core(clock)
    clock.sync(
        x.far,
        *shards_q.far_near,
        shards_u.second,
        shards_o.first,
        *before,
    )

    def send_keys(s):
        kv[s] = clock.go(kv[s])
        if two:
            kvp[s] = swap(kv[s], "ctx", 1, 2)[None]
        else:
            kvp[s] = lax.all_gather(kv[s], "ctx", axis=0, tiled=False)

    def attention_step(s):
        return attention(
            info,
            s,
            opening[:, None],
            q,
            kv[s],
            kvp[s],
            datt,
            tables,
            before,
            deps=clock.marks,
        )

    def returned(sent):
        if two:
            return swap(clock.go(sent[0]), "ctx", 1, 2)
        return lax.psum_scatter(clock.go(sent), "ctx", scatter_dimension=0, tiled=False)

    def back_in_step(s):
        return back_in(
            layout,
            info,
            s,
            x.parts,
            dq[s],
            dkv[s],
            sent[s],
            dup,
            shards_q.pieces,
            shards_u.pieces,
            gain,
            stats,
            deps=clock.marks,
        )

    layout = layout_of(two)
    kvp, att, dq, dkv, sent = ([None] * seqs for _ in range(5))

    shards_o.over_y(clock)
    shards_u.far_core(clock)
    ct = Gather(cotangent)
    ct.behind, ct.ahead = ring(ct.own, 1), ring(ct.own, -1)
    normed, stats, q, *kv = norm_qkv(
        layout, info, x.parts, gain, shift, shards_q.pieces, qkv_bias, tables, deps=clock.marks
    )
    clock.sync(normed, *shards_u.far_near, shards_u.near, ct.behind, shards_o.second)

    shards_o.near_core(clock)
    shards_o.far_core(clock)
    ct.onward(clock)
    hidden, slope = mlp_up(layout, info, normed, shards_u.pieces, up_shift, deps=clock.marks)
    clock.sync(hidden, shards_o.near, *shards_o.far_near)

    send_keys(0)
    send_keys(1)
    out_parts = out_hidden(layout, info, hidden, shards_o.pieces, deps=clock.marks)
    clock.sync(out_parts, ct.ahead)
    down_begun = grad_down(
        info, hidden, (ct.own, ct.behind, ct.ahead), (0, 3, 1), deps=clock.marks
    )
    clock.sync(down_begun[0], ct.far)

    cf, out_bias_sum, datt, dup = back_out(
        layout, info, ct.parts, shards_o.pieces, slope, deps=clock.marks
    )
    clock.sync(datt, kvp[0])

    def added(big, small=()):
        return combine(info, big, list(small), deps=clock.marks)

    up_kept, up_given, up_sum = grad_up(info, normed, dup, deps=clock.marks)
    clock.sync(up_kept, kvp[1])
    up = Reduction(up_kept, up_given, clock, two)
    att[0], dq[0], dkv[0], sent[0] = attention_step(0)
    clock.sync(att[0], up.got)

    sent[0] = returned(sent[0])
    across, across_1 = added([up.across(0), up.across(1)])
    up.over_x(0, across)
    clock.sync(across)
    down_kept, down_given = grad_down(
        info, hidden, (ct.far,), (2,), down_begun, deps=clock.marks
    )
    clock.sync(down_kept, *clock.marks)
    att[1], dq[1], dkv[1], sent[1] = attention_step(1)
    clock.sync(att[1], sent[0], up.moved[0])

    sent[1] = returned(sent[1])
    up.over_x(1, clock.go(across_1))
    down = Reduction(down_kept, down_given, clock, two)
    out = Scatter(out_heads(layout, info, att, out_parts, shards_o.pieces, deps=clock.marks))
    clock.sync(out.own, *clock.marks)
    head_kept, head_given, query_sum = grad_out_query(
        info, normed, cf, att, dq, deps=clock.marks
    )
    clock.sync(head_kept, down.got)
    across, across_1, here = added([down.across(0), down.across(1), up.here_sum(0)])
    clock.sync(across, sent[1])

    up.over_y(0, clock.go(here))
    out.forward(clock)
    clock.sync(up.moved[1])
    down.over_x(0, clock.go(across))
    head = Reduction(head_kept, head_given, clock, two)
    (here,) = added([up.here_sum(1)])
    clock.sync(here)
    back_0 = Scatter(back_in_step(0))
    clock.sync(back_0.own)
    clock.sync(up.there[0])

    up.over_y(1, clock.go(here))
    clock.sync(out.far)
    back_0.forward(clock)
    back_0.backward(clock)
    clock.sync(down.moved[0], head.got)
    down.over_x(1, clock.go(across_1))
    here, across, out_both = added([down.here_sum(0), head.across(0)], [out.both()])
    clock.sync(here)
    pair_kept, pair_given, pair_sum = grad_key_value(info, normed, dkv, sent, deps=clock.marks)
    clock.sync(pair_kept)
    clock.sync(up.there[1])

    down.over_y(0, clock.go(here))
    clock.sync(back_0.far, back_0.back)
    out.backward(clock)
    clock.sync(down.moved[1])
    head.over_x(0, clock.go(across))
    pair = Reduction(pair_kept, pair_given, clock, two)
    here, both_0 = added([down.here_sum(1)], [back_0.both()])
    clock.sync(here)
    back_1 = Scatter(back_in_step(1))
    clock.sync(back_1.own)
    clock.sync(down.there[0])

    down.over_y(1, clock.go(here))
    clock.sync(out.back)
    back_1.forward(clock)
    back_1.backward(clock)
    clock.sync(head.moved[0], pair.got)
    (across,) = added([pair.across(0)])
    pair.over_x(0, across)
    clock.sync(across)
    (here,) = added([head.here_sum(0)])
    clock.sync(here)
    up_wg = finish_blocks(info, [up.sums(0), up.sums(1)], 1, deps=clock.marks)
    clock.sync(up_wg)
    clock.sync(down.there[1])

    head.over_y(0, clock.go(here))
    back_0.onward(clock.go(both_0))
    clock.sync(back_1.far, back_1.back)
    (both_1,) = added([], [back_1.both()])
    back_1.onward(both_1)
    clock.sync(pair.moved[0])
    (here,) = added([pair.here_sum(0)])
    clock.sync(here, back_0.near)
    down_wg = finish_blocks(info, [down.sums(0), down.sums(1)], 0, deps=clock.marks)
    clock.sync(down_wg)
    clock.sync(head.there[0])

    pair.over_y(0, clock.go(here))
    clock.sync(back_1.near)
    out.onward(clock.go(out_both))
    in_grad, last = finish_in(
        info,
        (*back_0.shares(), *back_1.shares()),
        block_in,
        cotangent,
        stats,
        gain_here,
        deps=clock.marks,
    )
    clock.sync(in_grad)
    table = small_table(info, (query_sum, pair_sum, up_sum, out_bias_sum, last))
    output_wg, query_wg = finish_pair(info, *head.sums(0), deps=clock.marks)
    table = table + swap(table, "dp", 1, N_DP)
    table = table + swap(table, "dp", 2, N_DP)
    table = table + swap(table, "ctx", 1, 2) if two else lax.psum(table, "ctx")
    block_out, key_wg, value_wg = finish_last(
        info, out.shares(), block_in, output_shift, *pair.sums(0)
    )

    share = CH // N_DP
    mine = lax.dynamic_slice_in_dim(table, d * share, share, 1)
    query_bg, key_bg, value_bg = mine[0], mine[1], mine[2]
    output_bg, gain_g, shift_g = mine[7], mine[8], mine[9]
    up_bg = lax.dynamic_slice_in_dim(table, 3 + d, 1, 0).reshape(-1)
    return (
        block_out,
        in_grad,
        query_wg,
        key_wg,
        value_wg,
        output_wg,
        up_wg,
        down_wg,
        query_bg,
        key_bg,
        value_bg,
        up_bg,
        output_bg,
        gain_g,
        shift_g,
    )


def solution(mesh):
    return jax.shard_map(
        body,
        mesh=mesh,
        in_specs=(
            P("dp", "ctx", "tp"),
            P("dp", None),
            P("dp", "tp"),
            P("dp", "tp"),
            P("dp", "tp"),
            P("tp", "dp"),
            P("dp", "tp"),
            P("tp", "dp"),
        )
        + (P(("tp", "dp")),) * 7
        + (P("dp", "ctx", "tp"),),
        out_specs=(
            P("dp", "ctx", "tp"),
            P("dp", "ctx", "tp"),
            P("dp", "tp"),
            P("dp", "tp"),
            P("dp", "tp"),
            P("tp", "dp"),
            P("dp", "tp"),
            P("tp", "dp"),
        )
        + (P(("tp", "dp")),) * 7,
        check_vma=False,
    )
```

```python
import functools
import math

import jax
import jax.numpy as jnp
from jax import lax
from jax.experimental import pallas as pl
from jax.experimental.pallas import tpu as pltpu
from jax.sharding import PartitionSpec as P

HEAD_DIM = 64
ROT = 32
D = 2048
N_DP = 4
N_TP = 4
CH = D // N_TP
EPS = 1e-05
NEG = -1e30
VMEM = 127 * 2**19
COST = 0.02

bf16 = jnp.bfloat16
f32 = jnp.float32


def dot_nn(a, b):
    return lax.dot_general(a, b, (((1,), (0,)), ((), ())), preferred_element_type=f32)


def dot_nt(a, b):
    return lax.dot_general(a, b, (((1,), (1,)), ((), ())), preferred_element_type=f32)


def dot_tn(a, b):
    return lax.dot_general(a, b, (((0,), (0,)), ((), ())), preferred_element_type=f32)


def spec(block, index):
    return pl.BlockSpec(block, index)


def whole(*block):
    zeros = (0,) * len(block)
    return pl.BlockSpec(block, lambda g, *_: zeros)


def once(*block):
    zeros = (0,) * len(block)
    return pl.BlockSpec(block, lambda g, *_: zeros, pipeline_mode=pl.Buffered(1))


def one_of(s, *block):
    zeros = (0,) * len(block)
    return pl.BlockSpec((None, *block), lambda g, *_: (s, *zeros))


def shaped(shape, dtype=bf16):
    return jax.ShapeDtypeStruct(tuple(shape), dtype)


ANYWHERE = pl.BlockSpec(memory_space=pl.ANY)


def call(
    body, name, grid, info, ins, in_specs, outs, out_specs, flops, scratch=(), deps=(), aliases=()
):
    moved = sum(math.prod(a.shape) * a.dtype.itemsize for a in (*ins, *jax.tree.leaves(outs)))
    first, last = 1 + len(ins), 1 + len(ins) + len(deps)

    def without_deps(*refs):
        body(*refs[:first], *refs[last:])

    return pl.pallas_call(
        without_deps,
        grid_spec=pltpu.PrefetchScalarGridSpec(
            num_scalar_prefetch=1,
            grid=(grid,),
            in_specs=[*in_specs, *[ANYWHERE] * len(deps)],
            out_specs=out_specs,
            scratch_shapes=list(scratch),
        ),
        out_shape=outs,
        input_output_aliases={1 + n: m for n, m in aliases},
        compiler_params=pltpu.CompilerParams(vmem_limit_bytes=VMEM),
        cost_estimate=pl.CostEstimate(
            flops=int(flops * COST), bytes_accessed=int(moved * COST), transcendentals=0
        ),
        name=name,
    )(info, *ins, *deps)


def tie(value, *deps):
    def nothing(*refs):
        del refs

    return pl.pallas_call(
        nothing,
        in_specs=[ANYWHERE] * (1 + len(deps)),
        out_specs=ANYWHERE,
        out_shape=shaped(value.shape, value.dtype),
        input_output_aliases={0: 0},
        compiler_params=pltpu.CompilerParams(vmem_limit_bytes=VMEM),
        cost_estimate=pl.CostEstimate(flops=0, bytes_accessed=0, transcendentals=0),
        name="tie",
    )(value, *deps)


def columns(index, width=CH):
    return pl.ds(pl.multiple_of(index * width, width), width)


def layout_of(two):
    if two:
        halves = [("c", CH // 2), ("other", CH // 2)]
    else:
        halves = [("", CH)]
    return [(0, "", CH), (1, "", CH)] + [(r, *half) for r in (2, 3) for half in halves]


def piece_offset(info, half):
    return {"": 0, "c": info[1], "other": 1 - info[1]}[half] * (CH // 2)


def piece_window(info, piece):
    r, half, size = piece
    start = (info[2] ^ r) * CH + piece_offset(info, half)
    return pl.ds(pl.multiple_of(start, size), size)


class Clock:
    def __init__(self):
        self.marks = ()

    def go(self, value):
        return tie(value, *self.marks) if self.marks else value

    def sync(self, *arrays):
        def nothing(*refs):
            del refs

        self.marks = (
            pl.pallas_call(
                nothing,
                in_specs=[ANYWHERE] * (len(arrays) + len(self.marks)),
                out_specs=ANYWHERE,
                out_shape=shaped((8, 128), f32),
                compiler_params=pltpu.CompilerParams(vmem_limit_bytes=VMEM),
                cost_estimate=pl.CostEstimate(flops=0, bytes_accessed=0, transcendentals=0),
                name="sync",
            )(*arrays, *self.marks),
        )


def swap(array, axis, bit, size):
    return lax.ppermute(array, axis, [(i, i ^ bit) for i in range(size)])


class Shards:
    def __init__(self, own, axis, d, c, two, made=True):
        self.own, self.two, self.made = own, two, made
        size = own.shape[axis] // 2
        self.part = lax.dynamic_slice_in_dim(own, c * size, size, axis) if two else own

    def near_core(self, clock):
        self.own = clock.go(self.own) if self.made else self.own
        self.near = swap(self.own, "dp", 1, N_DP)

    def over_x(self, clock):
        self.first = swap(clock.go(self.part), "dp", 2, N_DP)

    def over_y(self, clock):
        self.first = clock.go(self.first)
        self.second = swap(self.first, "ctx", 1, 2) if self.two else self.first

    def far_core(self, clock):
        self.first = clock.go(self.first)
        far = [self.first]
        if self.two:
            self.second = clock.go(self.second)
            far.append(self.second)
        self.far_near = [swap(a, "dp", 1, N_DP) for a in far]
        self.pieces = [self.own, self.near, *far, *self.far_near]


def rotary_tables(starts, positions):
    before = starts[:, None, :] <= positions[None, :, None]
    opening = jnp.max(jnp.where(before, starts[:, None, :], 0), axis=2)
    relative = (positions[None, :] - opening).astype(f32)
    half = ROT // 2
    lane = jnp.arange(128, dtype=jnp.int32) % HEAD_DIM
    frequency = jnp.exp((lane % half).astype(f32) * (-math.log(10000.0) / half))
    angles = relative[:, :, None] * jnp.where(lane < ROT, frequency, 0.0)
    sine = jnp.sin(angles)
    return (
        jnp.cos(angles),
        jnp.where(lane < half, -sine, 0.0),
        jnp.where(lane >= half, sine, 0.0),
    ), opening


def add_rounded(a, b):
    return (a.astype(f32) + b.astype(f32)).astype(bf16)


def turn(x, own, up, down):
    return x * own + pltpu.roll(x, 112, 1) * up + pltpu.roll(x, 16, 1) * down


def turn_back(x, own, up, down):
    return x * own - pltpu.roll(x, 112, 1) * up - pltpu.roll(x, 16, 1) * down


def stream_pieces(layout, info, sources, held, sems, axis, blocks):
    j = pl.program_id(0)

    def copies(block):
        cut = pl.ds(pl.multiple_of(block * CH, CH), CH)
        for n, (piece, source) in enumerate(zip(layout, sources)):
            window = piece_window(info, piece)
            if axis == 0:
                pair = source.at[:, cut], held.at[window, cut]
            else:
                pair = source.at[cut, :], held.at[cut, window]
            yield pltpu.make_async_copy(*pair, sems.at[block, n])

    @pl.when(j == 0)
    def _():
        for block in range(blocks):
            for copy in copies(block):
                copy.start()

    for copy in copies(j):
        copy.wait()


def norm_qkv_body(layout, info, x0, xa, xc, xb, gain, shift, bias, own, up, down, *refs):
    *w, normed, stats, q, kv0, kv1, columns_held, held, sems = refs
    j = pl.program_id(0)
    t = info[0]
    seqs, rows, _ = x0.shape
    stream_pieces(layout, info, w, held, sems, 0, 3)

    @pl.when(j == 0)
    def _():
        parts = [(x0, t), (xa, (t + 3) % N_TP), (xc, (t + 1) % N_TP), (xb, (t + 2) % N_TP)]
        tile = 128

        def rows_of(i, carry):
            s = i // (rows // tile)
            window = pl.ds(pl.multiple_of((i % (rows // tile)) * tile, tile), tile)
            x = [part[s, window, :].astype(f32) for part, _ in parts]
            average = sum(jnp.sum(a, axis=1, keepdims=True) for a in x) * (1.0 / D)
            x = [a - average for a in x]
            variance = sum(jnp.sum(a * a, axis=1, keepdims=True) for a in x) * (1.0 / D)
            root = lax.rsqrt(variance + EPS)
            columns_held[s, window, 0:1] = average
            columns_held[s, window, 1:2] = root
            for a, (_, index) in zip(x, parts):
                at = columns(index)
                y = a * root * gain[:, at].astype(f32) + shift[:, at].astype(f32)
                normed[s, window, at] = y.astype(bf16)
            return carry

        columns_held[...] = jnp.zeros(columns_held.shape, f32)
        lax.fori_loop(0, seqs * rows // tile, rows_of, 0)
        for s in range(seqs):
            stats[s] = columns_held[s].T[: stats.shape[1]]

    for s, kv in ((0, kv0), (1, kv1)):
        y = dot_nn(normed[s], held[:, columns(j)]) + bias[...].astype(f32)

        def rotated(s=s, y=y):
            parts = [
                turn(y[:, 128 * n : 128 * n + 128], own[s], up[s], down[s])
                for n in range(CH // 128)
            ]
            return jnp.concatenate(parts, axis=1).astype(bf16)

        @pl.when(j == 0)
        def _(s=s, rotated=rotated):
            q[s] = rotated()

        @pl.when(j == 1)
        def _(kv=kv, rotated=rotated):
            kv[0] = rotated()

        @pl.when(j == 2)
        def _(kv=kv, y=y):
            kv[0] = y.astype(bf16)


def norm_qkv(layout, info, parts, gain, shift, w, bias, tables, deps=()):
    seqs, rows, _ = parts[0].shape
    outs = (
        shaped((seqs, rows, D)),
        shaped((seqs, 8, rows), f32),
        shaped((seqs, rows, CH)),
        shaped((2, rows, CH)),
        shaped((2, rows, CH)),
    )
    pair = spec((1, rows, CH), lambda j, *_: (jnp.maximum(j - 1, 0), 0, 0))
    return call(
        functools.partial(norm_qkv_body, layout),
        "norm_qkv",
        3,
        info,
        (*parts, gain, shift, bias, *tables, *w),
        [whole(seqs, rows, CH)] * 4
        + [whole(1, D)] * 2
        + [spec((1, CH), lambda j, *_: (0, j))]
        + [whole(seqs, rows, 128)] * 3
        + [ANYWHERE] * len(w),
        outs,
        [
            whole(seqs, rows, D),
            whole(seqs, 8, rows),
            whole(seqs, rows, CH),
            pair,
            pair,
        ],
        2 * seqs * rows * D * 3 * CH,
        [
            pltpu.VMEM((seqs, rows, 128), f32),
            pltpu.VMEM((D, 3 * CH), bf16),
            pltpu.SemaphoreType.DMA((3, len(w))),
        ],
        deps=deps,
    )


def mlp_up_body(layout, info, normed, bias, *refs):
    *w, hidden, grad, held, sems = refs
    j = pl.program_id(0)
    stream_pieces(layout, info, w, held, sems, 0, held.shape[1] // CH)
    root = math.sqrt(2.0 / math.pi)
    part = 512
    for s in range(normed.shape[0]):
        for row in range(0, normed.shape[1], part):
            window = slice(row, row + part)
            u = dot_nn(normed[s, window], held[:, columns(j)]) + bias[...].astype(f32)
            square = u * u
            t = jnp.tanh(u * (root + (root * 0.044715) * square))
            half = 0.5 + 0.5 * t
            value = u * half
            hidden[s, window] = value.astype(bf16)
            slope = 2 * root + (6 * 0.044715 * root) * square
            grad[s, window] = (half + value * (1.0 - half) * slope).astype(bf16)


def mlp_up(layout, info, normed, w, bias, deps=()):
    seqs, rows, _ = normed.shape
    units = w[0].shape[1]
    block = spec((seqs, rows, CH), lambda j, *_: (0, 0, j))
    return call(
        functools.partial(mlp_up_body, layout),
        "mlp_up",
        units // CH,
        info,
        (normed, bias, *w),
        [whole(seqs, rows, D), spec((1, CH), lambda j, *_: (0, j))] + [ANYWHERE] * len(w),
        (shaped((seqs, rows, units)),) * 2,
        [block] * 2,
        2 * seqs * rows * D * units,
        [pltpu.VMEM((D, units), bf16), pltpu.SemaphoreType.DMA((units // CH, len(w)))],
        deps=deps,
    )


def back_out_body(layout, info, c0, ca, cc, cb, slope, *refs):
    *w, cf, bias_grad, datt, dup, held, sems, cf_sems = refs
    j = pl.program_id(0)
    t = info[0]
    seqs = c0.shape[0]
    parts = [(c0, t), (ca, (t + 3) % N_TP), (cc, (t + 1) % N_TP), (cb, (t + 2) % N_TP)]
    stream_pieces(layout, info, w, held, sems, 1, held.shape[0] // CH)
    copies = [
        pltpu.make_async_copy(part, cf.at[:, :, columns(index)], cf_sems.at[n])
        for n, (part, index) in enumerate(parts)
    ]

    @pl.when(j == 0)
    def _():
        for copy in copies:
            copy.start()
        bias_grad[...] = sum(
            jnp.sum(c0[s].astype(f32), axis=0, keepdims=True) for s in range(seqs)
        )

    for s in range(seqs):
        y = sum(dot_nt(part[s], held[columns(j), columns(index)]) for part, index in parts)

        @pl.when(j == 0)
        def _(s=s, y=y):
            datt[s] = y.astype(bf16)

        @pl.when(j > 0)
        def _(s=s, y=y):
            dup[s] = (y * slope[s].astype(f32)).astype(bf16)

    @pl.when(j == pl.num_programs(0) - 1)
    def _():
        for copy in copies:
            copy.wait()


def back_out(layout, info, parts, w, slope, deps=()):
    seqs, rows, units = slope.shape
    later = spec((seqs, rows, CH), lambda j, *_: (0, 0, jnp.maximum(j - 1, 0)))
    return call(
        functools.partial(back_out_body, layout),
        "back_out",
        1 + units // CH,
        info,
        (*parts, slope, *w),
        [once(seqs, rows, CH)] * 4 + [later] + [ANYWHERE] * len(w),
        (
            shaped((seqs, rows, D)),
            shaped((1, CH), f32),
            shaped((seqs, rows, CH)),
            shaped((seqs, rows, units)),
        ),
        [ANYWHERE, whole(1, CH), whole(seqs, rows, CH), later],
        2 * seqs * rows * D * (CH + units),
        [
            pltpu.VMEM((CH + units, D), bf16),
            pltpu.SemaphoreType.DMA((1 + units // CH, len(w))),
            pltpu.SemaphoreType.DMA((len(parts),)),
        ],
        deps=deps,
    )


def attention_body(
    blocks, info, low, q, kv, kvp, do, own, up, down, ownp, upp, downp,
    att, dq, dkv, dkvp, scores, probs,
):
    rows = q.shape[0]
    before, start = info[1], info[1] * rows
    lane = lax.broadcasted_iota(jnp.int32, (rows, 128), 1)
    key_row = lax.broadcasted_iota(jnp.int32, (rows, 1), 0)
    query_at = start + lax.broadcasted_iota(jnp.int32, (1, rows), 1)
    first = low[0]
    do_t = do[...].astype(f32).T
    nothing = jnp.zeros((), bf16)
    outputs = []
    for head in range(2):
        mine = (lane < HEAD_DIM) if head == 0 else (lane >= HEAD_DIM)
        half = slice(HEAD_DIM * head, HEAD_DIM * (head + 1))
        qh = jnp.where(mine, q[...] * jnp.asarray(HEAD_DIM**-0.5, bf16), nothing)
        dh = jnp.where(mine, do[...], nothing)

        key_at = start + key_row
        s = dot_nt(kv[0], qh)
        s = jnp.where((key_at >= first) & (key_at <= query_at), s, NEG)
        scores[blocks] = s
        peak = jnp.max(s, axis=0, keepdims=True)

        def score(n, peak):
            s = dot_nt(kvp[n, 0], qh)
            s = jnp.where(n * rows + key_row >= first, s, NEG)
            scores[n] = s
            return jnp.maximum(peak, jnp.max(s, axis=0, keepdims=True))

        peak = lax.fori_loop(0, before, score, peak)

        def expo(n, total):
            e = jnp.exp(scores[n] - peak)
            scores[n] = e
            return total + jnp.sum(e, axis=0, keepdims=True)

        total = expo(blocks, jnp.zeros((1, rows), f32))
        total = lax.fori_loop(0, before, expo, total)
        scale = 1.0 / total

        def weigh(n, values):
            p = (scores[n] * scale).astype(bf16)
            probs[n] = p
            return dot_tn(values, p)

        out_t = weigh(blocks, kv[1])
        out_t = lax.fori_loop(0, before, lambda n, acc: acc + weigh(n, kvp[n, 1]), out_t)
        delta = jnp.sum(out_t[half] * do_t[half], axis=0, keepdims=True)

        def back(n, keys, values):
            dp = dot_nt(values, dh)
            ds = ((scores[n] * scale) * (dp - delta)).astype(bf16)
            return dot_nn(ds, qh), dot_nn(probs[n], dh), dot_tn(keys, ds)

        dk, dv, dq_t = back(blocks, kv[0], kv[1])
        if head == 0:
            dk_sum, dv_sum = dk, dv
        else:
            dk_sum, dv_sum = dk_sum + dk, dv_sum + dv

        def back_before(n, acc):
            dk, dv, more = back(n, kvp[n, 0], kvp[n, 1])
            dk = turn_back(dk, ownp[n], upp[n], downp[n])
            if head == 0:
                dkvp[n, 0] = dk.astype(bf16)
                dkvp[n, 1] = dv.astype(bf16)
            else:
                dkvp[n, 0] = (dkvp[n, 0].astype(f32) + dk).astype(bf16)
                dkvp[n, 1] = (dkvp[n, 1].astype(f32) + dv).astype(bf16)
            return acc + more

        dq_t = lax.fori_loop(0, before, back_before, dq_t)
        outputs.append((out_t[half], dq_t[half]))

    def clear(n, carry):
        dkvp[n] = jnp.zeros(dkvp.shape[1:], bf16)
        return carry

    lax.fori_loop(before, blocks, clear, 0)
    att[...] = jnp.concatenate([outputs[0][0], outputs[1][0]], axis=0).T.astype(bf16)
    grad = jnp.concatenate([outputs[0][1], outputs[1][1]], axis=0).T * HEAD_DIM**-0.5
    dq[...] = turn_back(grad, own[...], up[...], down[...]).astype(bf16)
    dkv[0] = turn_back(dk_sum, own[...], up[...], down[...]).astype(bf16)
    dkv[1] = dv_sum.astype(bf16)


def attention_two_body(
    info, low, q, kv, kvp, do, own, up, down, ownp, upp, downp, att, dq, dkv, dkvp
):
    rows = q.shape[0]
    part = rows // 2
    before, start = info[1], info[1] * rows

    def tail(x, skipped):
        return x[:, skipped:] if skipped else x

    def merge(acc, x, skipped, op):
        if acc is None:
            return x
        if not skipped:
            return op(acc, x)
        return jnp.concatenate([acc[:, :skipped], op(acc[:, skipped:], x)], axis=1)

    def run(with_before):
        lane = lax.broadcasted_iota(jnp.int32, (rows, 128), 1)
        key_row = lax.broadcasted_iota(jnp.int32, (part, 1), 0)
        query_at = start + lax.broadcasted_iota(jnp.int32, (1, rows), 1)
        first = low[...]
        do_t = do[...].astype(f32).T
        nothing = jnp.zeros((), bf16)
        blocks = []
        for n in range(2):
            if with_before:
                blocks.append((kvp.at[0], n * part, 0, False))
        for n in range(2):
            blocks.append((kv, n * part, n * part, True))
        dk_sum, dv_sum = [0.0] * len(blocks), [0.0] * len(blocks)
        heads = []
        for head in range(2):
            mine = (lane < HEAD_DIM) if head == 0 else (lane >= HEAD_DIM)
            qh = jnp.where(mine, q[...] * jnp.asarray(HEAD_DIM**-0.5, bf16), nothing)
            dh = jnp.where(mine, do[...], nothing)
            heads.append((qh, dh, slice(HEAD_DIM * head, HEAD_DIM * (head + 1))))

        def score(head):
            qh = heads[head][0]
            scores, peak = [], None
            for ref, row, skip, here in blocks:
                s = dot_nt(ref[0, row : row + part], qh[skip:])
                key_at = (start if here else start - rows) + row + key_row
                allowed = key_at >= tail(first, skip)
                if here:
                    allowed = allowed & (key_at <= tail(query_at, skip))
                s = jnp.where(allowed, s, NEG)
                scores.append(s)
                peak = merge(peak, jnp.max(s, axis=0, keepdims=True), skip, jnp.maximum)
            return scores, peak

        def grads(head):
            dh = heads[head][1]
            return [
                dot_nt(ref[1, row : row + part], dh[skip:]) for ref, row, skip, _ in blocks
            ]

        def soften(scores, peak):
            terms, total = [], None
            for s, (_, _, skip, _) in zip(scores, blocks):
                e = jnp.exp(s - tail(peak, skip))
                terms.append(e)
                total = merge(total, jnp.sum(e, axis=0, keepdims=True), skip, jnp.add)
            scale = 1.0 / total
            probs = [e * tail(scale, skip) for e, (_, _, skip, _) in zip(terms, blocks)]
            return probs, [p.astype(bf16) for p in probs]

        def weigh(head, rounded):
            out_t = None
            for n, (ref, row, skip, _) in enumerate(blocks):
                out_t = merge(
                    out_t, dot_tn(ref[1, row : row + part], rounded[n]), skip, jnp.add
                )
                dv_sum[n] = dv_sum[n] + dot_nn(rounded[n], heads[head][1][skip:])
            half = heads[head][2]
            return out_t[half], jnp.sum(out_t[half] * do_t[half], axis=0, keepdims=True)

        def differ(probs, dps, delta):
            return [
                (p * (dp - tail(delta, skip))).astype(bf16)
                for p, dp, (_, _, skip, _) in zip(probs, dps, blocks)
            ]

        def back(head, dss):
            dq_t = None
            for n, (ref, row, skip, _) in enumerate(blocks):
                dk_sum[n] = dk_sum[n] + dot_nn(dss[n], heads[head][0][skip:])
                dq_t = merge(dq_t, dot_tn(ref[0, row : row + part], dss[n]), skip, jnp.add)
            return dq_t[heads[head][2]]

        scores_0 = score(0)
        scores_1 = score(1)
        probs_0, rounded_0 = soften(*scores_0)
        out_0, delta_0 = weigh(0, rounded_0)
        dss_0 = differ(probs_0, grads(0), delta_0)
        probs_1, rounded_1 = soften(*scores_1)
        dq_0 = back(0, dss_0)
        out_1, delta_1 = weigh(1, rounded_1)
        dss_1 = differ(probs_1, grads(1), delta_1)
        dq_1 = back(1, dss_1)
        outputs = [(out_0, dq_0), (out_1, dq_1)]

        att[...] = jnp.concatenate([outputs[0][0], outputs[1][0]], axis=0).T.astype(bf16)
        grad = jnp.concatenate([outputs[0][1], outputs[1][1]], axis=0).T * HEAD_DIM**-0.5
        dq[...] = turn_back(grad, own[...], up[...], down[...]).astype(bf16)
        dk = jnp.concatenate(dk_sum[-2:], axis=0)
        dkv[0] = turn_back(dk, own[...], up[...], down[...]).astype(bf16)
        dkv[1] = jnp.concatenate(dv_sum[-2:], axis=0).astype(bf16)
        if with_before:
            dk = jnp.concatenate(dk_sum[:2], axis=0)
            dkvp[0, 0] = turn_back(dk, ownp[0], upp[0], downp[0]).astype(bf16)
            dkvp[0, 1] = jnp.concatenate(dv_sum[:2], axis=0).astype(bf16)
        else:
            dkvp[...] = jnp.zeros(dkvp.shape, bf16)

    @pl.when(before == 0)
    def _():
        run(False)

    @pl.when(before > 0)
    def _():
        run(True)


def attention(info, s, low, q, kv, kvp, do, tables, tables_before, deps=()):
    _, rows, width = q.shape
    blocks = kvp.shape[0]
    token = spec((rows, 128), lambda g, *_: (0, g))
    query = spec((None, rows, 128), lambda g, *_: (s, 0, g))
    pair = spec((2, rows, 128), lambda g, *_: (0, 0, g))
    pairs = spec((blocks, 2, rows, 128), lambda g, *_: (0, 0, 0, g))
    return call(
        attention_two_body if blocks == 1 else functools.partial(attention_body, blocks),
        "attention",
        width // 128,
        info,
        (low, q, kv, kvp, do, *tables, *tables_before),
        [one_of(s, 1, rows), query, pair, pairs, query]
        + [one_of(s, rows, 128)] * 3
        + [one_of(s, blocks, rows, 128)] * 3,
        (
            shaped((rows, width)),
            shaped((rows, width)),
            shaped((2, rows, width)),
            shaped((blocks, 2, rows, width)),
        ),
        [token, token, pair, pairs],
        48 * rows * rows * width,
        []
        if blocks == 1
        else [
            pltpu.VMEM((blocks + 1, rows, rows), f32),
            pltpu.VMEM((blocks + 1, rows, rows), bf16),
        ],
        deps=deps,
    )


TAIL = 16


def fetch_pieces(layout, sources, targets, sems, axis):
    copies = [[] for _ in range(N_DP)]
    at = [r * CH for r in range(N_DP)]
    n = 0
    for group, target in zip(sources, targets):
        at = [r * CH for r in range(N_DP)]
        for (r, _, size), source in zip(layout, group):
            window = pl.ds(at[r], size)
            place = target.at[window, :] if axis == 0 else target.at[:, window]
            copies[r].append(pltpu.make_async_copy(source, place, sems.at[n]))
            at[r] += size
            n += 1
    return copies


def with_chunk(layout, info, copies, work):
    j = pl.program_id(0)

    @pl.when(j == 0)
    def _():
        for group in copies:
            for copy in group:
                copy.start()

    for r in range(N_DP):

        @pl.when(j == r)
        def _(r=r):
            for copy in copies[r]:
                copy.wait()
            at = r * CH
            for s, half, size in layout:
                if s == r:
                    offset = pl.multiple_of(piece_offset(info, half), size)
                    work(pl.ds(at, size), pl.ds(offset, size))
                    at += size


def chunk_now(info):
    return ((info[2] ^ pl.program_id(0)) + N_TP - info[0]) % N_TP


def out_hidden_body(layout, info, hidden, *refs):
    *w, out, held, sems = refs

    def work(place, window):
        for s in range(hidden.shape[0]):
            out[0, s, :, window] = dot_nn(hidden[s], held[:, place]).astype(bf16)

    lower = [a.at[pl.ds(CH, held.shape[0]), :] for a in w]
    with_chunk(layout, info, fetch_pieces(layout, [lower], [held], sems, 1), work)


def out_hidden(layout, info, hidden, w, deps=()):
    seqs, rows, units = hidden.shape
    return call(
        functools.partial(out_hidden_body, layout),
        "out_hidden",
        N_DP,
        info,
        (hidden, *w),
        [once(seqs, rows, units)] + [ANYWHERE] * len(w),
        shaped((N_DP, seqs, rows, CH)),
        spec((1, seqs, rows, CH), lambda j, *_: (j, 0, 0, 0)),
        2 * seqs * rows * D * units,
        [pltpu.VMEM((units, D), bf16), pltpu.SemaphoreType.DMA((len(w),))],
        deps=deps,
    )


def out_heads_body(layout, info, a0, a1, part, *refs):
    count = len(layout)
    w, outs = refs[:count], refs[count : count + N_TP]
    held, y, sems, out_sems = refs[count + N_TP :]
    j = pl.program_id(0)

    def work(place, window):
        for s, att in ((0, a0), (1, a1)):
            total = dot_nn(att[...], held[:, place]) + part[0, s, :, window].astype(f32)
            y[j, s, :, window] = total.astype(bf16)

    upper = [a.at[pl.ds(0, CH), :] for a in w]
    with_chunk(layout, info, fetch_pieces(layout, [upper], [held], sems, 1), work)
    for r in range(N_TP):

        @pl.when(chunk_now(info) == r)
        def _(r=r):
            pltpu.make_async_copy(y.at[j], outs[r], out_sems.at[r]).start()

    @pl.when(j == N_TP - 1)
    def _():
        for r in range(N_TP):
            pltpu.make_async_copy(y.at[r], outs[r], out_sems.at[r]).wait()


def out_heads(layout, info, att, parts, w, deps=()):
    _, seqs, rows, _ = parts.shape
    return call(
        functools.partial(out_heads_body, layout),
        "out_heads",
        N_TP,
        info,
        (*att, parts, *w),
        [once(rows, CH)] * 2
        + [spec((1, seqs, rows, CH), lambda j, *_: (j, 0, 0, 0))]
        + [ANYWHERE] * len(w),
        (shaped((seqs, rows, CH)),) * N_TP,
        [ANYWHERE] * N_TP,
        2 * seqs * rows * D * CH,
        [
            pltpu.VMEM((CH, D), bf16),
            pltpu.VMEM((N_TP, seqs, rows, CH), bf16),
            pltpu.SemaphoreType.DMA((len(w),)),
            pltpu.SemaphoreType.DMA((N_TP,)),
        ],
        deps=deps,
    )


def back_in_body(layout, info, x0, xa, xc, xb, dq, dkv, back, dup, gain, stats, *refs):
    count = len(layout)
    wq, wu = refs[:count], refs[count : 2 * count]
    *chunks, held_q, held_u, y, xs, row_sums, column_sums, both, sems = refs[2 * count :]
    j = pl.program_id(0)
    rows = dq.shape[0]

    @pl.when(j == 0)
    def _():
        both[...] = add_rounded(dkv[...], back[...])


    def work(place, window):
        part = dot_nt(dup[...], held_u[place, :])
        part = part + dot_nt(dq[...], held_q[place, :CH])
        part = part + dot_nt(both[0], held_q[place, CH : 2 * CH])
        y[:, window] = part + dot_nt(both[1], held_q[place, 2 * CH :])

    copies = fetch_pieces(layout, [wq, wu], [held_q, held_u], sems, 0)
    with_chunk(layout, info, copies, work)
    for r, part in enumerate((x0, xc, xb, xa)):

        @pl.when(chunk_now(info) == r)
        def _(r=r, part=part):
            chunks[r][:rows, :] = y[...].astype(bf16)
            xs[...] = part[...]

    total = y[...]
    turned = stats[...].T
    standard = (xs[...].astype(f32) - turned[:, 0:1]) * turned[:, 1:2]
    cross = total * standard
    weight = gain[...].astype(f32)

    @pl.when(j == 0)
    def _():
        row_sums[...] = jnp.zeros(row_sums.shape, f32)
        column_sums[...] = jnp.zeros(column_sums.shape, f32)

    both = jnp.concatenate(
        [jnp.sum(cross, axis=0, keepdims=True), jnp.sum(total, axis=0, keepdims=True)], axis=0
    )
    column_sums[chunk_now(info), 0:2, :] = both
    row_sums[:, 0:1] += jnp.sum(total * weight, axis=1, keepdims=True)
    row_sums[:, 1:2] += jnp.sum(cross * weight, axis=1, keepdims=True)

    @pl.when(j == N_TP - 1)
    def _():
        turned = row_sums[...].T[: TAIL // 2]
        for r, chunk in enumerate(chunks):
            chunk[rows:, :] = jnp.concatenate([turned, column_sums[r]], axis=0).astype(bf16)


def back_in(layout, info, s, parts, dq, dkv, back, dup, wq, wu, gain, stats, deps=()):
    _, rows, units = dup.shape
    return call(
        functools.partial(back_in_body, layout),
        "back_in",
        N_TP,
        info,
        (*parts, dq, dkv, back, dup, gain, stats, *wq, *wu),
        [one_of(s, rows, CH)] * 4
        + [
            whole(rows, CH),
            whole(2, rows, CH),
            whole(2, rows, CH),
            one_of(s, rows, units),
            spec((1, CH), lambda j, info: (0, info[2] ^ j)),
            one_of(s, 8, rows),
        ]
        + [ANYWHERE] * (2 * len(wq)),
        (shaped((rows + TAIL, CH)),) * N_TP,
        [whole(rows + TAIL, CH)] * N_TP,
        2 * rows * D * (3 * CH + units),
        [
            pltpu.VMEM((D, 3 * CH), bf16),
            pltpu.VMEM((D, units), bf16),
            pltpu.VMEM((rows, CH), f32),
            pltpu.VMEM((rows, CH), bf16),
            pltpu.VMEM((rows, 128), f32),
            pltpu.VMEM((N_TP, TAIL // 2, CH), f32),
            pltpu.VMEM((2, rows, CH), bf16),
            pltpu.SemaphoreType.DMA((2 * len(wq),)),
        ],
        deps=deps,
    )


KEPT = ((0, 0), (2, 1))
GIVEN = ((1, 0), (3, 1))


def grad_up_body(info, normed, dup, kept, given, sums):
    d = info[2]
    rights = (dup[0], dup[1])
    store_by_rows(d, normed, rights, kept, given)
    sums[...] = sum(jnp.sum(b.astype(f32), axis=0, keepdims=True) for b in rights)


def grad_up(info, normed, dup, deps=()):
    _, rows, units = dup.shape
    count = units // CH
    message = spec((2, 1, CH, CH), lambda j, *_: (0, j, 0, 0))
    return call(
        grad_up_body,
        "grad_up",
        count,
        info,
        (normed, dup),
        [whole(2, rows, D), spec((2, rows, CH), lambda j, *_: (0, 0, j))],
        (shaped((2, count, CH, CH)),) * 2 + (shaped((1, units), f32),),
        [message, message, spec((1, CH), lambda j, *_: (0, j))],
        4 * rows * D * units,
        deps=deps,
    )


def grad_down_body(offsets, group, info, hidden, *refs):
    parts = refs[: len(offsets)]
    kept, given, tiles, sems = refs[-4:]
    for k in range(group):
        n = pl.program_id(0) * group + k
        units = slice(CH * k, CH * (k + 1))
        for i, (part, offset) in enumerate(zip(parts, offsets)):
            y = dot_tn(hidden[0, :, units], part[0]) + dot_tn(hidden[1, :, units], part[1])
            tiles[n, i] = y.astype(bf16)
            r = ((info[0] + offset) % N_TP) ^ info[2]
            for odd, target in ((0, kept), (1, given)):

                @pl.when(r % 2 == odd)
                def _(i=i, n=n, r=r, target=target):
                    place = target.at[r // 2, n]
                    pltpu.make_async_copy(tiles.at[n, i], place, sems.at[n, i]).start()

    @pl.when(pl.program_id(0) == tiles.shape[0] // group - 1)
    def _():
        for m in range(tiles.shape[0]):
            for i in range(len(offsets)):
                pltpu.make_async_copy(tiles.at[m, i], kept.at[0, 0], sems.at[m, i]).wait()


def grad_down(info, hidden, parts, offsets, begun=(), deps=()):
    _, rows, units = hidden.shape
    count = units // CH
    group = 2 if len(parts) == 1 else 1
    at = 1 + len(parts)
    return call(
        functools.partial(grad_down_body, offsets, group),
        "grad_down",
        count // group,
        info,
        (hidden, *parts, *begun),
        [spec((2, rows, group * CH), lambda j, *_: (0, 0, j))]
        + [once(2, rows, CH)] * len(parts)
        + [ANYWHERE] * len(begun),
        (shaped((2, count, CH, CH)),) * 2,
        [ANYWHERE] * 2,
        4 * rows * CH * units * len(parts),
        [
            pltpu.VMEM((count, len(parts), CH, CH), bf16),
            pltpu.SemaphoreType.DMA((count, len(parts))),
        ],
        deps=deps,
        aliases=[(at + n, n) for n in range(len(begun))],
    )


def store_by_rows(d, lefts, rights, kept, given):
    for target, which in ((given, GIVEN), (kept, KEPT)):
        for r, at in which:
            window = columns(d ^ r)
            y = sum(dot_tn(lefts[s, :, window], b) for s, b in enumerate(rights))
            target[at, 0] = y.astype(bf16)


def grad_out_query_body(info, normed, ct, a0, a1, q0, q1, kept, given, sums):
    j = pl.program_id(0)
    out = dot_tn(a0[...], ct[0]) + dot_tn(a1[...], ct[1])
    query = dot_tn(normed[0], q0[...]) + dot_tn(normed[1], q1[...])

    def store(target):
        target[0, 0] = out.astype(bf16)
        target[0, 1] = query.astype(bf16)

    @pl.when(j < 2)
    def _():
        store(given)

    @pl.when(j >= 2)
    def _():
        store(kept)

    @pl.when(j == 0)
    def _():
        sums[...] = sum(jnp.sum(b[...].astype(f32), axis=0, keepdims=True) for b in (q0, q1))


def grad_out_query(info, normed, ct, att, dq, deps=()):
    rows = normed.shape[1]

    def of_step(j, info):
        return 0, 0, info[2] ^ jnp.where(j < 2, 2 * j + 1, 2 * j - 4)

    return call(
        grad_out_query_body,
        "grad_out_query",
        N_DP,
        info,
        (normed, ct, *att, *dq),
        [spec((2, rows, CH), of_step)] * 2 + [once(rows, CH)] * 4,
        (shaped((2, 2, CH, CH)),) * 2 + (shaped((1, CH), f32),),
        [
            spec((1, 2, CH, CH), lambda j, *_: (jnp.maximum(j - 2, 0), 0, 0, 0)),
            spec((1, 2, CH, CH), lambda j, *_: (jnp.minimum(j, 1), 0, 0, 0)),
            whole(1, CH),
        ],
        4 * rows * D * 2 * CH,
        deps=deps,
    )


def grad_key_value_body(info, normed, kv0, back0, kv1, back1, kept, given, sums):
    rights = (add_rounded(kv0[0], back0[0]), add_rounded(kv1[0], back1[0]))
    store_by_rows(info[2], normed, rights, kept, given)
    sums[0] = sum(jnp.sum(b.astype(f32), axis=0, keepdims=True) for b in rights)


def grad_key_value(info, normed, dkv, sent, deps=()):
    rows = normed.shape[1]
    message = spec((2, 1, CH, CH), lambda j, *_: (0, j, 0, 0))
    pair = spec((1, rows, CH), lambda j, *_: (j, 0, 0))
    return call(
        grad_key_value_body,
        "grad_key_value",
        2,
        info,
        (normed, dkv[0], sent[0], dkv[1], sent[1]),
        [whole(2, rows, D)] + [pair] * 4,
        (shaped((2, 2, CH, CH)),) * 2 + (shaped((2, 1, CH), f32),),
        [message, message, spec((1, 1, CH), lambda j, *_: (j, 0, 0))],
        4 * rows * D * 2 * CH,
        deps=deps,
    )


def combine_body(counts, info, *refs):
    ins, outs = refs[: sum(counts)], refs[sum(counts) :]
    at = 0
    for count, out in zip(counts, outs):
        terms = ins[at : at + count]
        at += count

        def add(terms=terms, out=out):
            out[...] = sum(a[...].astype(f32) for a in terms).astype(bf16)

        if len(out.shape) == 3:
            add()
        else:
            pl.when(pl.program_id(0) == 0)(add)


def combine(info, big, small, deps=()):
    steps = 2
    part = 2 * CH // steps
    ins, in_specs, outs, out_specs = [], [], [], []
    for job in big:
        for array, row in job:
            ins.append(array.reshape(-1, part, CH))
            in_specs.append(spec((1, part, CH), lambda j, _, at=row // part: (at + j, 0, 0)))
        outs.append(shaped((steps, part, CH)))
        out_specs.append(spec((1, part, CH), lambda j, _: (j, 0, 0)))
    for job in small:
        ins += job
        in_specs += [whole(*a.shape) for a in job]
        outs.append(shaped(job[0].shape))
        out_specs.append(whole(*job[0].shape))
    results = call(
        functools.partial(combine_body, [len(job) for job in (*big, *small)]),
        "combine",
        steps,
        info,
        ins,
        in_specs,
        outs,
        out_specs,
        0,
        deps=deps,
    )
    count = len(big)
    return [a.reshape(2, CH, CH) for a in results[:count]] + list(results[count:])


def finish_blocks_body(info, *refs):
    *sums, out = refs
    j = pl.program_id(0)
    for n in range(len(sums) // 2):
        here, there = sums[2 * n : 2 * n + 2]

        @pl.when((j >= 2 * n) & (j < 2 * n + 2))
        def _(here=here, there=there):
            out[...] = here[0].astype(f32) + there[0].astype(f32)


def finish_blocks(info, sums, axis, deps=()):
    count = len(sums)
    arrays = [a for pair in sums for a in pair]
    blocks = [
        spec((1, CH, CH), lambda j, _, n=n: (jnp.clip(j - 2 * n, 0, 1), 0, 0))
        for n in range(count)
        for _ in range(2)
    ]
    return call(
        finish_blocks_body,
        "finish_blocks",
        2 * count,
        info,
        arrays,
        blocks,
        shaped((2 * count * CH, CH) if axis == 0 else (CH, 2 * count * CH), f32),
        spec((CH, CH), lambda j, _: (j, 0) if axis == 0 else (0, j)),
        0,
        deps=deps,
    )


def finish_pair_body(info, here, there, *outs):
    for n, out in enumerate(outs):
        out[...] = here[n].astype(f32) + there[n].astype(f32)


def finish_pair(info, here, there, deps=()):
    part = CH // 2
    return call(
        finish_pair_body,
        "finish_pair",
        2,
        info,
        (here, there),
        [spec((2, part, CH), lambda j, _: (0, j, 0))] * 2,
        (shaped((CH, CH), f32),) * 2,
        [spec((part, CH), lambda j, _: (j, 0))] * 2,
        0,
        deps=deps,
    )


def finish_last_body(info, own, back, near, x, shift, here, there, out, first, second):
    total = own[...].astype(f32) + back[...].astype(f32) + near[...].astype(f32)
    out[...] = (x[...].astype(f32) + total + shift[...].astype(f32)).astype(bf16)
    finish_pair_body(info, here, there, first, second)


def finish_last(info, shares, x, shift, here, there, deps=()):
    seqs, rows, _ = x.shape
    both = spec((seqs, rows // 2, CH), lambda j, _: (0, j, 0))
    pair = spec((2, CH // 2, CH), lambda j, _: (0, j, 0))
    half = spec((CH // 2, CH), lambda j, _: (j, 0))
    return call(
        finish_last_body,
        "finish_last",
        2,
        info,
        (*shares, x, shift, here, there),
        [both] * 4 + [whole(1, CH), pair, pair],
        (shaped(x.shape), shaped((CH, CH), f32), shaped((CH, CH), f32)),
        [both, half, half],
        0,
        deps=deps,
    )


def finish_in_body(info, *refs):
    shares, tails, wide = refs[:6], refs[6:12], refs[12:18]
    x, ct, stats, gain, out, sums = refs[18:]
    weight = gain[...].astype(f32)
    for s in range(2):
        at = slice(3 * s, 3 * s + 3)
        total = sum(a[...].astype(f32) for a in shares[at])
        tail = sum(a[...].astype(f32) for a in tails[at])
        column = jnp.concatenate([tail[:8], stats[s]], axis=0).T
        plain, cross = column[:, 0:1], column[:, 1:2]
        average, root = column[:, 8:9], column[:, 9:10]
        standard = (x[s].astype(f32) - average) * root
        scaled = total * weight - plain * (1.0 / D) - standard * (cross * (1.0 / D))
        out[s] = ct[s].astype(f32) + root * scaled

    @pl.when(pl.program_id(0) == 0)
    def _():
        sums[...] = sum(a[...].astype(f32)[8:] for a in wide)


def finish_in(info, shares, x, ct, stats, gain, deps=()):
    seqs, rows, _ = x.shape
    part = rows // 2
    both = spec((seqs, part, CH), lambda j, _: (0, j, 0))
    last = rows // TAIL
    return call(
        finish_in_body,
        "finish_in",
        2,
        info,
        (*shares, *shares, *shares, x, ct, stats, gain),
        [spec((part, CH), lambda j, _: (j, 0))] * 6
        + [spec((TAIL, part), lambda j, _: (last, j))] * 6
        + [spec((TAIL, CH), lambda j, _: (last, 0))] * 6
        + [both, both, spec((seqs, 8, part), lambda j, _: (0, 0, j)), whole(1, CH)],
        (shaped(x.shape, f32), shaped((TAIL // 2, CH), f32)),
        [both, whole(TAIL // 2, CH)],
        0,
        deps=deps,
    )


SMALL = 16


def small_table_body(info, query, pair, up, out, last, table):
    table[...] = jnp.zeros(table.shape, f32)
    table[0:1, :] = query[...]
    table[1:2, :] = pair[0]
    table[2:3, :] = pair[1]
    for n in range(4):
        table[3 + n : 4 + n, :] = up[:, CH * n : CH * (n + 1)]
    table[7:8, :] = out[...]
    table[8:10, :] = last[0:2, :]


def small_table(info, arrays):
    return call(
        small_table_body,
        "small_table",
        1,
        info,
        arrays,
        [whole(*a.shape) for a in arrays],
        shaped((SMALL, CH), f32),
        whole(SMALL, CH),
        0,
    )


def ring(array, step):
    return lax.ppermute(array, "tp", [(i, (i + step) % N_TP) for i in range(N_TP)])


class Gather:
    def __init__(self, own):
        self.own = own

    def forth(self, clock):
        self.own = clock.go(self.own)
        self.behind = ring(self.own, 1)

    def back(self):
        self.ahead = ring(self.own, -1)

    def sides(self, clock):
        self.forth(clock)
        self.ahead = ring(self.own, -1)

    def onward(self, clock):
        self.behind = clock.go(self.behind)
        self.far = ring(self.behind, 1)
        self.parts = (self.own, self.behind, self.ahead, self.far)


class Scatter:
    def __init__(self, chunks):
        self.own, self.share, self.first, self.given = chunks

    def forward(self, clock):
        self.far = ring(clock.go(self.first), 1)

    def backward(self, clock):
        self.back = ring(clock.go(self.given), -1)

    def both(self):
        return [self.share, self.far]

    def onward(self, both):
        self.near = ring(both, 1)

    def shares(self):
        return self.own, self.back, self.near


class Reduction:
    def __init__(self, kept, given, clock, two):
        self.kept, self.two = kept, two
        self.got = swap(clock.go(given), "dp", 1, N_DP)
        self.moved, self.here, self.there = {}, {}, {}

    def across(self, n):
        row = (self.kept.shape[1] + 2 * n) * CH
        return [(self.kept, row), (self.got, row)]

    def here_sum(self, n):
        row = 2 * n * CH
        return [(self.kept, row), (self.got, row), (self.moved[n], 0)]

    def over_x(self, n, across):
        self.moved[n] = swap(across, "dp", 2, N_DP)

    def over_y(self, n, here):
        self.here[n] = here
        self.there[n] = swap(here, "ctx", 1, 2) if self.two else lax.psum(here, "ctx")

    def sums(self, n):
        if self.two:
            return self.here[n], self.there[n]
        return self.there[n], jnp.zeros_like(self.there[n])


def body(
    block_in,
    doc_starts,
    query_weight,
    key_weight,
    value_weight,
    output_weight,
    up_weight,
    down_weight,
    query_bias,
    key_bias,
    value_bias,
    up_bias,
    output_bias,
    norm_gain,
    norm_shift,
    cotangent,
):
    seqs, rows, _ = block_in.shape
    d, c, t = lax.axis_index("dp"), lax.axis_index("ctx"), lax.axis_index("tp")
    n_ctx = lax.axis_size("ctx")
    two = n_ctx == 2
    info = jnp.stack([t, c, d]).astype(jnp.int32)

    clock = Clock()

    x = Gather(block_in)
    x.forth(clock)
    small = jnp.concatenate(
        [query_bias, key_bias, value_bias, up_bias, output_bias, norm_gain, norm_shift]
    )
    size = small.size
    near = swap(small, "dp", 1, N_DP)
    flip = (d & 1) == 1
    pair = jnp.concatenate([jnp.where(flip, near, small), jnp.where(flip, small, near)])
    across = swap(pair, "dp", 2, N_DP)
    flip = (d & 2) == 2
    small_here = jnp.concatenate([jnp.where(flip, across, pair), jnp.where(flip, pair, across)])
    small_here = small_here.reshape(N_DP, size)

    def small_of(first, length):
        return small_here[:, first : first + length].reshape(1, -1)

    share = query_bias.size
    share_units = up_bias.size
    qkv_bias = jnp.concatenate([small_of(n * share, share) for n in range(3)], axis=1)
    up_shift = small_of(3 * share, share_units)
    output_shift = small_of(3 * share + share_units, share)
    gain_here = small_of(4 * share + share_units, share)
    shift_here = small_of(5 * share + share_units, share)
    both = jnp.concatenate([gain_here, shift_here], axis=0)
    others = [ring(both, -r) for r in range(1, N_TP)]
    wq_shard = jnp.concatenate([query_weight, key_weight, value_weight], axis=1)
    shards_q = Shards(tie(wq_shard, across), 0, d, c, two)
    shards_q.over_x(clock)
    shards_u = Shards(up_weight, 0, d, c, two, made=False)
    wo_shard = jnp.concatenate([output_weight, down_weight], axis=0)
    shards_o = Shards(wo_shard, 1, d, c, two)
    clock.sync(x.behind, shards_q.first, *others, shards_u.part)

    x.back()
    shards_q.over_y(clock)
    shards_u.over_x(clock)
    shards_q.near_core(clock)
    circle = jnp.concatenate([both, *others] * 2, axis=1)
    gain_shift = lax.dynamic_slice_in_dim(circle, (N_TP - t) % N_TP * CH, D, 1)
    gain, shift = gain_shift[0:1], gain_shift[1:2]

    here = c * rows + jnp.arange(rows, dtype=jnp.int32)
    tables, opening = rotary_tables(doc_starts, here)
    blocks = 1 if two else n_ctx
    before, _ = rotary_tables(doc_starts, jnp.arange(blocks * rows, dtype=jnp.int32))
    before = [a.reshape(seqs, blocks, rows, 128) for a in before]

    clock.sync(shards_q.second, shards_u.first, x.ahead, shards_q.near, shards_o.part)
    shards_u.near_core(clock)

    x.onward(clock)
    shards_u.over_y(clock)
    shards_o.over_x(clock)
    shards_q.far_core(clock)
    clock.sync(
        x.far,
        *shards_q.far_near,
        shards_u.second,
        shards_o.first,
        *before,
    )

    def send_keys(s):
        kv[s] = clock.go(kv[s])
        if two:
            kvp[s] = swap(kv[s], "ctx", 1, 2)[None]
        else:
            kvp[s] = lax.all_gather(kv[s], "ctx", axis=0, tiled=False)

    def attention_step(s):
        return attention(
            info,
            s,
            opening[:, None],
            q,
            kv[s],
            kvp[s],
            datt,
            tables,
            before,
            deps=clock.marks,
        )

    def returned(sent):
        if two:
            return swap(clock.go(sent[0]), "ctx", 1, 2)
        return lax.psum_scatter(clock.go(sent), "ctx", scatter_dimension=0, tiled=False)

    def back_in_step(s):
        return back_in(
            layout,
            info,
            s,
            x.parts,
            dq[s],
            dkv[s],
            sent[s],
            dup,
            shards_q.pieces,
            shards_u.pieces,
            gain,
            stats,
            deps=clock.marks,
        )

    layout = layout_of(two)
    kvp, att, dq, dkv, sent = ([None] * seqs for _ in range(5))

    shards_o.over_y(clock)
    shards_u.far_core(clock)
    ct = Gather(cotangent)
    ct.behind, ct.ahead = ring(ct.own, 1), ring(ct.own, -1)
    normed, stats, q, *kv = norm_qkv(
        layout, info, x.parts, gain, shift, shards_q.pieces, qkv_bias, tables, deps=clock.marks
    )
    clock.sync(normed, *shards_u.far_near, shards_u.near, ct.behind, shards_o.second)

    shards_o.near_core(clock)
    shards_o.far_core(clock)
    ct.onward(clock)
    hidden, slope = mlp_up(layout, info, normed, shards_u.pieces, up_shift, deps=clock.marks)
    clock.sync(hidden, shards_o.near, *shards_o.far_near)

    send_keys(0)
    send_keys(1)
    out_parts = out_hidden(layout, info, hidden, shards_o.pieces, deps=clock.marks)
    clock.sync(out_parts, ct.ahead)
    down_begun = grad_down(
        info, hidden, (ct.own, ct.behind, ct.ahead), (0, 3, 1), deps=clock.marks
    )
    clock.sync(down_begun[0], ct.far)

    cf, out_bias_sum, datt, dup = back_out(
        layout, info, ct.parts, shards_o.pieces, slope, deps=clock.marks
    )
    clock.sync(datt, kvp[0])

    def added(big, small=()):
        return combine(info, big, list(small), deps=clock.marks)

    up_kept, up_given, up_sum = grad_up(info, normed, dup, deps=clock.marks)
    clock.sync(up_kept, kvp[1])
    up = Reduction(up_kept, up_given, clock, two)
    att[0], dq[0], dkv[0], sent[0] = attention_step(0)
    clock.sync(att[0], up.got)

    sent[0] = returned(sent[0])
    across, across_1 = added([up.across(0), up.across(1)])
    up.over_x(0, across)
    clock.sync(across)
    down_kept, down_given = grad_down(
        info, hidden, (ct.far,), (2,), down_begun, deps=clock.marks
    )
    clock.sync(down_kept, *clock.marks)
    att[1], dq[1], dkv[1], sent[1] = attention_step(1)
    clock.sync(att[1], sent[0], up.moved[0])

    sent[1] = returned(sent[1])
    up.over_x(1, clock.go(across_1))
    down = Reduction(down_kept, down_given, clock, two)
    out = Scatter(out_heads(layout, info, att, out_parts, shards_o.pieces, deps=clock.marks))
    clock.sync(out.own, *clock.marks)
    head_kept, head_given, query_sum = grad_out_query(
        info, normed, cf, att, dq, deps=clock.marks
    )
    clock.sync(head_kept, down.got)
    across, across_1, here = added([down.across(0), down.across(1), up.here_sum(0)])
    clock.sync(across, sent[1])

    up.over_y(0, clock.go(here))
    out.forward(clock)
    clock.sync(up.moved[1])
    down.over_x(0, clock.go(across))
    head = Reduction(head_kept, head_given, clock, two)
    (here,) = added([up.here_sum(1)])
    clock.sync(here)
    back_0 = Scatter(back_in_step(0))
    clock.sync(back_0.own)
    clock.sync(up.there[0])

    up.over_y(1, clock.go(here))
    clock.sync(out.far)
    back_0.forward(clock)
    back_0.backward(clock)
    clock.sync(down.moved[0], head.got)
    down.over_x(1, clock.go(across_1))
    here, across, out_both = added([down.here_sum(0), head.across(0)], [out.both()])
    clock.sync(here)
    pair_kept, pair_given, pair_sum = grad_key_value(info, normed, dkv, sent, deps=clock.marks)
    clock.sync(pair_kept)
    clock.sync(up.there[1])

    down.over_y(0, clock.go(here))
    clock.sync(back_0.far, back_0.back)
    out.backward(clock)
    clock.sync(down.moved[1])
    head.over_x(0, clock.go(across))
    pair = Reduction(pair_kept, pair_given, clock, two)
    here, both_0 = added([down.here_sum(1)], [back_0.both()])
    clock.sync(here)
    back_1 = Scatter(back_in_step(1))
    clock.sync(back_1.own)
    clock.sync(down.there[0])

    down.over_y(1, clock.go(here))
    clock.sync(out.back)
    back_1.forward(clock)
    back_1.backward(clock)
    clock.sync(head.moved[0], pair.got)
    (across,) = added([pair.across(0)])
    pair.over_x(0, across)
    clock.sync(across)
    (here,) = added([head.here_sum(0)])
    clock.sync(here)
    up_wg = finish_blocks(info, [up.sums(0), up.sums(1)], 1, deps=clock.marks)
    clock.sync(up_wg)
    clock.sync(down.there[1])

    head.over_y(0, clock.go(here))
    back_0.onward(clock.go(both_0))
    clock.sync(back_1.far, back_1.back)
    (both_1,) = added([], [back_1.both()])
    back_1.onward(both_1)
    clock.sync(pair.moved[0])
    (here,) = added([pair.here_sum(0)])
    clock.sync(here, back_0.near)
    down_wg = finish_blocks(info, [down.sums(0), down.sums(1)], 0, deps=clock.marks)
    clock.sync(down_wg)
    clock.sync(head.there[0])

    pair.over_y(0, clock.go(here))
    clock.sync(back_1.near)
    out.onward(clock.go(out_both))
    in_grad, last = finish_in(
        info,
        (*back_0.shares(), *back_1.shares()),
        block_in,
        cotangent,
        stats,
        gain_here,
        deps=clock.marks,
    )
    clock.sync(in_grad)
    table = small_table(info, (query_sum, pair_sum, up_sum, out_bias_sum, last))
    output_wg, query_wg = finish_pair(info, *head.sums(0), deps=clock.marks)
    table = table + swap(table, "dp", 1, N_DP)
    table = table + swap(table, "dp", 2, N_DP)
    table = table + swap(table, "ctx", 1, 2) if two else lax.psum(table, "ctx")
    block_out, key_wg, value_wg = finish_last(
        info, out.shares(), block_in, output_shift, *pair.sums(0)
    )

    share = CH // N_DP
    mine = lax.dynamic_slice_in_dim(table, d * share, share, 1)
    query_bg, key_bg, value_bg = mine[0], mine[1], mine[2]
    output_bg, gain_g, shift_g = mine[7], mine[8], mine[9]
    up_bg = lax.dynamic_slice_in_dim(table, 3 + d, 1, 0).reshape(-1)
    return (
        block_out,
        in_grad,
        query_wg,
        key_wg,
        value_wg,
        output_wg,
        up_wg,
        down_wg,
        query_bg,
        key_bg,
        value_bg,
        up_bg,
        output_bg,
        gain_g,
        shift_g,
    )


def solution(mesh):
    return jax.shard_map(
        body,
        mesh=mesh,
        in_specs=(
            P("dp", "ctx", "tp"),
            P("dp", None),
            P("dp", "tp"),
            P("dp", "tp"),
            P("dp", "tp"),
            P("tp", "dp"),
            P("dp", "tp"),
            P("tp", "dp"),
        )
        + (P(("tp", "dp")),) * 7
        + (P("dp", "ctx", "tp"),),
        out_specs=(
            P("dp", "ctx", "tp"),
            P("dp", "ctx", "tp"),
            P("dp", "tp"),
            P("dp", "tp"),
            P("dp", "tp"),
            P("tp", "dp"),
            P("dp", "tp"),
            P("tp", "dp"),
        )
        + (P(("tp", "dp")),) * 7,
        check_vma=False,
    )
```
